32 devices in a mesh: blk: 8 (over z, x), head: 4 (over y, core).
Axes of the slice: x: 2, y: 2, z: 4, core: 2. Of those that a mesh axis runs over, the one named last changes fastest.
Arguments:
- hidden_in: bfloat16 [4096, 768], P(('blk', 'head')), may hold values from -6 to 6
- out_grad: bfloat16 [4096, 768], P(('blk', 'head')), may hold values from -6 to 6
- segment_ids: int32 [4096], replicated, may hold values from 0 to 4, as said below
- alibi_slopes: float32 [12], replicated, may hold values from 0.00012207031 to 0.015625
- qkv_weight: bfloat16 [2, 768, 2304], P(None, ('blk', 'head')), may hold values from -0.21875 to 0.21875
- out_weight: bfloat16 [2, 768, 768], P(None, ('blk', 'head')), may hold values from -0.875 to 0.875
- gate_up_weight: bfloat16 [2, 768, 6144], P(None, ('blk', 'head')), may hold values from -0.21875 to 0.21875
- down_weight: bfloat16 [2, 3072, 768], P(None, ('blk', 'head')), may hold values from -0.109375 to 0.109375
- gains: bfloat16 [2, 2, 768], P(None, None, ('blk', 'head')), may hold values from 0.25 to 1.75
- biases: bfloat16 [2, 6, 768], P(None, None, ('blk', 'head')), may hold values from -3 to 3
Outputs:
- output: bfloat16 [4096, 768], P(('blk', 'head'))
- input_grad: float32 [4096, 768], P(('blk', 'head'))
- qkv_weight_grad: float32 [2, 768, 2304], P(None, ('blk', 'head'))
- out_weight_grad: float32 [2, 768, 768], P(None, ('blk', 'head'))
- gate_up_weight_grad: float32 [2, 768, 6144], P(None, ('blk', 'head'))
- down_weight_grad: float32 [2, 3072, 768], P(None, ('blk', 'head'))
- gains_grad: float32 [2, 2, 768], P(None, None, ('blk', 'head'))
- biases_grad: float32 [2, 6, 768], P(None, None, ('blk', 'head'))
The draws below stay inside these ranges and needn't reach their ends.
Inputs may be any that keep to these rules, and one draw needn't show every extreme that they name: `segment_ids`: segment numbers never fall along the tokens and all five documents occur. Document 1 starts within the first 512 tokens and document 2 starts within the last 512.
All inputs are finite; a program needn't handle non-finite values.
Results may differ from the reference program's by a relative error of at most 0.039.
Values may be sent and summed in bfloat16 or wider, within the bound.
A program may use at most 256 MiB of HBM per device.

```python
import math
import jax
import jax.numpy as jnp
from jax import lax

D = 768
H = 12
FF = 3072
HS = 64
L = 2
BLOCK_TOKENS = 512
TOKENS = 4096


def draw_segment_ids(key, part):
    key = jax.random.fold_in(key, 11)
    key_list = jax.random.split(key, 4)
    left_end = jax.random.randint(key_list[0], (), BLOCK_TOKENS // 4, BLOCK_TOKENS)
    right_len = jax.random.randint(key_list[1], (), BLOCK_TOKENS // 2, BLOCK_TOKENS)
    right_start = TOKENS - right_len
    third_cut = jax.random.randint(key_list[2], (), right_start + 1, TOKENS - 1)
    fourth_cut = jax.random.randint(key_list[3], (), third_cut + 1, TOKENS)
    position = jnp.arange(TOKENS, dtype=jnp.int32)
    segment = (position >= left_end).astype(jnp.int32) + (position >= right_start).astype(jnp.int32)
    segment = segment + (position >= third_cut).astype(jnp.int32) + (position >= fourth_cut).astype(jnp.int32)
    return segment


def shard_levels(stream_key, extent, cuts, low, high):
    loudness = 1.0
    for dim, parts in cuts:
        heights = jax.random.uniform(jax.random.fold_in(jax.random.fold_in(stream_key, 6), dim), (parts,), jnp.float32, low / len(cuts), high / len(cuts))
        loudness = loudness * jnp.repeat(jnp.exp(heights), extent[dim] // parts).reshape((-1,) + (1,) * (len(extent) - 1 - dim))
    return loudness


def gaussian(stream_key, shape, spread, reach, cuts=(), held_as=jnp.bfloat16):
    values = spread * jax.random.normal(stream_key, shape, jnp.float32)
    if cuts:
        values = values * shard_levels(stream_key, shape, cuts, -0.22, 0.18)
    return jnp.clip(values, -reach, reach).astype(held_as)


def setup_inputs(seed: int = 0) -> dict:
    splits = jax.random.split(jax.random.key(seed), 11)
    hidden_in = gaussian(splits[0], (TOKENS, D), 1.0, 6.0, ((0, 32),))
    out_grad = gaussian(splits[1], (TOKENS, D), 1.0, 6.0, ((0, 32),))
    segment_ids = draw_segment_ids(jax.random.fold_in(splits[10], 71), 0)
    alibi_slopes = jnp.clip(jnp.exp(jax.random.uniform(splits[3], (H,), jnp.float32, math.log(0.00012207031), math.log(0.015625))), 0.00012207031, 0.015625)
    qkv_weight = gaussian(splits[4], (L, D, 3 * D), D ** -0.5, 0.21875, ((1, 32),))
    out_weight = gaussian(splits[5], (L, D, D), (D // 16) ** -0.5, 0.875, ((1, 32),))
    gate_up_weight = gaussian(splits[6], (L, D, 2 * FF), D ** -0.5, 0.21875, ((1, 32),))
    down_weight = gaussian(splits[7], (L, FF, D), FF ** -0.5, 0.109375, ((1, 32),))
    gains = jnp.clip(1.0 + 0.15 * jax.random.normal(splits[8], (L, 2, D), jnp.float32), 0.25, 1.75).astype(jnp.bfloat16)
    biases = gaussian(splits[9], (L, 6, D), 0.5, 3.0, ((2, 32),))
    return {"hidden_in": hidden_in, "out_grad": out_grad, "segment_ids": segment_ids, "alibi_slopes": alibi_slopes, "qkv_weight": qkv_weight, "out_weight": out_weight, "gate_up_weight": gate_up_weight, "down_weight": down_weight, "gains": gains, "biases": biases}


@jax.custom_vjp
def low(v):
    return lax.optimization_barrier(v.astype(jnp.bfloat16)).astype(jnp.float32)

@jax.custom_vjp
def low_back(v):
    return v

def low_keep(v):
    return (low(v), None)

def low_pass(kept, grad):
    return (grad,)

def back_keep(v):
    return (v, None)

def back_low(kept, grad):
    return (low(grad),)
low.defvjp(low_keep, low_pass)
low_back.defvjp(back_keep, back_low)
epsilon = 1e-06
highest = lax.Precision.HIGHEST
masked_out = -1e+30

def layer_norm(hidden_state, ln_gain, ln_shift):
    row_mean = lax.optimization_barrier(jnp.mean(hidden_state, axis=-1, keepdims=True))
    centred = hidden_state - row_mean
    row_var = lax.optimization_barrier(jnp.mean(centred * centred, axis=-1, keepdims=True))
    return centred * lax.rsqrt(row_var + epsilon) * ln_gain + ln_shift

def attention(queries, key_rows, value_rows, segment_ids, slopes):
    block_count = TOKENS // BLOCK_TOKENS
    positions = jnp.arange(TOKENS, dtype=jnp.int32)

    def one_block(block_number):
        first_row = block_number * BLOCK_TOKENS
        query_block = lax.dynamic_slice_in_dim(queries, first_row, BLOCK_TOKENS, 0)
        query_seg = lax.dynamic_slice_in_dim(segment_ids, first_row, BLOCK_TOKENS, 0)
        query_pos = first_row + jnp.arange(BLOCK_TOKENS, dtype=jnp.int32)
        distance = jnp.abs(query_pos[:, None] - positions[None, :]).astype(jnp.float32)
        scores = jnp.einsum('qhd,khd->hqk', query_block, key_rows, precision=highest) * HS ** (-0.5)
        scores = scores - slopes[:, None, None] * distance[None]
        scores = low_back(scores)
        key_mask = (query_seg[:, None] == segment_ids[None, :])[None]
        masked = jnp.where(key_mask, scores, masked_out)
        row_top = lax.optimization_barrier(jnp.max(masked, axis=-1, keepdims=True))
        exponent = jnp.where(key_mask, jnp.exp(masked - row_top), 0.0)
        weights = exponent / lax.optimization_barrier(jnp.sum(exponent, axis=-1, keepdims=True))
        return jnp.einsum('hqk,khd->qhd', low(weights), value_rows, precision=highest)
    blocks = lax.map(jax.checkpoint(one_block), jnp.arange(block_count, dtype=jnp.int32))
    return blocks.reshape(TOKENS, H, HS)

def encoder_layer(hidden_state, qkv_w, out_w, gate_up_w, down_w, gain_rows, bias_rows, segment_ids, slopes):
    inputs = low(hidden_state)
    zero_bias = jnp.zeros((D,), jnp.float32)
    projected = jnp.dot(inputs, qkv_w, precision=highest) + jnp.concatenate([bias_rows[0], zero_bias, bias_rows[1]])
    projected = low(low_back(projected))
    queries = projected[:, :D].reshape(TOKENS, H, HS)
    key_rows = projected[:, D:2 * D].reshape(TOKENS, H, HS)
    value_rows = projected[:, 2 * D:].reshape(TOKENS, H, HS)
    context = attention(queries, key_rows, value_rows, segment_ids, slopes).reshape(TOKENS, D)
    context = low(low_back(context))
    branch = low_back(jnp.dot(context, out_w, precision=highest) + bias_rows[2])
    normed = layer_norm(hidden_state + branch, gain_rows[0], bias_rows[3])
    mixed_proj = low_back(jnp.dot(low(normed), gate_up_w, precision=highest))
    hidden_units = low(jax.nn.gelu(mixed_proj[:, :FF], approximate=False) * mixed_proj[:, FF:])
    feed_out = low_back(jnp.dot(hidden_units, down_w, precision=highest) + bias_rows[4])
    return layer_norm(normed + feed_out, gain_rows[1], bias_rows[5])

def reference(hidden_in, out_grad, segment_ids, alibi_slopes, qkv_weight, out_weight, gate_up_weight, down_weight, gains, biases):

    def forward(hidden_state, qkv_all, out_all, gate_up_all, down_all, gain_all, bias_all):
        for layer_number in range(L):
            hidden_state = encoder_layer(hidden_state, qkv_all[layer_number], out_all[layer_number], gate_up_all[layer_number], down_all[layer_number], gain_all[layer_number], bias_all[layer_number], segment_ids, alibi_slopes)
        return hidden_state
    primals = (hidden_in.astype(jnp.float32), qkv_weight.astype(jnp.float32), out_weight.astype(jnp.float32), gate_up_weight.astype(jnp.float32), down_weight.astype(jnp.float32), gains.astype(jnp.float32), biases.astype(jnp.float32))
    result, pullback = jax.vjp(forward, *primals)
    grads = pullback(out_grad.astype(jnp.float32))
    return (result.astype(jnp.bfloat16), grads[0], grads[1], grads[2], grads[3], grads[4], grads[5], grads[6])
```

```python
import functools
import jax
import jax.numpy as jnp
from jax import lax
from jax.experimental import pallas as pl
from jax.experimental.pallas import tpu as pltpu
from jax.sharding import PartitionSpec as P

MESH = pl.DeviceIdType.MESH
BF = jnp.bfloat16
F32 = jnp.float32
NT = (((1,), (1,)), ((), ()))
NN = (((1,), (0,)), ((), ()))
TN = (((0,), (0,)), ((), ()))


def dot(a, b, dims):
    return lax.dot_general(a, b, dims, preferred_element_type=F32)


def in_half(half, rows):
    lane = lax.broadcasted_iota(jnp.int32, (rows, 128), 1)
    return (lane >= 64) if half else (lane < 64)


def ones_half(half, rows, count):
    lane = lax.broadcasted_iota(jnp.int32, (rows, 128), 1)
    first = 0 if half else 64
    return jnp.where((lane >= first) & (lane < first + count), 1.0, 0.0).astype(BF)


def k_operand(kv_ref, kaug_ref, b, h):
    col = 128 * (h // 2)
    return jnp.where(in_half(h % 2, kv_ref.shape[1]), kv_ref[b, :, col : col + 128], kaug_ref[h, b])


def v_operand(kv_ref, b, h):
    col, half = 128 * ((3 + h) // 2), (3 + h) % 2
    rows = kv_ref.shape[1]
    return jnp.where(in_half(half, rows), kv_ref[b, :, col : col + 128], ones_half(half, rows, 3))


def fwd_block(side, diag, b, q_ref, kv_ref, kaug_ref, m_ref, acc_ref):
    for h in range(3):
        k = k_operand(kv_ref, kaug_ref, b, h)
        if diag:
            s = jnp.minimum(dot(q_ref[0, h], k, NT), dot(q_ref[1, h], k, NT))
        else:
            s = dot(q_ref[side, h], k, NT)
        m_old = m_ref[h]
        m_new = jnp.maximum(m_old, jnp.max(s, axis=1, keepdims=True))
        p = jnp.exp(s - m_new[:, :1]).astype(BF)
        acc_ref[h] = acc_ref[h] * jnp.exp(m_old - m_new) + dot(p, v_operand(kv_ref, b, h), NN)
        m_ref[h] = m_new


def fwd_finish(m_ref, acc_ref, ctx_ref, ctxf_ref, lse_ref):
    for h in range(3):
        half = (3 + h) % 2
        first = 0 if half else 64
        acc = acc_ref[h]
        total = acc[:, first : first + 1]
        ctx = acc[:, 64 * half : 64 * half + 64] / total
        ctxf_ref[:, 64 * h : 64 * h + 64] = ctx
        ctx_ref[:, 64 * h : 64 * h + 64] = ctx.astype(BF)
        lse_ref[h] = m_ref[h] + jnp.log(total)


def attn_fwd_kernel(nz, comm, q_ref, own_ref, kaug_ref, ctx_ref, ctxf_ref, lse_ref, kv_ref,
                    m_ref, acc_ref, zsend, xsend, recv):
    blk, head = lax.axis_index("blk"), lax.axis_index("head")
    z, x = blk // 2, blk % 2
    other = 1 - x

    def device(zz, xx):
        return (zz * 2 + xx, head)

    if comm:
        barrier = pltpu.get_barrier_semaphore()
        pl.semaphore_signal(barrier, inc=1, device_id=device(z, other), device_id_type=MESH)

        @pl.when(z > 0)
        def _():
            pl.semaphore_signal(barrier, inc=1, device_id=device(z - 1, x), device_id_type=MESH)

        @pl.when(z < nz - 1)
        def _():
            pl.semaphore_signal(barrier, inc=1, device_id=device(z + 1, x), device_id_type=MESH)

        kv_ref[blk] = own_ref[...]
        ends = (z == 0).astype(jnp.int32) + (z == nz - 1).astype(jnp.int32)
        pl.semaphore_wait(barrier, 3 - ends)

    def to_right(b):
        return pltpu.make_async_remote_copy(
            src_ref=kv_ref.at[b], dst_ref=kv_ref.at[b], send_sem=zsend.at[b], recv_sem=recv.at[b],
            device_id=device(z + 1, x), device_id_type=MESH)

    def to_left(b):
        return pltpu.make_async_remote_copy(
            src_ref=kv_ref.at[b], dst_ref=kv_ref.at[b], send_sem=zsend.at[nz * 2 + b], recv_sem=recv.at[b],
            device_id=device(z - 1, x), device_id_type=MESH)

    def to_other(b):
        return pltpu.make_async_remote_copy(
            src_ref=kv_ref.at[b], dst_ref=kv_ref.at[b], send_sem=xsend.at[b], recv_sem=recv.at[b],
            device_id=device(z, other), device_id_type=MESH)

    def arrived(b):
        if comm:
            to_other(b).wait_recv()

    if comm:
        @pl.when(z < nz - 1)
        def _():
            to_right(blk).start()

        @pl.when(z > 0)
        def _():
            to_left(blk).start()

        to_other(blk).start()

    def compute(b, diag=False):
        side = (b > blk).astype(jnp.int32)
        fwd_block(side, diag, b, q_ref, kv_ref, kaug_ref, m_ref, acc_ref)

    m_ref[...] = jnp.full(m_ref.shape, -1e30, F32)
    acc_ref[...] = jnp.zeros(acc_ref.shape, F32)
    compute(blk, True)

    def step(d, carry):
        zl, zr = z - d, z + d

        @pl.when(zl >= 0)
        def _():
            b = zl * 2 + x
            if comm:
                arrived(b)
                to_other(b).start()

                @pl.when(z < nz - 1)
                def _():
                    to_right(b).start()

        @pl.when(zr < nz)
        def _():
            b = zr * 2 + x
            if comm:
                arrived(b)
                to_other(b).start()

                @pl.when(z > 0)
                def _():
                    to_left(b).start()

        def visit(i, c):
            zz = jnp.where(i % 2 == 0, z - d + i // 2, z + d - i // 2)
            xx = jnp.where(i < 2, x, other)
            seen = (zz >= 0) & (zz < nz) & ((i != 3) | (d > 1))

            @pl.when(seen)
            def _():
                b = zz * 2 + xx

                @pl.when(i >= 2)
                def _():
                    arrived(b)
                compute(b)
            return c
        lax.fori_loop(0, 4, visit, 0)
        return carry

    lax.fori_loop(1, nz, step, 0)

    def last(i, c):
        zz = jnp.where(i == 0, z - (nz - 1), z + (nz - 1))

        @pl.when((zz >= 0) & (zz < nz))
        def _():
            b = zz * 2 + other
            arrived(b)
            compute(b)
        return c
    lax.fori_loop(0, 2, last, 0)
    fwd_finish(m_ref, acc_ref, ctx_ref, ctxf_ref, lse_ref)

    if comm:
        def drain(zz, c):
            b = zz * 2 + x
            to_other(b).wait_send()

            @pl.when((zz <= z) & (z < nz - 1))
            def _():
                to_right(b).wait_send()

            @pl.when((zz >= z) & (z > 0))
            def _():
                to_left(b).wait_send()
            return c
        lax.fori_loop(0, nz, drain, 0)


def attn_fwd(qa, own, kaug, comm=True, cid=0):
    n, rows = kaug.shape[1], kaug.shape[2]
    V = pl.BlockSpec(memory_space=pltpu.VMEM)
    return pl.pallas_call(
        functools.partial(attn_fwd_kernel, n // 2, comm),
        out_shape=(
            jax.ShapeDtypeStruct((rows, 192), BF),
            jax.ShapeDtypeStruct((rows, 192), F32),
            jax.ShapeDtypeStruct((3, rows, 128), F32),
            jax.ShapeDtypeStruct((n, rows, 384), BF),
        ),
        in_specs=[V] * 3,
        out_specs=(V,) * 4,
        scratch_shapes=[
            pltpu.VMEM((3, rows, 128), F32),
            pltpu.VMEM((3, rows, 128), F32),
            pltpu.SemaphoreType.DMA((2 * n,)),
            pltpu.SemaphoreType.DMA((n,)),
            pltpu.SemaphoreType.DMA((n,)),
        ],
        compiler_params=pltpu.CompilerParams(
            collective_id=cid if comm else None, has_side_effects=comm, vmem_limit_bytes=56 * 2**20),
        cost_estimate=pl.CostEstimate(flops=20 * 10**9, bytes_accessed=10**8, transcendentals=10**7),
        name="attn_fwd",
    )(qa, own, kaug)


def attn_bwd_kernel(nz, comm, q_ref, do_ref, kv_ref, kaug_ref, dq_ref, dkv_ref,
                    dqacc, part, stage, xin, zin, xsend, xrecv, zsend, zrecv):
    blk, head = lax.axis_index("blk"), lax.axis_index("head")
    z, x = blk // 2, blk % 2
    other = 1 - x
    rows = dq_ref.shape[0]

    def device(zz, xx):
        return (zz * 2 + xx, head)

    if comm:
        barrier = pltpu.get_barrier_semaphore()
        pl.semaphore_signal(barrier, inc=1, device_id=device(z, other), device_id_type=MESH)

        def greet(d, c):
            pl.semaphore_signal(barrier, inc=1, device_id=device((z + d) % nz, x), device_id_type=MESH)
            return c
        lax.fori_loop(1, nz, greet, 0)
        pl.semaphore_wait(barrier, nz)

    dqacc[...] = jnp.zeros(dqacc.shape, F32)

    def compute(b, diag):
        side = (b > blk).astype(jnp.int32)
        dks, dvs = [], []
        for h in range(3):
            k = k_operand(kv_ref, kaug_ref, b, h)
            v = v_operand(kv_ref, b, h)
            if diag:
                s = jnp.minimum(dot(k, q_ref[0, h], NT), dot(k, q_ref[1, h], NT))
            else:
                s = dot(k, q_ref[side, h], NT)
            p = jnp.exp(s)
            ds = (p * dot(v, do_ref[h], NT)).astype(BF)
            dvs.append(dot(p.astype(BF), do_ref[h], NN))
            dks.append(dot(ds, q_ref[side, h], NN))
            dqacc[h] += dot(ds, k, TN)
        low = in_half(0, rows)
        part[:, 0:128] = jnp.where(low, dks[0], dks[1])
        part[:, 128:256] = jnp.where(low, dks[2], dvs[0])
        part[:, 256:384] = jnp.where(low, dvs[1], dvs[2])

    def to_other(zz):
        return pltpu.make_async_remote_copy(
            src_ref=stage.at[zz, 0], dst_ref=xin.at[zz], send_sem=xsend.at[zz], recv_sem=xrecv.at[zz],
            device_id=device(z, other), device_id_type=MESH)

    def to_owner(zz):
        return pltpu.make_async_remote_copy(
            src_ref=stage.at[zz, 1], dst_ref=zin.at[z], send_sem=zsend.at[zz], recv_sem=zrecv.at[z],
            device_id=device(zz, x), device_id_type=MESH)

    def from_sender(zz):
        return pltpu.make_async_remote_copy(
            src_ref=stage.at[zz, 1], dst_ref=zin.at[zz], send_sem=zsend.at[zz], recv_sem=zrecv.at[zz],
            device_id=device(zz, x), device_id_type=MESH)

    def far(zz):
        compute(zz * 2 + other, False)
        stage[zz, 0] = part[...].astype(BF)
        if comm:
            to_other(zz).start()

    def step(i, c):
        zz = (z + 1 + i) % nz
        far(zz)
        compute(zz * 2 + x, False)
        if comm:
            to_other(zz).wait_recv()
        stage[zz, 1] = (part[...] + xin[zz].astype(F32)).astype(BF)
        if comm:
            to_owner(zz).start()
        return c

    lax.fori_loop(0, nz - 1, step, 0)
    far(z)
    compute(blk, True)
    for h in range(3):
        half = h % 2
        dq_ref[:, 64 * h : 64 * h + 64] = (dqacc[h][:, 64 * half : 64 * half + 64] * 0.125).astype(BF)
    if comm:
        to_other(z).wait_recv()
    part[...] += xin[z].astype(F32)

    def gather(i, c):
        zz = (z + nz - 1 - i) % nz
        if comm:
            from_sender(zz).wait_recv()
        part[...] += zin[zz].astype(F32)
        return c
    lax.fori_loop(0, nz - 1, gather, 0)
    dkv_ref[...] = part[...].astype(BF)

    if comm:
        def drain(i, c):
            zz = (z + 1 + i) % nz
            to_other(zz).wait_send()
            to_owner(zz).wait_send()
            return c
        lax.fori_loop(0, nz - 1, drain, 0)
        to_other(z).wait_send()


def attn_bwd(qb, do, kv, kaug, comm=True, cid=1):
    n, rows = kaug.shape[1], kaug.shape[2]
    nz = n // 2
    V = pl.BlockSpec(memory_space=pltpu.VMEM)
    return pl.pallas_call(
        functools.partial(attn_bwd_kernel, nz, comm),
        out_shape=(
            jax.ShapeDtypeStruct((rows, 192), BF),
            jax.ShapeDtypeStruct((rows, 384), BF),
        ),
        in_specs=[V] * 4,
        out_specs=(V,) * 2,
        scratch_shapes=[
            pltpu.VMEM((3, rows, 128), F32),
            pltpu.VMEM((rows, 384), F32),
            pltpu.VMEM((nz, 2, rows, 384), BF),
            pltpu.VMEM((nz, rows, 384), BF),
            pltpu.VMEM((nz, rows, 384), BF),
            pltpu.SemaphoreType.DMA((nz,)),
            pltpu.SemaphoreType.DMA((nz,)),
            pltpu.SemaphoreType.DMA((nz,)),
            pltpu.SemaphoreType.DMA((nz,)),
        ],
        compiler_params=pltpu.CompilerParams(
            collective_id=cid if comm else None, has_side_effects=comm, vmem_limit_bytes=60 * 2**20),
        cost_estimate=pl.CostEstimate(flops=40 * 10**9, bytes_accessed=2 * 10**8, transcendentals=10**7),
        name="attn_bwd",
    )(qb, do, kv, kaug)


EPS = 1e-06


def layer_norm(hidden_state, ln_gain, ln_shift):
    row_mean = jnp.mean(hidden_state, axis=-1, keepdims=True)
    centred = hidden_state - row_mean
    row_var = jnp.mean(centred * centred, axis=-1, keepdims=True)
    return centred * lax.rsqrt(row_var + EPS) * ln_gain + ln_shift


def norm_back(grad, total, gain):
    row_mean = jnp.mean(total, axis=-1, keepdims=True)
    centred = total - row_mean
    scale = lax.rsqrt(jnp.mean(centred * centred, axis=-1, keepdims=True) + EPS)
    n = centred * scale
    dn = grad * gain
    e = scale * (dn - jnp.mean(dn, axis=-1, keepdims=True) - n * jnp.mean(dn * n, axis=-1, keepdims=True))
    return e, jnp.sum(grad * n, axis=0), jnp.sum(grad, axis=0)


def gelu_parts(u):
    cdf = 0.5 * (1.0 + lax.erf(u * (0.5 ** 0.5)))
    pdf = jnp.exp(-0.5 * u * u) * ((2.0 * jnp.pi) ** -0.5)
    return cdf, pdf


def three(value):
    high = lax.reduce_precision(value, 8, 7)
    rest = value - high
    mid = lax.reduce_precision(rest, 8, 7)
    return [part.astype(BF) for part in (high, mid, rest - mid)]


def aug(columns, rows):
    out = jnp.stack(columns, axis=-1)
    return jnp.pad(out, ((0, 0), (0, 64 - out.shape[1])))


def shards(hidden_in, out_grad, segment_ids, alibi_slopes, qkv_weight, out_weight, gate_up_weight, down_weight, gains, biases):
    nh, nb = lax.axis_size("head"), lax.axis_size("blk")
    head, blk = lax.axis_index("head"), lax.axis_index("blk")
    token_rows, width = hidden_in.shape
    rows = token_rows * nh
    layers, wrows = qkv_weight.shape[:2]
    ff = gate_up_weight.shape[2] // 2
    ffd = down_weight.shape[1]
    group = width // nh
    quarter = ff // nh
    tokens = segment_ids.shape[0]

    small = jnp.concatenate([gains.reshape(layers, -1), biases.reshape(layers, -1)], axis=1)
    small = jnp.broadcast_to(small.reshape(layers, wrows, 1, 8), (layers, wrows, nh, 8))
    qkv_cols = qkv_weight.reshape(layers, wrows, 3, nh, group).transpose(0, 1, 3, 2, 4).reshape(layers, wrows, nh, 3 * group)
    gu_cols = gate_up_weight.reshape(layers, wrows, 2, nb, nh, ffd).transpose(0, 1, 4, 2, 3, 5).reshape(layers, wrows, nh, 2 * quarter)
    spread = lax.all_to_all(jnp.concatenate([qkv_cols, small, gu_cols], axis=3), "head", split_axis=2, concat_axis=1, tiled=True)
    spread = spread.reshape(layers, nh * wrows, -1)
    qk, gu0 = 3 * group, 3 * group + 8

    first = jnp.concatenate([spread[0, :, :gu0]] + [spread[l, :, qk:gu0] for l in range(1, layers)], axis=1)
    first = lax.all_gather(first, "blk", axis=0, tiled=True)
    qkv_w = [first[:, :qk]]
    smalls = []
    for l in range(layers):
        s = first[:, qk + 8 * l : qk + 8 * l + 8].astype(F32).reshape(nb * nh, 8, wrows)
        smalls.append(s.transpose(1, 0, 2).reshape(8, width))
    outs_all = lax.all_gather(out_weight, ("blk", "head"), axis=1, tiled=True)
    gu_w, down_w = [], []
    for l in range(layers):
        if l:
            qkv_w.append(lax.all_gather(spread[l, :, :qk], "blk", axis=0, tiled=True))
        gu_w.append(lax.all_gather(spread[l, :, gu0:], "blk", axis=0, tiled=True))
        down_w.append(lax.all_gather(down_weight[l], "blk", axis=0, tiled=True))
    out_w = [outs_all[l] for l in range(layers)]
    out_rows = [lax.dynamic_slice_in_dim(outs_all[l], head * group, group, 0) for l in range(layers)]

    slopes = lax.dynamic_slice_in_dim(alibi_slopes, head * 3, 3, 0)
    position = jnp.arange(tokens, dtype=jnp.int32).astype(F32)
    same = (segment_ids[:, None] == jnp.arange(5, dtype=jnp.int32)[None, :])
    apart = [jnp.where(same[:, s], 0.0, -1e30).astype(BF) for s in range(5)]
    inside = [same[:, s].astype(BF) for s in range(5)]
    one = jnp.ones((tokens,), BF)
    nothing = jnp.zeros((tokens, 64), BF)
    kaug = []
    for h in range(3):
        a = aug(three(slopes[h] * position) + [one] * 3 + apart, tokens)
        kaug.append(jnp.concatenate([nothing, a] if h % 2 == 0 else [a, nothing], axis=1))
    kaug = jnp.stack(kaug).reshape(3, nb, rows, 128)
    own_pos = (blk * rows).astype(F32) + jnp.arange(rows, dtype=jnp.int32).astype(F32)
    own_in = [lax.dynamic_slice_in_dim(v, blk * rows, rows, 0) for v in inside]
    own_one = jnp.ones((rows,), BF)

    def q_operand(q, lse):
        sides = []
        for sign in (1.0, -1.0):
            for h in range(3):
                row = -sign * slopes[h] * own_pos
                if lse is not None:
                    row = row - lse[h]
                a = aug([own_one * sign] * 3 + three(row) + own_in, rows)
                qh = q[:, 64 * h : 64 * h + 64] * jnp.asarray(0.125, BF)
                sides.append(jnp.concatenate([qh, a] if h % 2 == 0 else [a, qh], axis=1))
        return jnp.stack(sides).reshape(2, 3, rows, 128)

    def spread_rows(v):
        return lax.all_gather(v, "head", axis=0, tiled=True)

    def sum_rows(v):
        parts = lax.all_to_all(v.astype(BF).reshape(nh, token_rows, v.shape[1]), "head", split_axis=0, concat_axis=0, tiled=True)
        return jnp.sum(parts.astype(F32), axis=0)

    def mm(a, b, dims=NN):
        return lax.dot_general(a, b, dims, preferred_element_type=F32)

    state = hidden_in.astype(F32)
    saved = []
    for l in range(layers):
        gain, bias = smalls[l][:2], smalls[l][2:]
        xr = spread_rows(state.astype(BF))
        qb = lax.dynamic_slice_in_dim(bias[0], head * group, group, 0)
        vb = lax.dynamic_slice_in_dim(bias[1], head * group, group, 0)
        proj = (mm(xr, qkv_w[l]) + jnp.concatenate([qb, jnp.zeros((group,), F32), vb])).astype(BF)
        q = proj[:, :group]
        ctx, ctxf, lse, kv = attn_fwd(q_operand(q, None), proj[:, group:], kaug)
        lse = lse[:, :, 0]
        ctx_tok = lax.all_to_all(ctx, "head", split_axis=0, concat_axis=1, tiled=True)
        sum1 = state + (mm(ctx_tok, out_w[l]) + bias[2])
        y = layer_norm(sum1, gain[0], bias[3])
        yr = spread_rows(y.astype(BF))
        mixed = mm(yr, gu_w[l])
        gate, up = mixed[:, :quarter], mixed[:, quarter:]
        cdf, _ = gelu_parts(gate)
        hid = (gate * cdf * up).astype(BF)
        sum2 = y + (sum_rows(mm(hid, down_w[l])) + bias[4])
        state = layer_norm(sum2, gain[1], bias[5])
        saved.append((xr, q, ctx, ctxf, lse, kv, sum1, yr, gate, up, hid, sum2))
    output = state.astype(BF)

    grad = out_grad.astype(F32)
    done = [None] * layers
    for l in reversed(range(layers)):
        gain, bias = smalls[l][:2], smalls[l][2:]
        xr, q, ctx, ctxf, lse, kv, sum1, yr, gate, up, hid, sum2 = saved[l]
        e2, d_gain2, d_shift2 = norm_back(grad, sum2, gain[1])
        df_tok = e2.astype(BF)
        d_down_bias = jnp.sum(df_tok.astype(F32), axis=0)
        df = spread_rows(df_tok)
        dhid = mm(df, down_w[l], NT)
        cdf, pdf = gelu_parts(gate)
        dgu = jnp.concatenate([dhid * up * (cdf + gate * pdf), dhid * (gate * cdf)], axis=1).astype(BF)
        d_down = mm(hid, df, TN).astype(BF)
        d_gu = mm(yr, dgu, TN).astype(BF)
        ff_sum = lax.psum_scatter(jnp.concatenate([d_gu, d_down], axis=1), "blk", scatter_dimension=0, tiled=True)
        dy = e2 + sum_rows(mm(dgu, gu_w[l], NT))
        e1, d_gain1, d_shift1 = norm_back(dy, sum1, gain[0])
        da_tok = e1.astype(BF)
        d_out_bias = jnp.sum(da_tok.astype(F32), axis=0)
        da = spread_rows(da_tok)
        dctx = mm(da, out_rows[l], NT).astype(BF)
        d_out = mm(ctx, da, TN).astype(BF)
        delta = jnp.sum((dctx.astype(F32) * ctxf).reshape(rows, 3, 64), axis=2)
        do = []
        for h in range(3):
            a = aug(three(-delta[:, h]), rows)
            dh = dctx[:, 64 * h : 64 * h + 64]
            do.append(jnp.concatenate([a, dh] if h % 2 == 0 else [dh, a], axis=1))
        dq, dkv = attn_bwd(q_operand(q, lse), jnp.stack(do), kv, kaug)
        dproj = jnp.concatenate([dq, dkv], axis=1)
        d_qkv = mm(xr, dproj, TN).astype(BF)
        d_out = d_out.reshape(width, group)
        at_sum = lax.psum_scatter(jnp.concatenate([d_qkv, d_out], axis=1), "blk", scatter_dimension=0, tiled=True)
        d_bias = jnp.sum(dproj.astype(F32), axis=0)
        grad = e1 + sum_rows(mm(dproj, qkv_w[l], NT))
        tok_small = jnp.stack([d_gain1, d_gain2, d_out_bias, d_shift1, d_down_bias, d_shift2])
        zero = jnp.zeros((2, width), F32)
        head_small = jnp.stack([
            lax.dynamic_update_slice_in_dim(zero[0], d_bias[:group], head * group, 0),
            lax.dynamic_update_slice_in_dim(zero[1], d_bias[2 * group :], head * group, 0)])
        done[l] = (ff_sum, at_sum, tok_small, head_small)

    small_g = jnp.stack([jnp.concatenate([done[l][2], done[l][3]]) for l in range(layers)])
    small_g = small_g.reshape(layers * 8, nb * nh, wrows).transpose(1, 0, 2).reshape(nb * nh, layers * 8 * wrows)
    small_sum = lax.psum_scatter(small_g, ("blk", "head"), scatter_dimension=0, tiled=True).reshape(layers, 8, wrows)
    gains_grad = small_sum[:, 0:2]
    biases_grad = jnp.concatenate([small_sum[:, 6:8], small_sum[:, 2:6]], axis=1)

    def piece(index, lo, hi):
        return jnp.stack([done[l][index][:, lo:hi] for l in range(layers)])

    gu_piece = piece(0, 0, 2 * quarter)
    qkv_piece = piece(1, 0, qk)
    back = jnp.concatenate([qkv_piece, gu_piece], axis=2).reshape(layers, nh, wrows, -1)
    back = lax.all_to_all(back, "head", split_axis=1, concat_axis=1, tiled=True).astype(F32)
    qkv_grad = back[..., :qk].reshape(layers, nh, wrows, 3, group).transpose(0, 2, 3, 1, 4).reshape(layers, wrows, 3 * width)
    gu_grad = back[..., qk:].reshape(layers, nh, wrows, 2, nb, ffd).transpose(0, 2, 3, 4, 1, 5).reshape(layers, wrows, 2 * ff)
    down_grad = piece(0, 2 * quarter, 2 * quarter + width).astype(F32)
    out_piece = piece(1, qk, qk + group).reshape(layers, wrows, width)
    moves = [(b * nh + h, h * nb + b) for b in range(nb) for h in range(nh)]
    out_grad_w = lax.ppermute(out_piece, ("blk", "head"), moves).astype(F32)
    return output, grad, qkv_grad, out_grad_w, gu_grad, down_grad, gains_grad, biases_grad


def solution(mesh):
    both = ("blk", "head")
    tok, mid, last = P(both, None), P(None, both, None), P(None, None, both)
    return jax.shard_map(
        shards, mesh=mesh,
        in_specs=(tok, tok, P(), P(), mid, mid, mid, mid, last, last),
        out_specs=(tok, tok, mid, mid, mid, mid, last, last),
        check_vma=False,
    )
```

```python
import functools
import types

import jax
import jax.numpy as jnp
from jax import lax
from jax.experimental import pallas as pl
from jax.experimental.pallas import tpu as pltpu
from jax.sharding import PartitionSpec as P

MESH = pl.DeviceIdType.MESH
BF = jnp.bfloat16
F32 = jnp.float32
NT = (((1,), (1,)), ((), ()))
NN = (((1,), (0,)), ((), ()))
TN = (((0,), (0,)), ((), ()))
EPS = 1e-06
K_AT = ((0, 0), (0, 1), (2, 0))
V_AT = ((1, 0), (1, 1), (2, 1))
VMEM = pl.BlockSpec(memory_space=pltpu.VMEM)
ANY = pl.BlockSpec(memory_space=pl.ANY)


def dot(a, b, dims=NN):
    return lax.dot_general(a, b, dims, preferred_element_type=F32)


def lanes(rows):
    return lax.broadcasted_iota(jnp.int32, (rows, 128), 1)


def in_half(half, rows):
    return lanes(rows) >= 64 if half else lanes(rows) < 64


def ones_half(half, rows):
    first = 0 if half else 64
    lane = lanes(rows)
    return jnp.where((lane >= first) & (lane < first + 3), 1.0, 0.0).astype(BF)


def k_operand(kv, aug, h):
    col, half = K_AT[h]
    return jnp.where(in_half(half, kv.shape[0]), kv[:, 128 * col : 128 * col + 128], aug)


def v_operand(kv, h):
    col, half = V_AT[h]
    rows = kv.shape[0]
    return jnp.where(in_half(half, rows), kv[:, 128 * col : 128 * col + 128], ones_half(half, rows))


def split3(value):
    high = value.astype(BF).astype(F32)
    mid = (value - high).astype(BF).astype(F32)
    return high, mid, value - high - mid


def with_lanes(base, first, values):
    lane = lanes(base.shape[0])
    for i, v in enumerate(values):
        base = jnp.where(lane == first + i, v, base)
    return base


def layer_norm(total, gain, shift):
    centred = total - jnp.mean(total, axis=-1, keepdims=True)
    scale = lax.rsqrt(jnp.mean(centred * centred, axis=-1, keepdims=True) + EPS)
    return centred * scale * gain + shift


def norm_back(grad, total, gain):
    centred = total - jnp.mean(total, axis=-1, keepdims=True)
    scale = lax.rsqrt(jnp.mean(centred * centred, axis=-1, keepdims=True) + EPS)
    n = centred * scale
    dn = grad * gain
    e = scale * (dn - jnp.mean(dn, axis=-1, keepdims=True) - n * jnp.mean(dn * n, axis=-1, keepdims=True))
    return e, jnp.sum(grad * n, axis=0, keepdims=True), jnp.sum(grad, axis=0, keepdims=True)


def normal_cdf(u):
    return 0.5 * (1.0 + lax.erf(u * (0.5**0.5)))


def normal_pdf(u):
    return jnp.exp(-0.5 * u * u) * ((2.0 * jnp.pi) ** -0.5)


def remote(src, dst, send, recv, device):
    return pltpu.make_async_remote_copy(
        src_ref=src, dst_ref=dst, send_sem=send, recv_sem=recv, device_id=device, device_id_type=MESH)


class Place:
    def __init__(self, nb):
        self.nz = nb // 2
        self.blk, self.head = lax.axis_index("blk"), lax.axis_index("head")
        self.z, self.x = self.blk // 2, self.blk % 2
        self.y, self.c = self.head // 2, self.head % 2
        self.other = 1 - self.x
        self.near_head = 2 * self.y + 1 - self.c
        self.far_head = 2 * (1 - self.y) + self.c
        self.cross_head = 2 * (1 - self.y) + 1 - self.c
        self.core = (self.blk, self.near_head)
        self.across = (self.blk, self.far_head)
        self.beside = (self.z * 2 + self.other, self.head)

    def column(self, zz):
        return (zz * 2 + self.x, self.head)

    def turn(self, i):
        return (self.z + 1 + i) % self.nz

    def enter(self):
        barrier = pltpu.get_barrier_semaphore()
        for device in (self.core, self.across, self.beside):
            pl.semaphore_signal(barrier, inc=1, device_id=device, device_id_type=MESH)

        def greet(i, carry):
            pl.semaphore_signal(barrier, inc=1, device_id=self.column(self.turn(i)), device_id_type=MESH)
            return carry
        lax.fori_loop(0, self.nz - 1, greet, 0)
        pl.semaphore_wait(barrier, 3 + self.nz - 1)


class HeadGather:
    def __init__(self, at, buf, send, recv):
        self.near = remote(buf.at[at.head], buf.at[at.head], send.at[0], recv.at[0], at.core)
        self.far = remote(buf.at[at.head], buf.at[at.head], send.at[1], recv.at[1], at.across)
        self.pass_on = remote(buf.at[at.far_head], buf.at[at.far_head], send.at[2], recv.at[2], at.core)

    def start(self):
        self.far.start()
        self.near.start()

    def wait_near(self):
        self.near.wait_recv()

    def wait_far(self):
        self.far.wait_recv()
        self.pass_on.start()
        self.pass_on.wait_recv()

    def finish(self):
        self.near.wait_send()
        self.far.wait_send()
        self.pass_on.wait_send()


class HeadSum:
    def __init__(self, at, part, stage, inbox, send, recv):
        self.at, self.part, self.stage, self.inbox = at, part, stage, inbox
        to = (at.core, at.core, at.across)
        self.copies = [remote(stage.at[i], inbox.at[i], send.at[i], recv.at[i], to[i]) for i in range(3)]

    def send_cross(self):
        self.stage[0] = self.part[self.at.cross_head].astype(BF)
        self.copies[0].start()

    def send_near(self):
        self.stage[1] = self.part[self.at.near_head].astype(BF)
        self.copies[1].start()

    def relay(self):
        self.copies[0].wait_recv()
        self.stage[2] = (self.part[self.at.far_head] + self.inbox[0].astype(F32)).astype(BF)
        self.copies[2].start()

    def total(self):
        self.copies[1].wait_recv()
        near = self.part[self.at.head] + self.inbox[1].astype(F32)
        self.copies[2].wait_recv()
        return near + self.inbox[2].astype(F32)

    def finish(self):
        for copy in self.copies:
            copy.wait_send()


class BlockSum:
    def __init__(self, at, item):
        self.at, self.stage, self.xin, self.zin = at, item.stage, item.xin, item.zin
        self.xsend, self.xrecv, self.zsend, self.zrecv = item.xsend, item.xrecv, item.zsend, item.zrecv

    def to_beside(self, zz):
        return remote(self.stage.at[zz * 2 + self.at.other], self.xin.at[zz], self.xsend.at[zz], self.xrecv.at[zz], self.at.beside)

    def to_owner(self, zz):
        at = self.at
        return remote(self.stage.at[zz * 2 + at.x], self.zin.at[at.z], self.zsend.at[zz], self.zrecv.at[at.z], at.column(zz))

    def from_sender(self, zz):
        at = self.at
        return remote(self.stage.at[zz * 2 + at.x], self.zin.at[zz], self.zsend.at[zz], self.zrecv.at[zz], at.column(zz))

    def each(self, first, last, do):
        def step(i, carry):
            do(self.at.turn(i))
            return carry
        lax.fori_loop(first, last, step, 0)

    def start(self):
        self.each(0, self.at.nz, lambda zz: self.to_beside(zz).start())

    def relay_one(self, zz):
        self.to_beside(zz).wait_recv()
        own = zz * 2 + self.at.x
        self.stage[own] = (self.stage[own].astype(F32) + self.xin[zz].astype(F32)).astype(BF)
        self.to_owner(zz).start()

    def relay(self):
        self.each(0, self.at.nz - 1, self.relay_one)

    def total(self, emit):
        at = self.at
        self.to_beside(at.z).wait_recv()
        self.each(0, at.nz - 1, lambda zz: self.from_sender(zz).wait_recv())
        value = self.stage[at.blk].astype(F32) + self.xin[at.z].astype(F32)
        emit(lax.fori_loop(0, at.nz - 1, lambda i, v: v + self.zin[at.turn(i)].astype(F32), value))

    def finish(self):
        self.each(0, self.at.nz, lambda zz: self.to_beside(zz).wait_send())
        self.each(0, self.at.nz - 1, lambda zz: self.to_owner(zz).wait_send())


def box(tree):
    if isinstance(tree, dict):
        return types.SimpleNamespace(**{k: box(v) for k, v in tree.items()})
    return [box(v) for v in tree] if isinstance(tree, list) else tree


def call(body, name, collective_id, near=None, far=None, table=None, out=None, far_out=None, scratch=None):
    groups = [near or {}, far or {}, table or {}, out or {}, far_out or {}, scratch or {}]
    flat, trees = zip(*[jax.tree.flatten(g) for g in groups])
    counts = [len(f) for f in flat]

    def kernel(*refs):
        named, first = {}, 0
        for tree, count in zip(trees, counts):
            named.update(jax.tree.unflatten(tree, refs[first : first + count]))
            first += count
        body(box(named))

    smem = pl.BlockSpec(memory_space=pltpu.SMEM)
    results = pl.pallas_call(
        kernel,
        out_shape=tuple(flat[3]) + tuple(flat[4]),
        in_specs=[VMEM] * counts[0] + [ANY] * counts[1] + [smem] * counts[2],
        out_specs=(VMEM,) * counts[3] + (ANY,) * counts[4],
        scratch_shapes=list(flat[5]),
        compiler_params=pltpu.CompilerParams(
            collective_id=collective_id, has_side_effects=True, vmem_limit_bytes=63 * 2**20),
        cost_estimate=pl.CostEstimate(flops=10**11, bytes_accessed=2 * 10**8, transcendentals=10**7),
        name=name,
    )(*flat[0], *flat[1], *flat[2])
    done = jax.tree.unflatten(trees[3], results[: counts[3]])
    done.update(jax.tree.unflatten(trees[4], results[counts[3] :]))
    return box(done)


def shape(*dims, dtype=BF):
    return jax.ShapeDtypeStruct(dims, dtype)


def keep(*dims, dtype=BF):
    return pltpu.VMEM(dims, dtype)


def copies(*dims):
    return pltpu.SemaphoreType.DMA(dims)


Q_HALF = (0, 1, 0)
ROW_LANE = 9


def row_term(blk, slopes_ref, h, rows):
    position = (blk * rows + lax.broadcasted_iota(jnp.int32, (rows, 128), 0)).astype(F32)
    return position * slopes_ref[h]


def query_base(q_ref, qaug_ref, side, h, rows):
    if h < 2:
        data = q_ref[:, 0:128]
    else:
        data = jnp.concatenate([q_ref[:, 128:192], jnp.zeros((rows, 64), q_ref.dtype)], axis=1)
    half = Q_HALF[h]
    return jnp.where(in_half(half, rows), data.astype(F32) * 0.125, qaug_ref[side, h].astype(F32)), 0 if half else 64


def query_operand(at, q_ref, qaug_ref, slopes_ref, side, h, rows, lse=None):
    base, first = query_base(q_ref, qaug_ref, side, h, rows)
    term = row_term(at.blk, slopes_ref, h, rows)
    term = -term if side == 0 else term
    if lse is not None:
        term = term - lse
    return with_lanes(base, first + ROW_LANE, split3(term)).astype(BF)


def fwd_block(side, diag, kv, aug, q_ref, m_ref, acc_ref):
    for h in range(3):
        k = k_operand(kv, aug, h)
        if diag:
            s = jnp.minimum(dot(q_ref[0, h], k, NT), dot(q_ref[1, h], k, NT))
        else:
            s = dot(q_ref[side, h], k, NT)
        m_old = m_ref[h]
        m_new = jnp.maximum(m_old, jnp.max(s, axis=1, keepdims=True))
        p = jnp.exp(s - m_new[:, :1]).astype(BF)
        acc_ref[h] = acc_ref[h] * jnp.exp(m_old - m_new) + dot(p, v_operand(kv, h))
        m_ref[h] = m_new


class BlockGather:
    def __init__(self, at, item):
        self.at, self.buf, self.zsend, self.xsend, self.recv = at, item.buf, item.zsend, item.xsend, item.recv

    def copy(self, b, send, device):
        return remote(self.buf.at[b], self.buf.at[b], send, self.recv.at[b], device)

    def to_right(self, b):
        return self.copy(b, self.zsend.at[0, b], self.at.column(self.at.z + 1))

    def to_left(self, b):
        return self.copy(b, self.zsend.at[1, b], self.at.column(self.at.z - 1))

    def to_beside(self, b):
        return self.copy(b, self.xsend.at[b], self.at.beside)

    def start(self):
        at = self.at

        @pl.when(at.z < at.nz - 1)
        def _():
            self.to_right(at.blk).start()

        @pl.when(at.z > 0)
        def _():
            self.to_left(at.blk).start()
        self.to_beside(at.blk).start()

    def wait(self, b):
        self.to_beside(b).wait_recv()

    def serve(self, d):
        at = self.at

        @pl.when(at.z - d >= 0)
        def _():
            b = (at.z - d) * 2 + at.x
            self.wait(b)
            self.to_beside(b).start()

            @pl.when(at.z < at.nz - 1)
            def _():
                self.to_right(b).start()

        @pl.when(at.z + d < at.nz)
        def _():
            b = (at.z + d) * 2 + at.x
            self.wait(b)
            self.to_beside(b).start()

            @pl.when(at.z > 0)
            def _():
                self.to_left(b).start()

    def serve_all(self):
        def step(d, carry):
            self.serve(d)
            return carry
        lax.fori_loop(1, self.at.nz, step, 0)

    def collect(self):
        def step(zz, carry):
            self.wait(zz * 2 + self.at.other)
            return carry
        lax.fori_loop(0, self.at.nz, step, 0)

    def finish(self):
        at = self.at

        def drain(zz, carry):
            b = zz * 2 + at.x
            self.to_beside(b).wait_send()

            @pl.when((zz <= at.z) & (at.z < at.nz - 1))
            def _():
                self.to_right(b).wait_send()

            @pl.when((zz >= at.z) & (at.z > 0))
            def _():
                self.to_left(b).wait_send()
            return carry
        lax.fori_loop(0, at.nz, drain, 0)


def attention(at, gather, q_op, kaug, m_ref, acc_ref, behind):
    m_ref[...] = jnp.full(m_ref.shape, -1e30, F32)
    acc_ref[...] = jnp.zeros(acc_ref.shape, F32)
    kv = gather.buf
    nz = at.nz

    def compute(b, diag=False):
        fwd_block((b > at.blk).astype(jnp.int32), diag, kv.at[b], kaug[b], q_op, m_ref, acc_ref)

    compute(at.blk, True)

    def visit_step(d, first, last):
        def visit(i, carry):
            zz = jnp.where(i % 2 == 0, at.z - d + i // 2, at.z + d - i // 2)
            xx = jnp.where(i < 2, at.x, at.other)

            @pl.when((zz >= 0) & (zz < nz) & ((i != 3) | (d > 1)))
            def _():
                b = zz * 2 + xx

                @pl.when(i >= 2)
                def _():
                    gather.wait(b)
                compute(b)
            return carry
        lax.fori_loop(first, last, visit, 0)

    def step(d, carry):
        @pl.when(d < nz)
        def _():
            gather.serve(d)
            behind(d)
        visit_step(d, jnp.where(d < nz, 0, 2), 4)
        return carry
    lax.fori_loop(1, nz + 1, step, 0)


def attention_end(at, q_ref, qaug, slopes, m_ref, acc_ref, ctx_ref, ctxf_ref, qb_ref):
    rows = ctx_ref.shape[0]
    for h in range(3):
        half = V_AT[h][1]
        first = 0 if half else 64
        acc = acc_ref[h]
        total = acc[:, first : first + 1]
        ctx = acc[:, 64 * half : 64 * half + 64] / total
        ctxf_ref[:, 64 * h : 64 * h + 64] = ctx
        ctx_ref[:, 64 * h : 64 * h + 64] = ctx.astype(BF)
        lse = m_ref[h] + jnp.log(total)
        for side in range(2):
            qb_ref[side, h] = query_operand(at, q_ref, qaug, slopes, side, h, rows, lse)


def fwd_kernel(nb, layers, host, R):
    at = Place(nb)
    rows = R.kaug.shape[1]
    half_rows = rows // 2
    quarter = R.hid.shape[1]
    group = R.ctx_now[0].shape[1]
    at.enter()
    part = R.part
    head_sum = HeadSum(at, part, R.hs_stage, R.hs_in, R.hs_send, R.hs_recv)
    gather_x = [HeadGather(at, R.xr_now[l], R.x_send.at[l], R.x_recv.at[l]) for l in range(layers)]
    gather_y = [HeadGather(at, R.yr_now[l], R.y_send.at[l], R.y_recv.at[l]) for l in range(layers)]
    kv = BlockGather(at, R.kv_now)
    saves = []

    def save(source, target):
        saves.append(pltpu.make_async_copy(source, target, R.saved.at[len(saves)]))
        saves[-1].start()
        return len(saves) - 1

    waited = []

    def wait_saved(number):
        saves[number].wait()
        waited.append(number)

    if host:
        qkv, gu, down = [[BlockGather(at, item) for item in items] for items in (R.qkv_now, R.gu_now, R.down_now)]
        ow = BlockGather(at, R.ow_now)
        order = ((qkv, R.qkv_own), (gu, R.gu_own), (down, R.down_own))
        qkv[0].buf[at.blk] = R.qkv_own[0][...]
        qkv[0].start()

    R.xr_now[0][at.head] = R.x0[...]
    gather_x[0].start()
    if host:
        for gathers, owns in order:
            for l in range(layers):
                if gathers is not qkv or l:
                    gathers[l].buf[at.blk] = owns[l][...]
        ow.buf[at.blk] = R.ow_own[...]
    for side in range(2):
        for h in range(3):
            R.qaug_now[side, h] = R.qaug[side, h]

    def weight(gathers, given, l, lo=0, hi=None):
        if not host:
            return given[l][:, lo:hi]
        v = gathers[l].buf[:, :, lo:hi]
        return v.reshape(v.shape[0] * v.shape[1], v.shape[2])

    def small(l, t):
        return R.small[8 * l + t : 8 * l + t + 1, :]

    def of(buf, half):
        v = buf[pl.ds(2 * half, 2)]
        return v.reshape(half_rows, v.shape[2])

    def half_at(half):
        return pl.ds(pl.multiple_of(half * half_rows, half_rows), half_rows)

    def of_group(row):
        value = jnp.zeros((1, group), F32)
        for h in range(4):
            value = jnp.where(at.head == h, row[:, group * h : group * h + group], value)
        return value

    if host:
        qkv[0].serve_all()
        ow.start()
        gu[0].start()
        down[0].start()
        qkv[0].collect()
        tail = weight(qkv, None, 0, 512, 640).astype(F32).T
        R.small[...] = tail[64 : 64 + 8 * layers, :]
    else:
        R.small[...] = R.small_given[...]
    R.state[...] = R.x0[...].astype(F32)
    gather_x[0].wait_near()
    gather_x[0].wait_far()

    for l in range(layers):
        last = l == layers - 1
        x_all = R.xr_now[l][...].reshape(rows, -1)
        save(R.xr_now[l], R.xr[l])
        qb, vb = of_group(small(l, 2)), of_group(small(l, 3))
        none = jnp.zeros((1, 128), F32)
        kv_bias = jnp.concatenate([none, vb[:, :128], none[:, :64], vb[:, 128:192]], axis=1)
        if l:
            pl.semaphore_wait(R.kv_free, 3 - (at.z == 0).astype(jnp.int32) - (at.z == at.nz - 1).astype(jnp.int32))
        kv.buf[at.blk] = (dot(x_all, weight(qkv if host else None, R.qkv_given, l, 0, 384)) + kv_bias).astype(BF)
        kv.start()
        R.q[...] = (dot(x_all, weight(qkv if host else None, R.qkv_given, l, 384, 576)) + qb).astype(BF)
        for side in range(2):
            for h in range(3):
                R.q_op[side, h] = query_operand(at, R.q, R.qaug_now, R.slopes, side, h, rows)

        def behind(d, l=l):
            if host:
                if l == 0:
                    ow.serve(d)
                gu[l].serve(d)
                down[l].serve(d)
        attention(at, kv, R.q_op, R.kaug, R.m, R.acc, behind)
        attention_end(at, R.q, R.qaug_now, R.slopes, R.m, R.acc, R.ctx_now[l], R.ctxf_now[l], R.qb_now[l])
        kv_saved = save(kv.buf, R.kv[l])
        save(R.ctx_now[l], R.ctx[l])
        save(R.ctxf_now[l], R.ctxf[l])
        save(R.qb_now[l], R.qb[l])
        kv.finish()
        if l == 0 and host:
            ow.collect()
            for i in range(layers):
                step = group // nb
                for b in range(nb):
                    R.ow_wide[...] = ow.buf[b].astype(F32)
                    R.ow_flat[step * b : step * b + step, :] = R.ow_wide[step * i : step * i + step, :]
                R.out_now[i][...] = R.ow_flat[...].astype(BF)
                save(R.out_now[i], R.out_w[i])
        if not last and host:
            qkv[l + 1].start()
        out_w = R.out_now[l][...] if host else R.out_given[l][...]
        if l:
            head_sum.finish()
        for number, half in enumerate((1 - at.y, at.y)):
            a = dot(R.ctx_now[l][half_at(half), :], out_w)
            part[pl.ds(2 * half, 2)] = a.reshape(2, half_rows // 2, a.shape[1])
            if number == 0:
                head_sum.send_cross()
            else:
                head_sum.send_near()
        head_sum.relay()
        wait_saved(kv_saved)
        if not last:
            pl.semaphore_signal(R.kv_free, inc=1, device_id=at.beside, device_id_type=MESH)

            @pl.when(at.z > 0)
            def _():
                pl.semaphore_signal(R.kv_free, inc=1, device_id=at.column(at.z - 1), device_id_type=MESH)

            @pl.when(at.z < at.nz - 1)
            def _():
                pl.semaphore_signal(R.kv_free, inc=1, device_id=at.column(at.z + 1), device_id_type=MESH)
        R.sum1_now[l][...] = R.state[...] + (head_sum.total() + small(l, 4))
        save(R.sum1_now[l], R.sum1[l])
        y = layer_norm(R.sum1_now[l][...], small(l, 0), small(l, 5))
        R.yr_now[l][at.head] = y.astype(BF)
        gather_y[l].start()
        R.state[...] = y
        if host:
            gu[l].collect()
            down[l].collect()
        gather_y[l].wait_near()
        if l:
            wait_saved(mixed_saved)
        head_sum.finish()
        for number, half in enumerate((at.y, 1 - at.y)):
            if number == 1:
                if not last and host:
                    qkv[l + 1].serve_all()
                    gu[l + 1].start()
                    down[l + 1].start()
                gather_y[l].wait_far()
            here = half_at(half)
            y_half = of(R.yr_now[l], half)
            gu_w = lambda lo: weight(gu if host else None, R.gu_given, l, lo, lo + 256)
            for col in range(0, quarter, 256):
                gate = dot(y_half, gu_w(col))
                up = dot(y_half, gu_w(quarter + col))
                R.mixed_now[here, col : col + 256] = gate
                R.mixed_now[here, quarter + col : quarter + col + 256] = up
                R.hid[:, col : col + 256] = (gate * normal_cdf(gate) * up).astype(BF)
            f = dot(R.hid[...], weight(down if host else None, R.down_given, l))
            part[pl.ds(2 * half, 2)] = f.reshape(2, half_rows // 2, f.shape[1])
            if number == 0:
                head_sum.send_near()
            else:
                head_sum.send_cross()
        mixed_saved = save(R.mixed_now, R.mixed[l])
        save(R.yr_now[l], R.yr[l])
        if host:
            save(qkv[l].buf, R.qkv_w[l])
            save(gu[l].buf, R.gu_w[l])
            save(down[l].buf, R.down_w[l])
        head_sum.relay()
        if not last and host:
            qkv[l + 1].collect()
        R.sum2_now[l][...] = R.state[...] + (head_sum.total() + small(l, 6))
        save(R.sum2_now[l], R.sum2[l])
        state = layer_norm(R.sum2_now[l][...], small(l, 1), small(l, 7))
        R.state[...] = state
        if last:
            R.output[...] = state.astype(BF)
        else:
            R.xr_now[l + 1][at.head] = state.astype(BF)
            gather_x[l + 1].start()
            gather_x[l + 1].wait_near()
            gather_x[l + 1].wait_far()
    for l in range(layers):
        gather_x[l].finish()
        gather_y[l].finish()
    head_sum.finish()
    if host:
        for items in (qkv, gu, down):
            for item in items:
                item.finish()
        ow.finish()
    for number, copy in enumerate(saves):
        if number not in waited:
            copy.wait()


def block_gather_item(nb, *dims):
    return dict(buf=keep(nb, *dims), zsend=copies(2, nb), xsend=copies(nb), recv=copies(nb))


def fwd(x0, slopes, qaug, kaug, weights, layers, host):
    nb, rows = kaug.shape[:2]
    tokens, width = x0.shape
    group = width // 4
    each = range(layers)
    r = width // nb
    ff2 = (weights.gu_own if host else weights.gu_given)[0].shape[1]
    quarter = ff2 // 2
    keep_rows = lambda: [keep(4, tokens, width) for _ in each]
    scratch = dict(
        xr_now=keep_rows(), x_send=copies(layers, 3), x_recv=copies(layers, 3),
        yr_now=keep_rows(), y_send=copies(layers, 3), y_recv=copies(layers, 3),
        part=keep(4, tokens, width, dtype=F32), hs_stage=keep(3, tokens, width), hs_in=keep(3, tokens, width),
        hs_send=copies(3), hs_recv=copies(3), state=keep(tokens, width, dtype=F32),
        kv_now=block_gather_item(nb, rows, 384), kv_free=pltpu.SemaphoreType.REGULAR, saved=copies(16 * layers),
        q=keep(rows, group), q_op=keep(2, 3, rows, 128), qaug_now=keep(2, 3, rows, 128),
        m=keep(3, rows, 128, dtype=F32), acc=keep(3, rows, 128, dtype=F32),
        ctx_now=[keep(rows, group) for _ in each], ctxf_now=[keep(rows, group, dtype=F32) for _ in each],
        qb_now=[keep(2, 3, rows, 128) for _ in each],
        sum1_now=[keep(tokens, width, dtype=F32) for _ in each], sum2_now=[keep(tokens, width, dtype=F32) for _ in each],
        mixed_now=keep(rows, ff2, dtype=F32), hid=keep(rows // 2, quarter))
    far_out = dict(
        xr=[shape(4, tokens, width) for _ in each], yr=[shape(4, tokens, width) for _ in each],
        kv=[shape(nb, rows, 384) for _ in each], ctx=[shape(rows, group) for _ in each],
        ctxf=[shape(rows, group, dtype=F32) for _ in each], qb=[shape(2, 3, rows, 128) for _ in each],
        sum1=[shape(tokens, width, dtype=F32) for _ in each], sum2=[shape(tokens, width, dtype=F32) for _ in each],
        mixed=[shape(rows, ff2, dtype=F32) for _ in each])
    near = dict(x0=x0, qaug=qaug, kaug=kaug, **vars(weights))
    if host:
        far_out.update(qkv_w=[shape(nb, *w.shape) for w in weights.qkv_own], gu_w=[shape(nb, *w.shape) for w in weights.gu_own],
                       down_w=[shape(nb, *w.shape) for w in weights.down_own], out_w=[shape(group, width) for _ in each])
        scratch.update(
            qkv_now=[block_gather_item(nb, *w.shape) for w in weights.qkv_own],
            gu_now=[block_gather_item(nb, *w.shape) for w in weights.gu_own],
            down_now=[block_gather_item(nb, *w.shape) for w in weights.down_own],
            ow_now=block_gather_item(nb, *weights.ow_own.shape), out_now=[keep(group, width) for _ in each],
            ow_wide=keep(*weights.ow_own.shape, dtype=F32), ow_flat=keep(group, width, dtype=F32))
        near.update(qkv_given=[], gu_given=[], down_given=[], out_given=[])
    out = dict(output=shape(tokens, width), small=shape(8 * layers, width, dtype=F32))
    done = call(functools.partial(fwd_kernel, nb, layers, host), "forward", 0, near=near, table=dict(slopes=slopes),
                out=out, far_out=far_out, scratch=scratch)
    if host:
        done.qkv_w = [w.reshape(width, -1)[:, :576] for w in done.qkv_w]
        done.gu_w = [w.reshape(width, -1) for w in done.gu_w]
        done.down_w = [w.reshape(quarter, -1) for w in done.down_w]
    else:
        done.qkv_w, done.gu_w, done.down_w, done.out_w = weights.qkv_given, weights.gu_given, weights.down_given, weights.out_given
    done.xr = [v.reshape(rows, width) for v in done.xr]
    done.yr = [v.reshape(rows, width) for v in done.yr]
    return done


OW_ROWS = 32


def attn_back(at, R, l, dkv, top, ff_start, after_first):
    nz, rows = at.nz, R.kvbuf.shape[1]
    q_ref, kaug, do_ref, acc, dqacc = R.qb[l], R.kaug, R.do, R.dkv_acc, R.dqacc
    slots = R.dkv.stage.shape[0]

    def load(zz, slot):
        b = zz * 2 + (at.other if slot == 0 else at.x)
        return pltpu.make_async_copy(R.kv[l].at[b], R.kvbuf.at[slot], R.kvsem.at[slot])

    dqacc[...] = jnp.zeros(dqacc.shape, F32)

    def compute(b, slot, diag):
        side = (b > at.blk).astype(jnp.int32)
        kv, aug = R.kvbuf.at[slot], kaug[b]
        dks, dvs = [], []
        for h in range(3):
            k, v = k_operand(kv, aug, h), v_operand(kv, h)
            if diag:
                s = jnp.minimum(dot(k, q_ref[0, h], NT), dot(k, q_ref[1, h], NT))
            else:
                s = dot(k, q_ref[side, h], NT)
            p = jnp.exp(s)
            ds = (p * dot(v, do_ref[h], NT)).astype(BF)
            dvs.append(dot(p.astype(BF), do_ref[h]))
            dks.append(dot(ds, q_ref[side, h]))
            dqacc[h] += dot(ds, k, TN)
        low = in_half(0, rows)
        acc[:, 0:128] = jnp.where(low, dks[0], dks[1])
        acc[:, 128:256] = jnp.where(low, dvs[0], dvs[1])
        acc[:, 256:384] = jnp.where(low, dks[2], dvs[2])

    def to_beside(i):
        zz = at.turn(i)
        return remote(R.dkv.stage.at[i % slots, 0], R.dkv.xin.at[zz], R.dkv.xsend.at[zz], R.dkv.xrecv.at[zz], at.beside)

    def to_owner(i):
        zz = at.turn(i)
        return remote(R.dkv.stage.at[i % slots, 1], R.dkv.zin.at[at.z], R.dkv.zsend.at[zz], R.dkv.zrecv.at[at.z], at.column(zz))

    def from_sender(zz):
        return remote(R.dkv.stage.at[0, 1], R.dkv.zin.at[zz], R.dkv.zsend.at[zz], R.dkv.zrecv.at[zz], at.column(zz))

    def far(i):
        zz = at.turn(i)
        load(zz, 1).start()
        load(zz, 0).wait()
        compute(zz * 2 + at.other, 0, False)

        @pl.when(i >= slots)
        def _():
            to_beside(i - slots).wait_send()
        R.dkv.stage[i % slots, 0] = acc[...].astype(BF)
        to_beside(i).start()

    load(at.turn(0), 0).start()
    if not top:
        pl.semaphore_wait(R.dkv.free, nz)

    def step(i, carry):
        zz = at.turn(i)
        far(i)
        load(at.turn(i + 1), 0).start()
        load(zz, 1).wait()
        compute(zz * 2 + at.x, 1, False)

        @pl.when(i >= slots)
        def _():
            to_owner(i - slots).wait_send()
        to_beside(i).wait_recv()
        R.dkv.stage[i % slots, 1] = (acc[...] + R.dkv.xin[zz].astype(F32)).astype(BF)
        to_owner(i).start()

        @pl.when(i == 0)
        def _():
            after_first()
        return carry
    lax.fori_loop(0, nz - 1, step, 0)
    far(nz - 1)
    ff_start()
    load(at.z, 1).wait()
    compute(at.blk, 1, True)
    dq = jnp.where(in_half(0, rows), dqacc[0], dqacc[1]) * 0.125
    R.dproj[:, 384:512] = dq.astype(BF)
    R.dproj[:, 512:576] = (dqacc[2][:, 0:64] * 0.125).astype(BF)
    to_beside(nz - 1).wait_recv()
    acc[...] += R.dkv.xin[at.z].astype(F32)

    def add(i, carry):
        zz = at.turn(nz - 2 - i)
        from_sender(zz).wait_recv()
        acc[...] += R.dkv.zin[zz].astype(F32)
        return carry
    lax.fori_loop(0, nz - 1, add, 0)
    R.dproj[:, 0:384] = acc[...].astype(BF)
    if l > 0:
        pl.semaphore_signal(R.dkv.free, inc=1, device_id=at.beside, device_id_type=MESH)

        def free(i, carry):
            pl.semaphore_signal(R.dkv.free, inc=1, device_id=at.column(at.turn(i)), device_id_type=MESH)
            return carry
        lax.fori_loop(0, nz - 1, free, 0)

    def drain(i, carry):
        to_beside(i).wait_send()

        @pl.when(i < nz - 1)
        def _():
            to_owner(i).wait_send()
        return carry
    lax.fori_loop(max(0, nz - slots), nz, drain, 0)
    if nz > slots:
        to_owner(nz - 1 - slots).wait_send()


def bwd_kernel(nb, layers, host, R):
    at = Place(nb)
    rows = R.kvbuf.shape[1]
    half_rows = rows // 2
    quarter = R.hid.shape[1]

    mixed, yr, xr, gu_w, down_w = range(5)
    streams = ((R.mixed, R.mixed_now), (R.yr, R.yr_now), (R.xr, R.xr_now), (R.gu_w, R.gu_now), (R.down_w, R.down_now))

    def load(which, l):
        return pltpu.make_async_copy(streams[which][0][l], streams[which][1], R.load.at[which])

    for which in range(5):
        load(which, layers - 1).start()
    at.enter()

    gather_df = HeadGather(at, R.df, R.df_send, R.df_recv)
    gather_da = HeadGather(at, R.da, R.da_send, R.da_recv)
    part = R.part
    head_sum = HeadSum(at, part, R.hs_stage, R.hs_in, R.hs_send, R.hs_recv)

    if host:
        ff_sum, at_sum, ow_sum = [[BlockSum(at, item) for item in items] for items in (R.ff, R.at, R.ow)]

    def small(l, t):
        return R.small[8 * l + t : 8 * l + t + 1, :]

    def put_small(l, t, value):
        R.tok_small[8 * l + t : 8 * l + t + 1, :] = value

    def of(buf, half):
        v = buf[pl.ds(2 * half, 2)]
        return v.reshape(half_rows, v.shape[2])

    def half_at(half):
        return pl.ds(pl.multiple_of(half * half_rows, half_rows), half_rows)

    def wgrad(left, right, stage, lo):
        step = stage.shape[1]
        for first in range(0, left.shape[1], 384):
            for col in range(0, right.shape[1], 768):
                width = min(768, right.shape[1] - col)
                v = dot(left[:, first : first + 384], right[:, col : col + width], TN)
                for i in range(384 // step):
                    stage[first // step + i, :, lo + col : lo + col + width] = v[step * i : step * i + step].astype(BF)

    def emit_ff(l):
        def emit(v):
            R.gu_sum[l][...] = v[:, : 2 * quarter].astype(BF)
            R.down_sum[l][...] = v[:, 2 * quarter :]
        ff_sum[l].total(emit)

    def emit_at(l):
        def emit(v):
            R.qkv_sum[l][...] = v.astype(BF)

        def emit_out(v):
            R.out_sum[l][...] = v
        at_sum[l].total(emit)
        ow_sum[l].total(emit_out)

    R.g[...] = R.grad[...].astype(F32)
    for l in reversed(range(layers)):
        top = l == layers - 1
        relay_before = host and not top
        e2, d_gain, d_shift = norm_back(R.g[...], R.sum2[l][...], small(l, 1))
        put_small(l, 1, d_gain)
        put_small(l, 5, d_shift)
        low = e2.astype(BF)
        put_small(l, 4, jnp.sum(low.astype(F32), axis=0, keepdims=True))
        if not top:
            head_sum.finish()
        R.df[at.head] = low
        gather_df.start()
        R.e2[...] = e2
        for which in range(5):
            load(which, l).wait()
        if relay_before:
            ff_sum[l + 1].relay_one(at.turn(0))
        gather_df.wait_near()
        for number, half in enumerate((at.y, 1 - at.y)):
            if number == 1:
                gather_df.wait_far()
                if relay_before:
                    ff_sum[l + 1].relay_one(at.turn(1))
            here = half_at(half)
            df_half = of(R.df, half)
            for col in range(0, quarter, 256):
                dhid = dot(df_half, R.down_now[col : col + 256, :], NT)
                gate = R.mixed_now[here, col : col + 256]
                up = R.mixed_now[here, quarter + col : quarter + col + 256]
                cdf = normal_cdf(gate)
                act = gate * cdf
                R.hid[here, col : col + 256] = (act * up).astype(BF)
                R.dgu[here, col : col + 256] = (dhid * up * (cdf + gate * normal_pdf(gate))).astype(BF)
                R.dgu[here, quarter + col : quarter + col + 256] = (dhid * act).astype(BF)
            dy = dot(R.dgu[here, :], R.gu_now[...], NT)
            part[pl.ds(2 * half, 2)] = dy.reshape(2, half_rows // 2, dy.shape[1])
            if number == 0:
                head_sum.send_near()
            else:
                head_sum.send_cross()
        ff_stage = R.ff[l].stage
        wgrad(R.hid, R.df[...].reshape(rows, -1), ff_stage, 2 * quarter)
        head_sum.relay()
        if relay_before:
            def rest(i, carry):
                ff_sum[l + 1].relay_one(at.turn(i))
                return carry
            lax.fori_loop(2, at.nz - 1, rest, 0)
        dy = R.e2[...] + head_sum.total()
        e1, d_gain, d_shift = norm_back(dy, R.sum1[l][...], small(l, 0))
        put_small(l, 0, d_gain)
        put_small(l, 3, d_shift)
        low = e1.astype(BF)
        put_small(l, 2, jnp.sum(low.astype(F32), axis=0, keepdims=True))
        R.da[at.head] = low
        gather_da.start()
        R.e1[...] = e1
        wgrad(R.yr_now, R.dgu, ff_stage, 0)
        gather_da.wait_near()
        gather_da.wait_far()
        if l > 0:
            for which in (mixed, yr, gu_w, down_w):
                load(which, l - 1).start()
        da_all = R.da[...].reshape(rows, -1)
        dctx = dot(da_all, R.out_w[l][...], NT).astype(BF)
        d_out = dot(R.ctx[l][...], da_all, TN)
        if host:
            step = d_out.shape[0] // nb
            for b in range(nb):
                R.ow[l].stage[b] = jnp.concatenate(
                    [d_out[step * b : step * b + step], jnp.zeros((OW_ROWS - step, d_out.shape[1]), F32)]).astype(BF)
        else:
            R.ow[l].stage[...] = d_out.astype(BF)
        ctxf = R.ctxf[l]
        wide = dctx.astype(F32)
        first_two = wide[:, :128]
        third = jnp.concatenate([jnp.zeros((rows, 64), F32), wide[:, 128:192]], axis=1)
        prod = first_two * ctxf[:, :128]
        low_half = in_half(0, rows)
        deltas = [
            jnp.sum(jnp.where(low_half, prod, 0.0), axis=1, keepdims=True),
            jnp.sum(jnp.where(low_half, 0.0, prod), axis=1, keepdims=True),
            jnp.sum(wide[:, 128:192] * ctxf[:, 128:192], axis=1, keepdims=True),
        ]
        for h in range(3):
            half = V_AT[h][1]
            base = jnp.where(in_half(half, rows), first_two if h < 2 else third, 0.0)
            R.do[h] = with_lanes(base, 0 if half else 64, split3(-deltas[h])).astype(BF)

        def ff_start(l=l):
            if host:
                ff_sum[l].start()

        def after_first(l=l, relay_before=relay_before):
            if relay_before:
                at_sum[l + 1].relay()
                ow_sum[l + 1].relay()
        attn_back(at, R, l, None, top, ff_start, after_first)
        dproj = R.dproj
        R.bias_sum[l : l + 1, :] = jnp.sum(dproj[...].astype(F32), axis=0, keepdims=True)
        gather_df.finish()
        gather_da.finish()
        head_sum.finish()
        for number, half in enumerate((1 - at.y, at.y)):
            dx = dot(dproj[half_at(half), :], R.qkv_w[l][...], NT)
            part[pl.ds(2 * half, 2)] = dx.reshape(2, half_rows // 2, dx.shape[1])
            if number == 0:
                head_sum.send_cross()
            else:
                head_sum.send_near()
        head_sum.relay()
        wgrad(R.xr_now, dproj, R.at[l].stage, 0)
        if host:
            at_sum[l].start()
            ow_sum[l].start()
        if l > 0:
            load(xr, l - 1).start()
        if relay_before:
            emit_ff(l + 1)
            emit_at(l + 1)
        R.g[...] = R.e1[...] + head_sum.total()
    R.grad_in[...] = R.g[...]
    head_sum.finish()
    if host:
        ff_sum[0].relay()
        at_sum[0].relay()
        ow_sum[0].relay()
        emit_ff(0)
        emit_at(0)
        for l in range(layers):
            ff_sum[l].finish()
            at_sum[l].finish()
            ow_sum[l].finish()


def block_sum_item(nb, *dims):
    nz = nb // 2
    return dict(stage=keep(nb, *dims), xin=keep(nz, *dims), zin=keep(nz, *dims),
                xsend=copies(nz), xrecv=copies(nz), zsend=copies(nz), zrecv=copies(nz))


def bwd(grad, small, kaug, saved, host):
    layers = len(saved.qkv_w)
    nb, rows = kaug.shape[:2]
    nz = nb // 2
    tokens, width = grad.shape
    group3 = saved.qkv_w[0].shape[1]
    quarter = saved.down_w[0].shape[0]
    r = width // nb
    ff_width = 2 * quarter + width
    each = range(layers)
    slots = min(nz, 4)
    out = dict(grad_in=shape(tokens, width, dtype=F32), tok_small=shape(8 * layers, width, dtype=F32),
               bias_sum=shape(layers, group3, dtype=F32))
    scratch = {}
    if host:
        out.update(
            gu_sum=[shape(r, 2 * quarter) for _ in each], down_sum=[shape(r, width, dtype=F32) for _ in each],
            qkv_sum=[shape(r, group3) for _ in each], out_sum=[shape(OW_ROWS, width, dtype=F32) for _ in each])
        scratch.update(
            ff=[block_sum_item(nb, r, ff_width) for _ in each], at=[block_sum_item(nb, r, group3) for _ in each],
            ow=[block_sum_item(nb, OW_ROWS, width) for _ in each])
    else:
        out.update(
            ff=[dict(stage=shape(nb, r, ff_width)) for _ in each], at=[dict(stage=shape(nb, r, group3)) for _ in each],
            ow=[dict(stage=shape(group3 // 3, width)) for _ in each])
    like = lambda arrays: keep(*arrays[0].shape, dtype=arrays[0].dtype)
    scratch.update(
        mixed_now=like(saved.mixed), yr_now=like(saved.yr), xr_now=like(saved.xr), gu_now=like(saved.gu_w),
        down_now=like(saved.down_w), load=copies(5), kvbuf=keep(2, rows, 384), kvsem=copies(2),
        df=keep(4, tokens, width), df_send=copies(3), df_recv=copies(3),
        da=keep(4, tokens, width), da_send=copies(3), da_recv=copies(3),
        part=keep(4, tokens, width, dtype=F32),
        hs_stage=keep(3, tokens, width), hs_in=keep(3, tokens, width), hs_send=copies(3), hs_recv=copies(3),
        g=keep(tokens, width, dtype=F32), e1=keep(tokens, width, dtype=F32), e2=keep(tokens, width, dtype=F32),
        hid=keep(rows, quarter), dgu=keep(rows, 2 * quarter), do=keep(3, rows, 128),
        dqacc=keep(3, rows, 128, dtype=F32), dkv_acc=keep(rows, 384, dtype=F32), dproj=keep(rows, group3),
        dkv=dict(stage=keep(slots, 2, rows, 384), xin=keep(nz, rows, 384), zin=keep(nz, rows, 384), xsend=copies(nz),
                 xrecv=copies(nz), zsend=copies(nz), zrecv=copies(nz), free=pltpu.SemaphoreType.REGULAR))
    near = dict(grad=grad, small=small, kaug=kaug, sum1=saved.sum1, sum2=saved.sum2, ctx=saved.ctx, ctxf=saved.ctxf,
                qb=saved.qb, out_w=saved.out_w, qkv_w=saved.qkv_w)
    far = dict(mixed=saved.mixed, yr=saved.yr, xr=saved.xr, gu_w=saved.gu_w, down_w=saved.down_w, kv=saved.kv)
    return call(functools.partial(bwd_kernel, nb, layers, host), "backward", 1, near=near, far=far, out=out, scratch=scratch)


def three(value):
    high = lax.reduce_precision(value, 8, 7)
    rest = value - high
    mid = lax.reduce_precision(rest, 8, 7)
    return [part.astype(BF) for part in (high, mid, rest - mid)]


def shards(hidden_in, out_grad, segment_ids, alibi_slopes, qkv_weight, out_weight, gate_up_weight, down_weight, gains, biases):
    nh, nb = lax.axis_size("head"), lax.axis_size("blk")
    head, blk = lax.axis_index("head"), lax.axis_index("blk")
    token_rows, width = hidden_in.shape
    rows = token_rows * nh
    layers, wrows = qkv_weight.shape[:2]
    ff = gate_up_weight.shape[2] // 2
    ffd = down_weight.shape[1]
    group = width // nh
    quarter = ff // nh
    tokens = segment_ids.shape[0]
    qk = 3 * group
    host = (width // nb) % 16 == 0

    def to_groups(w):
        w = w.reshape(layers, wrows, 3, nh, 3, 64)
        q, k, v = w[:, :, 0], w[:, :, 1], w[:, :, 2]
        kv = jnp.stack([k[..., 0, :], k[..., 1, :], v[..., 0, :], v[..., 1, :], k[..., 2, :], v[..., 2, :]], axis=3)
        return jnp.concatenate([kv, q], axis=3).reshape(layers, wrows, nh, qk)

    def from_groups(g):
        g = g.reshape(layers, nh, wrows, 9, 64)
        pick = lambda *index: jnp.stack([g[:, :, :, i] for i in index], axis=3)
        all3 = jnp.stack([pick(6, 7, 8), pick(0, 1, 4), pick(2, 3, 5)], axis=1)
        return all3.transpose(0, 3, 1, 2, 4, 5).reshape(layers, wrows, 3 * width)

    small = jnp.concatenate([gains, biases], axis=1).transpose(0, 2, 1)
    small = jnp.concatenate([small[l] for l in range(layers)], axis=1)
    small = jnp.pad(small, ((0, 0), (0, 64 - small.shape[1])))
    small = jnp.broadcast_to(small[:, None], (wrows, nh, 64))
    gu_cols = gate_up_weight.reshape(layers, wrows, 2, nb, nh, ffd).transpose(0, 1, 4, 2, 3, 5).reshape(layers, wrows, nh, 2 * quarter)
    qkv_cols = to_groups(qkv_weight)
    pieces = [qkv_cols[0], small] + [qkv_cols[l] for l in range(1, layers)] + [gu_cols[l] for l in range(layers)]
    spread = lax.all_to_all(jnp.concatenate(pieces, axis=2), "head", split_axis=1, concat_axis=0, tiled=True)
    spread = spread.reshape(nh * wrows, -1)
    qkv0 = spread[:, : qk + 64]
    qkv_own = [qkv0] + [spread[:, qk * l + 64 : qk * l + qk + 64] for l in range(1, layers)]
    gu0 = qk * layers + 64
    gu_own = [spread[:, gu0 + 2 * quarter * l : gu0 + 2 * quarter * (l + 1)] for l in range(layers)]
    moves = [(b * nh + h, h * nb + b) for b in range(nb) for h in range(nh)]
    ow_own = lax.ppermute(out_weight, ("blk", "head"), [(target, source) for source, target in moves])
    if host:
        weights = types.SimpleNamespace(qkv_own=qkv_own, gu_own=gu_own, down_own=[down_weight[l] for l in range(layers)],
                                        ow_own=ow_own.reshape(layers * wrows, width))
    else:
        whole = lambda v: lax.all_gather(v, "blk", axis=0, tiled=True)
        qkv_all = [whole(v) for v in qkv_own]
        out_all = lax.all_gather(ow_own, "blk", axis=1, tiled=True)
        weights = types.SimpleNamespace(
            qkv_given=[v[:, :qk] for v in qkv_all], gu_given=[whole(v) for v in gu_own],
            down_given=[whole(down_weight[l]) for l in range(layers)], out_given=[out_all[l] for l in range(layers)],
            small_given=qkv_all[0][:, qk : qk + 8 * layers].astype(F32).T)

    slopes = lax.dynamic_slice_in_dim(alibi_slopes, head * 3, 3, 0)
    position = jnp.arange(tokens, dtype=jnp.int32).astype(F32)
    same = (segment_ids[:, None] == jnp.arange(5, dtype=jnp.int32)[None, :])
    apart = [jnp.where(same[:, s], 0.0, -1e30).astype(BF) for s in range(5)]
    one = jnp.ones((tokens,), BF)
    columns = [part for h in range(3) for part in three(slopes[h] * position)] + [one] * 3 + apart
    columns = jnp.pad(jnp.stack(columns, axis=-1), ((0, 0), (0, 64 - len(columns))))
    kaug = jnp.concatenate([columns, columns], axis=1).reshape(nb, rows, 128)
    inside = lax.dynamic_slice_in_dim(same, blk * rows, rows, 0).astype(BF)
    qaug = []
    for sign in (1.0, -1.0):
        for h in range(3):
            ones = [jnp.full((rows,), sign if i // 3 == h else 0.0, BF) for i in range(9)]
            a = jnp.concatenate([jnp.stack(ones, axis=-1), jnp.zeros((rows, 3), BF), inside, jnp.zeros((rows, 47), BF)], axis=1)
            qaug.append(jnp.concatenate([a, a], axis=1))
    qaug = jnp.stack(qaug).reshape(2, 3, rows, 128)

    saved = fwd(hidden_in, slopes, qaug, kaug, weights, layers, host)
    done = bwd(out_grad, saved.small, kaug, saved, host)
    if not host:
        done.gu_sum, done.down_sum, done.qkv_sum, done.out_sum = [], [], [], []
        for l in range(layers):
            ff_sum, at_sum, ow_sum = [
                lax.psum_scatter(items[l].stage.reshape(width, -1), "blk", scatter_dimension=0, tiled=True)
                for items in (done.ff, done.at, done.ow)]
            done.gu_sum.append(ff_sum[:, : 2 * quarter])
            done.down_sum.append(ff_sum[:, 2 * quarter :])
            done.qkv_sum.append(at_sum)
            done.out_sum.append(ow_sum.reshape(wrows, width))

    tok_small = done.tok_small.reshape(layers, 8, width)
    bias_sum = done.bias_sum
    rows_of = jnp.zeros((layers, 2, width), F32)
    dqb = bias_sum[:, 384:]
    dvb = jnp.concatenate([bias_sum[:, 128:256], bias_sum[:, 320:384]], axis=1)
    rows_of = lax.dynamic_update_slice_in_dim(rows_of, jnp.stack([dqb, dvb], axis=1), head * group, 2)
    small_g = jnp.concatenate([tok_small[:, :6], rows_of], axis=1)
    small_g = small_g.reshape(layers * 8, nb * nh, wrows).transpose(1, 0, 2).reshape(nb * nh, layers * 8 * wrows)
    small_sum = lax.psum_scatter(small_g, ("blk", "head"), scatter_dimension=0, tiled=True).reshape(layers, 8, wrows)
    gains_grad = small_sum[:, 0:2]
    biases_grad = jnp.concatenate([small_sum[:, 6:8], small_sum[:, 2:6]], axis=1)

    back = jnp.concatenate([jnp.stack(done.qkv_sum), jnp.stack(done.gu_sum)], axis=2).reshape(layers, nh, wrows, -1)
    back = lax.all_to_all(back, "head", split_axis=1, concat_axis=1, tiled=True).astype(F32)
    qkv_grad = from_groups(back[..., :qk])
    gu_grad = back[..., qk:].reshape(layers, nh, wrows, 2, nb, ffd).transpose(0, 2, 3, 4, 1, 5).reshape(layers, wrows, 2 * ff)
    out_grad_w = lax.ppermute(jnp.stack(done.out_sum)[:, :wrows], ("blk", "head"), moves).astype(F32)
    return saved.output, done.grad_in, qkv_grad, out_grad_w, gu_grad, jnp.stack(done.down_sum).astype(F32), gains_grad, biases_grad


def solution(mesh):
    both = ("blk", "head")
    tok, mid, last = P(both, None), P(None, both, None), P(None, None, both)
    return jax.shard_map(
        shards, mesh=mesh,
        in_specs=(tok, tok, P(), P(), mid, mid, mid, mid, last, last),
        out_specs=(tok, tok, mid, mid, mid, mid, last, last),
        check_vma=False,
    )
```

```python
import functools
import types

import jax
import jax.numpy as jnp
from jax import lax
from jax.experimental import pallas as pl
from jax.experimental.pallas import tpu as pltpu
from jax.sharding import Mesh
from jax.sharding import PartitionSpec as P

MESH = pl.DeviceIdType.MESH
BF = jnp.bfloat16
F32 = jnp.float32
NT = (((1,), (1,)), ((), ()))
NN = (((1,), (0,)), ((), ()))
TN = (((0,), (0,)), ((), ()))
EPS = 1e-06
K_AT = ((0, 0), (0, 1), (2, 0))
V_AT = ((1, 0), (1, 1), (2, 1))
ROW_LANE, SEGMENT_LANE = 9, 12
OW_ROWS = 32
VMEM = pl.BlockSpec(memory_space=pltpu.VMEM)
ANY = pl.BlockSpec(memory_space=pl.ANY)


def dot(a, b, dims=NN):
    return lax.dot_general(a, b, dims, preferred_element_type=F32)


def lanes(rows):
    return lax.broadcasted_iota(jnp.int32, (rows, 128), 1)


def in_half(half, rows):
    return lanes(rows) >= 64 if half else lanes(rows) < 64


def ones_half(half, rows):
    first = 0 if half else 64
    lane = lanes(rows)
    return jnp.where((lane >= first) & (lane < first + 3), 1.0, 0.0).astype(BF)


def k_operand(kv, aug, h):
    col, half = K_AT[h]
    return jnp.where(in_half(half, kv.shape[0]), kv[:, 128 * col : 128 * col + 128], aug)


def v_operand(kv, h):
    col, half = V_AT[h]
    rows = kv.shape[0]
    return jnp.where(in_half(half, rows), kv[:, 128 * col : 128 * col + 128], ones_half(half, rows))


def split3(value):
    high = value.astype(BF).astype(F32)
    mid = (value - high).astype(BF).astype(F32)
    return high, mid, value - high - mid


def with_lanes(base, first, values):
    lane = lanes(base.shape[0])
    for i, v in enumerate(values):
        base = jnp.where(lane == first + i, v, base)
    return base


def layer_norm(total, gain, shift):
    centred = total - jnp.mean(total, axis=-1, keepdims=True)
    scale = lax.rsqrt(jnp.mean(centred * centred, axis=-1, keepdims=True) + EPS)
    return centred * scale * gain + shift


def norm_back(grad, total, gain):
    centred = total - jnp.mean(total, axis=-1, keepdims=True)
    scale = lax.rsqrt(jnp.mean(centred * centred, axis=-1, keepdims=True) + EPS)
    n = centred * scale
    dn = grad * gain
    e = scale * (dn - jnp.mean(dn, axis=-1, keepdims=True) - n * jnp.mean(dn * n, axis=-1, keepdims=True))
    return e, jnp.sum(grad * n, axis=0, keepdims=True), jnp.sum(grad, axis=0, keepdims=True)


def normal_cdf(u):
    return 0.5 * (1.0 + lax.erf(u * (0.5**0.5)))


def normal_pdf(u):
    return jnp.exp(-0.5 * u * u) * ((2.0 * jnp.pi) ** -0.5)


def remote(src, dst, send, recv, device):
    return pltpu.make_async_remote_copy(
        src_ref=src, dst_ref=dst, send_sem=send, recv_sem=recv, device_id=device, device_id_type=MESH)


def loop(first, last, do):
    def step(i, carry):
        do(i)
        return carry
    lax.fori_loop(first, last, step, 0)


class Place:
    def __init__(self, nz):
        self.nz = nz
        self.z, self.x, self.y, self.c = [lax.axis_index(name) for name in "zxyc"]
        self.g = 2 * self.x + self.y
        self.gx, self.gy = 2 * (1 - self.x) + self.y, 2 * self.x + 1 - self.y
        self.gd = 2 * (1 - self.x) + 1 - self.y
        self.oc = 1 - self.c
        self.beside = (self.z, self.x, self.y, self.oc)
        self.across_x = (self.z, 1 - self.x, self.y, self.c)
        self.across_y = (self.z, self.x, 1 - self.y, self.c)
        self.block = 2 * self.z + self.c
        self.has_left, self.has_right = self.z > 0, self.z < nz - 1

    def column(self, zz):
        return (zz, self.x, self.y, self.c)

    def neighbours(self):
        return 3 - (self.z == 0).astype(jnp.int32) - (self.z == self.nz - 1).astype(jnp.int32)

    def signal_neighbours(self, semaphore):
        pl.semaphore_signal(semaphore, inc=1, device_id=self.beside, device_id_type=MESH)

        @pl.when(self.has_left)
        def _():
            pl.semaphore_signal(semaphore, inc=1, device_id=self.column(self.z - 1), device_id_type=MESH)

        @pl.when(self.has_right)
        def _():
            pl.semaphore_signal(semaphore, inc=1, device_id=self.column(self.z + 1), device_id_type=MESH)

    def enter(self):
        barrier = pltpu.get_barrier_semaphore()
        for device in (self.across_x, self.across_y):
            pl.semaphore_signal(barrier, inc=1, device_id=device, device_id_type=MESH)
        self.signal_neighbours(barrier)
        pl.semaphore_wait(barrier, 2 + self.neighbours())

    def positions(self, zz, cc, tokens, rows):
        row = lax.broadcasted_iota(jnp.int32, (rows, 128), 0)
        return ((zz * 8 + (row // tokens) * 2 + cc) * tokens + row % tokens).astype(F32)


class SquareGather:
    def __init__(self, at, buf, send, recv):
        half = buf.shape[1] // 2
        first, second = pl.ds(0, half), pl.ds(half, half)
        own = buf.at[at.g]
        self.to_x = remote(own, own, send.at[0], recv.at[0], at.across_x)
        self.to_y = remote(own, own, send.at[1], recv.at[1], at.across_y)
        self.on_y = remote(buf.at[at.gx, first], buf.at[at.gx, first], send.at[2], recv.at[2], at.across_y)
        self.on_x = remote(buf.at[at.gy, second], buf.at[at.gy, second], send.at[3], recv.at[3], at.across_x)

    def start(self):
        self.to_x.start()
        self.to_y.start()

    def wait_near(self):
        self.to_x.wait_recv()
        self.on_y.start()
        self.to_y.wait_recv()
        self.on_x.start()

    def wait_far(self):
        self.on_x.wait_recv()
        self.on_y.wait_recv()

    def finish(self):
        for copy in (self.to_x, self.to_y, self.on_x, self.on_y):
            copy.wait_send()


class SquareSum:
    def __init__(self, at, part, pair, single, send, recv):
        self.at, self.part = at, part
        self.pair, self.single = pair, single
        self.half = part.shape[2] // 2
        to = (at.across_x, at.across_y, at.across_y, at.across_y, at.across_x)
        refs = [(pair.stage, pair.inbox)] + [(single.stage.at[i], single.inbox.at[i]) for i in range(4)]
        self.copies = [remote(refs[i][0], refs[i][1], send.at[i], recv.at[i], to[i]) for i in range(5)]

    def left(self, g):
        return self.part[g, :, : self.half]

    def right(self, g):
        return self.part[g, :, self.half :]

    def send_far(self):
        at = self.at
        self.pair.stage[...] = self.part[pl.ds(2 * (1 - at.x), 2), :, : self.half].astype(BF)
        self.copies[0].start()
        self.single.stage[1] = self.right(at.gd).astype(BF)
        self.copies[2].start()

    def send_near(self):
        self.single.stage[0] = self.right(self.at.gy).astype(BF)
        self.copies[1].start()

    def relay(self):
        at = self.at
        self.copies[0].wait_recv()
        self.single.stage[2] = (self.left(at.gy) + self.pair.inbox[1 - at.y].astype(F32)).astype(BF)
        self.copies[3].start()
        self.copies[2].wait_recv()
        self.single.stage[3] = (self.right(at.gx) + self.single.inbox[1].astype(F32)).astype(BF)
        self.copies[4].start()

    def total(self):
        at = self.at
        self.copies[1].wait_recv()
        left = self.left(at.g) + self.pair.inbox[at.y].astype(F32)
        right = self.right(at.g) + self.single.inbox[0].astype(F32)
        self.copies[3].wait_recv()
        self.copies[4].wait_recv()
        return jnp.concatenate(
            [left + self.single.inbox[2].astype(F32), right + self.single.inbox[3].astype(F32)], axis=1)

    def finish(self):
        for copy in self.copies:
            copy.wait_send()


class BlockGather:
    def __init__(self, at, item):
        self.at, self.buf, self.zsend, self.csend, self.recv = at, item.buf, item.zsend, item.csend, item.recv

    def copy(self, zz, send, device):
        at = self.at
        return remote(self.buf.at[zz, at.c], self.buf.at[zz, at.c], send, self.recv.at[zz, at.c], device)

    def to_right(self, zz):
        return self.copy(zz, self.zsend.at[0, zz], self.at.column(self.at.z + 1))

    def to_left(self, zz):
        return self.copy(zz, self.zsend.at[1, zz], self.at.column(self.at.z - 1))

    def to_beside(self, zz):
        return self.copy(zz, self.csend.at[zz], self.at.beside)

    def wait(self, zz, cc):
        at = self.at
        remote(self.buf.at[zz, cc], self.buf.at[zz, cc], self.csend.at[zz], self.recv.at[zz, cc], at.beside).wait_recv()

    def put(self, value):
        self.buf[self.at.z, self.at.c] = value

    def start(self):
        at = self.at

        @pl.when(at.has_right)
        def _():
            self.to_right(at.z).start()

        @pl.when(at.has_left)
        def _():
            self.to_left(at.z).start()
        self.to_beside(at.z).start()

    def serve(self, d):
        at = self.at

        @pl.when(at.z - d >= 0)
        def _():
            self.wait(at.z - d, at.c)

            @pl.when(at.has_right)
            def _():
                self.to_right(at.z - d).start()
            self.to_beside(at.z - d).start()

        @pl.when(at.z + d < at.nz)
        def _():
            self.wait(at.z + d, at.c)

            @pl.when(at.has_left)
            def _():
                self.to_left(at.z + d).start()
            self.to_beside(at.z + d).start()

    def serve_all(self):
        loop(1, self.at.nz, self.serve)

    def collect(self):
        loop(0, self.at.nz, lambda zz: self.wait(zz, self.at.oc))

    def finish(self):
        at = self.at

        def drain(zz):
            self.to_beside(zz).wait_send()

            @pl.when((zz <= at.z) & at.has_right)
            def _():
                self.to_right(zz).wait_send()

            @pl.when((zz >= at.z) & at.has_left)
            def _():
                self.to_left(zz).wait_send()
        loop(0, at.nz, drain)


def block_gather_item(nz, *dims):
    return dict(buf=keep(nz, 2, *dims), zsend=copies(2, nz), csend=copies(nz), recv=copies(nz, 2))


class BlockSum:
    def __init__(self, at, item):
        self.at, self.stage, self.cin, self.zin = at, item.stage, item.cin, item.zin
        self.csend, self.crecv, self.zsend, self.zrecv = item.csend, item.crecv, item.zsend, item.zrecv

    def to_beside(self, t):
        return remote(self.stage.at[t, self.at.oc], self.cin.at[t], self.csend.at[t], self.crecv.at[t], self.at.beside)

    def to_right(self, t):
        return remote(self.stage.at[t, self.at.c], self.zin.at[t + 1], self.zsend.at[t], self.zrecv.at[t + 1], self.at.column(self.at.z + 1))

    def to_left(self, t):
        return remote(self.stage.at[t, self.at.c], self.zin.at[t], self.zsend.at[t], self.zrecv.at[t], self.at.column(self.at.z - 1))

    def arrived(self, slot):
        at = self.at
        remote(self.zin.at[slot], self.zin.at[slot], self.zsend.at[0], self.zrecv.at[slot], at.beside).wait_recv()

    def start(self):
        loop(0, self.at.nz, lambda t: self.to_beside(t).start())

    def add(self, t, slot=None):
        value = self.stage[t, self.at.c].astype(F32) + self.cin[t].astype(F32)
        if slot is not None:
            value = value + self.zin[slot].astype(F32)
        self.stage[t, self.at.c] = value.astype(self.stage.dtype)

    def go_right(self, t):
        self.to_beside(t).wait_recv()

        @pl.when(self.at.has_left)
        def _():
            self.arrived(t + 1)
            self.add(t, t + 1)

        @pl.when(jnp.logical_not(self.at.has_left))
        def _():
            self.add(t)
        self.to_right(t).start()

    def go_left(self, t):
        self.to_beside(t).wait_recv()

        @pl.when(self.at.has_right)
        def _():
            self.arrived(t)
            self.add(t, t)

        @pl.when(jnp.logical_not(self.at.has_right))
        def _():
            self.add(t)
        self.to_left(t).start()

    def serve(self, p, source=True, relay=True):
        at = self.at
        right, left = p - at.z, p - (at.nz - 1 - at.z)
        go_r = (right >= 0) & (right < at.nz - 1 - at.z)
        go_l = (left >= 0) & (left < at.z)
        if not source:
            go_r, go_l = go_r & at.has_left, go_l & at.has_right
        if not relay:
            go_r, go_l = go_r & jnp.logical_not(at.has_left), go_l & jnp.logical_not(at.has_right)

        @pl.when(go_r)
        def _():
            self.go_right(at.nz - 1 - right)

        @pl.when(go_l)
        def _():
            self.go_left(left)

    def total(self):
        at = self.at
        self.to_beside(at.z).wait_recv()

        @pl.when(at.has_left)
        def _():
            self.arrived(at.z + 1)

        @pl.when(at.has_right)
        def _():
            self.arrived(at.z)
        value = self.stage[at.z, at.c].astype(F32) + self.cin[at.z].astype(F32)
        from_left = jnp.where(at.has_left, self.zin[at.z + 1].astype(F32), 0.0)
        from_right = jnp.where(at.has_right, self.zin[at.z].astype(F32), 0.0)
        return value + from_left + from_right

    def finish(self):
        at = self.at

        def drain(t):
            self.to_beside(t).wait_send()

            @pl.when(t > at.z)
            def _():
                self.to_right(t).wait_send()

            @pl.when(t < at.z)
            def _():
                self.to_left(t).wait_send()
        loop(0, at.nz, drain)


def box(tree):
    if isinstance(tree, dict):
        return types.SimpleNamespace(**{k: box(v) for k, v in tree.items()})
    return [box(v) for v in tree] if isinstance(tree, list) else tree


def call(body, name, collective_id, near=None, far=None, table=None, out=None, far_out=None, scratch=None):
    groups = [near or {}, far or {}, table or {}, out or {}, far_out or {}, scratch or {}]
    flat, trees = zip(*[jax.tree.flatten(g) for g in groups])
    counts = [len(f) for f in flat]

    def kernel(*refs):
        named, first = {}, 0
        for tree, count in zip(trees, counts):
            named.update(jax.tree.unflatten(tree, refs[first : first + count]))
            first += count
        body(box(named))

    smem = pl.BlockSpec(memory_space=pltpu.SMEM)
    results = pl.pallas_call(
        kernel,
        out_shape=tuple(flat[3]) + tuple(flat[4]),
        in_specs=[VMEM] * counts[0] + [ANY] * counts[1] + [smem] * counts[2],
        out_specs=(VMEM,) * counts[3] + (ANY,) * counts[4],
        scratch_shapes=list(flat[5]),
        compiler_params=pltpu.CompilerParams(
            collective_id=collective_id, has_side_effects=True, vmem_limit_bytes=63 * 2**20),
        cost_estimate=pl.CostEstimate(flops=10**11, bytes_accessed=2 * 10**8, transcendentals=10**7),
        name=name,
    )(*flat[0], *flat[1], *flat[2])
    done = jax.tree.unflatten(trees[3], results[: counts[3]])
    done.update(jax.tree.unflatten(trees[4], results[counts[3] :]))
    return box(done)


def shape(*dims, dtype=BF):
    return jax.ShapeDtypeStruct(dims, dtype)


def keep(*dims, dtype=BF):
    return pltpu.VMEM(dims, dtype)


def copies(*dims):
    return pltpu.SemaphoreType.DMA(dims)


def square_sum_items(tokens, width):
    half = width // 2
    return dict(
        pair=dict(stage=keep(2, tokens, half), inbox=keep(2, tokens, half)),
        single=dict(stage=keep(4, tokens, half), inbox=keep(4, tokens, half)), ss_send=copies(5), ss_recv=copies(5))


def flat_weight(ref, lo=0, hi=None):
    if len(ref.shape) == 2:
        return ref[:, lo:hi]
    v = ref[:, :, :, lo:hi]
    return v.reshape(v.shape[0] * v.shape[1] * v.shape[2], v.shape[3])


def side_weight(ref, cc, lo=0, hi=None):
    v = ref[:, cc, :, lo:hi]
    return v.reshape(v.shape[0] * v.shape[1], v.shape[2])


def block_sum_item(nz, *dims, dtype=BF):
    return dict(stage=keep(nz, 2, *dims, dtype=dtype), cin=keep(nz, *dims, dtype=dtype), zin=keep(nz + 1, *dims, dtype=dtype),
                csend=copies(nz), crecv=copies(nz), zsend=copies(nz), zrecv=copies(nz + 1))


def key_columns(at, slopes, seg, zz, cc, tokens):
    rows = 4 * tokens
    column = lax.broadcasted_iota(jnp.int32, (128, rows), 0) % 64
    row = lax.broadcasted_iota(jnp.int32, (128, rows), 1)
    position = ((zz * 8 + (row // tokens) * 2 + cc) * tokens + row % tokens).astype(F32)
    value = jnp.where(seg[2 * zz + cc] == column - SEGMENT_LANE, 0.0, -1e30)
    value = jnp.where(column < SEGMENT_LANE + 5, value, 0.0)
    value = jnp.where(column < SEGMENT_LANE, 1.0, value)
    for h in range(3):
        for i, term in enumerate(split3(position * slopes[3 * at.g + h])):
            value = jnp.where(column == 3 * h + i, term, value)
    return value.T.astype(BF)


def segment_columns(at, seg, rows):
    column = lax.broadcasted_iota(jnp.int32, (128, rows), 0) % 64
    return jnp.where(seg[at.block] == column - SEGMENT_LANE, 1.0, 0.0).T


def query_operand(at, q_ref, inside, slopes, side, h, tokens, lse=None):
    rows = 4 * tokens
    if h < 2:
        data = q_ref[:, 0:128]
    else:
        data = jnp.concatenate([q_ref[:, 128:192], jnp.zeros((rows, 64), q_ref.dtype)], axis=1)
    half = K_AT[h][1]
    sign = 1.0 if side == 0 else -1.0
    column = lanes(rows) % 64
    aug = jnp.where((column >= 3 * h) & (column < 3 * h + 3), sign, inside[...])
    term = at.positions(at.z, at.c, tokens, rows) * (slopes[3 * at.g + h] * -sign)
    if lse is not None:
        term = term - lse
    aug = with_lanes(aug, ROW_LANE if half else 64 + ROW_LANE, split3(term))
    return jnp.where(in_half(half, rows), data.astype(F32) * 0.125, aug).astype(BF)


def attention(at, gather, q_op, kaug, m_ref, acc_ref, behind):
    m_ref[...] = jnp.full(m_ref.shape, -1e30, F32)
    acc_ref[...] = jnp.zeros(acc_ref.shape, F32)

    def compute(zz, cc, same):
        kv, aug = gather.buf.at[zz, cc], kaug[zz, cc]
        side = (zz > at.z).astype(jnp.int32)
        for h in range(3):
            k = k_operand(kv, aug, h)
            if same:
                s = jnp.minimum(dot(q_op[0, h], k, NT), dot(q_op[1, h], k, NT))
            else:
                s = dot(q_op[side, h], k, NT)
            m_old = m_ref[h]
            m_new = jnp.maximum(m_old, jnp.max(s, axis=1, keepdims=True))
            p = jnp.exp(s - m_new[:, :1]).astype(BF)
            acc_ref[h] = acc_ref[h] * jnp.exp(m_old - m_new) + dot(p, v_operand(kv, h))
            m_ref[h] = m_new

    def here(i):
        cc = jnp.where(i == 0, at.c, at.oc)

        @pl.when(i == 1)
        def _():
            gather.wait(at.z, at.oc)
        compute(at.z, cc, True)
    loop(0, 2, here)

    def step(d):
        gather.serve(d)
        behind(d)

        def visit(i):
            zz = jnp.where(i % 2 == 0, at.z - d, at.z + d)

            @pl.when((zz >= 0) & (zz < at.nz))
            def _():
                @pl.when(i >= 2)
                def _():
                    gather.wait(zz, at.oc)
                compute(zz, jnp.where(i < 2, at.c, at.oc), False)
        loop(0, 4, visit)
    loop(1, at.nz, step)


def attention_end(at, q_ref, inside, slopes, tokens, m_ref, acc_ref, ctx_ref, ctxf_ref, qb_ref):
    for h in range(3):
        half = V_AT[h][1]
        first = 0 if half else 64
        acc = acc_ref[h]
        total = acc[:, first : first + 1]
        ctx = acc[:, 64 * half : 64 * half + 64] / total
        ctxf_ref[:, 64 * h : 64 * h + 64] = ctx
        ctx_ref[:, 64 * h : 64 * h + 64] = ctx.astype(BF)
        lse = m_ref[h] + jnp.log(total)
        for side in range(2):
            qb_ref[side, h] = query_operand(at, q_ref, inside, slopes, side, h, tokens, lse)


def fwd_kernel(nz, layers, host, R):
    at = Place(nz)
    tokens = R.x0.shape[0]
    rows, half_rows = 4 * tokens, 2 * tokens
    quarter = R.hid.shape[1]
    group = R.ctx_now[0].shape[1]
    at.enter()
    part = R.part
    square_sum = SquareSum(at, part, R.pair, R.single, R.ss_send, R.ss_recv)
    gather_x = [SquareGather(at, R.xr_now[l], R.x_send.at[l], R.x_recv.at[l]) for l in range(layers)]
    gather_y = [SquareGather(at, R.yr_now[l], R.y_send.at[l], R.y_recv.at[l]) for l in range(layers)]
    kv = BlockGather(at, R.kv_now)
    saves, waited = [], []

    def save(source, target):
        saves.append(pltpu.make_async_copy(source, target, R.saved.at[len(saves)]))
        saves[-1].start()
        return len(saves) - 1

    def wait_saved(number):
        saves[number].wait()
        waited.append(number)

    if host:
        qkv, gu, down = [[BlockGather(at, item) for item in items] for items in (R.qkv_now, R.gu_now, R.down_now)]
        ow = BlockGather(at, R.ow_now)
        qkv_w, gu_w, down_w, out_w = [g.buf for g in qkv], [g.buf for g in gu], [g.buf for g in down], R.out_now
        qkv[0].put(R.qkv_own[0][...])
        qkv[0].start()
    else:
        qkv_w, gu_w, down_w, out_w = R.qkv_given, R.gu_given, R.down_given, R.out_given

    R.xr_now[0][at.g] = R.x0[...]
    gather_x[0].start()
    if host:
        for l in range(layers):
            if l:
                qkv[l].put(R.qkv_own[l][...])
            gu[l].put(R.gu_own[l][...])
            down[l].put(R.down_own[l][...])
        ow.put(R.ow_own[...])

    def columns(b):
        R.kaug_now[b // 2, b % 2] = key_columns(at, R.slopes, R.seg, b // 2, b % 2, tokens)
    loop(0, 2 * nz, columns)
    save(R.kaug_now, R.kaug)
    R.inside[...] = segment_columns(at, R.seg, rows)

    def small(l, t):
        return R.small[8 * l + t : 8 * l + t + 1, :]

    def of(buf, half):
        v = buf[pl.ds(2 * half, 2)]
        return v.reshape(half_rows, v.shape[2])

    def half_at(half):
        return pl.ds(pl.multiple_of(half * half_rows, half_rows), half_rows)

    def put_part(half, value):
        part[pl.ds(2 * half, 2)] = value.reshape(2, tokens, value.shape[1])

    def of_group(row):
        value = jnp.zeros((1, group), F32)
        for g in range(4):
            value = jnp.where(at.g == g, row[:, group * g : group * g + group], value)
        return value

    if host:
        qkv[0].serve_all()
        ow.start()
        gu[0].start()
        down[0].start()
        qkv[0].collect()
    R.small[...] = side_weight(qkv_w[0], 1, 128, 256).astype(F32).T[64 : 64 + 8 * layers, :]
    R.state[...] = R.x0[...].astype(F32)
    gather_x[0].wait_near()
    gather_x[0].wait_far()

    for l in range(layers):
        last = l == layers - 1
        x_all = R.xr_now[l][...].reshape(rows, -1)
        save(R.xr_now[l], R.xr[l])
        qb, vb = of_group(small(l, 2)), of_group(small(l, 3))
        none = jnp.zeros((1, 128), F32)
        kv_bias = jnp.concatenate([none, vb[:, :128], none[:, :64], vb[:, 128:192]], axis=1)
        if l:
            pl.semaphore_wait(R.kv_free, at.neighbours())
        kv.put((dot(x_all, side_weight(qkv_w[l], 0)) + kv_bias).astype(BF))
        kv.start()
        R.q[...] = (dot(x_all, side_weight(qkv_w[l], 1, 0, group)) + qb).astype(BF)
        for side in range(2):
            for h in range(3):
                R.q_op[side, h] = query_operand(at, R.q, R.inside, R.slopes, side, h, tokens)

        def behind(d, l=l):
            if host:
                if l == 0:
                    ow.serve(d)
                gu[l].serve(d)
                down[l].serve(d)
        attention(at, kv, R.q_op, R.kaug_now, R.m, R.acc, behind)
        attention_end(at, R.q, R.inside, R.slopes, tokens, R.m, R.acc, R.ctx_now[l], R.ctxf_now[l], R.qb_now[l])
        kv_saved = save(kv.buf, R.kv[l])
        save(R.ctx_now[l], R.ctx[l])
        save(R.ctxf_now[l], R.ctxf[l])
        save(R.qb_now[l], R.qb[l])
        kv.finish()
        if l == 0 and host:
            ow.collect()
            step = group // (2 * nz)
            for i in range(layers):
                for b in range(2 * nz):
                    R.ow_wide[...] = ow.buf[b // 2, b % 2].astype(F32)
                    R.ow_flat[step * b : step * b + step, :] = R.ow_wide[step * i : step * i + step, :]
                R.out_now[i][...] = R.ow_flat[...].astype(BF)
                save(R.out_now[i], R.out_w[i])
        if not last and host:
            qkv[l + 1].start()
        if l:
            square_sum.finish()
        for number, half in enumerate((1 - at.x, at.x)):
            put_part(half, dot(R.ctx_now[l][half_at(half), :], out_w[l][...]))
            if number == 0:
                square_sum.send_far()
            else:
                square_sum.send_near()
        square_sum.relay()
        wait_saved(kv_saved)
        if not last:
            at.signal_neighbours(R.kv_free)
        R.sum1_now[l][...] = R.state[...] + (square_sum.total() + small(l, 4))
        save(R.sum1_now[l], R.sum1[l])
        y = layer_norm(R.sum1_now[l][...], small(l, 0), small(l, 5))
        R.yr_now[l][at.g] = y.astype(BF)
        gather_y[l].start()
        R.state[...] = y
        if host:
            gu[l].collect()
            down[l].collect()
        gather_y[l].wait_near()
        if l:
            wait_saved(mixed_saved)
        square_sum.finish()
        for number, half in enumerate((at.x, 1 - at.x)):
            if number == 1:
                if not last and host:
                    qkv[l + 1].serve_all()
                    gu[l + 1].start()
                    down[l + 1].start()
                gather_y[l].wait_far()
            here = half_at(half)
            y_half = of(R.yr_now[l], half)
            for col in range(0, quarter, 256):
                gate = dot(y_half, side_weight(gu_w[l], 0, col, col + 256))
                up = dot(y_half, side_weight(gu_w[l], 1, col, col + 256))
                R.mixed_now[here, col : col + 256] = gate
                R.mixed_now[here, quarter + col : quarter + col + 256] = up
                R.hid[:, col : col + 256] = (gate * normal_cdf(gate) * up).astype(BF)
            put_part(half, dot(R.hid[...], flat_weight(down_w[l])))
            if number == 0:
                square_sum.send_near()
            else:
                square_sum.send_far()
        mixed_saved = save(R.mixed_now, R.mixed[l])
        save(R.yr_now[l], R.yr[l])
        if host:
            save(qkv[l].buf, R.qkv_w[l])
            save(gu[l].buf, R.gu_w[l])
            save(down[l].buf, R.down_w[l])
        square_sum.relay()
        if not last and host:
            qkv[l + 1].collect()
        R.sum2_now[l][...] = R.state[...] + (square_sum.total() + small(l, 6))
        save(R.sum2_now[l], R.sum2[l])
        state = layer_norm(R.sum2_now[l][...], small(l, 1), small(l, 7))
        R.state[...] = state
        if last:
            R.output[...] = state.astype(BF)
        else:
            R.xr_now[l + 1][at.g] = state.astype(BF)
            gather_x[l + 1].start()
            gather_x[l + 1].wait_near()
            gather_x[l + 1].wait_far()
    for l in range(layers):
        gather_x[l].finish()
        gather_y[l].finish()
    square_sum.finish()
    if host:
        for items in (qkv, gu, down):
            for item in items:
                item.finish()
        ow.finish()
    for number, copy in enumerate(saves):
        if number not in waited:
            copy.wait()


def fwd(x0, slopes, seg, weights, layers, host):
    nb, _, rows = seg.shape
    nz = nb // 2
    tokens, width = x0.shape
    group = width // 4
    each = range(layers)
    quarter = (weights.gu_own[0].shape if host else weights.gu_given[0].shape)[-1]
    keep_rows = lambda: [keep(4, tokens, width) for _ in each]
    keep_wide = lambda: [keep(tokens, width, dtype=F32) for _ in each]
    scratch = dict(
        xr_now=keep_rows(), x_send=copies(layers, 4), x_recv=copies(layers, 4),
        yr_now=keep_rows(), y_send=copies(layers, 4), y_recv=copies(layers, 4),
        part=keep(4, tokens, width, dtype=F32), state=keep(tokens, width, dtype=F32), **square_sum_items(tokens, width),
        kv_now=block_gather_item(nz, rows, 384), kv_free=pltpu.SemaphoreType.REGULAR, saved=copies(16 * layers),
        kaug_now=keep(nz, 2, rows, 128), inside=keep(rows, 128, dtype=F32),
        q=keep(rows, group), q_op=keep(2, 3, rows, 128),
        m=keep(3, rows, 128, dtype=F32), acc=keep(3, rows, 128, dtype=F32),
        ctx_now=[keep(rows, group) for _ in each], ctxf_now=[keep(rows, group, dtype=F32) for _ in each],
        qb_now=[keep(2, 3, rows, 128) for _ in each], sum1_now=keep_wide(), sum2_now=keep_wide(),
        mixed_now=keep(rows, 2 * quarter, dtype=F32), hid=keep(2 * tokens, quarter))
    far_out = dict(
        xr=[shape(4, tokens, width) for _ in each], yr=[shape(4, tokens, width) for _ in each],
        kv=[shape(nz, 2, rows, 384) for _ in each], ctx=[shape(rows, group) for _ in each],
        ctxf=[shape(rows, group, dtype=F32) for _ in each], qb=[shape(2, 3, rows, 128) for _ in each],
        sum1=[shape(tokens, width, dtype=F32) for _ in each], sum2=[shape(tokens, width, dtype=F32) for _ in each],
        mixed=[shape(rows, 2 * quarter, dtype=F32) for _ in each], kaug=shape(nz, 2, rows, 128))
    near = dict(x0=x0, seg=seg, **vars(weights))
    if host:
        gathered = lambda arrays: [shape(nz, 2, *w.shape) for w in arrays]
        items = lambda arrays: [block_gather_item(nz, *w.shape) for w in arrays]
        far_out.update(qkv_w=gathered(weights.qkv_own), gu_w=gathered(weights.gu_own), down_w=gathered(weights.down_own),
                       out_w=[shape(group, width) for _ in each])
        scratch.update(
            qkv_now=items(weights.qkv_own), gu_now=items(weights.gu_own), down_now=items(weights.down_own),
            ow_now=block_gather_item(nz, *weights.ow_own.shape), out_now=[keep(group, width) for _ in each],
            ow_wide=keep(*weights.ow_own.shape, dtype=F32), ow_flat=keep(group, width, dtype=F32))
    out = dict(output=shape(tokens, width), small=shape(8 * layers, width, dtype=F32))
    done = call(functools.partial(fwd_kernel, nz, layers, host), "forward", 0, near=near, table=dict(slopes=slopes),
                out=out, far_out=far_out, scratch=scratch)
    if not host:
        done.qkv_w, done.gu_w, done.down_w, done.out_w = weights.qkv_given, weights.gu_given, weights.down_given, weights.out_given
    done.down_w = [w.reshape(quarter, width) for w in done.down_w]
    done.xr = [v.reshape(rows, width) for v in done.xr]
    done.yr = [v.reshape(rows, width) for v in done.yr]
    return done


def attn_back(at, R, l, top, begin, behind, at_end):
    nz, rows = at.nz, R.kvbuf.shape[1]
    q_ref, do_ref, dqacc = R.qb[l], R.do, R.dqacc
    dkv = BlockSum(at, R.dkv)

    def target(i):
        right = nz - 1 - at.z
        from_right = jnp.where(i < right, nz - 1 - i, i - right)
        from_left = jnp.where(i < at.z, i, nz - 1 - (i - at.z))
        return jnp.where(i == nz - 1, at.z, jnp.where(at.z < nz // 2, from_right, from_left))

    class Load:
        def __init__(self, t, slot):
            cc = at.oc if slot == 0 else at.c
            self.copies = [pltpu.make_async_copy(source.at[t, cc], target.at[slot], R.kvsem.at[i, slot])
                           for i, (source, target) in enumerate(((R.kv[l], R.kvbuf), (R.kaug, R.augbuf)))]

        def start(self):
            for copy in self.copies:
                copy.start()

        def wait(self):
            for copy in self.copies:
                copy.wait()

    load = Load

    dqacc[...] = jnp.zeros(dqacc.shape, F32)

    def compute(t, slot, same):
        cc = at.oc if slot == 0 else at.c
        side = (t > at.z).astype(jnp.int32)
        kv, aug = R.kvbuf.at[slot], R.augbuf[slot]
        dks, dvs = [], []
        for h in range(3):
            k, v = k_operand(kv, aug, h), v_operand(kv, h)
            if same:
                s = jnp.minimum(dot(k, q_ref[0, h], NT), dot(k, q_ref[1, h], NT))
            else:
                s = dot(k, q_ref[side, h], NT)
            p = jnp.exp(s)
            ds = (p * dot(v, do_ref[h], NT)).astype(BF)
            dvs.append(dot(p.astype(BF), do_ref[h]))
            dks.append(dot(ds, q_ref[side, h]))
            dqacc[h] += dot(ds, k, TN)
        low = in_half(0, rows)
        dkv.stage[t, cc, :, 0:128] = jnp.where(low, dks[0], dks[1]).astype(BF)
        dkv.stage[t, cc, :, 128:256] = jnp.where(low, dvs[0], dvs[1]).astype(BF)
        dkv.stage[t, cc, :, 256:384] = jnp.where(low, dks[2], dvs[2]).astype(BF)

    def far(t, same):
        load(t, 1).start()
        load(t, 0).wait()
        compute(t, 0, same)
        dkv.to_beside(t).start()

    load(target(0), 0).start()
    begin()
    if not top:
        pl.semaphore_wait(R.dkv.free, at.neighbours())

    def step(i):
        t = target(i)
        far(t, False)
        load(target(i + 1), 0).start()
        load(t, 1).wait()
        compute(t, 1, False)
        dkv.serve(i, relay=False)

        @pl.when(i > 0)
        def _():
            dkv.serve(i - 1, source=False)
        behind(i)
    loop(0, nz - 1, step)
    far(at.z, True)
    dkv.serve(nz - 2, source=False)
    load(at.z, 1).wait()
    compute(at.z, 1, True)
    at_end()
    dq = jnp.where(in_half(0, rows), dqacc[0], dqacc[1]) * 0.125
    R.dproj[:, 384:512] = dq.astype(BF)
    R.dproj[:, 512:576] = (dqacc[2][:, 0:64] * 0.125).astype(BF)
    R.dproj[:, 0:384] = dkv.total().astype(BF)
    if l > 0:
        at.signal_neighbours(R.dkv.free)
    dkv.finish()


def bwd_kernel(nz, layers, host, R):
    at = Place(nz)
    tokens = R.grad.shape[0]
    rows, half_rows = 4 * tokens, 2 * tokens
    quarter = R.hid.shape[1]
    width = R.grad.shape[1]
    mixed, yr, xr, gu_w, down_w, qkv_w = range(6)
    streams = ((R.mixed, R.mixed_now), (R.yr, R.yr_now), (R.xr, R.xr_now), (R.gu_w, R.gu_now), (R.down_w, R.down_now),
               (R.qkv_w, R.qkv_now))

    def load(which, l):
        return pltpu.make_async_copy(streams[which][0][l], streams[which][1], R.load.at[which])

    for which in range(6):
        load(which, layers - 1).start()
    at.enter()
    R.dproj[:, 576:768] = jnp.zeros((rows, 192), BF)
    gather_df = SquareGather(at, R.df, R.df_send, R.df_recv)
    gather_da = SquareGather(at, R.da, R.da_send, R.da_recv)
    part = R.part
    square_sum = SquareSum(at, part, R.pair, R.single, R.ss_send, R.ss_recv)
    if host:
        gu_sum, dn_sum, qk_sum, ow_sum = [[BlockSum(at, item) for item in items] for items in (R.gu, R.dn, R.qk, R.ow)]
        sm_sum = BlockSum(at, R.sm)

    def small(l, t):
        return R.small[8 * l + t : 8 * l + t + 1, :]

    def put_small(l, t, value):
        R.tok_small[8 * l + t : 8 * l + t + 1, :] = value

    def of(buf, half):
        v = buf[pl.ds(2 * half, 2)]
        return v.reshape(half_rows, v.shape[2])

    def half_at(half):
        return pl.ds(pl.multiple_of(half * half_rows, half_rows), half_rows)

    def put_part(half, value):
        part[pl.ds(2 * half, 2)] = value.reshape(2, tokens, value.shape[1])

    def wgrad(left, right, stage, cc, lo, hi):
        for first in range(0, left.shape[1], 384):
            v = dot(left[:, first : first + 384], right[:, lo:hi], TN)
            if len(stage.shape) == 2:
                stage[first : first + 384, :] = v.astype(BF)
                continue
            step = stage.shape[2]
            for i in range(384 // step):
                b = first // step + i
                zz, side = (b // 2, b % 2) if cc is None else (b, cc)
                stage[zz, side] = v[step * i : step * i + step].astype(BF)

    def feed_forward_sums(l):
        return (gu_sum[l], dn_sum[l]) if host and l < layers else ()

    def attention_sums(l):
        return (qk_sum[l], ow_sum[l]) if host and l < layers else ()

    def serve(items, p):
        for item in items:
            item.serve(p)

    def emit(l):
        if host and l < layers:
            R.gu_sum[l][...] = gu_sum[l].total().astype(BF)
            R.dn_sum[l][...] = dn_sum[l].total()
            R.qk_sum[l][...] = qk_sum[l].total().astype(BF)
            R.ow_sum[l][...] = ow_sum[l].total()

    R.g[...] = R.grad[...].astype(F32)
    for l in reversed(range(layers)):
        top = l == layers - 1
        e2, d_gain, d_shift = norm_back(R.g[...], R.sum2[l][...], small(l, 1))
        put_small(l, 1, d_gain)
        put_small(l, 5, d_shift)
        low = e2.astype(BF)
        put_small(l, 4, jnp.sum(low.astype(F32), axis=0, keepdims=True))
        if not top:
            square_sum.finish()
        R.df[at.g] = low
        gather_df.start()
        R.e2[...] = e2
        for which in range(6):
            load(which, l).wait()
        serve(feed_forward_sums(l + 1), 1)
        gather_df.wait_near()
        for number, half in enumerate((at.x, 1 - at.x)):
            if number == 1:
                gather_df.wait_far()
                serve(attention_sums(l + 1), 1)
            here = half_at(half)
            dhid_all = dot(of(R.df, half), R.down_now[...], NT)
            for col in range(0, quarter, 256):
                dhid = dhid_all[:, col : col + 256]
                gate = R.mixed_now[here, col : col + 256]
                up = R.mixed_now[here, quarter + col : quarter + col + 256]
                cdf = normal_cdf(gate)
                act = gate * cdf
                R.hid[here, col : col + 256] = (act * up).astype(BF)
                R.dgu[here, col : col + 256] = (dhid * up * (cdf + gate * normal_pdf(gate))).astype(BF)
                R.dgu[here, quarter + col : quarter + col + 256] = (dhid * act).astype(BF)
            put_part(half, dot(R.dgu[here, :quarter], side_weight(R.gu_now, 0), NT)
                     + dot(R.dgu[here, quarter:], side_weight(R.gu_now, 1), NT))
            if number == 0:
                square_sum.send_near()
            else:
                square_sum.send_far()
        wgrad(R.hid, R.df[...].reshape(rows, width), R.dn[l].stage, None, 0, width)
        square_sum.relay()
        serve(feed_forward_sums(l + 1), 2)
        for p in range(3, nz - 1):
            serve(feed_forward_sums(l + 1), p)
        dy = R.e2[...] + square_sum.total()
        e1, d_gain, d_shift = norm_back(dy, R.sum1[l][...], small(l, 0))
        put_small(l, 0, d_gain)
        put_small(l, 3, d_shift)
        low = e1.astype(BF)
        put_small(l, 2, jnp.sum(low.astype(F32), axis=0, keepdims=True))
        R.da[at.g] = low
        gather_da.start()
        R.e1[...] = e1
        for cc in range(2):
            wgrad(R.yr_now, R.dgu, R.gu[l].stage, cc, quarter * cc, quarter * cc + quarter)
        gather_da.wait_near()
        gather_da.wait_far()
        for item in feed_forward_sums(l):
            item.start()
        if l > 0:
            for which in (mixed, yr, gu_w, down_w):
                load(which, l - 1).start()
        da_all = R.da[...].reshape(rows, width)
        dctx = dot(da_all, R.out_w[l][...], NT).astype(BF)
        d_out = dot(R.ctx[l][...], da_all, TN)
        if host:
            step = d_out.shape[0] // (2 * nz)
            for b in range(2 * nz):
                R.ow[l].stage[b // 2, b % 2] = jnp.concatenate(
                    [d_out[step * b : step * b + step], jnp.zeros((OW_ROWS - step, width), F32)]).astype(BF)
        else:
            R.ow[l].stage[...] = d_out.astype(BF)
        ctxf = R.ctxf[l]
        wide = dctx.astype(F32)
        first_two = wide[:, :128]
        third = jnp.concatenate([jnp.zeros((rows, 64), F32), wide[:, 128:192]], axis=1)
        prod = first_two * ctxf[:, :128]
        low_half = in_half(0, rows)
        deltas = [
            jnp.sum(jnp.where(low_half, prod, 0.0), axis=1, keepdims=True),
            jnp.sum(jnp.where(low_half, 0.0, prod), axis=1, keepdims=True),
            jnp.sum(wide[:, 128:192] * ctxf[:, 128:192], axis=1, keepdims=True),
        ]
        for h in range(3):
            half = V_AT[h][1]
            base = jnp.where(in_half(half, rows), first_two if h < 2 else third, 0.0)
            R.do[h] = with_lanes(base, 0 if half else 64, split3(-deltas[h])).astype(BF)

        def begin(l=l):
            serve(attention_sums(l + 1), 2)
            for p in range(3, nz - 1):
                serve(attention_sums(l + 1), p)

        def behind(i):
            pass

        def at_end(l=l):
            serve(feed_forward_sums(l), 0)
        attn_back(at, R, l, top, begin, behind, at_end)
        dproj = R.dproj
        bias_sum = jnp.sum(dproj[...].astype(F32), axis=0, keepdims=True)
        for t, row in ((6, bias_sum[:, 384:576]), (7, jnp.concatenate([bias_sum[:, 128:256], bias_sum[:, 320:384]], axis=1))):
            put_small(l, t, jnp.concatenate([jnp.where(at.g == g, row, 0.0) for g in range(4)], axis=1))
        gather_df.finish()
        gather_da.finish()
        square_sum.finish()
        for number, half in enumerate((1 - at.x, at.x)):
            put_part(half, dot(dproj[half_at(half), :384], side_weight(R.qkv_now, 0), NT)
                     + dot(dproj[half_at(half), 384:], side_weight(R.qkv_now, 1), NT))
            if number == 0:
                square_sum.send_far()
            else:
                square_sum.send_near()
        square_sum.relay()
        for cc in range(2):
            wgrad(R.xr_now, dproj, R.qk[l].stage, cc, 384 * cc, 384 * cc + 384)
        for item in attention_sums(l):
            item.start()
        serve(attention_sums(l), 0)
        if l > 0:
            load(xr, l - 1).start()
            load(qkv_w, l - 1).start()
        emit(l + 1)
        R.g[...] = R.e1[...] + square_sum.total()
    R.grad_in[...] = R.g[...]
    square_sum.finish()
    if host:
        for b in range(2 * nz):
            step = width // (2 * nz)
            sm_sum.stage[b // 2, b % 2, :, 0:step] = R.tok_small[:, step * b : step * b + step]
        sm_sum.start()
        last = feed_forward_sums(0) + attention_sums(0) + (sm_sum,)
        sm_sum.serve(0)
        for p in range(1, nz - 1):
            serve(last, p)
        R.sm_sum[...] = sm_sum.total()
        emit(0)
        for l in range(layers):
            for item in feed_forward_sums(l) + attention_sums(l):
                item.finish()
        sm_sum.finish()


def bwd(grad, saved, host):
    layers = len(saved.qkv_w)
    nz, _, rows, _ = saved.kaug.shape
    tokens, width = grad.shape
    quarter, group = width, width // 4
    quarter = saved.down_w[0].shape[0]
    r, rd = width // nz, quarter // (2 * nz)
    each = range(layers)
    out = dict(grad_in=shape(tokens, width, dtype=F32))
    scratch = {}
    if host:
        out.update(
            gu_sum=[shape(r, quarter) for _ in each], dn_sum=[shape(rd, width, dtype=F32) for _ in each],
            qk_sum=[shape(r, 384) for _ in each], ow_sum=[shape(OW_ROWS, width, dtype=F32) for _ in each],
            sm_sum=shape(8 * layers, 128, dtype=F32))
        scratch.update(
            gu=[block_sum_item(nz, r, quarter) for _ in each], dn=[block_sum_item(nz, rd, width) for _ in each],
            qk=[block_sum_item(nz, r, 384) for _ in each], ow=[block_sum_item(nz, OW_ROWS, width) for _ in each],
            sm=block_sum_item(nz, 8 * layers, 128, dtype=F32), tok_small=keep(8 * layers, width, dtype=F32))
    else:
        out.update(
            gu=[dict(stage=shape(nz, 2, r, quarter)) for _ in each], dn=[dict(stage=shape(quarter, width)) for _ in each],
            qk=[dict(stage=shape(nz, 2, r, 384)) for _ in each], ow=[dict(stage=shape(group, width)) for _ in each],
            tok_small=shape(8 * layers, width, dtype=F32))
    like = lambda arrays: keep(*arrays[0].shape, dtype=arrays[0].dtype)
    scratch.update(
        mixed_now=like(saved.mixed), yr_now=like(saved.yr), xr_now=like(saved.xr), gu_now=like(saved.gu_w),
        down_now=like(saved.down_w), qkv_now=like(saved.qkv_w), load=copies(6), kvbuf=keep(2, rows, 384), augbuf=keep(2, rows, 128), kvsem=copies(2, 2),
        df=keep(4, tokens, width), df_send=copies(4), df_recv=copies(4),
        da=keep(4, tokens, width), da_send=copies(4), da_recv=copies(4),
        part=keep(4, tokens, width, dtype=F32), **square_sum_items(tokens, width),
        g=keep(tokens, width, dtype=F32), e1=keep(tokens, width, dtype=F32), e2=keep(tokens, width, dtype=F32),
        hid=keep(rows, quarter), dgu=keep(rows, 2 * quarter), do=keep(3, rows, 128),
        dqacc=keep(3, rows, 128, dtype=F32), dproj=keep(rows, 768),
        dkv=dict(block_sum_item(nz, rows, 384), free=pltpu.SemaphoreType.REGULAR))
    near = dict(grad=grad, small=saved.small, sum1=saved.sum1, sum2=saved.sum2, ctx=saved.ctx,
                ctxf=saved.ctxf, qb=saved.qb, out_w=saved.out_w)
    far = dict(mixed=saved.mixed, yr=saved.yr, xr=saved.xr, gu_w=saved.gu_w, down_w=saved.down_w, kv=saved.kv, kaug=saved.kaug,
               qkv_w=saved.qkv_w)
    return call(functools.partial(bwd_kernel, nz, layers, host), "backward", 1, near=near, far=far, out=out, scratch=scratch)


def shards(hidden_in, out_grad, segment_ids, alibi_slopes, qkv_weight, out_weight, gate_up_weight, down_weight, gains, biases):
    nz = lax.axis_size("z")
    nb = 2 * nz
    square, everyone, blocks = ("x", "y", "c"), ("z", "x", "y", "c"), ("z", "c")
    z, c = lax.axis_index("z"), lax.axis_index("c")
    tokens, width = hidden_in.shape
    layers, wrows = qkv_weight.shape[:2]
    ff = gate_up_weight.shape[2] // 2
    group, quarter = width // 4, ff // 4
    host = (width // nz) % 16 == 0 and down_weight.shape[1] % 16 == 0

    def to_groups(w):
        w = w.reshape(wrows, 3, 4, 3, 64)
        q, k, v = w[:, 0], w[:, 1], w[:, 2]
        kv = jnp.stack([k[:, :, 0], k[:, :, 1], v[:, :, 0], v[:, :, 1], k[:, :, 2], v[:, :, 2]], axis=2)
        return kv.reshape(wrows, 4, 384), q.reshape(wrows, 4, group)

    def from_groups(kv, q):
        kv, q = kv.reshape(4, wrows, 6, 64), q.reshape(4, wrows, 3, 64)
        k = jnp.stack([kv[:, :, 0], kv[:, :, 1], kv[:, :, 4]], axis=2)
        v = jnp.stack([kv[:, :, 2], kv[:, :, 3], kv[:, :, 5]], axis=2)
        return jnp.stack([q, k, v]).transpose(2, 0, 1, 3, 4).reshape(wrows, 3 * width)

    small = jnp.concatenate([gains, biases], axis=1).transpose(0, 2, 1)
    small = jnp.concatenate([small[l] for l in range(layers)], axis=1)
    small = jnp.pad(small, ((0, 0), (0, 192 - small.shape[1])))
    small = jnp.broadcast_to(small[:, None], (wrows, 4, 192))
    nothing = jnp.zeros((wrows, 4, 192), BF)
    gu = gate_up_weight.reshape(layers, wrows, 2, nz, 4, quarter // nz).transpose(0, 1, 4, 2, 3, 5).reshape(layers, wrows, 4, 2, quarter)
    sides = [[], []]
    for l in range(layers):
        kv, q = to_groups(qkv_weight[l])
        sides[0].append(kv)
        sides[1] += [q, nothing if l else small]
    for l in range(layers):
        for side in range(2):
            sides[side].append(gu[l, :, :, side])
    both = jnp.stack([jnp.concatenate(side, axis=2) for side in sides], axis=2).reshape(wrows, 8, -1)
    spread = lax.all_to_all(both, square, split_axis=1, concat_axis=0, tiled=True).reshape(8 * wrows, -1)
    qkv_own = [spread[:, 384 * l : 384 * l + 384] for l in range(layers)]
    gu0 = 384 * layers
    gu_own = [spread[:, gu0 + quarter * l : gu0 + quarter * l + quarter] for l in range(layers)]
    places = [(8 * zz + 2 * g + cc, g * nb + 2 * zz + cc) for zz in range(nz) for g in range(4) for cc in range(2)]
    ow_own = lax.ppermute(out_weight, everyone, [(chunk, device) for device, chunk in places])
    if host:
        weights = types.SimpleNamespace(qkv_own=qkv_own, gu_own=gu_own, down_own=[down_weight[l] for l in range(layers)],
                                        ow_own=ow_own.reshape(layers * wrows, width))
    else:
        whole = lambda v: lax.all_gather(v, blocks, axis=0).reshape(nz, 2, *v.shape)
        flat = lambda v: lax.all_gather(v, blocks, axis=0, tiled=True)
        weights = types.SimpleNamespace(
            qkv_given=[whole(v) for v in qkv_own], gu_given=[whole(v) for v in gu_own],
            down_given=[flat(down_weight[l]) for l in range(layers)], out_given=[flat(ow_own[l]) for l in range(layers)])

    seg = segment_ids.reshape(nz, 4, 2, tokens).transpose(0, 2, 1, 3).reshape(nb, 1, 4 * tokens)
    saved = fwd(hidden_in, alibi_slopes, seg, weights, layers, host)
    done = bwd(out_grad, saved, host)

    step = width // nb
    if host:
        sm = done.sm_sum[:, :step]
    else:
        blocks_sum = lambda v: lax.psum_scatter(v, blocks, scatter_dimension=0, tiled=True)
        done.gu_sum = [blocks_sum(item.stage.reshape(nb, -1, quarter))[0] for item in done.gu]
        done.qk_sum = [blocks_sum(item.stage.reshape(nb, -1, 384))[0] for item in done.qk]
        done.dn_sum = [blocks_sum(item.stage) for item in done.dn]
        done.ow_sum = [blocks_sum(item.stage) for item in done.ow]
        sm = lax.psum_scatter(done.tok_small.reshape(-1, nb, step), blocks, scatter_dimension=1, tiled=True)[:, 0]
    sm = sm.T.reshape(4, wrows, 8 * layers)
    high = lax.reduce_precision(sm, 8, 7)
    sm = jnp.concatenate([high, sm - high], axis=2).astype(BF)
    sm = lax.dynamic_update_slice_in_dim(jnp.zeros((8, wrows, 16 * layers), BF), sm, 4 * c, 0)
    rows_of = lambda v: v.reshape(8, wrows, -1)
    back = jnp.concatenate([rows_of(v) for v in done.qk_sum + done.gu_sum] + [sm], axis=2)
    back = lax.all_to_all(back, square, split_axis=0, concat_axis=0, tiled=True)
    sides = back.astype(F32).reshape(4, 2, wrows, -1)
    qkv_grad = jnp.stack([from_groups(sides[:, 0, :, 384 * l : 384 * l + 384], sides[:, 1, :, 384 * l : 384 * l + group])
                          for l in range(layers)])
    gu_grad = jnp.stack([sides[:, :, :, gu0 + quarter * l : gu0 + quarter * l + quarter] for l in range(layers)])
    gu_grad = gu_grad.reshape(layers, 4, 2, wrows, nz, quarter // nz).transpose(0, 3, 2, 4, 1, 5).reshape(layers, wrows, 2 * ff)
    sm = jnp.sum(sides[..., gu0 + quarter * layers :], axis=(0, 1))
    sm = (sm[:, : 8 * layers] + sm[:, 8 * layers :]).T.reshape(layers, 8, wrows)
    out_grad_w = lax.ppermute(jnp.stack(done.ow_sum)[:, :wrows].astype(F32), everyone, places)
    return (saved.output, done.grad_in, qkv_grad, out_grad_w, gu_grad, jnp.stack(done.dn_sum).astype(F32), sm[:, 0:2],
            jnp.concatenate([sm[:, 6:8], sm[:, 2:6]], axis=1))


def solution(mesh):
    nb, nh = mesh.devices.shape
    everyone = ("z", "x", "y", "c")
    tok, mid, last = P(everyone, None), P(None, everyone, None), P(None, None, everyone)
    return jax.shard_map(
        shards, mesh=Mesh(mesh.devices.reshape(nb // 2, 2, nh // 2, 2), everyone),
        in_specs=(tok, tok, P(), P(), mid, mid, mid, mid, last, last),
        out_specs=(tok, tok, mid, mid, mid, mid, last, last),
        check_vma=False,
    )
```

```python
import functools
import types

import jax
import jax.numpy as jnp
from jax import lax
from jax.experimental import pallas as pl
from jax.experimental.pallas import tpu as pltpu
from jax.sharding import Mesh
from jax.sharding import PartitionSpec as P

MESH = pl.DeviceIdType.MESH
BF = jnp.bfloat16
F32 = jnp.float32
NT = (((1,), (1,)), ((), ()))
NN = (((1,), (0,)), ((), ()))
TN = (((0,), (0,)), ((), ()))
EPS = 1e-06
K_AT = ((0, 0), (0, 1), (2, 0))
V_AT = ((1, 0), (1, 1), (2, 1))
ROW_LANE, SEGMENT_LANE = 9, 12
OW_ROWS = 32
VMEM = pl.BlockSpec(memory_space=pltpu.VMEM)
ANY = pl.BlockSpec(memory_space=pl.ANY)


def dot(a, b, dims=NN):
    return lax.dot_general(a, b, dims, preferred_element_type=F32)


def lanes(rows):
    return lax.broadcasted_iota(jnp.int32, (rows, 128), 1)


def in_half(half, rows):
    return lanes(rows) >= 64 if half else lanes(rows) < 64


def ones_half(half, rows):
    first = 0 if half else 64
    lane = lanes(rows)
    return jnp.where((lane >= first) & (lane < first + 3), 1.0, 0.0).astype(BF)


def k_operand(kv, aug, h):
    col, half = K_AT[h]
    return jnp.where(in_half(half, kv.shape[0]), kv[:, 128 * col : 128 * col + 128], aug)


def v_operand(kv, h):
    col, half = V_AT[h]
    rows = kv.shape[0]
    return jnp.where(in_half(half, rows), kv[:, 128 * col : 128 * col + 128], ones_half(half, rows))


def split3(value):
    high = value.astype(BF).astype(F32)
    mid = (value - high).astype(BF).astype(F32)
    return high, mid, value - high - mid


def with_lanes(base, first, values):
    lane = lanes(base.shape[0])
    for i, v in enumerate(values):
        base = jnp.where(lane == first + i, v, base)
    return base


def layer_norm(total, gain, shift):
    centred = total - jnp.mean(total, axis=-1, keepdims=True)
    scale = lax.rsqrt(jnp.mean(centred * centred, axis=-1, keepdims=True) + EPS)
    return centred * scale * gain + shift


def norm_back(grad, total, gain):
    centred = total - jnp.mean(total, axis=-1, keepdims=True)
    scale = lax.rsqrt(jnp.mean(centred * centred, axis=-1, keepdims=True) + EPS)
    n = centred * scale
    dn = grad * gain
    e = scale * (dn - jnp.mean(dn, axis=-1, keepdims=True) - n * jnp.mean(dn * n, axis=-1, keepdims=True))
    return e, jnp.sum(grad * n, axis=0, keepdims=True), jnp.sum(grad, axis=0, keepdims=True)


def normal_cdf(u):
    return 0.5 * (1.0 + lax.erf(u * (0.5**0.5)))


def normal_pdf(u):
    return jnp.exp(-0.5 * u * u) * ((2.0 * jnp.pi) ** -0.5)


def remote(src, dst, send, recv, device):
    return pltpu.make_async_remote_copy(
        src_ref=src, dst_ref=dst, send_sem=send, recv_sem=recv, device_id=device, device_id_type=MESH)


def loop(first, last, do):
    def step(i, carry):
        do(i)
        return carry
    lax.fori_loop(first, last, step, 0)


class Place:
    def __init__(self, nz):
        self.nz = nz
        self.z, self.x, self.y, self.c = [lax.axis_index(name) for name in "zxyc"]
        self.g = 2 * self.x + self.y
        self.gx, self.gy = 2 * (1 - self.x) + self.y, 2 * self.x + 1 - self.y
        self.gd = 2 * (1 - self.x) + 1 - self.y
        self.oc = 1 - self.c
        self.beside = (self.z, self.x, self.y, self.oc)
        self.across_x = (self.z, 1 - self.x, self.y, self.c)
        self.across_y = (self.z, self.x, 1 - self.y, self.c)
        self.block = 2 * self.z + self.c
        self.member = 2 * self.g + self.c
        self.number = 8 * self.z + self.member
        nb = 2 * nz
        self.chunk = self.g * nb + self.block
        self.chunk_device = self.device(self.chunk)
        place = self.number % nb
        self.holder = (place // 2, self.number // nb // 2, self.number // nb % 2, place % 2)
        self.moves = self.chunk != self.number
        self.has_left, self.has_right = self.z > 0, self.z < nz - 1

    def column(self, zz):
        return (zz, self.x, self.y, self.c)

    def device(self, number):
        k = number % 8
        return (number // 8, k // 4, k // 2 % 2, k % 2)

    def of_plane(self, k):
        return (self.z, k // 4, k // 2 % 2, k % 2)

    def neighbours(self):
        return 3 - (self.z == 0).astype(jnp.int32) - (self.z == self.nz - 1).astype(jnp.int32)

    def signal_neighbours(self, semaphore):
        pl.semaphore_signal(semaphore, inc=1, device_id=self.beside, device_id_type=MESH)

        @pl.when(self.has_left)
        def _():
            pl.semaphore_signal(semaphore, inc=1, device_id=self.column(self.z - 1), device_id_type=MESH)

        @pl.when(self.has_right)
        def _():
            pl.semaphore_signal(semaphore, inc=1, device_id=self.column(self.z + 1), device_id_type=MESH)

    def enter(self, plane):
        barrier = pltpu.get_barrier_semaphore()

        def greet(device):
            pl.semaphore_signal(barrier, inc=1, device_id=device, device_id_type=MESH)

        if not plane:
            greet(self.across_x)
            greet(self.across_y)
            self.signal_neighbours(barrier)
            pl.semaphore_wait(barrier, 2 + self.neighbours())
            return
        loop(1, 8, lambda j: greet(self.of_plane((self.member + j) % 8)))
        self.signal_neighbours(barrier)

        @pl.when(self.moves)
        def _():
            greet(self.chunk_device)
            greet(self.holder)
        pl.semaphore_wait(barrier, 7 + self.neighbours() + 2 * self.moves.astype(jnp.int32))

    def positions(self, zz, cc, tokens, rows):
        row = lax.broadcasted_iota(jnp.int32, (rows, 128), 0)
        return ((zz * 8 + (row // tokens) * 2 + cc) * tokens + row % tokens).astype(F32)


class SquareGather:
    def __init__(self, at, buf, send, recv):
        half = buf.shape[1] // 2
        first, second = pl.ds(0, half), pl.ds(half, half)
        own = buf.at[at.g]
        self.to_x = remote(own, own, send.at[0], recv.at[0], at.across_x)
        self.to_y = remote(own, own, send.at[1], recv.at[1], at.across_y)
        self.on_y = remote(buf.at[at.gx, first], buf.at[at.gx, first], send.at[2], recv.at[2], at.across_y)
        self.on_x = remote(buf.at[at.gy, second], buf.at[at.gy, second], send.at[3], recv.at[3], at.across_x)

    def start(self):
        self.to_x.start()
        self.to_y.start()

    def wait_near(self):
        self.to_x.wait_recv()
        self.on_y.start()
        self.to_y.wait_recv()
        self.on_x.start()

    def wait_far(self):
        self.on_x.wait_recv()
        self.on_y.wait_recv()

    def finish(self):
        for copy in (self.to_x, self.to_y, self.on_x, self.on_y):
            copy.wait_send()


class SquareSum:
    def __init__(self, at, part, pair, single, send, recv):
        self.at, self.part = at, part
        self.pair, self.single = pair, single
        self.half = part.shape[2] // 2
        to = (at.across_x, at.across_y, at.across_y, at.across_y, at.across_x)
        refs = [(pair.stage, pair.inbox)] + [(single.stage.at[i], single.inbox.at[i]) for i in range(4)]
        self.copies = [remote(refs[i][0], refs[i][1], send.at[i], recv.at[i], to[i]) for i in range(5)]

    def left(self, g):
        return self.part[g, :, : self.half]

    def right(self, g):
        return self.part[g, :, self.half :]

    def send_far(self):
        at = self.at
        self.pair.stage[...] = self.part[pl.ds(2 * (1 - at.x), 2), :, : self.half].astype(BF)
        self.copies[0].start()
        self.single.stage[1] = self.right(at.gd).astype(BF)
        self.copies[2].start()

    def send_near(self):
        self.single.stage[0] = self.right(self.at.gy).astype(BF)
        self.copies[1].start()

    def relay(self):
        at = self.at
        self.copies[0].wait_recv()
        self.single.stage[2] = (self.left(at.gy) + self.pair.inbox[1 - at.y].astype(F32)).astype(BF)
        self.copies[3].start()
        self.copies[2].wait_recv()
        self.single.stage[3] = (self.right(at.gx) + self.single.inbox[1].astype(F32)).astype(BF)
        self.copies[4].start()

    def total(self):
        at = self.at
        self.copies[1].wait_recv()
        left = self.left(at.g) + self.pair.inbox[at.y].astype(F32)
        right = self.right(at.g) + self.single.inbox[0].astype(F32)
        self.copies[3].wait_recv()
        self.copies[4].wait_recv()
        return jnp.concatenate(
            [left + self.single.inbox[2].astype(F32), right + self.single.inbox[3].astype(F32)], axis=1)

    def finish(self):
        for copy in self.copies:
            copy.wait_send()


class BlockGather:
    def __init__(self, at, item):
        self.at, self.buf, self.zsend, self.csend, self.recv = at, item.buf, item.zsend, item.csend, item.recv

    def copy(self, zz, send, device):
        at = self.at
        return remote(self.buf.at[zz, at.c], self.buf.at[zz, at.c], send, self.recv.at[zz, at.c], device)

    def to_right(self, zz):
        return self.copy(zz, self.zsend.at[0, zz], self.at.column(self.at.z + 1))

    def to_left(self, zz):
        return self.copy(zz, self.zsend.at[1, zz], self.at.column(self.at.z - 1))

    def to_beside(self, zz):
        return self.copy(zz, self.csend.at[zz], self.at.beside)

    def wait(self, zz, cc):
        at = self.at
        remote(self.buf.at[zz, cc], self.buf.at[zz, cc], self.csend.at[zz], self.recv.at[zz, cc], at.beside).wait_recv()

    def put(self, value):
        self.buf[self.at.z, self.at.c] = value

    def start(self):
        at = self.at

        @pl.when(at.has_right)
        def _():
            self.to_right(at.z).start()

        @pl.when(at.has_left)
        def _():
            self.to_left(at.z).start()
        self.to_beside(at.z).start()

    def serve(self, d):
        at = self.at

        @pl.when(at.z - d >= 0)
        def _():
            self.wait(at.z - d, at.c)

            @pl.when(at.has_right)
            def _():
                self.to_right(at.z - d).start()
            self.to_beside(at.z - d).start()

        @pl.when(at.z + d < at.nz)
        def _():
            self.wait(at.z + d, at.c)

            @pl.when(at.has_left)
            def _():
                self.to_left(at.z + d).start()
            self.to_beside(at.z + d).start()

    def serve_all(self):
        loop(1, self.at.nz, self.serve)

    def collect(self):
        loop(0, self.at.nz, lambda zz: self.wait(zz, self.at.oc))

    def finish(self):
        at = self.at

        def drain(zz):
            self.to_beside(zz).wait_send()

            @pl.when((zz <= at.z) & at.has_right)
            def _():
                self.to_right(zz).wait_send()

            @pl.when((zz >= at.z) & at.has_left)
            def _():
                self.to_left(zz).wait_send()
        loop(0, at.nz, drain)


def block_gather_item(nz, *dims):
    return dict(buf=keep(nz, 2, *dims), zsend=copies(2, nz), csend=copies(nz), recv=copies(nz, 2))


class BlockSum:
    def __init__(self, at, item):
        self.at, self.stage, self.cin, self.zin = at, item.stage, item.cin, item.zin
        self.csend, self.crecv, self.zsend, self.zrecv = item.csend, item.crecv, item.zsend, item.zrecv

    def to_beside(self, t):
        return remote(self.stage.at[t, self.at.oc], self.cin.at[t], self.csend.at[t], self.crecv.at[t], self.at.beside)

    def to_right(self, t):
        return remote(self.stage.at[t, self.at.c], self.zin.at[t + 1], self.zsend.at[t], self.zrecv.at[t + 1], self.at.column(self.at.z + 1))

    def to_left(self, t):
        return remote(self.stage.at[t, self.at.c], self.zin.at[t], self.zsend.at[t], self.zrecv.at[t], self.at.column(self.at.z - 1))

    def arrived(self, slot):
        at = self.at
        remote(self.zin.at[slot], self.zin.at[slot], self.zsend.at[0], self.zrecv.at[slot], at.beside).wait_recv()

    def start(self):
        loop(0, self.at.nz, lambda t: self.to_beside(t).start())

    def add(self, t, slot=None):
        value = self.stage[t, self.at.c].astype(F32) + self.cin[t].astype(F32)
        if slot is not None:
            value = value + self.zin[slot].astype(F32)
        self.stage[t, self.at.c] = value.astype(self.stage.dtype)

    def go_right(self, t):
        self.to_beside(t).wait_recv()

        @pl.when(self.at.has_left)
        def _():
            self.arrived(t + 1)
            self.add(t, t + 1)

        @pl.when(jnp.logical_not(self.at.has_left))
        def _():
            self.add(t)
        self.to_right(t).start()

    def go_left(self, t):
        self.to_beside(t).wait_recv()

        @pl.when(self.at.has_right)
        def _():
            self.arrived(t)
            self.add(t, t)

        @pl.when(jnp.logical_not(self.at.has_right))
        def _():
            self.add(t)
        self.to_left(t).start()

    def serve(self, p, source=True, relay=True):
        at = self.at
        right, left = p - at.z, p - (at.nz - 1 - at.z)
        go_r = (right >= 0) & (right < at.nz - 1 - at.z)
        go_l = (left >= 0) & (left < at.z)
        if not source:
            go_r, go_l = go_r & at.has_left, go_l & at.has_right
        if not relay:
            go_r, go_l = go_r & jnp.logical_not(at.has_left), go_l & jnp.logical_not(at.has_right)

        @pl.when(go_r)
        def _():
            self.go_right(at.nz - 1 - right)

        @pl.when(go_l)
        def _():
            self.go_left(left)

    def total(self):
        at = self.at
        self.to_beside(at.z).wait_recv()

        @pl.when(at.has_left)
        def _():
            self.arrived(at.z + 1)

        @pl.when(at.has_right)
        def _():
            self.arrived(at.z)
        value = self.stage[at.z, at.c].astype(F32) + self.cin[at.z].astype(F32)
        from_left = jnp.where(at.has_left, self.zin[at.z + 1].astype(F32), 0.0)
        from_right = jnp.where(at.has_right, self.zin[at.z].astype(F32), 0.0)
        return value + from_left + from_right

    def finish(self):
        at = self.at

        def drain(t):
            self.to_beside(t).wait_send()

            @pl.when(t > at.z)
            def _():
                self.to_right(t).wait_send()

            @pl.when(t < at.z)
            def _():
                self.to_left(t).wait_send()
        loop(0, at.nz, drain)


class PlaneExchange:
    def __init__(self, at, out, inbox, send, recv, columns=None):
        self.at, self.out, self.inbox, self.send, self.recv, self.columns = at, out, inbox, send, recv, columns

    def source(self, k):
        return self.out.at[k] if self.columns is None else self.out.at[k, :, self.columns]

    def start(self):
        at = self.at

        def step(j):
            k = (at.member + j) % 8
            remote(self.source(k), self.inbox.at[at.member], self.send.at[k], self.recv.at[at.member], at.of_plane(k)).start()
        loop(1, 8, step)
        self.inbox[at.member] = self.source(at.member)[...]

    def each(self, do):
        at = self.at

        def step(j):
            k = (at.member + j) % 8
            do(remote(self.source(k), self.inbox.at[k], self.send.at[k], self.recv.at[k], at.of_plane(k)))
        loop(1, 8, step)

    def wait(self):
        self.each(lambda copy: copy.wait_recv())

    def finish(self):
        self.each(lambda copy: copy.wait_send())

    def rows(self, count):
        return jnp.concatenate([self.inbox[k].astype(F32)[0:count] for k in range(8)], axis=0)


def box(tree):
    if isinstance(tree, dict):
        return types.SimpleNamespace(**{k: box(v) for k, v in tree.items()})
    return [box(v) for v in tree] if isinstance(tree, list) else tree


def call(body, name, collective_id, near=None, far=None, table=None, out=None, far_out=None, scratch=None):
    groups = [near or {}, far or {}, table or {}, out or {}, far_out or {}, scratch or {}]
    flat, trees = zip(*[jax.tree.flatten(g) for g in groups])
    counts = [len(f) for f in flat]

    def kernel(*refs):
        named, first = {}, 0
        for tree, count in zip(trees, counts):
            named.update(jax.tree.unflatten(tree, refs[first : first + count]))
            first += count
        body(box(named))

    smem = pl.BlockSpec(memory_space=pltpu.SMEM)
    results = pl.pallas_call(
        kernel,
        out_shape=tuple(flat[3]) + tuple(flat[4]),
        in_specs=[VMEM] * counts[0] + [ANY] * counts[1] + [smem] * counts[2],
        out_specs=(VMEM,) * counts[3] + (ANY,) * counts[4],
        scratch_shapes=list(flat[5]),
        compiler_params=pltpu.CompilerParams(
            collective_id=collective_id, has_side_effects=True, vmem_limit_bytes=63 * 2**20),
        cost_estimate=pl.CostEstimate(flops=10**11, bytes_accessed=2 * 10**8, transcendentals=10**7),
        name=name,
    )(*flat[0], *flat[1], *flat[2])
    done = jax.tree.unflatten(trees[3], results[: counts[3]])
    done.update(jax.tree.unflatten(trees[4], results[counts[3] :]))
    return box(done)


def shape(*dims, dtype=BF):
    return jax.ShapeDtypeStruct(dims, dtype)


def keep(*dims, dtype=BF):
    return pltpu.VMEM(dims, dtype)


def copies(*dims):
    return pltpu.SemaphoreType.DMA(dims)


def square_sum_items(tokens, width):
    half = width // 2
    return dict(
        pair=dict(stage=keep(2, tokens, half), inbox=keep(2, tokens, half)),
        single=dict(stage=keep(4, tokens, half), inbox=keep(4, tokens, half)), ss_send=copies(5), ss_recv=copies(5))


def flat_weight(ref, lo=0, hi=None):
    if len(ref.shape) == 2:
        return ref[:, lo:hi]
    v = ref[:, :, :, lo:hi]
    return v.reshape(v.shape[0] * v.shape[1] * v.shape[2], v.shape[3])


def side_weight(ref, cc, lo=0, hi=None):
    v = ref[:, cc, :, lo:hi]
    return v.reshape(v.shape[0] * v.shape[1], v.shape[2])


def block_sum_item(nz, *dims, dtype=BF):
    return dict(stage=keep(nz, 2, *dims, dtype=dtype), cin=keep(nz, *dims, dtype=dtype), zin=keep(nz + 1, *dims, dtype=dtype),
                csend=copies(nz), crecv=copies(nz), zsend=copies(nz), zrecv=copies(nz + 1))


def key_columns(at, slopes, seg, zz, cc, tokens):
    rows = 4 * tokens
    column = lax.broadcasted_iota(jnp.int32, (128, rows), 0) % 64
    row = lax.broadcasted_iota(jnp.int32, (128, rows), 1)
    position = ((zz * 8 + (row // tokens) * 2 + cc) * tokens + row % tokens).astype(F32)
    value = jnp.where(seg[2 * zz + cc] == column - SEGMENT_LANE, 0.0, -1e30)
    value = jnp.where(column < SEGMENT_LANE + 5, value, 0.0)
    value = jnp.where(column < SEGMENT_LANE, 1.0, value)
    for h in range(3):
        for i, term in enumerate(split3(position * slopes[3 * at.g + h])):
            value = jnp.where(column == 3 * h + i, term, value)
    return value.T.astype(BF)


def segment_columns(at, seg, rows):
    column = lax.broadcasted_iota(jnp.int32, (128, rows), 0) % 64
    return jnp.where(seg[at.block] == column - SEGMENT_LANE, 1.0, 0.0).T


def query_operand(at, q_ref, inside, slopes, side, h, tokens, lse=None):
    rows = 4 * tokens
    if h < 2:
        data = q_ref[:, 0:128]
    else:
        data = jnp.concatenate([q_ref[:, 128:192], jnp.zeros((rows, 64), q_ref.dtype)], axis=1)
    half = K_AT[h][1]
    sign = 1.0 if side == 0 else -1.0
    column = lanes(rows) % 64
    aug = jnp.where((column >= 3 * h) & (column < 3 * h + 3), sign, inside[...])
    term = at.positions(at.z, at.c, tokens, rows) * (slopes[3 * at.g + h] * -sign)
    if lse is not None:
        term = term - lse
    aug = with_lanes(aug, ROW_LANE if half else 64 + ROW_LANE, split3(term))
    return jnp.where(in_half(half, rows), data.astype(F32) * 0.125, aug).astype(BF)


def attention(at, gather, q_op, kaug, m_ref, acc_ref, behind):
    m_ref[...] = jnp.full(m_ref.shape, -1e30, F32)
    acc_ref[...] = jnp.zeros(acc_ref.shape, F32)

    def compute(zz, cc, same):
        kv, aug = gather.buf.at[zz, cc], kaug[zz, cc]
        side = (zz > at.z).astype(jnp.int32)
        for h in range(3):
            k = k_operand(kv, aug, h)
            if same:
                s = jnp.minimum(dot(q_op[0, h], k, NT), dot(q_op[1, h], k, NT))
            else:
                s = dot(q_op[side, h], k, NT)
            m_old = m_ref[h]
            m_new = jnp.maximum(m_old, jnp.max(s, axis=1, keepdims=True))
            p = jnp.exp(s - m_new[:, :1]).astype(BF)
            acc_ref[h] = acc_ref[h] * jnp.exp(m_old - m_new) + dot(p, v_operand(kv, h))
            m_ref[h] = m_new

    def here(i):
        cc = jnp.where(i == 0, at.c, at.oc)

        @pl.when(i == 1)
        def _():
            gather.wait(at.z, at.oc)
        compute(at.z, cc, True)
    loop(0, 2, here)

    def step(d):
        gather.serve(d)
        behind(d)

        def visit(i):
            zz = jnp.where(i % 2 == 0, at.z - d, at.z + d)

            @pl.when((zz >= 0) & (zz < at.nz))
            def _():
                @pl.when(i >= 2)
                def _():
                    gather.wait(zz, at.oc)
                compute(zz, jnp.where(i < 2, at.c, at.oc), False)
        loop(0, 4, visit)
    loop(1, at.nz, step)


def attention_end(at, q_ref, inside, slopes, tokens, m_ref, acc_ref, ctx_ref, ctxf_ref, qb_ref):
    for h in range(3):
        half = V_AT[h][1]
        first = 0 if half else 64
        acc = acc_ref[h]
        total = acc[:, first : first + 1]
        ctx = acc[:, 64 * half : 64 * half + 64] / total
        ctxf_ref[:, 64 * h : 64 * h + 64] = ctx
        ctx_ref[:, 64 * h : 64 * h + 64] = ctx.astype(BF)
        lse = m_ref[h] + jnp.log(total)
        for side in range(2):
            qb_ref[side, h] = query_operand(at, q_ref, inside, slopes, side, h, tokens, lse)


def fwd_kernel(nz, layers, host, R):
    at = Place(nz)
    tokens = R.x0.shape[0]
    rows, half_rows = 4 * tokens, 2 * tokens
    quarter = R.hid.shape[1]
    group = R.ctx_now[0].shape[1]
    at.enter(host)
    part = R.part
    square_sum = SquareSum(at, part, R.pair, R.single, R.ss_send, R.ss_recv)
    gather_x = [SquareGather(at, R.xr_now[l], R.x_send.at[l], R.x_recv.at[l]) for l in range(layers)]
    gather_y = [SquareGather(at, R.yr_now[l], R.y_send.at[l], R.y_recv.at[l]) for l in range(layers)]
    kv = BlockGather(at, R.kv_now)
    saves, waited = [], []

    def save(source, target):
        saves.append(pltpu.make_async_copy(source, target, R.saved.at[len(saves)]))
        saves[-1].start()
        return len(saves) - 1

    def wait_saved(number):
        saves[number].wait()
        waited.append(number)

    if host:
        qkv, gu, down = [[BlockGather(at, item) for item in items] for items in (R.qkv_now, R.gu_now, R.down_now)]
        ow = BlockGather(at, R.ow_now)
        qkv_w, gu_w, down_w, out_w = [g.buf for g in qkv], [g.buf for g in gu], [g.buf for g in down], R.out_now
        wrows = R.ow_now.buf.shape[2] // layers
        lists = [qkv[l] for l in range(layers)] + [gu[l] for l in range(layers)]
        columns, first = [], 0
        for item in lists:
            columns.append(pl.ds(first, item.buf.shape[3]))
            first += item.buf.shape[3]
        spread = [PlaneExchange(at, R.spread, R.spread_in[i], R.spread_send.at[i], R.spread_recv.at[i], columns[i])
                  for i in range(len(lists))]

        def arrive(i):
            spread[i].wait()
            lists[i].put(spread[i].rows(wrows).astype(BF))

        to_holder = remote(R.ow_mine, R.ow_in, R.ow_send, R.ow_recv, at.holder)
        spread[0].start()
    else:
        qkv_w, gu_w, down_w, out_w = R.qkv_given, R.gu_given, R.down_given, R.out_given

    R.xr_now[0][at.g] = R.x0[...]
    gather_x[0].start()
    if host:
        spread[layers].start()

        @pl.when(at.moves)
        def _():
            to_holder.start()

        @pl.when(jnp.logical_not(at.moves))
        def _():
            R.ow_in[...] = R.ow_mine[...]
        arrive(0)
        qkv[0].start()
        for l in range(layers):
            down[l].put(R.down_own[l][...])

        @pl.when(at.moves)
        def _():
            to_holder.wait_recv()
        ow.put(R.ow_in[...])
        ow.start()

    def columns(b):
        R.kaug_now[b // 2, b % 2] = key_columns(at, R.slopes, R.seg, b // 2, b % 2, tokens)
    loop(0, 2 * nz, columns)
    save(R.kaug_now, R.kaug)
    R.inside[...] = segment_columns(at, R.seg, rows)

    def small(l, t):
        return R.small[8 * l + t : 8 * l + t + 1, :]

    def of(buf, half):
        v = buf[pl.ds(2 * half, 2)]
        return v.reshape(half_rows, v.shape[2])

    def half_at(half):
        return pl.ds(pl.multiple_of(half * half_rows, half_rows), half_rows)

    def put_part(half, value):
        part[pl.ds(2 * half, 2)] = value.reshape(2, tokens, value.shape[1])

    def of_group(row):
        value = jnp.zeros((1, group), F32)
        for g in range(4):
            value = jnp.where(at.g == g, row[:, group * g : group * g + group], value)
        return value

    if host:
        qkv[0].serve_all()
        arrive(layers)
        gu[0].start()
        down[0].start()
        qkv[0].collect()
    R.small[...] = side_weight(qkv_w[0], 1, 128, 256).astype(F32).T[64 : 64 + 8 * layers, :]
    R.state[...] = R.x0[...].astype(F32)
    gather_x[0].wait_near()
    gather_x[0].wait_far()

    for l in range(layers):
        last = l == layers - 1
        x_all = R.xr_now[l][...].reshape(rows, -1)
        save(R.xr_now[l], R.xr[l])
        qb, vb = of_group(small(l, 2)), of_group(small(l, 3))
        none = jnp.zeros((1, 128), F32)
        kv_bias = jnp.concatenate([none, vb[:, :128], none[:, :64], vb[:, 128:192]], axis=1)
        if l:
            pl.semaphore_wait(R.kv_free, at.neighbours())
        kv.put((dot(x_all, side_weight(qkv_w[l], 0)) + kv_bias).astype(BF))
        kv.start()
        if host and not last:
            spread[l + 1].start()
            spread[layers + l + 1].start()
        R.q[...] = (dot(x_all, side_weight(qkv_w[l], 1, 0, group)) + qb).astype(BF)
        for side in range(2):
            for h in range(3):
                R.q_op[side, h] = query_operand(at, R.q, R.inside, R.slopes, side, h, tokens)

        def behind(d, l=l):
            if host and l == 0:
                ow.serve(d)
                gu[l].serve(d)
                down[l].serve(d)

        def ahead(d, l=l):
            if host and l < layers - 1:
                for p in range(d, nz if d == 3 else d + 1):
                    gu[l + 1].serve(p)
                    down[l + 1].serve(p)
        attention(at, kv, R.q_op, R.kaug_now, R.m, R.acc, behind)
        attention_end(at, R.q, R.inside, R.slopes, tokens, R.m, R.acc, R.ctx_now[l], R.ctxf_now[l], R.qb_now[l])
        kv_saved = save(kv.buf, R.kv[l])
        save(R.ctx_now[l], R.ctx[l])
        save(R.ctxf_now[l], R.ctxf[l])
        save(R.qb_now[l], R.qb[l])
        kv.finish()
        if l == 0 and host:
            ow.collect()
            step = group // (2 * nz)
            for i in range(layers):
                for b in range(2 * nz):
                    R.ow_wide[...] = ow.buf[b // 2, b % 2].astype(F32)
                    R.ow_flat[step * b : step * b + step, :] = R.ow_wide[step * i : step * i + step, :]
                R.out_now[i][...] = R.ow_flat[...].astype(BF)
                save(R.out_now[i], R.out_w[i])
        if not last and host:
            arrive(l + 1)
            qkv[l + 1].start()
            arrive(layers + l + 1)
            gu[l + 1].start()
            down[l + 1].start()
        if l:
            square_sum.finish()
        for number, half in enumerate((1 - at.x, at.x)):
            put_part(half, dot(R.ctx_now[l][half_at(half), :], out_w[l][...]))
            if number == 0:
                square_sum.send_far()
            else:
                square_sum.send_near()
        square_sum.relay()
        wait_saved(kv_saved)
        if not last:
            at.signal_neighbours(R.kv_free)
        R.sum1_now[l][...] = R.state[...] + (square_sum.total() + small(l, 4))
        save(R.sum1_now[l], R.sum1[l])
        y = layer_norm(R.sum1_now[l][...], small(l, 0), small(l, 5))
        R.yr_now[l][at.g] = y.astype(BF)
        gather_y[l].start()
        R.state[...] = y
        if host:
            gu[l].collect()
            down[l].collect()
        gather_y[l].wait_near()
        if l:
            wait_saved(mixed_saved)
        square_sum.finish()
        for number, half in enumerate((at.x, 1 - at.x)):
            if number == 1:
                if not last and host:
                    qkv[l + 1].serve_all()
                gather_y[l].wait_far()
                ahead(1)
            here = half_at(half)
            y_half = of(R.yr_now[l], half)
            for col in range(0, quarter, 256):
                gate = dot(y_half, side_weight(gu_w[l], 0, col, col + 256))
                up = dot(y_half, side_weight(gu_w[l], 1, col, col + 256))
                R.mixed_now[here, col : col + 256] = gate
                R.mixed_now[here, quarter + col : quarter + col + 256] = up
                R.hid[:, col : col + 256] = (gate * normal_cdf(gate) * up).astype(BF)
            put_part(half, dot(R.hid[...], flat_weight(down_w[l])))
            if number == 0:
                square_sum.send_near()
            else:
                square_sum.send_far()
        mixed_saved = save(R.mixed_now, R.mixed[l])
        save(R.yr_now[l], R.yr[l])
        if host:
            save(qkv[l].buf, R.qkv_w[l])
            save(gu[l].buf, R.gu_w[l])
            save(down[l].buf, R.down_w[l])
        square_sum.relay()
        ahead(2)
        if not last and host:
            qkv[l + 1].collect()
        R.sum2_now[l][...] = R.state[...] + (square_sum.total() + small(l, 6))
        save(R.sum2_now[l], R.sum2[l])
        state = layer_norm(R.sum2_now[l][...], small(l, 1), small(l, 7))
        R.state[...] = state
        if last:
            R.output[...] = state.astype(BF)
        else:
            R.xr_now[l + 1][at.g] = state.astype(BF)
            gather_x[l + 1].start()
            gather_x[l + 1].wait_near()
            ahead(3)
            gather_x[l + 1].wait_far()
    for l in range(layers):
        gather_x[l].finish()
        gather_y[l].finish()
    square_sum.finish()
    if host:
        for items in (qkv, gu, down):
            for item in items:
                item.finish()
        ow.finish()
        for item in spread:
            item.finish()

        @pl.when(at.moves)
        def _():
            to_holder.wait_send()
    for number, copy in enumerate(saves):
        if number not in waited:
            copy.wait()


def fwd(x0, slopes, seg, weights, layers, host):
    nb, _, rows = seg.shape
    nz = nb // 2
    tokens, width = x0.shape
    group = width // 4
    each = range(layers)
    quarter = weights.spread.shape[2] // layers - 384 if host else weights.gu_given[0].shape[3]
    r = width // nz
    keep_rows = lambda: [keep(4, tokens, width) for _ in each]
    keep_wide = lambda: [keep(tokens, width, dtype=F32) for _ in each]
    scratch = dict(
        xr_now=keep_rows(), x_send=copies(layers, 4), x_recv=copies(layers, 4),
        yr_now=keep_rows(), y_send=copies(layers, 4), y_recv=copies(layers, 4),
        part=keep(4, tokens, width, dtype=F32), state=keep(tokens, width, dtype=F32), **square_sum_items(tokens, width),
        kv_now=block_gather_item(nz, rows, 384), kv_free=pltpu.SemaphoreType.REGULAR, saved=copies(16 * layers),
        kaug_now=keep(nz, 2, rows, 128), inside=keep(rows, 128, dtype=F32),
        q=keep(rows, group), q_op=keep(2, 3, rows, 128),
        m=keep(3, rows, 128, dtype=F32), acc=keep(3, rows, 128, dtype=F32),
        ctx_now=[keep(rows, group) for _ in each], ctxf_now=[keep(rows, group, dtype=F32) for _ in each],
        qb_now=[keep(2, 3, rows, 128) for _ in each], sum1_now=keep_wide(), sum2_now=keep_wide(),
        mixed_now=keep(rows, 2 * quarter, dtype=F32), hid=keep(2 * tokens, quarter))
    far_out = dict(
        xr=[shape(4, tokens, width) for _ in each], yr=[shape(4, tokens, width) for _ in each],
        kv=[shape(nz, 2, rows, 384) for _ in each], ctx=[shape(rows, group) for _ in each],
        ctxf=[shape(rows, group, dtype=F32) for _ in each], qb=[shape(2, 3, rows, 128) for _ in each],
        sum1=[shape(tokens, width, dtype=F32) for _ in each], sum2=[shape(tokens, width, dtype=F32) for _ in each],
        mixed=[shape(rows, 2 * quarter, dtype=F32) for _ in each], kaug=shape(nz, 2, rows, 128))
    near = dict(x0=x0, seg=seg, **vars(weights))
    if host:
        gathered = lambda *dims: [shape(nz, 2, *dims) for _ in each]
        items = lambda *dims: [block_gather_item(nz, *dims) for _ in each]
        rd = weights.down_own[0].shape[0]
        padded = weights.spread.shape[1]
        far_out.update(qkv_w=gathered(r, 384), gu_w=gathered(r, quarter), down_w=gathered(rd, width),
                       out_w=[shape(group, width) for _ in each])
        scratch.update(
            qkv_now=items(r, 384), gu_now=items(r, quarter), down_now=items(rd, width),
            spread_in=[keep(8, padded, 384) for _ in each] + [keep(8, padded, quarter) for _ in each],
            spread_send=copies(2 * layers, 8), spread_recv=copies(2 * layers, 8),
            ow_in=keep(*weights.ow_mine.shape), ow_send=pltpu.SemaphoreType.DMA, ow_recv=pltpu.SemaphoreType.DMA,
            ow_now=block_gather_item(nz, *weights.ow_mine.shape), out_now=[keep(group, width) for _ in each],
            ow_wide=keep(*weights.ow_mine.shape, dtype=F32), ow_flat=keep(group, width, dtype=F32))
    out = dict(output=shape(tokens, width), small=shape(8 * layers, width, dtype=F32))
    done = call(functools.partial(fwd_kernel, nz, layers, host), "forward", 0, near=near, table=dict(slopes=slopes),
                out=out, far_out=far_out, scratch=scratch)
    if not host:
        done.qkv_w, done.gu_w, done.down_w, done.out_w = weights.qkv_given, weights.gu_given, weights.down_given, weights.out_given
    done.down_w = [w.reshape(quarter, width) for w in done.down_w]
    done.xr = [v.reshape(rows, width) for v in done.xr]
    done.yr = [v.reshape(rows, width) for v in done.yr]
    return done


def attn_back(at, R, l, top, begin, behind, at_end):
    nz, rows = at.nz, R.kvbuf.shape[1]
    q_ref, do_ref, dqacc = R.qb[l], R.do, R.dqacc
    dkv = BlockSum(at, R.dkv)

    def target(i):
        right = nz - 1 - at.z
        from_right = jnp.where(i < right, nz - 1 - i, i - right)
        from_left = jnp.where(i < at.z, i, nz - 1 - (i - at.z))
        return jnp.where(i == nz - 1, at.z, jnp.where(at.z < nz // 2, from_right, from_left))

    class Load:
        def __init__(self, t, slot):
            cc = at.oc if slot == 0 else at.c
            self.copies = [pltpu.make_async_copy(source.at[t, cc], target.at[slot], R.kvsem.at[i, slot])
                           for i, (source, target) in enumerate(((R.kv[l], R.kvbuf), (R.kaug, R.augbuf)))]

        def start(self):
            for copy in self.copies:
                copy.start()

        def wait(self):
            for copy in self.copies:
                copy.wait()

    load = Load

    dqacc[...] = jnp.zeros(dqacc.shape, F32)

    def compute(t, slot, same):
        cc = at.oc if slot == 0 else at.c
        side = (t > at.z).astype(jnp.int32)
        kv, aug = R.kvbuf.at[slot], R.augbuf[slot]
        dks, dvs = [], []
        for h in range(3):
            k, v = k_operand(kv, aug, h), v_operand(kv, h)
            if same:
                s = jnp.minimum(dot(k, q_ref[0, h], NT), dot(k, q_ref[1, h], NT))
            else:
                s = dot(k, q_ref[side, h], NT)
            p = jnp.exp(s)
            ds = (p * dot(v, do_ref[h], NT)).astype(BF)
            dvs.append(dot(p.astype(BF), do_ref[h]))
            dks.append(dot(ds, q_ref[side, h]))
            dqacc[h] += dot(ds, k, TN)
        low = in_half(0, rows)
        dkv.stage[t, cc, :, 0:128] = jnp.where(low, dks[0], dks[1]).astype(BF)
        dkv.stage[t, cc, :, 128:256] = jnp.where(low, dvs[0], dvs[1]).astype(BF)
        dkv.stage[t, cc, :, 256:384] = jnp.where(low, dks[2], dvs[2]).astype(BF)

    def far(t, same):
        load(t, 1).start()
        load(t, 0).wait()
        compute(t, 0, same)
        dkv.to_beside(t).start()

    load(target(0), 0).start()
    begin()
    if not top:
        pl.semaphore_wait(R.dkv.free, at.neighbours())

    def step(i):
        t = target(i)
        far(t, False)
        load(target(i + 1), 0).start()
        load(t, 1).wait()
        compute(t, 1, False)
        dkv.serve(i, relay=False)

        @pl.when(i > 0)
        def _():
            dkv.serve(i - 1, source=False)
        behind(i)
    loop(0, nz - 1, step)
    far(at.z, True)
    dkv.serve(nz - 2, source=False)
    load(at.z, 1).wait()
    compute(at.z, 1, True)
    at_end()
    dq = jnp.where(in_half(0, rows), dqacc[0], dqacc[1]) * 0.125
    R.dproj[:, 384:512] = dq.astype(BF)
    R.dproj[:, 512:576] = (dqacc[2][:, 0:64] * 0.125).astype(BF)
    R.dproj[:, 0:384] = dkv.total().astype(BF)
    if l > 0:
        at.signal_neighbours(R.dkv.free)
    dkv.finish()


def bwd_kernel(nz, layers, host, R):
    at = Place(nz)
    tokens = R.grad.shape[0]
    rows, half_rows = 4 * tokens, 2 * tokens
    quarter = R.hid.shape[1]
    width = R.grad.shape[1]
    mixed, yr, xr, gu_w, down_w, qkv_w = range(6)
    streams = ((R.mixed, R.mixed_now), (R.yr, R.yr_now), (R.xr, R.xr_now), (R.gu_w, R.gu_now), (R.down_w, R.down_now),
               (R.qkv_w, R.qkv_now))

    def load(which, l):
        return pltpu.make_async_copy(streams[which][0][l], streams[which][1], R.load.at[which])

    for which in range(6):
        load(which, layers - 1).start()
    at.enter(host)
    R.dproj[:, 576:768] = jnp.zeros((rows, 192), BF)
    gather_df = SquareGather(at, R.df, R.df_send, R.df_recv)
    gather_da = SquareGather(at, R.da, R.da_send, R.da_recv)
    part = R.part
    square_sum = SquareSum(at, part, R.pair, R.single, R.ss_send, R.ss_recv)
    if host:
        gu_sum, dn_sum, qk_sum, ow_sum = [[BlockSum(at, item) for item in items] for items in (R.gu, R.dn, R.qk, R.ow)]
        sm_sum = BlockSum(at, R.sm)
        back = [PlaneExchange(at, item.out, item.inbox, item.send, item.recv) for item in R.back]
        wrows = R.out_grad.shape[1]
        moved = [remote(R.ow_out.at[l], R.ow_in.at[l], R.ow_send.at[l], R.ow_recv.at[l], at.chunk_device) for l in range(layers)]

    def small(l, t):
        return R.small[8 * l + t : 8 * l + t + 1, :]

    def put_small(l, t, value):
        R.tok_small[8 * l + t : 8 * l + t + 1, :] = value

    def of(buf, half):
        v = buf[pl.ds(2 * half, 2)]
        return v.reshape(half_rows, v.shape[2])

    def half_at(half):
        return pl.ds(pl.multiple_of(half * half_rows, half_rows), half_rows)

    def put_part(half, value):
        part[pl.ds(2 * half, 2)] = value.reshape(2, tokens, value.shape[1])

    def wgrad(left, right, stage, cc, lo, hi):
        for first in range(0, left.shape[1], 384):
            v = dot(left[:, first : first + 384], right[:, lo:hi], TN)
            if len(stage.shape) == 2:
                stage[first : first + 384, :] = v.astype(BF)
                continue
            step = stage.shape[2]
            for i in range(384 // step):
                b = first // step + i
                zz, side = (b // 2, b % 2) if cc is None else (b, cc)
                stage[zz, side] = v[step * i : step * i + step].astype(BF)

    def feed_forward_sums(l):
        return (gu_sum[l], dn_sum[l]) if host and l < layers else ()

    def attention_sums(l):
        return (qk_sum[l], ow_sum[l]) if host and l < layers else ()

    def serve(items, p):
        for item in items:
            item.serve(p)

    def emit(l):
        if not host or l == layers:
            return
        pad = lambda v: jnp.concatenate([v, jnp.zeros((R.back[l].out.shape[1] - wrows, v.shape[1]), F32)], axis=0).astype(BF)
        for item, lo in ((gu_sum[l], 0), (qk_sum[l], quarter)):
            v = item.total()
            for k in range(8):
                R.back[l].out[k, :, lo : lo + v.shape[1]] = pad(v[wrows * k : wrows * k + wrows])
        back[l].start()
        R.dn_grad[l] = dn_sum[l].total()
        R.ow_out[l] = ow_sum[l].total()

        @pl.when(at.moves)
        def _():
            moved[l].start()

        @pl.when(jnp.logical_not(at.moves))
        def _():
            R.ow_in[l] = R.ow_out[l]

    def assemble(l):
        back[l].wait()
        piece = [R.back[l].inbox[k].astype(F32)[0:wrows] for k in range(8)]
        join = lambda side, *spans: jnp.concatenate(
            [piece[2 * g + side][:, lo:hi] for g in range(4) for lo, hi in spans], axis=1)
        at_kv = quarter
        R.qkv_grad[l, :, 0:width] = join(1, (at_kv, at_kv + 192))
        R.qkv_grad[l, :, width : 2 * width] = join(0, (at_kv, at_kv + 128), (at_kv + 256, at_kv + 320))
        R.qkv_grad[l, :, 2 * width : 3 * width] = join(0, (at_kv + 128, at_kv + 256), (at_kv + 320, at_kv + 384))
        step = quarter // nz
        for side in range(2):
            for zz in range(nz):
                lo = (side * nz + zz) * 4 * step
                R.gu_grad[l, :, lo : lo + 4 * step] = join(side, (step * zz, step * zz + step))

        @pl.when(at.moves)
        def _():
            moved[l].wait_recv()
        R.out_grad[l] = R.ow_in[l, 0:wrows, :]

    def small_copy(j):
        k = 4 * at.c + j
        return remote(R.sm_out, R.sm_in.at[at.g], R.sm_send.at[j], R.sm_recv.at[at.g], at.of_plane(k)), k != at.member

    def small_from(g):
        k = 2 * g + at.x
        return remote(R.sm_out, R.sm_in.at[g], R.sm_send.at[0], R.sm_recv.at[g], at.of_plane(k)), k != at.member

    R.g[...] = R.grad[...].astype(F32)
    for l in reversed(range(layers)):
        top = l == layers - 1
        e2, d_gain, d_shift = norm_back(R.g[...], R.sum2[l][...], small(l, 1))
        put_small(l, 1, d_gain)
        put_small(l, 5, d_shift)
        low = e2.astype(BF)
        put_small(l, 4, jnp.sum(low.astype(F32), axis=0, keepdims=True))
        if not top:
            square_sum.finish()
        R.df[at.g] = low
        gather_df.start()
        R.e2[...] = e2
        for which in range(6):
            load(which, l).wait()
        serve(feed_forward_sums(l + 1), 1)
        gather_df.wait_near()
        for number, half in enumerate((at.x, 1 - at.x)):
            if number == 1:
                gather_df.wait_far()
                serve(attention_sums(l + 1), 1)
            here = half_at(half)
            dhid_all = dot(of(R.df, half), R.down_now[...], NT)
            for col in range(0, quarter, 256):
                dhid = dhid_all[:, col : col + 256]
                gate = R.mixed_now[here, col : col + 256]
                up = R.mixed_now[here, quarter + col : quarter + col + 256]
                cdf = normal_cdf(gate)
                act = gate * cdf
                R.hid[here, col : col + 256] = (act * up).astype(BF)
                R.dgu[here, col : col + 256] = (dhid * up * (cdf + gate * normal_pdf(gate))).astype(BF)
                R.dgu[here, quarter + col : quarter + col + 256] = (dhid * act).astype(BF)
            put_part(half, dot(R.dgu[here, :quarter], side_weight(R.gu_now, 0), NT)
                     + dot(R.dgu[here, quarter:], side_weight(R.gu_now, 1), NT))
            if number == 0:
                square_sum.send_near()
            else:
                square_sum.send_far()
        wgrad(R.hid, R.df[...].reshape(rows, width), R.dn[l].stage, None, 0, width)
        square_sum.relay()
        serve(feed_forward_sums(l + 1), 2)
        for p in range(3, nz - 1):
            serve(feed_forward_sums(l + 1), p)
        dy = R.e2[...] + square_sum.total()
        e1, d_gain, d_shift = norm_back(dy, R.sum1[l][...], small(l, 0))
        put_small(l, 0, d_gain)
        put_small(l, 3, d_shift)
        low = e1.astype(BF)
        put_small(l, 2, jnp.sum(low.astype(F32), axis=0, keepdims=True))
        R.da[at.g] = low
        gather_da.start()
        R.e1[...] = e1
        for cc in range(2):
            wgrad(R.yr_now, R.dgu, R.gu[l].stage, cc, quarter * cc, quarter * cc + quarter)
        gather_da.wait_near()
        gather_da.wait_far()
        for item in feed_forward_sums(l):
            item.start()
        if l > 0:
            for which in (mixed, yr, gu_w, down_w):
                load(which, l - 1).start()
        da_all = R.da[...].reshape(rows, width)
        dctx = dot(da_all, R.out_w[l][...], NT).astype(BF)
        d_out = dot(R.ctx[l][...], da_all, TN)
        if host:
            step = d_out.shape[0] // (2 * nz)
            for b in range(2 * nz):
                R.ow[l].stage[b // 2, b % 2] = jnp.concatenate(
                    [d_out[step * b : step * b + step], jnp.zeros((OW_ROWS - step, width), F32)]).astype(BF)
        else:
            R.ow[l].stage[...] = d_out.astype(BF)
        ctxf = R.ctxf[l]
        wide = dctx.astype(F32)
        first_two = wide[:, :128]
        third = jnp.concatenate([jnp.zeros((rows, 64), F32), wide[:, 128:192]], axis=1)
        prod = first_two * ctxf[:, :128]
        low_half = in_half(0, rows)
        deltas = [
            jnp.sum(jnp.where(low_half, prod, 0.0), axis=1, keepdims=True),
            jnp.sum(jnp.where(low_half, 0.0, prod), axis=1, keepdims=True),
            jnp.sum(wide[:, 128:192] * ctxf[:, 128:192], axis=1, keepdims=True),
        ]
        for h in range(3):
            half = V_AT[h][1]
            base = jnp.where(in_half(half, rows), first_two if h < 2 else third, 0.0)
            R.do[h] = with_lanes(base, 0 if half else 64, split3(-deltas[h])).astype(BF)

        def begin(l=l):
            serve(attention_sums(l + 1), 2)
            for p in range(3, nz - 1):
                serve(attention_sums(l + 1), p)

        def behind(i):
            pass

        def at_end(l=l):
            serve(feed_forward_sums(l), 0)
        attn_back(at, R, l, top, begin, behind, at_end)
        dproj = R.dproj
        bias_sum = jnp.sum(dproj[...].astype(F32), axis=0, keepdims=True)
        for t, row in ((6, bias_sum[:, 384:576]), (7, jnp.concatenate([bias_sum[:, 128:256], bias_sum[:, 320:384]], axis=1))):
            put_small(l, t, jnp.concatenate([jnp.where(at.g == g, row, 0.0) for g in range(4)], axis=1))
        gather_df.finish()
        gather_da.finish()
        square_sum.finish()
        for number, half in enumerate((1 - at.x, at.x)):
            put_part(half, dot(dproj[half_at(half), :384], side_weight(R.qkv_now, 0), NT)
                     + dot(dproj[half_at(half), 384:], side_weight(R.qkv_now, 1), NT))
            if number == 0:
                square_sum.send_far()
            else:
                square_sum.send_near()
        square_sum.relay()
        for cc in range(2):
            wgrad(R.xr_now, dproj, R.qk[l].stage, cc, 384 * cc, 384 * cc + 384)
        for item in attention_sums(l):
            item.start()
        serve(attention_sums(l), 0)
        if l > 0:
            load(xr, l - 1).start()
            load(qkv_w, l - 1).start()
        emit(l + 1)
        R.g[...] = R.e1[...] + square_sum.total()
    R.grad_in[...] = R.g[...]
    square_sum.finish()
    if host:
        for b in range(2 * nz):
            step = width // (2 * nz)
            sm_sum.stage[b // 2, b % 2, :, 0:step] = R.tok_small[:, step * b : step * b + step]
        sm_sum.start()
        last = feed_forward_sums(0) + attention_sums(0) + (sm_sum,)
        sm_sum.serve(0)
        for p in range(1, nz - 1):
            serve(last, p)
        R.sm_out[...] = sm_sum.total()
        for j in range(4):
            copy, away = small_copy(j)

            @pl.when(away)
            def _(copy=copy):
                copy.start()

            @pl.when(jnp.logical_not(away))
            def _():
                R.sm_in[at.g] = R.sm_out[...]
        emit(0)
        for l in range(1, layers):
            assemble(l)
        total = jnp.zeros(R.sm_out.shape, F32)
        for g in range(4):
            copy, away = small_from(g)

            @pl.when(away)
            def _(copy=copy):
                copy.wait_recv()
            total = total + R.sm_in[g]
        mine = jnp.zeros((8 * layers, wrows), F32)
        for k in range(4):
            mine = jnp.where(2 * at.y + at.c == k, total[:, wrows * k : wrows * k + wrows], mine)
        for l in range(layers):
            R.gains_grad[l] = mine[8 * l : 8 * l + 2]
            R.biases_grad[l] = jnp.concatenate([mine[8 * l + 6 : 8 * l + 8], mine[8 * l + 2 : 8 * l + 6]], axis=0)
        assemble(0)
        for l in range(layers):
            for item in feed_forward_sums(l) + attention_sums(l) + (back[l],):
                item.finish()

            @pl.when(at.moves)
            def _(l=l):
                moved[l].wait_send()
        for j in range(4):
            copy, away = small_copy(j)

            @pl.when(away)
            def _(copy=copy):
                copy.wait_send()
        sm_sum.finish()


def bwd(grad, saved, host):
    layers = len(saved.qkv_w)
    nz, _, rows, _ = saved.kaug.shape
    tokens, width = grad.shape
    quarter, group = width, width // 4
    quarter = saved.down_w[0].shape[0]
    r, rd = width // nz, quarter // (2 * nz)
    each = range(layers)
    out = dict(grad_in=shape(tokens, width, dtype=F32))
    scratch = {}
    if host:
        wrows, padded = width // (8 * nz), 32
        out.update(
            qkv_grad=shape(layers, wrows, 3 * width, dtype=F32), out_grad=shape(layers, wrows, width, dtype=F32),
            gu_grad=shape(layers, wrows, 8 * quarter, dtype=F32), dn_grad=shape(layers, rd, width, dtype=F32),
            gains_grad=shape(layers, 2, wrows, dtype=F32), biases_grad=shape(layers, 6, wrows, dtype=F32))
        scratch.update(
            back=[dict(out=keep(8, padded, quarter + 384), inbox=keep(8, padded, quarter + 384), send=copies(8), recv=copies(8))
                  for _ in each],
            ow_out=keep(layers, OW_ROWS, width, dtype=F32), ow_in=keep(layers, OW_ROWS, width, dtype=F32),
            ow_send=copies(layers), ow_recv=copies(layers),
            sm_out=keep(8 * layers, 128, dtype=F32), sm_in=keep(4, 8 * layers, 128, dtype=F32), sm_send=copies(4), sm_recv=copies(4))
        scratch.update(
            gu=[block_sum_item(nz, r, quarter) for _ in each], dn=[block_sum_item(nz, rd, width) for _ in each],
            qk=[block_sum_item(nz, r, 384) for _ in each], ow=[block_sum_item(nz, OW_ROWS, width) for _ in each],
            sm=block_sum_item(nz, 8 * layers, 128, dtype=F32), tok_small=keep(8 * layers, width, dtype=F32))
    else:
        out.update(
            gu=[dict(stage=shape(nz, 2, r, quarter)) for _ in each], dn=[dict(stage=shape(quarter, width)) for _ in each],
            qk=[dict(stage=shape(nz, 2, r, 384)) for _ in each], ow=[dict(stage=shape(group, width)) for _ in each],
            tok_small=shape(8 * layers, width, dtype=F32))
    like = lambda arrays: keep(*arrays[0].shape, dtype=arrays[0].dtype)
    scratch.update(
        mixed_now=like(saved.mixed), yr_now=like(saved.yr), xr_now=like(saved.xr), gu_now=like(saved.gu_w),
        down_now=like(saved.down_w), qkv_now=like(saved.qkv_w), load=copies(6), kvbuf=keep(2, rows, 384), augbuf=keep(2, rows, 128), kvsem=copies(2, 2),
        df=keep(4, tokens, width), df_send=copies(4), df_recv=copies(4),
        da=keep(4, tokens, width), da_send=copies(4), da_recv=copies(4),
        part=keep(4, tokens, width, dtype=F32), **square_sum_items(tokens, width),
        g=keep(tokens, width, dtype=F32), e1=keep(tokens, width, dtype=F32), e2=keep(tokens, width, dtype=F32),
        hid=keep(rows, quarter), dgu=keep(rows, 2 * quarter), do=keep(3, rows, 128),
        dqacc=keep(3, rows, 128, dtype=F32), dproj=keep(rows, 768),
        dkv=dict(block_sum_item(nz, rows, 384), free=pltpu.SemaphoreType.REGULAR))
    near = dict(grad=grad, small=saved.small, sum1=saved.sum1, sum2=saved.sum2, ctx=saved.ctx,
                ctxf=saved.ctxf, qb=saved.qb, out_w=saved.out_w)
    far = dict(mixed=saved.mixed, yr=saved.yr, xr=saved.xr, gu_w=saved.gu_w, down_w=saved.down_w, kv=saved.kv, kaug=saved.kaug,
               qkv_w=saved.qkv_w)
    return call(functools.partial(bwd_kernel, nz, layers, host), "backward", 1, near=near, far=far, out=out, scratch=scratch)


def shards(hidden_in, out_grad, segment_ids, alibi_slopes, qkv_weight, out_weight, gate_up_weight, down_weight, gains, biases):
    nz = lax.axis_size("z")
    nb = 2 * nz
    square, everyone, blocks = ("x", "y", "c"), ("z", "x", "y", "c"), ("z", "c")
    z, c = lax.axis_index("z"), lax.axis_index("c")
    tokens, width = hidden_in.shape
    layers, wrows = qkv_weight.shape[:2]
    ff = gate_up_weight.shape[2] // 2
    group, quarter = width // 4, ff // 4
    host = (width // nz) % 16 == 0 and down_weight.shape[1] % 16 == 0

    def to_groups(w):
        w = w.reshape(wrows, 3, 4, 3, 64)
        q, k, v = w[:, 0], w[:, 1], w[:, 2]
        kv = jnp.stack([k[:, :, 0], k[:, :, 1], v[:, :, 0], v[:, :, 1], k[:, :, 2], v[:, :, 2]], axis=2)
        return kv.reshape(wrows, 4, 384), q.reshape(wrows, 4, group)

    def from_groups(kv, q):
        kv, q = kv.reshape(4, wrows, 6, 64), q.reshape(4, wrows, 3, 64)
        k = jnp.stack([kv[:, :, 0], kv[:, :, 1], kv[:, :, 4]], axis=2)
        v = jnp.stack([kv[:, :, 2], kv[:, :, 3], kv[:, :, 5]], axis=2)
        return jnp.stack([q, k, v]).transpose(2, 0, 1, 3, 4).reshape(wrows, 3 * width)

    places = [(8 * zz + 2 * g + cc, g * nb + 2 * zz + cc) for zz in range(nz) for g in range(4) for cc in range(2)]
    gu0 = 384 * layers

    def gathered_outside(both, out_weight, down_weight):
        spread = lax.all_to_all(both, square, split_axis=1, concat_axis=0, tiled=True).reshape(8 * wrows, -1)
        ow_own = lax.ppermute(out_weight, everyone, [(chunk, device) for device, chunk in places])
        whole = lambda v: lax.all_gather(v, blocks, axis=0).reshape(nz, 2, *v.shape)
        flat = lambda v: lax.all_gather(v, blocks, axis=0, tiled=True)
        return types.SimpleNamespace(
            qkv_given=[whole(spread[:, 384 * l : 384 * l + 384]) for l in range(layers)],
            gu_given=[whole(spread[:, gu0 + quarter * l : gu0 + quarter * l + quarter]) for l in range(layers)],
            down_given=[flat(down_weight[l]) for l in range(layers)], out_given=[flat(ow_own[l]) for l in range(layers)])

    small = jnp.concatenate([gains, biases], axis=1).transpose(0, 2, 1)
    small = jnp.concatenate([small[l] for l in range(layers)], axis=1)
    small = jnp.pad(small, ((0, 0), (0, 192 - small.shape[1])))
    small = jnp.broadcast_to(small[:, None], (wrows, 4, 192))
    nothing = jnp.zeros((wrows, 4, 192), BF)
    gu = gate_up_weight.reshape(layers, wrows, 2, nz, 4, quarter // nz).transpose(0, 1, 4, 2, 3, 5).reshape(layers, wrows, 4, 2, quarter)
    sides = [[], []]
    for l in range(layers):
        kv, q = to_groups(qkv_weight[l])
        sides[0].append(kv)
        sides[1] += [q, nothing if l else small]
    for l in range(layers):
        for side in range(2):
            sides[side].append(gu[l, :, :, side])
    both = jnp.stack([jnp.concatenate(side, axis=2) for side in sides], axis=2).reshape(wrows, 8, -1)
    if host:
        spread = jnp.pad(both.transpose(1, 0, 2), ((0, 0), (0, 32 - wrows), (0, 0)))
        weights = types.SimpleNamespace(
            spread=spread, down_own=[down_weight[l] for l in range(layers)], ow_mine=out_weight.reshape(layers * wrows, width))
    else:
        weights = gathered_outside(both, out_weight, down_weight)

    seg = segment_ids.reshape(nz, 4, 2, tokens).transpose(0, 2, 1, 3).reshape(nb, 1, 4 * tokens)
    saved = fwd(hidden_in, alibi_slopes, seg, weights, layers, host)
    done = bwd(out_grad, saved, host)
    if host:
        return (saved.output, done.grad_in, done.qkv_grad, done.out_grad, done.gu_grad, done.dn_grad, done.gains_grad,
                done.biases_grad)
    step = width // nb
    blocks_sum = lambda v: lax.psum_scatter(v, blocks, scatter_dimension=0, tiled=True)
    done.gu_sum = [blocks_sum(item.stage.reshape(nb, -1, quarter))[0] for item in done.gu]
    done.qk_sum = [blocks_sum(item.stage.reshape(nb, -1, 384))[0] for item in done.qk]
    done.dn_sum = [blocks_sum(item.stage) for item in done.dn]
    done.ow_sum = [blocks_sum(item.stage) for item in done.ow]
    sm = lax.psum_scatter(done.tok_small.reshape(-1, nb, step), blocks, scatter_dimension=1, tiled=True)[:, 0]
    sm = sm.T.reshape(4, wrows, 8 * layers)
    high = lax.reduce_precision(sm, 8, 7)
    sm = jnp.concatenate([high, sm - high], axis=2).astype(BF)
    sm = lax.dynamic_update_slice_in_dim(jnp.zeros((8, wrows, 16 * layers), BF), sm, 4 * c, 0)
    rows_of = lambda v: v.reshape(8, wrows, -1)
    back = jnp.concatenate([rows_of(v) for v in done.qk_sum + done.gu_sum] + [sm], axis=2)
    back = lax.all_to_all(back, square, split_axis=0, concat_axis=0, tiled=True)
    sides = back.astype(F32).reshape(4, 2, wrows, -1)
    qkv_grad = jnp.stack([from_groups(sides[:, 0, :, 384 * l : 384 * l + 384], sides[:, 1, :, 384 * l : 384 * l + group])
                          for l in range(layers)])
    gu_grad = jnp.stack([sides[:, :, :, gu0 + quarter * l : gu0 + quarter * l + quarter] for l in range(layers)])
    gu_grad = gu_grad.reshape(layers, 4, 2, wrows, nz, quarter // nz).transpose(0, 3, 2, 4, 1, 5).reshape(layers, wrows, 2 * ff)
    sm = jnp.sum(sides[..., gu0 + quarter * layers :], axis=(0, 1))
    sm = (sm[:, : 8 * layers] + sm[:, 8 * layers :]).T.reshape(layers, 8, wrows)
    out_grad_w = lax.ppermute(jnp.stack(done.ow_sum)[:, :wrows].astype(F32), everyone, places)
    return (saved.output, done.grad_in, qkv_grad, out_grad_w, gu_grad, jnp.stack(done.dn_sum).astype(F32), sm[:, 0:2],
            jnp.concatenate([sm[:, 6:8], sm[:, 2:6]], axis=1))


def solution(mesh):
    nb, nh = mesh.devices.shape
    everyone = ("z", "x", "y", "c")
    tok, mid, last = P(everyone, None), P(None, everyone, None), P(None, None, everyone)
    return jax.shard_map(
        shards, mesh=Mesh(mesh.devices.reshape(nb // 2, 2, nh // 2, 2), everyone),
        in_specs=(tok, tok, P(), P(), mid, mid, mid, mid, last, last),
        out_specs=(tok, tok, mid, mid, mid, mid, last, last),
        check_vma=False,
    )
```

```python
import functools
import types

import jax
import jax.numpy as jnp
from jax import lax
from jax.experimental import pallas as pl
from jax.experimental.pallas import tpu as pltpu
from jax.sharding import Mesh
from jax.sharding import PartitionSpec as P

MESH = pl.DeviceIdType.MESH
BF = jnp.bfloat16
F32 = jnp.float32
NT = (((1,), (1,)), ((), ()))
NN = (((1,), (0,)), ((), ()))
TN = (((0,), (0,)), ((), ()))
EPS = 1e-06
K_AT = ((0, 0), (0, 1), (2, 0))
V_AT = ((1, 0), (1, 1), (2, 1))
ROW_LANE, SEGMENT_LANE = 9, 12
OW_ROWS = 32
VMEM = pl.BlockSpec(memory_space=pltpu.VMEM)
ANY = pl.BlockSpec(memory_space=pl.ANY)


def dot(a, b, dims=NN):
    return lax.dot_general(a, b, dims, preferred_element_type=F32)


def lanes(rows):
    return lax.broadcasted_iota(jnp.int32, (rows, 128), 1)


def in_half(half, rows):
    return lanes(rows) >= 64 if half else lanes(rows) < 64


def ones_half(half, rows):
    first = 0 if half else 64
    lane = lanes(rows)
    return jnp.where((lane >= first) & (lane < first + 3), 1.0, 0.0).astype(BF)


def k_operand(kv, aug, h):
    col, half = K_AT[h]
    return jnp.where(in_half(half, kv.shape[0]), kv[:, 128 * col : 128 * col + 128], aug)


def v_operand(kv, h):
    col, half = V_AT[h]
    rows = kv.shape[0]
    return jnp.where(in_half(half, rows), kv[:, 128 * col : 128 * col + 128], ones_half(half, rows))


def split3(value):
    high = value.astype(BF).astype(F32)
    mid = (value - high).astype(BF).astype(F32)
    return high, mid, value - high - mid


def with_lanes(base, first, values):
    lane = lanes(base.shape[0])
    for i, v in enumerate(values):
        base = jnp.where(lane == first + i, v, base)
    return base


def layer_norm(total, gain, shift):
    centred = total - jnp.mean(total, axis=-1, keepdims=True)
    scale = lax.rsqrt(jnp.mean(centred * centred, axis=-1, keepdims=True) + EPS)
    return centred * scale * gain + shift


def norm_back(grad, total, gain):
    centred = total - jnp.mean(total, axis=-1, keepdims=True)
    scale = lax.rsqrt(jnp.mean(centred * centred, axis=-1, keepdims=True) + EPS)
    n = centred * scale
    dn = grad * gain
    e = scale * (dn - jnp.mean(dn, axis=-1, keepdims=True) - n * jnp.mean(dn * n, axis=-1, keepdims=True))
    return e, jnp.sum(grad * n, axis=0, keepdims=True), jnp.sum(grad, axis=0, keepdims=True)


def normal_cdf(u):
    return 0.5 * (1.0 + lax.erf(u * (0.5**0.5)))


def normal_pdf(u):
    return jnp.exp(-0.5 * u * u) * ((2.0 * jnp.pi) ** -0.5)


def remote(src, dst, send, recv, device):
    return pltpu.make_async_remote_copy(
        src_ref=src, dst_ref=dst, send_sem=send, recv_sem=recv, device_id=device, device_id_type=MESH)


def loop(first, last, do):
    def step(i, carry):
        do(i)
        return carry
    lax.fori_loop(first, last, step, 0)


class Place:
    def __init__(self, nz):
        self.nz = nz
        self.z, self.x, self.y, self.c = [lax.axis_index(name) for name in "zxyc"]
        self.g = 2 * self.x + self.y
        self.gx, self.gy = 2 * (1 - self.x) + self.y, 2 * self.x + 1 - self.y
        self.gd = 2 * (1 - self.x) + 1 - self.y
        self.oc = 1 - self.c
        self.beside = (self.z, self.x, self.y, self.oc)
        self.across_x = (self.z, 1 - self.x, self.y, self.c)
        self.across_y = (self.z, self.x, 1 - self.y, self.c)
        self.block = 2 * self.z + self.c
        self.member = 2 * self.g + self.c
        self.number = 8 * self.z + self.member
        nb = 2 * nz
        self.chunk = self.g * nb + self.block
        self.chunk_device = self.device(self.chunk)
        place = self.number % nb
        self.holder = (place // 2, self.number // nb // 2, self.number // nb % 2, place % 2)
        self.moves = self.chunk != self.number
        self.has_left, self.has_right = self.z > 0, self.z < nz - 1

    def column(self, zz):
        return (zz, self.x, self.y, self.c)

    def device(self, number):
        k = number % 8
        return (number // 8, k // 4, k // 2 % 2, k % 2)

    def of_plane(self, k):
        return (self.z, k // 4, k // 2 % 2, k % 2)

    def neighbours(self):
        return 3 - (self.z == 0).astype(jnp.int32) - (self.z == self.nz - 1).astype(jnp.int32)

    def signal_neighbours(self, semaphore):
        pl.semaphore_signal(semaphore, inc=1, device_id=self.beside, device_id_type=MESH)

        @pl.when(self.has_left)
        def _():
            pl.semaphore_signal(semaphore, inc=1, device_id=self.column(self.z - 1), device_id_type=MESH)

        @pl.when(self.has_right)
        def _():
            pl.semaphore_signal(semaphore, inc=1, device_id=self.column(self.z + 1), device_id_type=MESH)

    def enter(self, plane):
        barrier = pltpu.get_barrier_semaphore()

        def greet(device):
            pl.semaphore_signal(barrier, inc=1, device_id=device, device_id_type=MESH)

        if not plane:
            greet(self.across_x)
            greet(self.across_y)
            self.signal_neighbours(barrier)
            return lambda: pl.semaphore_wait(barrier, 2 + self.neighbours())
        loop(1, 8, lambda j: greet(self.of_plane((self.member + j) % 8)))
        self.signal_neighbours(barrier)

        @pl.when(self.moves)
        def _():
            greet(self.chunk_device)
            greet(self.holder)
        return lambda: pl.semaphore_wait(barrier, 7 + self.neighbours() + 2 * self.moves.astype(jnp.int32))

    def positions(self, zz, cc, tokens, rows):
        row = lax.broadcasted_iota(jnp.int32, (rows, 128), 0)
        return ((zz * 8 + (row // tokens) * 2 + cc) * tokens + row % tokens).astype(F32)


class SquareGather:
    def __init__(self, at, buf, send, recv):
        half = buf.shape[1] // 2
        first, second = pl.ds(0, half), pl.ds(half, half)

        def copy(i, g, rows, device):
            return remote(buf.at[g, rows], buf.at[g, rows], send.at[i], recv.at[i], device)
        self.x_first, self.x_second = copy(0, at.g, first, at.across_x), copy(1, at.g, second, at.across_x)
        self.y_second, self.y_first = copy(2, at.g, second, at.across_y), copy(3, at.g, first, at.across_y)
        self.on_y = copy(4, at.gx, first, at.across_y)
        self.on_x = copy(5, at.gy, second, at.across_x)

    def start(self):
        for copy in (self.x_first, self.y_second, self.x_second, self.y_first):
            copy.start()

    def wait_near(self):
        self.x_first.wait_recv()
        self.on_y.start()
        self.y_second.wait_recv()
        self.on_x.start()
        self.y_first.wait_recv()

    def wait_far(self):
        self.x_second.wait_recv()
        self.on_x.wait_recv()
        self.on_y.wait_recv()

    def finish(self):
        for copy in (self.x_first, self.x_second, self.y_first, self.y_second, self.on_x, self.on_y):
            copy.wait_send()


class SquareSum:
    def __init__(self, at, part, stage, inbox, send, recv):
        self.at, self.part, self.stage, self.inbox = at, part, stage, inbox
        self.half = part.shape[2] // 2
        to = (at.across_x, at.across_x, at.across_y, at.across_y, at.across_y, at.across_x)
        self.copies = [remote(stage.at[i], inbox.at[i], send.at[i], recv.at[i], to[i]) for i in range(6)]

    def left(self, g):
        return self.part[g, :, : self.half]

    def right(self, g):
        return self.part[g, :, self.half :]

    def post(self, i, value):
        self.stage[i] = value.astype(BF)
        self.copies[i].start()

    def came(self, i):
        self.copies[i].wait_recv()
        return self.inbox[i].astype(F32)

    def send_far(self):
        self.post(0, self.left(self.at.gd))
        self.post(2, self.right(self.at.gd))
        self.post(1, self.left(self.at.gx))

    def send_near(self):
        self.post(3, self.right(self.at.gy))

    def relay(self):
        self.post(4, self.left(self.at.gy) + self.came(0))
        self.post(5, self.right(self.at.gx) + self.came(2))

    def total(self):
        left = self.left(self.at.g) + self.came(1)
        right = self.right(self.at.g) + self.came(3)
        return jnp.concatenate([left + self.came(4), right + self.came(5)], axis=1)

    def finish(self):
        for copy in self.copies:
            copy.wait_send()


class BlockGather:
    def __init__(self, at, item):
        self.at, self.buf, self.zsend, self.csend, self.recv = at, item.buf, item.zsend, item.csend, item.recv

    def copy(self, zz, send, device):
        at = self.at
        return remote(self.buf.at[zz, at.c], self.buf.at[zz, at.c], send, self.recv.at[zz, at.c], device)

    def to_right(self, zz):
        return self.copy(zz, self.zsend.at[0, zz], self.at.column(self.at.z + 1))

    def to_left(self, zz):
        return self.copy(zz, self.zsend.at[1, zz], self.at.column(self.at.z - 1))

    def to_beside(self, zz):
        return self.copy(zz, self.csend.at[zz], self.at.beside)

    def wait(self, zz, cc):
        at = self.at
        remote(self.buf.at[zz, cc], self.buf.at[zz, cc], self.csend.at[zz], self.recv.at[zz, cc], at.beside).wait_recv()

    def put(self, value):
        self.buf[self.at.z, self.at.c] = value

    def start(self):
        at = self.at

        @pl.when(at.has_right)
        def _():
            self.to_right(at.z).start()

        @pl.when(at.has_left)
        def _():
            self.to_left(at.z).start()
        self.to_beside(at.z).start()

    def serve(self, d):
        at = self.at

        @pl.when(at.z - d >= 0)
        def _():
            self.wait(at.z - d, at.c)

            @pl.when(at.has_right)
            def _():
                self.to_right(at.z - d).start()
            self.to_beside(at.z - d).start()

        @pl.when(at.z + d < at.nz)
        def _():
            self.wait(at.z + d, at.c)

            @pl.when(at.has_left)
            def _():
                self.to_left(at.z + d).start()
            self.to_beside(at.z + d).start()

    def serve_all(self):
        loop(1, self.at.nz, self.serve)

    def collect(self):
        loop(0, self.at.nz, lambda zz: self.wait(zz, self.at.oc))

    def finish(self):
        at = self.at

        def drain(zz):
            self.to_beside(zz).wait_send()

            @pl.when((zz <= at.z) & at.has_right)
            def _():
                self.to_right(zz).wait_send()

            @pl.when((zz >= at.z) & at.has_left)
            def _():
                self.to_left(zz).wait_send()
        loop(0, at.nz, drain)


def block_gather_item(nz, *dims):
    return dict(buf=keep(nz, 2, *dims), zsend=copies(2, nz), csend=copies(nz), recv=copies(nz, 2))


class BlockSum:
    def __init__(self, at, item):
        self.at, self.stage, self.cin, self.zin = at, item.stage, item.cin, item.zin
        self.csend, self.crecv, self.zsend, self.zrecv = item.csend, item.crecv, item.zsend, item.zrecv

    def to_beside(self, t):
        return remote(self.stage.at[t, self.at.oc], self.cin.at[t], self.csend.at[t], self.crecv.at[t], self.at.beside)

    def to_right(self, t):
        return remote(self.stage.at[t, self.at.c], self.zin.at[t + 1], self.zsend.at[t], self.zrecv.at[t + 1], self.at.column(self.at.z + 1))

    def to_left(self, t):
        return remote(self.stage.at[t, self.at.c], self.zin.at[t], self.zsend.at[t], self.zrecv.at[t], self.at.column(self.at.z - 1))

    def arrived(self, slot):
        at = self.at
        remote(self.zin.at[slot], self.zin.at[slot], self.zsend.at[0], self.zrecv.at[slot], at.beside).wait_recv()

    def start(self):
        loop(0, self.at.nz, lambda t: self.to_beside(t).start())

    def add(self, t, slot=None):
        value = self.stage[t, self.at.c].astype(F32) + self.cin[t].astype(F32)
        if slot is not None:
            value = value + self.zin[slot].astype(F32)
        self.stage[t, self.at.c] = value.astype(self.stage.dtype)

    def go_right(self, t):
        self.to_beside(t).wait_recv()

        @pl.when(self.at.has_left)
        def _():
            self.arrived(t + 1)
            self.add(t, t + 1)

        @pl.when(jnp.logical_not(self.at.has_left))
        def _():
            self.add(t)
        self.to_right(t).start()

    def go_left(self, t):
        self.to_beside(t).wait_recv()

        @pl.when(self.at.has_right)
        def _():
            self.arrived(t)
            self.add(t, t)

        @pl.when(jnp.logical_not(self.at.has_right))
        def _():
            self.add(t)
        self.to_left(t).start()

    def serve(self, p, source=True, relay=True):
        at = self.at
        right, left = p - at.z, p - (at.nz - 1 - at.z)
        go_r = (right >= 0) & (right < at.nz - 1 - at.z)
        go_l = (left >= 0) & (left < at.z)
        if not source:
            go_r, go_l = go_r & at.has_left, go_l & at.has_right
        if not relay:
            go_r, go_l = go_r & jnp.logical_not(at.has_left), go_l & jnp.logical_not(at.has_right)

        @pl.when(go_r)
        def _():
            self.go_right(at.nz - 1 - right)

        @pl.when(go_l)
        def _():
            self.go_left(left)

    def total(self):
        at = self.at
        self.to_beside(at.z).wait_recv()

        @pl.when(at.has_left)
        def _():
            self.arrived(at.z + 1)

        @pl.when(at.has_right)
        def _():
            self.arrived(at.z)
        value = self.stage[at.z, at.c].astype(F32) + self.cin[at.z].astype(F32)
        from_left = jnp.where(at.has_left, self.zin[at.z + 1].astype(F32), 0.0)
        from_right = jnp.where(at.has_right, self.zin[at.z].astype(F32), 0.0)
        return value + from_left + from_right

    def finish(self):
        at = self.at

        def drain(t):
            self.to_beside(t).wait_send()

            @pl.when(t > at.z)
            def _():
                self.to_right(t).wait_send()

            @pl.when(t < at.z)
            def _():
                self.to_left(t).wait_send()
        loop(0, at.nz, drain)


class PlaneExchange:
    def __init__(self, at, out, inbox, send, recv, columns=None):
        self.at, self.out, self.inbox, self.send, self.recv, self.columns = at, out, inbox, send, recv, columns

    def source(self, k):
        return self.out.at[k] if self.columns is None else self.out.at[k, :, self.columns]

    def start(self):
        at = self.at

        def step(j):
            k = (at.member + j) % 8
            remote(self.source(k), self.inbox.at[at.member], self.send.at[k], self.recv.at[at.member], at.of_plane(k)).start()
        loop(1, 8, step)
        self.inbox[at.member] = self.source(at.member)[...]

    def each(self, do):
        at = self.at

        def step(j):
            k = (at.member + j) % 8
            do(remote(self.source(k), self.inbox.at[k], self.send.at[k], self.recv.at[k], at.of_plane(k)))
        loop(1, 8, step)

    def wait(self):
        self.each(lambda copy: copy.wait_recv())

    def finish(self):
        self.each(lambda copy: copy.wait_send())

    def rows(self, count):
        return jnp.concatenate([self.inbox[k].astype(F32)[0:count] for k in range(8)], axis=0)


def box(tree):
    if isinstance(tree, dict):
        return types.SimpleNamespace(**{k: box(v) for k, v in tree.items()})
    return [box(v) for v in tree] if isinstance(tree, list) else tree


def call(body, name, collective_id, near=None, far=None, table=None, out=None, far_out=None, scratch=None):
    groups = [near or {}, far or {}, table or {}, out or {}, far_out or {}, scratch or {}]
    flat, trees = zip(*[jax.tree.flatten(g) for g in groups])
    counts = [len(f) for f in flat]

    def kernel(*refs):
        named, first = {}, 0
        for tree, count in zip(trees, counts):
            named.update(jax.tree.unflatten(tree, refs[first : first + count]))
            first += count
        body(box(named))

    smem = pl.BlockSpec(memory_space=pltpu.SMEM)
    results = pl.pallas_call(
        kernel,
        out_shape=tuple(flat[3]) + tuple(flat[4]),
        in_specs=[VMEM] * counts[0] + [ANY] * counts[1] + [smem] * counts[2],
        out_specs=(VMEM,) * counts[3] + (ANY,) * counts[4],
        scratch_shapes=list(flat[5]),
        compiler_params=pltpu.CompilerParams(
            collective_id=collective_id, has_side_effects=True, vmem_limit_bytes=63 * 2**20),
        cost_estimate=pl.CostEstimate(flops=10**11, bytes_accessed=2 * 10**8, transcendentals=10**7),
        name=name,
    )(*flat[0], *flat[1], *flat[2])
    done = jax.tree.unflatten(trees[3], results[: counts[3]])
    done.update(jax.tree.unflatten(trees[4], results[counts[3] :]))
    return box(done)


def shape(*dims, dtype=BF):
    return jax.ShapeDtypeStruct(dims, dtype)


def keep(*dims, dtype=BF):
    return pltpu.VMEM(dims, dtype)


def copies(*dims):
    return pltpu.SemaphoreType.DMA(dims)


def square_sum_items(tokens, width):
    half = width // 2
    return dict(ss_stage=keep(6, tokens, half), ss_inbox=keep(6, tokens, half), ss_send=copies(6), ss_recv=copies(6))


def flat_weight(ref, lo=0, hi=None):
    if len(ref.shape) == 2:
        return ref[:, lo:hi]
    v = ref[:, :, :, lo:hi]
    return v.reshape(v.shape[0] * v.shape[1] * v.shape[2], v.shape[3])


def side_weight(ref, cc, lo=0, hi=None):
    v = ref[:, cc, :, lo:hi]
    return v.reshape(v.shape[0] * v.shape[1], v.shape[2])


def block_sum_item(nz, *dims, dtype=BF):
    return dict(stage=keep(nz, 2, *dims, dtype=dtype), cin=keep(nz, *dims, dtype=dtype), zin=keep(nz + 1, *dims, dtype=dtype),
                csend=copies(nz), crecv=copies(nz), zsend=copies(nz), zrecv=copies(nz + 1))


def segment_row(seg, zz, cc):
    return jnp.concatenate([seg[pl.ds(zz * 8 + 2 * k + cc, 1), :] for k in range(4)], axis=1)


def key_columns(at, slopes, seg, zz, cc, tokens):
    rows = 4 * tokens
    column = lax.broadcasted_iota(jnp.int32, (128, rows), 0) % 64
    row = lax.broadcasted_iota(jnp.int32, (128, rows), 1)
    position = ((zz * 8 + (row // tokens) * 2 + cc) * tokens + row % tokens).astype(F32)
    value = jnp.where(segment_row(seg, zz, cc) == column - SEGMENT_LANE, 0.0, -1e30)
    value = jnp.where(column < SEGMENT_LANE + 5, value, 0.0)
    value = jnp.where(column < SEGMENT_LANE, 1.0, value)
    for h in range(3):
        for i, term in enumerate(split3(position * slopes[3 * at.g + h])):
            value = jnp.where(column == 3 * h + i, term, value)
    return value.T.astype(BF)


def segment_columns(at, seg, rows):
    column = lax.broadcasted_iota(jnp.int32, (128, rows), 0) % 64
    return jnp.where(segment_row(seg, at.z, at.c) == column - SEGMENT_LANE, 1.0, 0.0).T


def query_operand(at, q_ref, inside, slopes, side, h, tokens, lse=None):
    rows = 4 * tokens
    if h < 2:
        data = q_ref[:, 0:128]
    else:
        data = jnp.concatenate([q_ref[:, 128:192], jnp.zeros((rows, 64), q_ref.dtype)], axis=1)
    half = K_AT[h][1]
    sign = 1.0 if side == 0 else -1.0
    column = lanes(rows) % 64
    aug = jnp.where((column >= 3 * h) & (column < 3 * h + 3), sign, inside[...])
    term = at.positions(at.z, at.c, tokens, rows) * (slopes[3 * at.g + h] * -sign)
    if lse is not None:
        term = term - lse
    aug = with_lanes(aug, ROW_LANE if half else 64 + ROW_LANE, split3(term))
    return jnp.where(in_half(half, rows), data.astype(F32) * 0.125, aug).astype(BF)


def attention(at, gather, q_op, kaug, m_ref, acc_ref, behind):
    m_ref[...] = jnp.full(m_ref.shape, -1e30, F32)
    acc_ref[...] = jnp.zeros(acc_ref.shape, F32)

    def compute(zz, cc, same):
        kv, aug = gather.buf.at[zz, cc], kaug[zz, cc]
        side = (zz > at.z).astype(jnp.int32)
        for h in range(3):
            k = k_operand(kv, aug, h)
            if same:
                s = jnp.minimum(dot(q_op[0, h], k, NT), dot(q_op[1, h], k, NT))
            else:
                s = dot(q_op[side, h], k, NT)
            m_old = m_ref[h]
            m_new = jnp.maximum(m_old, jnp.max(s, axis=1, keepdims=True))
            p = jnp.exp(s - m_new[:, :1]).astype(BF)
            acc_ref[h] = acc_ref[h] * jnp.exp(m_old - m_new) + dot(p, v_operand(kv, h))
            m_ref[h] = m_new

    def here(i):
        cc = jnp.where(i == 0, at.c, at.oc)

        @pl.when(i == 1)
        def _():
            gather.wait(at.z, at.oc)
        compute(at.z, cc, True)
    loop(0, 2, here)

    def step(d):
        gather.serve(d)
        behind(d)

        def visit(i):
            zz = jnp.where(i % 2 == 0, at.z - d, at.z + d)

            @pl.when((zz >= 0) & (zz < at.nz))
            def _():
                @pl.when(i >= 2)
                def _():
                    gather.wait(zz, at.oc)
                compute(zz, jnp.where(i < 2, at.c, at.oc), False)
        loop(0, 4, visit)
    loop(1, at.nz, step)


def attention_end(at, q_ref, inside, slopes, tokens, m_ref, acc_ref, ctx_ref, ctxf_ref, qb_ref):
    for h in range(3):
        half = V_AT[h][1]
        first = 0 if half else 64
        acc = acc_ref[h]
        total = acc[:, first : first + 1]
        ctx = acc[:, 64 * half : 64 * half + 64] / total
        ctxf_ref[:, 64 * h : 64 * h + 64] = ctx
        ctx_ref[:, 64 * h : 64 * h + 64] = ctx.astype(BF)
        lse = m_ref[h] + jnp.log(total)
        for side in range(2):
            qb_ref[side, h] = query_operand(at, q_ref, inside, slopes, side, h, tokens, lse)


def fwd_kernel(nz, layers, host, R):
    at = Place(nz)
    tokens = R.x0.shape[0]
    rows, half_rows = 4 * tokens, 2 * tokens
    quarter = R.hid.shape[1]
    group = R.ctx_now[0].shape[1]
    arrived = at.enter(host)
    part = R.part
    square_sum = SquareSum(at, part, R.ss_stage, R.ss_inbox, R.ss_send, R.ss_recv)
    gather_x = [SquareGather(at, R.xr_now[l], R.x_send.at[l], R.x_recv.at[l]) for l in range(layers)]
    gather_y = [SquareGather(at, R.yr_now[l], R.y_send.at[l], R.y_recv.at[l]) for l in range(layers)]
    kv = BlockGather(at, R.kv_now)
    saves, waited = [], []

    def save(source, target):
        saves.append(pltpu.make_async_copy(source, target, R.saved.at[len(saves)]))
        saves[-1].start()
        return len(saves) - 1

    def wait_saved(number):
        saves[number].wait()
        waited.append(number)

    if host:
        qkv, gu, down = [[BlockGather(at, item) for item in items] for items in (R.qkv_now, R.gu_now, R.down_now)]
        ow = BlockGather(at, R.ow_now)
        qkv_w, gu_w, down_w, out_w = [g.buf for g in qkv], [g.buf for g in gu], [g.buf for g in down], R.out_now
        wrows = R.ow_now.buf.shape[2] // layers
        lists = [qkv[l] for l in range(layers)] + [gu[l] for l in range(layers)]
        columns, first = [], 0
        for item in lists:
            columns.append(pl.ds(first, item.buf.shape[3]))
            first += item.buf.shape[3]
        spread = [PlaneExchange(at, R.spread, R.spread_in[i], R.spread_send.at[i], R.spread_recv.at[i], columns[i])
                  for i in range(len(lists))]

        def arrive(i):
            spread[i].wait()
            lists[i].put(spread[i].rows(wrows).astype(BF))

        def regroup():
            join = lambda *parts: jnp.concatenate(parts, axis=1)
            part_width = quarter // nz
            for l in range(layers):
                w = R.qkv_mine[l].astype(F32)
                for g in range(4):
                    q, k, v = [w[:, part * 4 * group + group * g : part * 4 * group + group * g + group] for part in range(3)]
                    beside = jnp.zeros(q.shape, F32) if l else R.small_mine[...].astype(F32)
                    at_l = 384 * l
                    R.spread[2 * g, 0:wrows, at_l : at_l + 384] = join(k[:, :128], v[:, :128], k[:, 128:], v[:, 128:]).astype(BF)
                    R.spread[2 * g + 1, 0:wrows, at_l : at_l + 384] = join(q, beside).astype(BF)
            for l in range(layers):
                w = R.gu_mine[l].astype(F32)
                lo = 384 * layers + quarter * l
                for g in range(4):
                    for side in range(2):
                        firsts = [((side * nz + zz) * 4 + g) * part_width for zz in range(nz)]
                        R.spread[2 * g + side, 0:wrows, lo : lo + quarter] = join(*[w[:, i : i + part_width] for i in firsts]).astype(BF)

        regroup()
        arrived()
        to_holder = remote(R.ow_mine, R.ow_in, R.ow_send, R.ow_recv, at.holder)
        spread[0].start()
    else:
        arrived()
        qkv_w, gu_w, down_w, out_w = R.qkv_given, R.gu_given, R.down_given, R.out_given

    R.xr_now[0][at.g] = R.x0[...]
    gather_x[0].start()
    if host:
        spread[layers].start()

        @pl.when(at.moves)
        def _():
            to_holder.start()

        @pl.when(jnp.logical_not(at.moves))
        def _():
            R.ow_in[...] = R.ow_mine[...]
        arrive(0)
        qkv[0].start()
        for l in range(layers):
            down[l].put(R.down_mine[l])

        @pl.when(at.moves)
        def _():
            to_holder.wait_recv()
        ow.put(R.ow_in[...])
        ow.start()

    def columns(b):
        R.kaug_now[b // 2, b % 2] = key_columns(at, R.slopes, R.seg, b // 2, b % 2, tokens)
    loop(0, 2 * nz, columns)
    save(R.kaug_now, R.kaug)
    R.inside[...] = segment_columns(at, R.seg, rows)

    def small(l, t):
        return R.small[8 * l + t : 8 * l + t + 1, :]

    def of(buf, half):
        v = buf[pl.ds(2 * half, 2)]
        return v.reshape(half_rows, v.shape[2])

    def half_at(half):
        return pl.ds(pl.multiple_of(half * half_rows, half_rows), half_rows)

    def put_part(half, value):
        part[pl.ds(2 * half, 2)] = value.reshape(2, tokens, value.shape[1])

    def of_group(row):
        value = jnp.zeros((1, group), F32)
        for g in range(4):
            value = jnp.where(at.g == g, row[:, group * g : group * g + group], value)
        return value

    if host:
        qkv[0].serve_all()
        arrive(layers)
        gu[0].start()
        down[0].start()
        qkv[0].collect()
    R.small[...] = side_weight(qkv_w[0], 1, 128, 256).astype(F32).T[64 : 64 + 8 * layers, :]
    R.state[...] = R.x0[...].astype(F32)
    gather_x[0].wait_near()
    gather_x[0].wait_far()

    for l in range(layers):
        last = l == layers - 1
        x_all = R.xr_now[l][...].reshape(rows, -1)
        save(R.xr_now[l], R.xr[l])
        qb, vb = of_group(small(l, 2)), of_group(small(l, 3))
        none = jnp.zeros((1, 128), F32)
        kv_bias = jnp.concatenate([none, vb[:, :128], none[:, :64], vb[:, 128:192]], axis=1)
        if l:
            pl.semaphore_wait(R.kv_free, at.neighbours())
        kv.put((dot(x_all, side_weight(qkv_w[l], 0)) + kv_bias).astype(BF))
        kv.start()
        if host and not last:
            spread[l + 1].start()
            spread[layers + l + 1].start()
        R.q[...] = (dot(x_all, side_weight(qkv_w[l], 1, 0, group)) + qb).astype(BF)
        for side in range(2):
            for h in range(3):
                R.q_op[side, h] = query_operand(at, R.q, R.inside, R.slopes, side, h, tokens)

        def behind(d, l=l):
            if host and l == 0:
                ow.serve(d)
                gu[l].serve(d)
                down[l].serve(d)

        def ahead(d, l=l):
            if host and l < layers - 1:
                for p in range(d, nz if d == 3 else d + 1):
                    gu[l + 1].serve(p)
                    down[l + 1].serve(p)
        attention(at, kv, R.q_op, R.kaug_now, R.m, R.acc, behind)
        attention_end(at, R.q, R.inside, R.slopes, tokens, R.m, R.acc, R.ctx_now[l], R.ctxf_now[l], R.qb_now[l])
        kv_saved = save(kv.buf, R.kv[l])
        save(R.ctx_now[l], R.ctx[l])
        save(R.ctxf_now[l], R.ctxf[l])
        save(R.qb_now[l], R.qb[l])
        kv.finish()
        if l == 0 and host:
            ow.collect()
            step = group // (2 * nz)
            for i in range(layers):
                for b in range(2 * nz):
                    R.ow_wide[...] = ow.buf[b // 2, b % 2].astype(F32)
                    R.ow_flat[step * b : step * b + step, :] = R.ow_wide[step * i : step * i + step, :]
                R.out_now[i][...] = R.ow_flat[...].astype(BF)
                save(R.out_now[i], R.out_w[i])
        if not last and host:
            arrive(l + 1)
            qkv[l + 1].start()
            arrive(layers + l + 1)
            gu[l + 1].start()
            down[l + 1].start()
        if l:
            square_sum.finish()
        for number, half in enumerate((1 - at.x, at.x)):
            put_part(half, dot(R.ctx_now[l][half_at(half), :], out_w[l][...]))
            if number == 0:
                square_sum.send_far()
            else:
                square_sum.send_near()
        square_sum.relay()
        wait_saved(kv_saved)
        if not last:
            at.signal_neighbours(R.kv_free)
        R.sum1_now[l][...] = R.state[...] + (square_sum.total() + small(l, 4))
        save(R.sum1_now[l], R.sum1[l])
        y = layer_norm(R.sum1_now[l][...], small(l, 0), small(l, 5))
        R.yr_now[l][at.g] = y.astype(BF)
        gather_y[l].start()
        R.state[...] = y
        if host:
            gu[l].collect()
            down[l].collect()
        gather_y[l].wait_near()
        if l:
            wait_saved(mixed_saved)
        square_sum.finish()
        for number, half in enumerate((at.x, 1 - at.x)):
            if number == 1:
                if not last and host:
                    qkv[l + 1].serve_all()
                gather_y[l].wait_far()
                ahead(1)
            here = half_at(half)
            y_half = of(R.yr_now[l], half)
            for col in range(0, quarter, 256):
                gate = dot(y_half, side_weight(gu_w[l], 0, col, col + 256))
                up = dot(y_half, side_weight(gu_w[l], 1, col, col + 256))
                R.mixed_now[here, col : col + 256] = gate
                R.mixed_now[here, quarter + col : quarter + col + 256] = up
                R.hid[:, col : col + 256] = (gate * normal_cdf(gate) * up).astype(BF)
            put_part(half, dot(R.hid[...], flat_weight(down_w[l])))
            if number == 0:
                square_sum.send_near()
            else:
                square_sum.send_far()
        mixed_saved = save(R.mixed_now, R.mixed[l])
        save(R.yr_now[l], R.yr[l])
        if host:
            save(qkv[l].buf, R.qkv_w[l])
            save(gu[l].buf, R.gu_w[l])
            save(down[l].buf, R.down_w[l])
        square_sum.relay()
        ahead(2)
        if not last and host:
            qkv[l + 1].collect()
        R.sum2_now[l][...] = R.state[...] + (square_sum.total() + small(l, 6))
        save(R.sum2_now[l], R.sum2[l])
        state = layer_norm(R.sum2_now[l][...], small(l, 1), small(l, 7))
        R.state[...] = state
        if last:
            R.output[...] = state.astype(BF)
        else:
            R.xr_now[l + 1][at.g] = state.astype(BF)
            gather_x[l + 1].start()
            gather_x[l + 1].wait_near()
            ahead(3)
            gather_x[l + 1].wait_far()
    for l in range(layers):
        gather_x[l].finish()
        gather_y[l].finish()
    square_sum.finish()
    if host:
        for items in (qkv, gu, down):
            for item in items:
                item.finish()
        ow.finish()
        for item in spread:
            item.finish()

        @pl.when(at.moves)
        def _():
            to_holder.wait_send()
    for number, copy in enumerate(saves):
        if number not in waited:
            copy.wait()


def fwd(x0, slopes, seg, weights, layers, host):
    nz = seg.shape[0] // 8
    tokens, width = x0.shape
    rows = 4 * tokens
    group = width // 4
    each = range(layers)
    quarter = weights.gu_mine.shape[2] // 8 if host else weights.gu_given[0].shape[3]
    r = width // nz
    keep_rows = lambda: [keep(4, tokens, width) for _ in each]
    keep_wide = lambda: [keep(tokens, width, dtype=F32) for _ in each]
    scratch = dict(
        xr_now=keep_rows(), x_send=copies(layers, 6), x_recv=copies(layers, 6),
        yr_now=keep_rows(), y_send=copies(layers, 6), y_recv=copies(layers, 6),
        part=keep(4, tokens, width, dtype=F32), state=keep(tokens, width, dtype=F32), **square_sum_items(tokens, width),
        kv_now=block_gather_item(nz, rows, 384), kv_free=pltpu.SemaphoreType.REGULAR, saved=copies(16 * layers),
        kaug_now=keep(nz, 2, rows, 128), inside=keep(rows, 128, dtype=F32),
        q=keep(rows, group), q_op=keep(2, 3, rows, 128),
        m=keep(3, rows, 128, dtype=F32), acc=keep(3, rows, 128, dtype=F32),
        ctx_now=[keep(rows, group) for _ in each], ctxf_now=[keep(rows, group, dtype=F32) for _ in each],
        qb_now=[keep(2, 3, rows, 128) for _ in each], sum1_now=keep_wide(), sum2_now=keep_wide(),
        mixed_now=keep(rows, 2 * quarter, dtype=F32), hid=keep(2 * tokens, quarter))
    far_out = dict(
        xr=[shape(4, tokens, width) for _ in each], yr=[shape(4, tokens, width) for _ in each],
        kv=[shape(nz, 2, rows, 384) for _ in each], ctx=[shape(rows, group) for _ in each],
        ctxf=[shape(rows, group, dtype=F32) for _ in each], qb=[shape(2, 3, rows, 128) for _ in each],
        sum1=[shape(tokens, width, dtype=F32) for _ in each], sum2=[shape(tokens, width, dtype=F32) for _ in each],
        mixed=[shape(rows, 2 * quarter, dtype=F32) for _ in each], kaug=shape(nz, 2, rows, 128))
    near = dict(x0=x0, seg=seg, **vars(weights))
    if host:
        gathered = lambda *dims: [shape(nz, 2, *dims) for _ in each]
        items = lambda *dims: [block_gather_item(nz, *dims) for _ in each]
        rd = weights.down_mine.shape[1]
        padded = 32
        far_out.update(qkv_w=gathered(r, 384), gu_w=gathered(r, quarter), down_w=gathered(rd, width),
                       out_w=[shape(group, width) for _ in each])
        scratch.update(
            qkv_now=items(r, 384), gu_now=items(r, quarter), down_now=items(rd, width),
            spread=keep(8, padded, layers * (384 + quarter)), spread_in=[keep(8, padded, 384) for _ in each] + [keep(8, padded, quarter) for _ in each],
            spread_send=copies(2 * layers, 8), spread_recv=copies(2 * layers, 8),
            ow_in=keep(*weights.ow_mine.shape), ow_send=pltpu.SemaphoreType.DMA, ow_recv=pltpu.SemaphoreType.DMA,
            ow_now=block_gather_item(nz, *weights.ow_mine.shape), out_now=[keep(group, width) for _ in each],
            ow_wide=keep(*weights.ow_mine.shape, dtype=F32), ow_flat=keep(group, width, dtype=F32))
    out = dict(output=shape(tokens, width), small=shape(8 * layers, width, dtype=F32))
    done = call(functools.partial(fwd_kernel, nz, layers, host), "forward", 0, near=near, table=dict(slopes=slopes),
                out=out, far_out=far_out, scratch=scratch)
    if not host:
        done.qkv_w, done.gu_w, done.down_w, done.out_w = weights.qkv_given, weights.gu_given, weights.down_given, weights.out_given
    done.down_w = [w.reshape(quarter, width) for w in done.down_w]
    done.xr = [v.reshape(rows, width) for v in done.xr]
    done.yr = [v.reshape(rows, width) for v in done.yr]
    return done


def attn_back(at, R, l, top, begin, behind, at_end):
    nz, rows = at.nz, R.kvbuf.shape[1]
    q_ref, do_ref, dqacc = R.qb[l], R.do, R.dqacc
    dkv = BlockSum(at, R.dkv)

    def target(i):
        right = nz - 1 - at.z
        from_right = jnp.where(i < right, nz - 1 - i, i - right)
        from_left = jnp.where(i < at.z, i, nz - 1 - (i - at.z))
        return jnp.where(i == nz - 1, at.z, jnp.where(at.z < nz // 2, from_right, from_left))

    class Load:
        def __init__(self, t, slot):
            cc = at.oc if slot == 0 else at.c
            self.copies = [pltpu.make_async_copy(source.at[t, cc], target.at[slot], R.kvsem.at[i, slot])
                           for i, (source, target) in enumerate(((R.kv[l], R.kvbuf), (R.kaug, R.augbuf)))]

        def start(self):
            for copy in self.copies:
                copy.start()

        def wait(self):
            for copy in self.copies:
                copy.wait()

    load = Load

    dqacc[...] = jnp.zeros(dqacc.shape, F32)

    def compute(t, slot, same):
        cc = at.oc if slot == 0 else at.c
        side = (t > at.z).astype(jnp.int32)
        kv, aug = R.kvbuf.at[slot], R.augbuf[slot]
        dks, dvs = [], []
        for h in range(3):
            k, v = k_operand(kv, aug, h), v_operand(kv, h)
            if same:
                s = jnp.minimum(dot(k, q_ref[0, h], NT), dot(k, q_ref[1, h], NT))
            else:
                s = dot(k, q_ref[side, h], NT)
            p = jnp.exp(s)
            ds = (p * dot(v, do_ref[h], NT)).astype(BF)
            dvs.append(dot(p.astype(BF), do_ref[h]))
            dks.append(dot(ds, q_ref[side, h]))
            dqacc[h] += dot(ds, k, TN)
        low = in_half(0, rows)
        dkv.stage[t, cc, :, 0:128] = jnp.where(low, dks[0], dks[1]).astype(BF)
        dkv.stage[t, cc, :, 128:256] = jnp.where(low, dvs[0], dvs[1]).astype(BF)
        dkv.stage[t, cc, :, 256:384] = jnp.where(low, dks[2], dvs[2]).astype(BF)

    def far(t, same):
        load(t, 1).start()
        load(t, 0).wait()
        compute(t, 0, same)
        dkv.to_beside(t).start()

    load(target(0), 0).start()
    begin()
    if not top:
        pl.semaphore_wait(R.dkv.free, at.neighbours())

    def step(i):
        t = target(i)
        far(t, False)
        load(target(i + 1), 0).start()
        load(t, 1).wait()
        compute(t, 1, False)
        dkv.serve(i, relay=False)

        @pl.when(i > 0)
        def _():
            dkv.serve(i - 1, source=False)
        behind(i)
    loop(0, nz - 1, step)
    far(at.z, True)
    dkv.serve(nz - 2, source=False)
    load(at.z, 1).wait()
    compute(at.z, 1, True)
    at_end()
    dq = jnp.where(in_half(0, rows), dqacc[0], dqacc[1]) * 0.125
    R.dproj[:, 384:512] = dq.astype(BF)
    R.dproj[:, 512:576] = (dqacc[2][:, 0:64] * 0.125).astype(BF)
    R.dproj[:, 0:384] = dkv.total().astype(BF)
    if l > 0:
        at.signal_neighbours(R.dkv.free)
    dkv.finish()


def bwd_kernel(nz, layers, host, R):
    at = Place(nz)
    tokens = R.grad.shape[0]
    rows, half_rows = 4 * tokens, 2 * tokens
    quarter = R.hid.shape[1]
    width = R.grad.shape[1]
    mixed, yr, xr, gu_w, down_w, qkv_w = range(6)
    streams = ((R.mixed, R.mixed_now), (R.yr, R.yr_now), (R.xr, R.xr_now), (R.gu_w, R.gu_now), (R.down_w, R.down_now),
               (R.qkv_w, R.qkv_now))

    def load(which, l):
        return pltpu.make_async_copy(streams[which][0][l], streams[which][1], R.load.at[which])

    for which in range(6):
        load(which, layers - 1).start()
    at.enter(host)()
    R.dproj[:, 576:768] = jnp.zeros((rows, 192), BF)
    gather_df = SquareGather(at, R.df, R.df_send, R.df_recv)
    gather_da = SquareGather(at, R.da, R.da_send, R.da_recv)
    part = R.part
    square_sum = SquareSum(at, part, R.ss_stage, R.ss_inbox, R.ss_send, R.ss_recv)
    if host:
        gu_sum, dn_sum, qk_sum, ow_sum = [[BlockSum(at, item) for item in items] for items in (R.gu, R.dn, R.qk, R.ow)]
        sm_sum = BlockSum(at, R.sm)
        back = [PlaneExchange(at, item.out, item.inbox, item.send, item.recv) for item in R.back]
        wrows = R.out_grad.shape[1]
        moved = [remote(R.ow_out.at[l], R.ow_in.at[l], R.ow_send.at[l], R.ow_recv.at[l], at.chunk_device) for l in range(layers)]

    def small(l, t):
        return R.small[8 * l + t : 8 * l + t + 1, :]

    def put_small(l, t, value):
        R.tok_small[8 * l + t : 8 * l + t + 1, :] = value

    def of(buf, half):
        v = buf[pl.ds(2 * half, 2)]
        return v.reshape(half_rows, v.shape[2])

    def half_at(half):
        return pl.ds(pl.multiple_of(half * half_rows, half_rows), half_rows)

    def put_part(half, value):
        part[pl.ds(2 * half, 2)] = value.reshape(2, tokens, value.shape[1])

    def wgrad(left, right, stage, cc, lo, hi):
        for first in range(0, left.shape[1], 384):
            v = dot(left[:, first : first + 384], right[:, lo:hi], TN)
            if len(stage.shape) == 2:
                stage[first : first + 384, :] = v.astype(BF)
                continue
            step = stage.shape[2]
            for i in range(384 // step):
                b = first // step + i
                zz, side = (b // 2, b % 2) if cc is None else (b, cc)
                stage[zz, side] = v[step * i : step * i + step].astype(BF)

    def feed_forward_sums(l):
        return (gu_sum[l], dn_sum[l]) if host and l < layers else ()

    def attention_sums(l):
        return (qk_sum[l], ow_sum[l]) if host and l < layers else ()

    def serve(items, p):
        for item in items:
            item.serve(p)

    def emit(l):
        if not host or l == layers:
            return
        pad = lambda v: jnp.concatenate([v, jnp.zeros((R.back[l].out.shape[1] - wrows, v.shape[1]), F32)], axis=0).astype(BF)
        for item, lo in ((gu_sum[l], 0), (qk_sum[l], quarter)):
            v = item.total()
            for k in range(8):
                R.back[l].out[k, :, lo : lo + v.shape[1]] = pad(v[wrows * k : wrows * k + wrows])
        back[l].start()
        R.dn_grad[l] = dn_sum[l].total()
        R.ow_out[l] = ow_sum[l].total()

        @pl.when(at.moves)
        def _():
            moved[l].start()

        @pl.when(jnp.logical_not(at.moves))
        def _():
            R.ow_in[l] = R.ow_out[l]

    def assemble(l):
        back[l].wait()
        piece = [R.back[l].inbox[k].astype(F32)[0:wrows] for k in range(8)]
        join = lambda side, *spans: jnp.concatenate(
            [piece[2 * g + side][:, lo:hi] for g in range(4) for lo, hi in spans], axis=1)
        at_kv = quarter
        R.qkv_grad[l, :, 0:width] = join(1, (at_kv, at_kv + 192))
        R.qkv_grad[l, :, width : 2 * width] = join(0, (at_kv, at_kv + 128), (at_kv + 256, at_kv + 320))
        R.qkv_grad[l, :, 2 * width : 3 * width] = join(0, (at_kv + 128, at_kv + 256), (at_kv + 320, at_kv + 384))
        step = quarter // nz
        for side in range(2):
            for zz in range(nz):
                lo = (side * nz + zz) * 4 * step
                R.gu_grad[l, :, lo : lo + 4 * step] = join(side, (step * zz, step * zz + step))

        @pl.when(at.moves)
        def _():
            moved[l].wait_recv()
        R.out_grad[l] = R.ow_in[l, 0:wrows, :]

    def small_copy(j):
        k = 4 * at.c + j
        return remote(R.sm_out, R.sm_in.at[at.g], R.sm_send.at[j], R.sm_recv.at[at.g], at.of_plane(k)), k != at.member

    def small_from(g):
        k = 2 * g + at.x
        return remote(R.sm_out, R.sm_in.at[g], R.sm_send.at[0], R.sm_recv.at[g], at.of_plane(k)), k != at.member

    R.g[...] = R.grad[...].astype(F32)
    for l in reversed(range(layers)):
        top = l == layers - 1
        e2, d_gain, d_shift = norm_back(R.g[...], R.sum2[l][...], small(l, 1))
        put_small(l, 1, d_gain)
        put_small(l, 5, d_shift)
        low = e2.astype(BF)
        put_small(l, 4, jnp.sum(low.astype(F32), axis=0, keepdims=True))
        if not top:
            square_sum.finish()
        R.df[at.g] = low
        gather_df.start()
        R.e2[...] = e2
        for which in range(6):
            load(which, l).wait()
        serve(feed_forward_sums(l + 1), 1)
        gather_df.wait_near()
        for number, half in enumerate((at.x, 1 - at.x)):
            if number == 1:
                gather_df.wait_far()
                serve(attention_sums(l + 1), 1)
            here = half_at(half)
            dhid_all = dot(of(R.df, half), R.down_now[...], NT)
            for col in range(0, quarter, 256):
                dhid = dhid_all[:, col : col + 256]
                gate = R.mixed_now[here, col : col + 256]
                up = R.mixed_now[here, quarter + col : quarter + col + 256]
                cdf = normal_cdf(gate)
                act = gate * cdf
                R.hid[here, col : col + 256] = (act * up).astype(BF)
                R.dgu[here, col : col + 256] = (dhid * up * (cdf + gate * normal_pdf(gate))).astype(BF)
                R.dgu[here, quarter + col : quarter + col + 256] = (dhid * act).astype(BF)
            put_part(half, dot(R.dgu[here, :quarter], side_weight(R.gu_now, 0), NT)
                     + dot(R.dgu[here, quarter:], side_weight(R.gu_now, 1), NT))
            if number == 0:
                square_sum.send_near()
            else:
                square_sum.send_far()
        wgrad(R.hid, R.df[...].reshape(rows, width), R.dn[l].stage, None, 0, width)
        square_sum.relay()
        serve(feed_forward_sums(l + 1), 2)
        for p in range(3, nz - 1):
            serve(feed_forward_sums(l + 1), p)
        dy = R.e2[...] + square_sum.total()
        e1, d_gain, d_shift = norm_back(dy, R.sum1[l][...], small(l, 0))
        put_small(l, 0, d_gain)
        put_small(l, 3, d_shift)
        low = e1.astype(BF)
        put_small(l, 2, jnp.sum(low.astype(F32), axis=0, keepdims=True))
        R.da[at.g] = low
        gather_da.start()
        R.e1[...] = e1
        for cc in range(2):
            wgrad(R.yr_now, R.dgu, R.gu[l].stage, cc, quarter * cc, quarter * cc + quarter)
        gather_da.wait_near()
        gather_da.wait_far()
        for item in feed_forward_sums(l):
            item.start()
        if l > 0:
            for which in (mixed, yr, gu_w, down_w):
                load(which, l - 1).start()
        da_all = R.da[...].reshape(rows, width)
        dctx = dot(da_all, R.out_w[l][...], NT).astype(BF)
        d_out = dot(R.ctx[l][...], da_all, TN)
        if host:
            step = d_out.shape[0] // (2 * nz)
            for b in range(2 * nz):
                R.ow[l].stage[b // 2, b % 2] = jnp.concatenate(
                    [d_out[step * b : step * b + step], jnp.zeros((OW_ROWS - step, width), F32)]).astype(BF)
        else:
            R.ow[l].stage[...] = d_out.astype(BF)
        ctxf = R.ctxf[l]
        wide = dctx.astype(F32)
        first_two = wide[:, :128]
        third = jnp.concatenate([jnp.zeros((rows, 64), F32), wide[:, 128:192]], axis=1)
        prod = first_two * ctxf[:, :128]
        low_half = in_half(0, rows)
        deltas = [
            jnp.sum(jnp.where(low_half, prod, 0.0), axis=1, keepdims=True),
            jnp.sum(jnp.where(low_half, 0.0, prod), axis=1, keepdims=True),
            jnp.sum(wide[:, 128:192] * ctxf[:, 128:192], axis=1, keepdims=True),
        ]
        for h in range(3):
            half = V_AT[h][1]
            base = jnp.where(in_half(half, rows), first_two if h < 2 else third, 0.0)
            R.do[h] = with_lanes(base, 0 if half else 64, split3(-deltas[h])).astype(BF)

        def begin(l=l):
            serve(attention_sums(l + 1), 2)
            for p in range(3, nz - 1):
                serve(attention_sums(l + 1), p)

        def behind(i):
            pass

        def at_end(l=l):
            serve(feed_forward_sums(l), 0)
        attn_back(at, R, l, top, begin, behind, at_end)
        dproj = R.dproj
        bias_sum = jnp.sum(dproj[...].astype(F32), axis=0, keepdims=True)
        for t, row in ((6, bias_sum[:, 384:576]), (7, jnp.concatenate([bias_sum[:, 128:256], bias_sum[:, 320:384]], axis=1))):
            put_small(l, t, jnp.concatenate([jnp.where(at.g == g, row, 0.0) for g in range(4)], axis=1))
        gather_df.finish()
        gather_da.finish()
        square_sum.finish()
        for number, half in enumerate((1 - at.x, at.x)):
            put_part(half, dot(dproj[half_at(half), :384], side_weight(R.qkv_now, 0), NT)
                     + dot(dproj[half_at(half), 384:], side_weight(R.qkv_now, 1), NT))
            if number == 0:
                square_sum.send_far()
            else:
                square_sum.send_near()
        square_sum.relay()
        for cc in range(2):
            wgrad(R.xr_now, dproj, R.qk[l].stage, cc, 384 * cc, 384 * cc + 384)
        for item in attention_sums(l):
            item.start()
        serve(attention_sums(l), 0)
        if l > 0:
            load(xr, l - 1).start()
            load(qkv_w, l - 1).start()
        emit(l + 1)
        R.g[...] = R.e1[...] + square_sum.total()
    R.grad_in[...] = R.g[...]
    square_sum.finish()
    if host:
        for b in range(2 * nz):
            step = width // (2 * nz)
            sm_sum.stage[b // 2, b % 2, :, 0:step] = R.tok_small[:, step * b : step * b + step]
        sm_sum.start()
        last = feed_forward_sums(0) + attention_sums(0) + (sm_sum,)
        sm_sum.serve(0)
        for p in range(1, nz - 1):
            serve(last, p)
        R.sm_out[...] = sm_sum.total()
        for j in range(4):
            copy, away = small_copy(j)

            @pl.when(away)
            def _(copy=copy):
                copy.start()

            @pl.when(jnp.logical_not(away))
            def _():
                R.sm_in[at.g] = R.sm_out[...]
        emit(0)
        for l in range(1, layers):
            assemble(l)
        total = jnp.zeros(R.sm_out.shape, F32)
        for g in range(4):
            copy, away = small_from(g)

            @pl.when(away)
            def _(copy=copy):
                copy.wait_recv()
            total = total + R.sm_in[g]
        mine = jnp.zeros((8 * layers, wrows), F32)
        for k in range(4):
            mine = jnp.where(2 * at.y + at.c == k, total[:, wrows * k : wrows * k + wrows], mine)
        for l in range(layers):
            R.gains_grad[l] = mine[8 * l : 8 * l + 2]
            R.biases_grad[l] = jnp.concatenate([mine[8 * l + 6 : 8 * l + 8], mine[8 * l + 2 : 8 * l + 6]], axis=0)
        assemble(0)
        for l in range(layers):
            for item in feed_forward_sums(l) + attention_sums(l) + (back[l],):
                item.finish()

            @pl.when(at.moves)
            def _(l=l):
                moved[l].wait_send()
        for j in range(4):
            copy, away = small_copy(j)

            @pl.when(away)
            def _(copy=copy):
                copy.wait_send()
        sm_sum.finish()


def bwd(grad, saved, host):
    layers = len(saved.qkv_w)
    nz, _, rows, _ = saved.kaug.shape
    tokens, width = grad.shape
    quarter, group = width, width // 4
    quarter = saved.down_w[0].shape[0]
    r, rd = width // nz, quarter // (2 * nz)
    each = range(layers)
    out = dict(grad_in=shape(tokens, width, dtype=F32))
    scratch = {}
    if host:
        wrows, padded = width // (8 * nz), 32
        out.update(
            qkv_grad=shape(layers, wrows, 3 * width, dtype=F32), out_grad=shape(layers, wrows, width, dtype=F32),
            gu_grad=shape(layers, wrows, 8 * quarter, dtype=F32), dn_grad=shape(layers, rd, width, dtype=F32),
            gains_grad=shape(layers, 2, wrows, dtype=F32), biases_grad=shape(layers, 6, wrows, dtype=F32))
        scratch.update(
            back=[dict(out=keep(8, padded, quarter + 384), inbox=keep(8, padded, quarter + 384), send=copies(8), recv=copies(8))
                  for _ in each],
            ow_out=keep(layers, OW_ROWS, width, dtype=F32), ow_in=keep(layers, OW_ROWS, width, dtype=F32),
            ow_send=copies(layers), ow_recv=copies(layers),
            sm_out=keep(8 * layers, 128, dtype=F32), sm_in=keep(4, 8 * layers, 128, dtype=F32), sm_send=copies(4), sm_recv=copies(4))
        scratch.update(
            gu=[block_sum_item(nz, r, quarter) for _ in each], dn=[block_sum_item(nz, rd, width) for _ in each],
            qk=[block_sum_item(nz, r, 384) for _ in each], ow=[block_sum_item(nz, OW_ROWS, width) for _ in each],
            sm=block_sum_item(nz, 8 * layers, 128, dtype=F32), tok_small=keep(8 * layers, width, dtype=F32))
    else:
        out.update(
            gu=[dict(stage=shape(nz, 2, r, quarter)) for _ in each], dn=[dict(stage=shape(quarter, width)) for _ in each],
            qk=[dict(stage=shape(nz, 2, r, 384)) for _ in each], ow=[dict(stage=shape(group, width)) for _ in each],
            tok_small=shape(8 * layers, width, dtype=F32))
    like = lambda arrays: keep(*arrays[0].shape, dtype=arrays[0].dtype)
    scratch.update(
        mixed_now=like(saved.mixed), yr_now=like(saved.yr), xr_now=like(saved.xr), gu_now=like(saved.gu_w),
        down_now=like(saved.down_w), qkv_now=like(saved.qkv_w), load=copies(6), kvbuf=keep(2, rows, 384), augbuf=keep(2, rows, 128), kvsem=copies(2, 2),
        df=keep(4, tokens, width), df_send=copies(6), df_recv=copies(6),
        da=keep(4, tokens, width), da_send=copies(6), da_recv=copies(6),
        part=keep(4, tokens, width, dtype=F32), **square_sum_items(tokens, width),
        g=keep(tokens, width, dtype=F32), e1=keep(tokens, width, dtype=F32), e2=keep(tokens, width, dtype=F32),
        hid=keep(rows, quarter), dgu=keep(rows, 2 * quarter), do=keep(3, rows, 128),
        dqacc=keep(3, rows, 128, dtype=F32), dproj=keep(rows, 768),
        dkv=dict(block_sum_item(nz, rows, 384), free=pltpu.SemaphoreType.REGULAR))
    near = dict(grad=grad, small=saved.small, sum1=saved.sum1, sum2=saved.sum2, ctx=saved.ctx,
                ctxf=saved.ctxf, qb=saved.qb, out_w=saved.out_w)
    far = dict(mixed=saved.mixed, yr=saved.yr, xr=saved.xr, gu_w=saved.gu_w, down_w=saved.down_w, kv=saved.kv, kaug=saved.kaug,
               qkv_w=saved.qkv_w)
    return call(functools.partial(bwd_kernel, nz, layers, host), "backward", 1, near=near, far=far, out=out, scratch=scratch)


def shards(hidden_in, out_grad, segment_ids, alibi_slopes, qkv_weight, out_weight, gate_up_weight, down_weight, gains, biases):
    nz = lax.axis_size("z")
    nb = 2 * nz
    square, everyone, blocks = ("x", "y", "c"), ("z", "x", "y", "c"), ("z", "c")
    z, c = lax.axis_index("z"), lax.axis_index("c")
    tokens, width = hidden_in.shape
    layers, wrows = qkv_weight.shape[:2]
    ff = gate_up_weight.shape[2] // 2
    group, quarter = width // 4, ff // 4
    host = (width // nz) % 16 == 0 and down_weight.shape[1] % 16 == 0

    def to_groups(w):
        w = w.reshape(wrows, 3, 4, 3, 64)
        q, k, v = w[:, 0], w[:, 1], w[:, 2]
        kv = jnp.stack([k[:, :, 0], k[:, :, 1], v[:, :, 0], v[:, :, 1], k[:, :, 2], v[:, :, 2]], axis=2)
        return kv.reshape(wrows, 4, 384), q.reshape(wrows, 4, group)

    def from_groups(kv, q):
        kv, q = kv.reshape(4, wrows, 6, 64), q.reshape(4, wrows, 3, 64)
        k = jnp.stack([kv[:, :, 0], kv[:, :, 1], kv[:, :, 4]], axis=2)
        v = jnp.stack([kv[:, :, 2], kv[:, :, 3], kv[:, :, 5]], axis=2)
        return jnp.stack([q, k, v]).transpose(2, 0, 1, 3, 4).reshape(wrows, 3 * width)

    places = [(8 * zz + 2 * g + cc, g * nb + 2 * zz + cc) for zz in range(nz) for g in range(4) for cc in range(2)]
    gu0 = 384 * layers

    def gathered_outside():
        beside = jnp.broadcast_to(small[:, None], (wrows, 4, 192))
        nothing = jnp.zeros((wrows, 4, 192), BF)
        gu = gate_up_weight.reshape(layers, wrows, 2, nz, 4, quarter // nz).transpose(0, 1, 4, 2, 3, 5)
        gu = gu.reshape(layers, wrows, 4, 2, quarter)
        sides = [[], []]
        for l in range(layers):
            kv, q = to_groups(qkv_weight[l])
            sides[0].append(kv)
            sides[1] += [q, nothing if l else beside]
        for l in range(layers):
            for side in range(2):
                sides[side].append(gu[l, :, :, side])
        both = jnp.stack([jnp.concatenate(side, axis=2) for side in sides], axis=2).reshape(wrows, 8, -1)
        spread = lax.all_to_all(both, square, split_axis=1, concat_axis=0, tiled=True).reshape(8 * wrows, -1)
        ow_own = lax.ppermute(out_weight, everyone, [(chunk, device) for device, chunk in places])
        whole = lambda v: lax.all_gather(v, blocks, axis=0).reshape(nz, 2, *v.shape)
        flat = lambda v: lax.all_gather(v, blocks, axis=0, tiled=True)
        return types.SimpleNamespace(
            qkv_given=[whole(spread[:, 384 * l : 384 * l + 384]) for l in range(layers)],
            gu_given=[whole(spread[:, gu0 + quarter * l : gu0 + quarter * l + quarter]) for l in range(layers)],
            down_given=[flat(down_weight[l]) for l in range(layers)], out_given=[flat(ow_own[l]) for l in range(layers)])

    small = jnp.concatenate([gains, biases], axis=1).transpose(0, 2, 1)
    small = jnp.concatenate([small[l] for l in range(layers)], axis=1)
    small = jnp.pad(small, ((0, 0), (0, 192 - small.shape[1])))
    if host:
        weights = types.SimpleNamespace(
            qkv_mine=qkv_weight, gu_mine=gate_up_weight, down_mine=down_weight, small_mine=small,
            ow_mine=out_weight.reshape(layers * wrows, width))
    else:
        weights = gathered_outside()
    seg = segment_ids.reshape(8 * nz, tokens)
    saved = fwd(hidden_in, alibi_slopes, seg, weights, layers, host)
    done = bwd(out_grad, saved, host)
    if host:
        return (saved.output, done.grad_in, done.qkv_grad, done.out_grad, done.gu_grad, done.dn_grad, done.gains_grad,
                done.biases_grad)
    step = width // nb
    blocks_sum = lambda v: lax.psum_scatter(v, blocks, scatter_dimension=0, tiled=True)
    done.gu_sum = [blocks_sum(item.stage.reshape(nb, -1, quarter))[0] for item in done.gu]
    done.qk_sum = [blocks_sum(item.stage.reshape(nb, -1, 384))[0] for item in done.qk]
    done.dn_sum = [blocks_sum(item.stage) for item in done.dn]
    done.ow_sum = [blocks_sum(item.stage) for item in done.ow]
    sm = lax.psum_scatter(done.tok_small.reshape(-1, nb, step), blocks, scatter_dimension=1, tiled=True)[:, 0]
    sm = sm.T.reshape(4, wrows, 8 * layers)
    high = lax.reduce_precision(sm, 8, 7)
    sm = jnp.concatenate([high, sm - high], axis=2).astype(BF)
    sm = lax.dynamic_update_slice_in_dim(jnp.zeros((8, wrows, 16 * layers), BF), sm, 4 * c, 0)
    rows_of = lambda v: v.reshape(8, wrows, -1)
    back = jnp.concatenate([rows_of(v) for v in done.qk_sum + done.gu_sum] + [sm], axis=2)
    back = lax.all_to_all(back, square, split_axis=0, concat_axis=0, tiled=True)
    sides = back.astype(F32).reshape(4, 2, wrows, -1)
    qkv_grad = jnp.stack([from_groups(sides[:, 0, :, 384 * l : 384 * l + 384], sides[:, 1, :, 384 * l : 384 * l + group])
                          for l in range(layers)])
    gu_grad = jnp.stack([sides[:, :, :, gu0 + quarter * l : gu0 + quarter * l + quarter] for l in range(layers)])
    gu_grad = gu_grad.reshape(layers, 4, 2, wrows, nz, quarter // nz).transpose(0, 3, 2, 4, 1, 5).reshape(layers, wrows, 2 * ff)
    sm = jnp.sum(sides[..., gu0 + quarter * layers :], axis=(0, 1))
    sm = (sm[:, : 8 * layers] + sm[:, 8 * layers :]).T.reshape(layers, 8, wrows)
    out_grad_w = lax.ppermute(jnp.stack(done.ow_sum)[:, :wrows].astype(F32), everyone, places)
    return (saved.output, done.grad_in, qkv_grad, out_grad_w, gu_grad, jnp.stack(done.dn_sum).astype(F32), sm[:, 0:2],
            jnp.concatenate([sm[:, 6:8], sm[:, 2:6]], axis=1))


def solution(mesh):
    nb, nh = mesh.devices.shape
    everyone = ("z", "x", "y", "c")
    tok, mid, last = P(everyone, None), P(None, everyone, None), P(None, None, everyone)
    return jax.shard_map(
        shards, mesh=Mesh(mesh.devices.reshape(nb // 2, 2, nh // 2, 2), everyone),
        in_specs=(tok, tok, P(), P(), mid, mid, mid, mid, last, last),
        out_specs=(tok, tok, mid, mid, mid, mid, last, last),
        check_vma=False,
    )
```

```python
import functools
import types

import jax
import jax.numpy as jnp
from jax import lax
from jax.experimental import pallas as pl
from jax.experimental.pallas import tpu as pltpu
from jax.sharding import Mesh
from jax.sharding import PartitionSpec as P

MESH = pl.DeviceIdType.MESH
BF = jnp.bfloat16
F32 = jnp.float32
NT = (((1,), (1,)), ((), ()))
NN = (((1,), (0,)), ((), ()))
TN = (((0,), (0,)), ((), ()))
EPS = 1e-06
K_AT = ((0, 0), (0, 1), (2, 0))
V_AT = ((1, 0), (1, 1), (2, 1))
ROW_LANE, SEGMENT_LANE = 9, 12
OW_ROWS = 32
VMEM = pl.BlockSpec(memory_space=pltpu.VMEM)
ANY = pl.BlockSpec(memory_space=pl.ANY)


def dot(a, b, dims=NN):
    return lax.dot_general(a, b, dims, preferred_element_type=F32)


def lanes(rows):
    return lax.broadcasted_iota(jnp.int32, (rows, 128), 1)


def in_half(half, rows):
    return lanes(rows) >= 64 if half else lanes(rows) < 64


def ones_half(half, rows):
    first = 0 if half else 64
    lane = lanes(rows)
    return jnp.where((lane >= first) & (lane < first + 3), 1.0, 0.0).astype(BF)


def k_operand(kv, aug, h):
    col, half = K_AT[h]
    return jnp.where(in_half(half, kv.shape[0]), kv[:, 128 * col : 128 * col + 128], aug)


def v_operand(kv, h):
    col, half = V_AT[h]
    rows = kv.shape[0]
    return jnp.where(in_half(half, rows), kv[:, 128 * col : 128 * col + 128], ones_half(half, rows))


def split3(value):
    high = value.astype(BF).astype(F32)
    mid = (value - high).astype(BF).astype(F32)
    return high, mid, value - high - mid


def with_lanes(base, first, values):
    lane = lanes(base.shape[0])
    for i, v in enumerate(values):
        base = jnp.where(lane == first + i, v, base)
    return base


def layer_norm(total, gain, shift):
    centred = total - jnp.mean(total, axis=-1, keepdims=True)
    scale = lax.rsqrt(jnp.mean(centred * centred, axis=-1, keepdims=True) + EPS)
    return centred * scale * gain + shift


def norm_back(grad, total, gain):
    centred = total - jnp.mean(total, axis=-1, keepdims=True)
    scale = lax.rsqrt(jnp.mean(centred * centred, axis=-1, keepdims=True) + EPS)
    n = centred * scale
    dn = grad * gain
    e = scale * (dn - jnp.mean(dn, axis=-1, keepdims=True) - n * jnp.mean(dn * n, axis=-1, keepdims=True))
    return e, jnp.sum(grad * n, axis=0, keepdims=True), jnp.sum(grad, axis=0, keepdims=True)


def normal_cdf(u):
    return 0.5 * (1.0 + lax.erf(u * (0.5**0.5)))


def normal_pdf(u):
    return jnp.exp(-0.5 * u * u) * ((2.0 * jnp.pi) ** -0.5)


def remote(src, dst, send, recv, device):
    return pltpu.make_async_remote_copy(
        src_ref=src, dst_ref=dst, send_sem=send, recv_sem=recv, device_id=device, device_id_type=MESH)


def loop(first, last, do):
    def step(i, carry):
        do(i)
        return carry
    lax.fori_loop(first, last, step, 0)


class Place:
    def __init__(self, nz):
        self.nz = nz
        self.z, self.x, self.y, self.c = [lax.axis_index(name) for name in "zxyc"]
        self.g = 2 * self.x + self.y
        self.gx, self.gy = 2 * (1 - self.x) + self.y, 2 * self.x + 1 - self.y
        self.gd = 2 * (1 - self.x) + 1 - self.y
        self.oc = 1 - self.c
        self.beside = (self.z, self.x, self.y, self.oc)
        self.across_x = (self.z, 1 - self.x, self.y, self.c)
        self.across_y = (self.z, self.x, 1 - self.y, self.c)
        self.block = 2 * self.z + self.c
        self.member = 2 * self.g + self.c
        self.number = 8 * self.z + self.member
        nb = 2 * nz
        self.chunk = self.g * nb + self.block
        self.chunk_device = self.device(self.chunk)
        place = self.number % nb
        self.holder = (place // 2, self.number // nb // 2, self.number // nb % 2, place % 2)
        self.moves = self.chunk != self.number
        self.has_left, self.has_right = self.z > 0, self.z < nz - 1

    def column(self, zz):
        return (zz, self.x, self.y, self.c)

    def device(self, number):
        k = number % 8
        return (number // 8, k // 4, k // 2 % 2, k % 2)

    def of_plane(self, k):
        return (self.z, k // 4, k // 2 % 2, k % 2)

    def neighbours(self):
        return 3 - (self.z == 0).astype(jnp.int32) - (self.z == self.nz - 1).astype(jnp.int32)

    def signal_neighbours(self, semaphore):
        pl.semaphore_signal(semaphore, inc=1, device_id=self.beside, device_id_type=MESH)

        @pl.when(self.has_left)
        def _():
            pl.semaphore_signal(semaphore, inc=1, device_id=self.column(self.z - 1), device_id_type=MESH)

        @pl.when(self.has_right)
        def _():
            pl.semaphore_signal(semaphore, inc=1, device_id=self.column(self.z + 1), device_id_type=MESH)

    def enter(self, plane):
        barrier = pltpu.get_barrier_semaphore()

        def greet(device):
            pl.semaphore_signal(barrier, inc=1, device_id=device, device_id_type=MESH)

        if not plane:
            greet(self.across_x)
            greet(self.across_y)
            self.signal_neighbours(barrier)
            return lambda: pl.semaphore_wait(barrier, 2 + self.neighbours())
        loop(1, 8, lambda j: greet(self.of_plane((self.member + j) % 8)))
        self.signal_neighbours(barrier)

        @pl.when(self.moves)
        def _():
            greet(self.chunk_device)
            greet(self.holder)
        return lambda: pl.semaphore_wait(barrier, 7 + self.neighbours() + 2 * self.moves.astype(jnp.int32))

    def positions(self, zz, cc, tokens, rows):
        row = lax.broadcasted_iota(jnp.int32, (rows, 128), 0)
        return ((zz * 8 + (row // tokens) * 2 + cc) * tokens + row % tokens).astype(F32)


class SquareGather:
    def __init__(self, at, buf, send, recv):
        half = buf.shape[1] // 2
        first, second = pl.ds(0, half), pl.ds(half, half)

        def copy(i, g, rows, device):
            return remote(buf.at[g, rows], buf.at[g, rows], send.at[i], recv.at[i], device)
        self.x_first, self.x_second = copy(0, at.g, first, at.across_x), copy(1, at.g, second, at.across_x)
        self.y_second, self.y_first = copy(2, at.g, second, at.across_y), copy(3, at.g, first, at.across_y)
        self.on_y = copy(4, at.gx, first, at.across_y)
        self.on_x = copy(5, at.gy, second, at.across_x)

    def start(self):
        for copy in (self.x_first, self.y_second, self.x_second, self.y_first):
            copy.start()

    def wait_near(self):
        self.x_first.wait_recv()
        self.on_y.start()
        self.y_second.wait_recv()
        self.on_x.start()
        self.y_first.wait_recv()

    def wait_far(self):
        self.x_second.wait_recv()
        self.on_x.wait_recv()
        self.on_y.wait_recv()

    def finish(self):
        for copy in (self.x_first, self.x_second, self.y_first, self.y_second, self.on_x, self.on_y):
            copy.wait_send()


class SquareSum:
    def __init__(self, at, part, stage, inbox, send, recv):
        self.at, self.part, self.stage, self.inbox = at, part, stage, inbox
        self.half = part.shape[2] // 2
        to = (at.across_x, at.across_x, at.across_y, at.across_y, at.across_y, at.across_x)
        self.copies = [remote(stage.at[i], inbox.at[i], send.at[i], recv.at[i], to[i]) for i in range(6)]

    def left(self, g):
        return self.part[g, :, : self.half]

    def right(self, g):
        return self.part[g, :, self.half :]

    def post(self, i, value):
        self.stage[i] = value.astype(BF)
        self.copies[i].start()

    def came(self, i):
        self.copies[i].wait_recv()
        return self.inbox[i].astype(F32)

    def send_far(self):
        self.post(0, self.left(self.at.gd))
        self.post(2, self.right(self.at.gd))
        self.post(1, self.left(self.at.gx))

    def send_near(self):
        self.post(3, self.right(self.at.gy))

    def relay(self):
        self.post(4, self.left(self.at.gy) + self.came(0))
        self.post(5, self.right(self.at.gx) + self.came(2))

    def total(self):
        left = self.left(self.at.g) + self.came(1)
        right = self.right(self.at.g) + self.came(3)
        return jnp.concatenate([left + self.came(4), right + self.came(5)], axis=1)

    def finish(self):
        for copy in self.copies:
            copy.wait_send()


class BlockGather:
    def __init__(self, at, item):
        self.at, self.buf, self.zsend, self.csend, self.recv = at, item.buf, item.zsend, item.csend, item.recv

    def copy(self, zz, send, device):
        at = self.at
        return remote(self.buf.at[zz, at.c], self.buf.at[zz, at.c], send, self.recv.at[zz, at.c], device)

    def to_right(self, zz):
        return self.copy(zz, self.zsend.at[0, zz], self.at.column(self.at.z + 1))

    def to_left(self, zz):
        return self.copy(zz, self.zsend.at[1, zz], self.at.column(self.at.z - 1))

    def to_beside(self, zz):
        return self.copy(zz, self.csend.at[zz], self.at.beside)

    def wait(self, zz, cc):
        at = self.at
        remote(self.buf.at[zz, cc], self.buf.at[zz, cc], self.csend.at[zz], self.recv.at[zz, cc], at.beside).wait_recv()

    def put(self, value):
        self.buf[self.at.z, self.at.c] = value

    def start(self):
        at = self.at

        @pl.when(at.has_right)
        def _():
            self.to_right(at.z).start()

        @pl.when(at.has_left)
        def _():
            self.to_left(at.z).start()
        self.to_beside(at.z).start()

    def serve(self, d):
        at = self.at

        @pl.when(at.z - d >= 0)
        def _():
            self.wait(at.z - d, at.c)

            @pl.when(at.has_right)
            def _():
                self.to_right(at.z - d).start()
            self.to_beside(at.z - d).start()

        @pl.when(at.z + d < at.nz)
        def _():
            self.wait(at.z + d, at.c)

            @pl.when(at.has_left)
            def _():
                self.to_left(at.z + d).start()
            self.to_beside(at.z + d).start()

    def serve_all(self):
        loop(1, self.at.nz, self.serve)

    def collect(self):
        loop(0, self.at.nz, lambda zz: self.wait(zz, self.at.oc))

    def finish(self):
        at = self.at

        def drain(zz):
            self.to_beside(zz).wait_send()

            @pl.when((zz <= at.z) & at.has_right)
            def _():
                self.to_right(zz).wait_send()

            @pl.when((zz >= at.z) & at.has_left)
            def _():
                self.to_left(zz).wait_send()
        loop(0, at.nz, drain)


def block_gather_item(nz, *dims):
    return dict(buf=keep(nz, 2, *dims), zsend=copies(2, nz), csend=copies(nz), recv=copies(nz, 2))


class BlockSum:
    def __init__(self, at, item):
        self.at, self.stage, self.cin, self.zin = at, item.stage, item.cin, item.zin
        self.csend, self.crecv, self.zsend, self.zrecv = item.csend, item.crecv, item.zsend, item.zrecv

    def to_beside(self, t):
        return remote(self.stage.at[t, self.at.oc], self.cin.at[t], self.csend.at[t], self.crecv.at[t], self.at.beside)

    def to_right(self, t):
        return remote(self.stage.at[t, self.at.c], self.zin.at[t + 1], self.zsend.at[t], self.zrecv.at[t + 1], self.at.column(self.at.z + 1))

    def to_left(self, t):
        return remote(self.stage.at[t, self.at.c], self.zin.at[t], self.zsend.at[t], self.zrecv.at[t], self.at.column(self.at.z - 1))

    def arrived(self, slot):
        at = self.at
        remote(self.zin.at[slot], self.zin.at[slot], self.zsend.at[0], self.zrecv.at[slot], at.beside).wait_recv()

    def start(self):
        loop(0, self.at.nz, lambda t: self.to_beside(t).start())

    def add(self, t, slot=None):
        value = self.stage[t, self.at.c].astype(F32) + self.cin[t].astype(F32)
        if slot is not None:
            value = value + self.zin[slot].astype(F32)
        self.stage[t, self.at.c] = value.astype(self.stage.dtype)

    def go_right(self, t):
        self.to_beside(t).wait_recv()

        @pl.when(self.at.has_left)
        def _():
            self.arrived(t + 1)
            self.add(t, t + 1)

        @pl.when(jnp.logical_not(self.at.has_left))
        def _():
            self.add(t)
        self.to_right(t).start()

    def go_left(self, t):
        self.to_beside(t).wait_recv()

        @pl.when(self.at.has_right)
        def _():
            self.arrived(t)
            self.add(t, t)

        @pl.when(jnp.logical_not(self.at.has_right))
        def _():
            self.add(t)
        self.to_left(t).start()

    def serve(self, p, source=True, relay=True):
        at = self.at
        right, left = p - at.z, p - (at.nz - 1 - at.z)
        go_r = (right >= 0) & (right < at.nz - 1 - at.z)
        go_l = (left >= 0) & (left < at.z)
        if not source:
            go_r, go_l = go_r & at.has_left, go_l & at.has_right
        if not relay:
            go_r, go_l = go_r & jnp.logical_not(at.has_left), go_l & jnp.logical_not(at.has_right)

        @pl.when(go_r)
        def _():
            self.go_right(at.nz - 1 - right)

        @pl.when(go_l)
        def _():
            self.go_left(left)

    def total(self):
        at = self.at
        self.to_beside(at.z).wait_recv()

        @pl.when(at.has_left)
        def _():
            self.arrived(at.z + 1)

        @pl.when(at.has_right)
        def _():
            self.arrived(at.z)
        value = self.stage[at.z, at.c].astype(F32) + self.cin[at.z].astype(F32)
        from_left = jnp.where(at.has_left, self.zin[at.z + 1].astype(F32), 0.0)
        from_right = jnp.where(at.has_right, self.zin[at.z].astype(F32), 0.0)
        return value + from_left + from_right

    def finish(self):
        at = self.at

        def drain(t):
            self.to_beside(t).wait_send()

            @pl.when(t > at.z)
            def _():
                self.to_right(t).wait_send()

            @pl.when(t < at.z)
            def _():
                self.to_left(t).wait_send()
        loop(0, at.nz, drain)


class PlaneExchange:
    def __init__(self, at, out, inbox, send, recv, columns=None):
        self.at, self.out, self.inbox, self.send, self.recv, self.columns = at, out, inbox, send, recv, columns

    def source(self, k):
        return self.out.at[k] if self.columns is None else self.out.at[k, :, self.columns]

    def start(self):
        at = self.at

        def step(j):
            k = (at.member + j) % 8
            remote(self.source(k), self.inbox.at[at.member], self.send.at[k], self.recv.at[at.member], at.of_plane(k)).start()
        loop(1, 8, step)
        self.inbox[at.member] = self.source(at.member)[...]

    def each(self, do):
        at = self.at

        def step(j):
            k = (at.member + j) % 8
            do(remote(self.source(k), self.inbox.at[k], self.send.at[k], self.recv.at[k], at.of_plane(k)))
        loop(1, 8, step)

    def wait(self):
        self.each(lambda copy: copy.wait_recv())

    def finish(self):
        self.each(lambda copy: copy.wait_send())

    def rows(self, count):
        return jnp.concatenate([self.inbox[k].astype(F32)[0:count] for k in range(8)], axis=0)


def box(tree):
    if isinstance(tree, dict):
        return types.SimpleNamespace(**{k: box(v) for k, v in tree.items()})
    return [box(v) for v in tree] if isinstance(tree, list) else tree


def call(body, name, collective_id, near=None, far=None, table=None, out=None, far_out=None, scratch=None):
    groups = [near or {}, far or {}, table or {}, out or {}, far_out or {}, scratch or {}]
    flat, trees = zip(*[jax.tree.flatten(g) for g in groups])
    counts = [len(f) for f in flat]

    def kernel(*refs):
        named, first = {}, 0
        for tree, count in zip(trees, counts):
            named.update(jax.tree.unflatten(tree, refs[first : first + count]))
            first += count
        body(box(named))

    smem = pl.BlockSpec(memory_space=pltpu.SMEM)
    results = pl.pallas_call(
        kernel,
        out_shape=tuple(flat[3]) + tuple(flat[4]),
        in_specs=[VMEM] * counts[0] + [ANY] * counts[1] + [smem] * counts[2],
        out_specs=(VMEM,) * counts[3] + (ANY,) * counts[4],
        scratch_shapes=list(flat[5]),
        compiler_params=pltpu.CompilerParams(
            collective_id=collective_id, has_side_effects=True, vmem_limit_bytes=63 * 2**20),
        cost_estimate=pl.CostEstimate(flops=10**11, bytes_accessed=2 * 10**8, transcendentals=10**7),
        name=name,
    )(*flat[0], *flat[1], *flat[2])
    done = jax.tree.unflatten(trees[3], results[: counts[3]])
    done.update(jax.tree.unflatten(trees[4], results[counts[3] :]))
    return box(done)


def shape(*dims, dtype=BF):
    return jax.ShapeDtypeStruct(dims, dtype)


def keep(*dims, dtype=BF):
    return pltpu.VMEM(dims, dtype)


def copies(*dims):
    return pltpu.SemaphoreType.DMA(dims)


def square_sum_items(tokens, width):
    half = width // 2
    return dict(ss_stage=keep(6, tokens, half), ss_inbox=keep(6, tokens, half), ss_send=copies(6), ss_recv=copies(6))


def flat_weight(ref, lo=0, hi=None):
    if len(ref.shape) == 2:
        return ref[:, lo:hi]
    v = ref[:, :, :, lo:hi]
    return v.reshape(v.shape[0] * v.shape[1] * v.shape[2], v.shape[3])


def side_weight(ref, cc, lo=0, hi=None):
    v = ref[:, cc, :, lo:hi]
    return v.reshape(v.shape[0] * v.shape[1], v.shape[2])


def block_sum_item(nz, *dims, dtype=BF):
    return dict(stage=keep(nz, 2, *dims, dtype=dtype), cin=keep(nz, *dims, dtype=dtype), zin=keep(nz + 1, *dims, dtype=dtype),
                csend=copies(nz), crecv=copies(nz), zsend=copies(nz), zrecv=copies(nz + 1))


def segment_row(seg, zz, cc):
    return jnp.concatenate([seg[pl.ds(zz * 8 + 2 * k + cc, 1), :] for k in range(4)], axis=1)


def key_columns(at, slopes, seg, zz, cc, tokens):
    rows = 4 * tokens
    column = lax.broadcasted_iota(jnp.int32, (128, rows), 0) % 64
    row = lax.broadcasted_iota(jnp.int32, (128, rows), 1)
    position = ((zz * 8 + (row // tokens) * 2 + cc) * tokens + row % tokens).astype(F32)
    value = jnp.where(segment_row(seg, zz, cc) == column - SEGMENT_LANE, 0.0, -1e30)
    value = jnp.where(column < SEGMENT_LANE + 5, value, 0.0)
    value = jnp.where(column < SEGMENT_LANE, 1.0, value)
    for h in range(3):
        for i, term in enumerate(split3(position * slopes[3 * at.g + h])):
            value = jnp.where(column == 3 * h + i, term, value)
    return value.T.astype(BF)


def segment_columns(at, seg, rows):
    column = lax.broadcasted_iota(jnp.int32, (128, rows), 0) % 64
    return jnp.where(segment_row(seg, at.z, at.c) == column - SEGMENT_LANE, 1.0, 0.0).T


def query_operand(at, q_ref, inside, slopes, side, h, tokens, lse=None):
    rows = 4 * tokens
    if h < 2:
        data = q_ref[:, 0:128]
    else:
        data = jnp.concatenate([q_ref[:, 128:192], jnp.zeros((rows, 64), q_ref.dtype)], axis=1)
    half = K_AT[h][1]
    sign = 1.0 if side == 0 else -1.0
    column = lanes(rows) % 64
    aug = jnp.where((column >= 3 * h) & (column < 3 * h + 3), sign, inside[...])
    term = at.positions(at.z, at.c, tokens, rows) * (slopes[3 * at.g + h] * -sign)
    if lse is not None:
        term = term - lse
    aug = with_lanes(aug, ROW_LANE if half else 64 + ROW_LANE, split3(term))
    return jnp.where(in_half(half, rows), data.astype(F32) * 0.125, aug).astype(BF)


def attention(at, gather, q_op, kaug, m_ref, acc_ref, behind):
    m_ref[...] = jnp.full(m_ref.shape, -1e30, F32)
    acc_ref[...] = jnp.zeros(acc_ref.shape, F32)

    def compute(zz, cc, same):
        kv, aug = gather.buf.at[zz, cc], kaug[zz, cc]
        side = (zz > at.z).astype(jnp.int32)
        for h in range(3):
            k = k_operand(kv, aug, h)
            if same:
                s = jnp.minimum(dot(q_op[0, h], k, NT), dot(q_op[1, h], k, NT))
            else:
                s = dot(q_op[side, h], k, NT)
            m_old = m_ref[h]
            m_new = jnp.maximum(m_old, jnp.max(s, axis=1, keepdims=True))
            p = jnp.exp(s - m_new[:, :1]).astype(BF)
            acc_ref[h] = acc_ref[h] * jnp.exp(m_old - m_new) + dot(p, v_operand(kv, h))
            m_ref[h] = m_new

    def here(i):
        cc = jnp.where(i == 0, at.c, at.oc)

        @pl.when(i == 1)
        def _():
            gather.wait(at.z, at.oc)
        compute(at.z, cc, True)
    loop(0, 2, here)

    def step(d):
        gather.serve(d)
        behind(d)

        def visit(i):
            zz = jnp.where(i % 2 == 0, at.z - d, at.z + d)

            @pl.when((zz >= 0) & (zz < at.nz))
            def _():
                @pl.when(i >= 2)
                def _():
                    gather.wait(zz, at.oc)
                compute(zz, jnp.where(i < 2, at.c, at.oc), False)
        loop(0, 4, visit)
    loop(1, at.nz, step)


def attention_end(m_ref, acc_ref, ctx_ref, ctxf_ref):
    for h in range(3):
        half = V_AT[h][1]
        first = 0 if half else 64
        acc = acc_ref[h]
        total = acc[:, first : first + 1]
        ctx = acc[:, 64 * half : 64 * half + 64] / total
        ctxf_ref[:, 64 * h : 64 * h + 64] = ctx
        ctx_ref[:, 64 * h : 64 * h + 64] = ctx.astype(BF)
        m_ref[h] = m_ref[h] + jnp.log(total)


def fwd_kernel(nz, layers, host, R):
    at = Place(nz)
    tokens = R.x0.shape[0]
    rows, half_rows = 4 * tokens, 2 * tokens
    quarter = R.hid.shape[1]
    group = R.ctx_now[0].shape[1]
    arrived = at.enter(host)
    part = R.part
    square_sum = SquareSum(at, part, R.ss_stage, R.ss_inbox, R.ss_send, R.ss_recv)
    gather_x = [SquareGather(at, R.xr_now[l], R.x_send.at[l], R.x_recv.at[l]) for l in range(layers)]
    gather_y = [SquareGather(at, R.yr_now[l], R.y_send.at[l], R.y_recv.at[l]) for l in range(layers)]
    kv = BlockGather(at, R.kv_now)
    saves, waited = [], []

    def save(source, target):
        saves.append(pltpu.make_async_copy(source, target, R.saved.at[len(saves)]))
        saves[-1].start()
        return len(saves) - 1

    def wait_saved(number):
        saves[number].wait()
        waited.append(number)

    if host:
        qkv, gu, down = [[BlockGather(at, item) for item in items] for items in (R.qkv_now, R.gu_now, R.down_now)]
        ow = BlockGather(at, R.ow_now)
        qkv_w, gu_w, down_w, out_w = [g.buf for g in qkv], [g.buf for g in gu], [g.buf for g in down], R.out_now
        wrows = R.ow_now.buf.shape[2] // layers
        lists = [qkv[l] for l in range(layers)] + [gu[l] for l in range(layers)]
        columns, first = [], 0
        for item in lists:
            columns.append(pl.ds(first, item.buf.shape[3]))
            first += item.buf.shape[3]
        spread = [PlaneExchange(at, R.spread, R.spread_in[i], R.spread_send.at[i], R.spread_recv.at[i], columns[i])
                  for i in range(len(lists))]

        def arrive(i):
            spread[i].wait()
            lists[i].put(spread[i].rows(wrows).astype(BF))

        def regroup():
            join = lambda *parts: jnp.concatenate(parts, axis=1)
            part_width = quarter // nz
            for l in range(layers):
                w = R.qkv_mine[l].astype(F32)
                for g in range(4):
                    q, k, v = [w[:, part * 4 * group + group * g : part * 4 * group + group * g + group] for part in range(3)]
                    beside = jnp.zeros(q.shape, F32) if l else R.small_mine[...].astype(F32)
                    at_l = 384 * l
                    R.spread[2 * g, 0:wrows, at_l : at_l + 384] = join(k[:, :128], v[:, :128], k[:, 128:], v[:, 128:]).astype(BF)
                    R.spread[2 * g + 1, 0:wrows, at_l : at_l + 384] = join(q, beside).astype(BF)
            for l in range(layers):
                w = R.gu_mine[l].astype(F32)
                lo = 384 * layers + quarter * l
                for g in range(4):
                    for side in range(2):
                        firsts = [((side * nz + zz) * 4 + g) * part_width for zz in range(nz)]
                        R.spread[2 * g + side, 0:wrows, lo : lo + quarter] = join(*[w[:, i : i + part_width] for i in firsts]).astype(BF)

        regroup()
        for l in range(layers):
            down[l].put(R.down_mine[l])
        arrived()
        down[0].start()
        to_holder = remote(R.ow_mine, R.ow_in, R.ow_send, R.ow_recv, at.holder)
        spread[0].start()
    else:
        arrived()
        qkv_w, gu_w, down_w, out_w = R.qkv_given, R.gu_given, R.down_given, R.out_given

    R.xr_now[0][at.g] = R.x0[...]
    gather_x[0].start()
    if host:
        spread[layers].start()

        @pl.when(at.moves)
        def _():
            to_holder.start()

        @pl.when(jnp.logical_not(at.moves))
        def _():
            R.ow_in[...] = R.ow_mine[...]
        arrive(0)
        qkv[0].start()

        @pl.when(at.moves)
        def _():
            to_holder.wait_recv()
        ow.put(R.ow_in[...])
        ow.start()

    def columns(b):
        R.kaug_now[b // 2, b % 2] = key_columns(at, R.slopes, R.seg, b // 2, b % 2, tokens)

    def columns_and_serve(zz):
        columns(2 * zz)
        columns(2 * zz + 1)
        if host:
            @pl.when(zz > 0)
            def _():
                qkv[0].serve(zz)
    loop(0, nz, columns_and_serve)
    save(R.kaug_now, R.kaug)
    R.inside[...] = segment_columns(at, R.seg, rows)

    def small(l, t):
        return R.small[8 * l + t : 8 * l + t + 1, :]

    def of(buf, half):
        v = buf[pl.ds(2 * half, 2)]
        return v.reshape(half_rows, v.shape[2])

    def half_at(half):
        return pl.ds(pl.multiple_of(half * half_rows, half_rows), half_rows)

    def put_part(half, value):
        part[pl.ds(2 * half, 2)] = value.reshape(2, tokens, value.shape[1])

    def of_group(row):
        value = jnp.zeros((1, group), F32)
        for g in range(4):
            value = jnp.where(at.g == g, row[:, group * g : group * g + group], value)
        return value

    if host:
        qkv[0].collect()
    R.small[...] = side_weight(qkv_w[0], 1, 128, 256).astype(F32).T[64 : 64 + 8 * layers, :]
    R.state[...] = R.x0[...].astype(F32)
    gather_x[0].wait_near()
    gather_x[0].wait_far()

    for l in range(layers):
        last = l == layers - 1
        x_all = R.xr_now[l][...].reshape(rows, -1)
        save(R.xr_now[l], R.xr[l])
        qb, vb = of_group(small(l, 2)), of_group(small(l, 3))
        none = jnp.zeros((1, 128), F32)
        kv_bias = jnp.concatenate([none, vb[:, :128], none[:, :64], vb[:, 128:192]], axis=1)
        if l:
            pl.semaphore_wait(R.kv_free, at.neighbours())
        kv.put((dot(x_all, side_weight(qkv_w[l], 0)) + kv_bias).astype(BF))
        kv.start()
        if host and not last:
            spread[l + 1].start()
            spread[layers + l + 1].start()
        R.q[...] = (dot(x_all, side_weight(qkv_w[l], 1, 0, group)) + qb).astype(BF)
        for side in range(2):
            for h in range(3):
                R.q_op[side, h] = query_operand(at, R.q, R.inside, R.slopes, side, h, tokens)

        def behind(d, l=l):
            if host:
                if l == 0:
                    ow.serve(d)

                @pl.when(d == min(2, nz - 1))
                def _():
                    arrive(layers + l)
                    gu[l].start()

        def later(p, l=l):
            if host:
                for step in range(p, nz if p == 3 else p + 1):
                    gu[l].serve(step)
                    if l == 0:
                        down[l].serve(step)

        def ahead(p, l=l):
            if host and l < layers - 1:
                if p == 0:
                    arrive(l + 1)
                    qkv[l + 1].start()
                    down[l + 1].start()
                for step in range(p, nz if p == 3 else p + 1):
                    if step:
                        qkv[l + 1].serve(step)
                        down[l + 1].serve(step)
        attention(at, kv, R.q_op, R.kaug_now, R.m, R.acc, behind)
        attention_end(R.m, R.acc, R.ctx_now[l], R.ctxf_now[l])
        kv_saved = save(kv.buf, R.kv[l])
        save(R.ctx_now[l], R.ctx[l])
        save(R.ctxf_now[l], R.ctxf[l])
        if l == 0 and host:
            ow.collect()
            step = group // (2 * nz)
            for i in range(layers):
                for b in range(2 * nz):
                    R.ow_wide[...] = ow.buf[b // 2, b % 2].astype(F32)
                    R.ow_flat[step * b : step * b + step, :] = R.ow_wide[step * i : step * i + step, :]
                R.out_now[i][...] = R.ow_flat[...].astype(BF)
                save(R.out_now[i], R.out_w[i])
        if l:
            square_sum.finish()
        for number, half in enumerate((1 - at.x, at.x)):
            put_part(half, dot(R.ctx_now[l][half_at(half), :], out_w[l][...]))
            if number == 0:
                square_sum.send_far()
            else:
                square_sum.send_near()
        later(1)
        square_sum.relay()
        kv.finish()
        for side in range(2):
            for h in range(3):
                R.qb_now[l][side, h] = query_operand(at, R.q, R.inside, R.slopes, side, h, tokens, R.m[h])
        save(R.qb_now[l], R.qb[l])
        later(2)
        wait_saved(kv_saved)
        if not last:
            at.signal_neighbours(R.kv_free)
        R.sum1_now[l][...] = R.state[...] + (square_sum.total() + small(l, 4))
        save(R.sum1_now[l], R.sum1[l])
        y = layer_norm(R.sum1_now[l][...], small(l, 0), small(l, 5))
        R.yr_now[l][at.g] = y.astype(BF)
        gather_y[l].start()
        R.state[...] = y
        later(3)
        ahead(0)
        if host:
            gu[l].collect()
            down[l].collect()
        gather_y[l].wait_near()
        if l:
            wait_saved(mixed_saved)
        square_sum.finish()
        for number, half in enumerate((at.x, 1 - at.x)):
            if number == 1:
                gather_y[l].wait_far()
                ahead(1)
            here = half_at(half)
            y_half = of(R.yr_now[l], half)
            for col in range(0, quarter, 256):
                gate = dot(y_half, side_weight(gu_w[l], 0, col, col + 256))
                up = dot(y_half, side_weight(gu_w[l], 1, col, col + 256))
                R.mixed_now[here, col : col + 256] = gate
                R.mixed_now[here, quarter + col : quarter + col + 256] = up
                R.hid[:, col : col + 256] = (gate * normal_cdf(gate) * up).astype(BF)
            put_part(half, dot(R.hid[...], flat_weight(down_w[l])))
            if number == 0:
                square_sum.send_near()
            else:
                square_sum.send_far()
        mixed_saved = save(R.mixed_now, R.mixed[l])
        save(R.yr_now[l], R.yr[l])
        if host:
            save(qkv[l].buf, R.qkv_w[l])
            save(gu[l].buf, R.gu_w[l])
            save(down[l].buf, R.down_w[l])
        square_sum.relay()
        ahead(2)
        R.sum2_now[l][...] = R.state[...] + (square_sum.total() + small(l, 6))
        save(R.sum2_now[l], R.sum2[l])
        state = layer_norm(R.sum2_now[l][...], small(l, 1), small(l, 7))
        R.state[...] = state
        if last:
            R.output[...] = state.astype(BF)
        else:
            R.xr_now[l + 1][at.g] = state.astype(BF)
            gather_x[l + 1].start()
            ahead(3)
            gather_x[l + 1].wait_near()
            gather_x[l + 1].wait_far()
            if host:
                qkv[l + 1].collect()
    for l in range(layers):
        gather_x[l].finish()
        gather_y[l].finish()
    square_sum.finish()
    if host:
        for items in (qkv, gu, down):
            for item in items:
                item.finish()
        ow.finish()
        for item in spread:
            item.finish()

        @pl.when(at.moves)
        def _():
            to_holder.wait_send()
    for number, copy in enumerate(saves):
        if number not in waited:
            copy.wait()


def fwd(x0, slopes, seg, weights, layers, host):
    nz = seg.shape[0] // 8
    tokens, width = x0.shape
    rows = 4 * tokens
    group = width // 4
    each = range(layers)
    quarter = weights.gu_mine.shape[2] // 8 if host else weights.gu_given[0].shape[3]
    r = width // nz
    keep_rows = lambda: [keep(4, tokens, width) for _ in each]
    keep_wide = lambda: [keep(tokens, width, dtype=F32) for _ in each]
    scratch = dict(
        xr_now=keep_rows(), x_send=copies(layers, 6), x_recv=copies(layers, 6),
        yr_now=keep_rows(), y_send=copies(layers, 6), y_recv=copies(layers, 6),
        part=keep(4, tokens, width, dtype=F32), state=keep(tokens, width, dtype=F32), **square_sum_items(tokens, width),
        kv_now=block_gather_item(nz, rows, 384), kv_free=pltpu.SemaphoreType.REGULAR, saved=copies(16 * layers),
        kaug_now=keep(nz, 2, rows, 128), inside=keep(rows, 128, dtype=F32),
        q=keep(rows, group), q_op=keep(2, 3, rows, 128),
        m=keep(3, rows, 128, dtype=F32), acc=keep(3, rows, 128, dtype=F32),
        ctx_now=[keep(rows, group) for _ in each], ctxf_now=[keep(rows, group, dtype=F32) for _ in each],
        qb_now=[keep(2, 3, rows, 128) for _ in each], sum1_now=keep_wide(), sum2_now=keep_wide(),
        mixed_now=keep(rows, 2 * quarter, dtype=F32), hid=keep(2 * tokens, quarter))
    far_out = dict(
        xr=[shape(4, tokens, width) for _ in each], yr=[shape(4, tokens, width) for _ in each],
        kv=[shape(nz, 2, rows, 384) for _ in each], ctx=[shape(rows, group) for _ in each],
        ctxf=[shape(rows, group, dtype=F32) for _ in each], qb=[shape(2, 3, rows, 128) for _ in each],
        sum1=[shape(tokens, width, dtype=F32) for _ in each], sum2=[shape(tokens, width, dtype=F32) for _ in each],
        mixed=[shape(rows, 2 * quarter, dtype=F32) for _ in each], kaug=shape(nz, 2, rows, 128))
    near = dict(x0=x0, seg=seg, **vars(weights))
    if host:
        gathered = lambda *dims: [shape(nz, 2, *dims) for _ in each]
        items = lambda *dims: [block_gather_item(nz, *dims) for _ in each]
        rd = weights.down_mine.shape[1]
        padded = 32
        far_out.update(qkv_w=gathered(r, 384), gu_w=gathered(r, quarter), down_w=gathered(rd, width),
                       out_w=[shape(group, width) for _ in each])
        scratch.update(
            qkv_now=items(r, 384), gu_now=items(r, quarter), down_now=items(rd, width),
            spread=keep(8, padded, layers * (384 + quarter)), spread_in=[keep(8, padded, 384) for _ in each] + [keep(8, padded, quarter) for _ in each],
            spread_send=copies(2 * layers, 8), spread_recv=copies(2 * layers, 8),
            ow_in=keep(*weights.ow_mine.shape), ow_send=pltpu.SemaphoreType.DMA, ow_recv=pltpu.SemaphoreType.DMA,
            ow_now=block_gather_item(nz, *weights.ow_mine.shape), out_now=[keep(group, width) for _ in each],
            ow_wide=keep(*weights.ow_mine.shape, dtype=F32), ow_flat=keep(group, width, dtype=F32))
    out = dict(output=shape(tokens, width), small=shape(8 * layers, width, dtype=F32))
    done = call(functools.partial(fwd_kernel, nz, layers, host), "forward", 0, near=near, table=dict(slopes=slopes),
                out=out, far_out=far_out, scratch=scratch)
    if not host:
        done.qkv_w, done.gu_w, done.down_w, done.out_w = weights.qkv_given, weights.gu_given, weights.down_given, weights.out_given
    done.down_w = [w.reshape(quarter, width) for w in done.down_w]
    done.xr = [v.reshape(rows, width) for v in done.xr]
    done.yr = [v.reshape(rows, width) for v in done.yr]
    return done


def attn_back(at, R, l, top, begin, behind, at_end):
    nz, rows = at.nz, R.kvbuf.shape[1]
    q_ref, do_ref, dqacc = R.qb[l], R.do, R.dqacc
    dkv = BlockSum(at, R.dkv)

    def target(i):
        right = nz - 1 - at.z
        from_right = jnp.where(i < right, nz - 1 - i, i - right)
        from_left = jnp.where(i < at.z, i, nz - 1 - (i - at.z))
        return jnp.where(i == nz - 1, at.z, jnp.where(at.z < nz // 2, from_right, from_left))

    class Load:
        def __init__(self, t, slot):
            cc = at.oc if slot == 0 else at.c
            self.copies = [pltpu.make_async_copy(source.at[t, cc], target.at[slot], R.kvsem.at[i, slot])
                           for i, (source, target) in enumerate(((R.kv[l], R.kvbuf), (R.kaug, R.augbuf)))]

        def start(self):
            for copy in self.copies:
                copy.start()

        def wait(self):
            for copy in self.copies:
                copy.wait()

    load = Load

    dqacc[...] = jnp.zeros(dqacc.shape, F32)

    def compute(t, slot, same):
        cc = at.oc if slot == 0 else at.c
        side = (t > at.z).astype(jnp.int32)
        kv, aug = R.kvbuf.at[slot], R.augbuf[slot]
        dks, dvs = [], []
        for h in range(3):
            k, v = k_operand(kv, aug, h), v_operand(kv, h)
            if same:
                s = jnp.minimum(dot(k, q_ref[0, h], NT), dot(k, q_ref[1, h], NT))
            else:
                s = dot(k, q_ref[side, h], NT)
            p = jnp.exp(s)
            ds = (p * dot(v, do_ref[h], NT)).astype(BF)
            dvs.append(dot(p.astype(BF), do_ref[h]))
            dks.append(dot(ds, q_ref[side, h]))
            dqacc[h] += dot(ds, k, TN)
        low = in_half(0, rows)
        dkv.stage[t, cc, :, 0:128] = jnp.where(low, dks[0], dks[1]).astype(BF)
        dkv.stage[t, cc, :, 128:256] = jnp.where(low, dvs[0], dvs[1]).astype(BF)
        dkv.stage[t, cc, :, 256:384] = jnp.where(low, dks[2], dvs[2]).astype(BF)

    def far(t, same):
        load(t, 1).start()
        load(t, 0).wait()
        compute(t, 0, same)
        dkv.to_beside(t).start()

    load(target(0), 0).start()
    begin()
    if not top:
        pl.semaphore_wait(R.dkv.free, at.neighbours())

    def step(i):
        t = target(i)
        far(t, False)
        load(target(i + 1), 0).start()
        load(t, 1).wait()
        compute(t, 1, False)
        dkv.serve(i, relay=False)

        @pl.when(i > 0)
        def _():
            dkv.serve(i - 1, source=False)
        behind(i)
    loop(0, nz - 1, step)
    far(at.z, True)
    dkv.serve(nz - 2, source=False)
    load(at.z, 1).wait()
    compute(at.z, 1, True)
    at_end()
    dq = jnp.where(in_half(0, rows), dqacc[0], dqacc[1]) * 0.125
    R.dproj[:, 384:512] = dq.astype(BF)
    R.dproj[:, 512:576] = (dqacc[2][:, 0:64] * 0.125).astype(BF)
    R.dproj[:, 0:384] = dkv.total().astype(BF)
    if l > 0:
        at.signal_neighbours(R.dkv.free)
    dkv.finish()


def bwd_kernel(nz, layers, host, R):
    at = Place(nz)
    tokens = R.grad.shape[0]
    rows, half_rows = 4 * tokens, 2 * tokens
    quarter = R.hid.shape[1]
    width = R.grad.shape[1]
    mixed, yr, xr, gu_w, down_w, qkv_w = range(6)
    streams = ((R.mixed, R.mixed_now), (R.yr, R.yr_now), (R.xr, R.xr_now), (R.gu_w, R.gu_now), (R.down_w, R.down_now),
               (R.qkv_w, R.qkv_now))

    def load(which, l):
        return pltpu.make_async_copy(streams[which][0][l], streams[which][1], R.load.at[which])

    for which in range(6):
        load(which, layers - 1).start()
    at.enter(host)()
    R.dproj[:, 576:768] = jnp.zeros((rows, 192), BF)
    gather_df = SquareGather(at, R.df, R.df_send, R.df_recv)
    gather_da = SquareGather(at, R.da, R.da_send, R.da_recv)
    part = R.part
    square_sum = SquareSum(at, part, R.ss_stage, R.ss_inbox, R.ss_send, R.ss_recv)
    if host:
        gu_sum, dn_sum, qk_sum, ow_sum = [[BlockSum(at, item) for item in items] for items in (R.gu, R.dn, R.qk, R.ow)]
        sm_sum = BlockSum(at, R.sm)
        back = [PlaneExchange(at, item.out, item.inbox, item.send, item.recv) for item in R.back]
        wrows = R.out_grad.shape[1]
        moved = [remote(R.ow_out.at[l], R.ow_in.at[l], R.ow_send.at[l], R.ow_recv.at[l], at.chunk_device) for l in range(layers)]

    def small(l, t):
        return R.small[8 * l + t : 8 * l + t + 1, :]

    def put_small(l, t, value):
        R.tok_small[8 * l + t : 8 * l + t + 1, :] = value

    def of(buf, half):
        v = buf[pl.ds(2 * half, 2)]
        return v.reshape(half_rows, v.shape[2])

    def half_at(half):
        return pl.ds(pl.multiple_of(half * half_rows, half_rows), half_rows)

    def put_part(half, value):
        part[pl.ds(2 * half, 2)] = value.reshape(2, tokens, value.shape[1])

    def wgrad(left, right, stage, cc, lo, hi):
        for first in range(0, left.shape[1], 384):
            v = dot(left[:, first : first + 384], right[:, lo:hi], TN)
            if len(stage.shape) == 2:
                stage[first : first + 384, :] = v.astype(BF)
                continue
            step = stage.shape[2]
            for i in range(384 // step):
                b = first // step + i
                zz, side = (b // 2, b % 2) if cc is None else (b, cc)
                stage[zz, side] = v[step * i : step * i + step].astype(BF)

    def feed_forward_sums(l):
        return (gu_sum[l], dn_sum[l]) if host and l < layers else ()

    def attention_sums(l):
        return (qk_sum[l], ow_sum[l]) if host and l < layers else ()

    def serve(items, p):
        for item in items:
            item.serve(p)

    def emit(l):
        if not host or l == layers:
            return
        pad = lambda v: jnp.concatenate([v, jnp.zeros((R.back[l].out.shape[1] - wrows, v.shape[1]), F32)], axis=0).astype(BF)
        for item, lo in ((gu_sum[l], 0), (qk_sum[l], quarter)):
            v = item.total()
            for k in range(8):
                R.back[l].out[k, :, lo : lo + v.shape[1]] = pad(v[wrows * k : wrows * k + wrows])
        back[l].start()
        R.dn_grad[l] = dn_sum[l].total()
        R.ow_out[l] = ow_sum[l].total()

        @pl.when(at.moves)
        def _():
            moved[l].start()

        @pl.when(jnp.logical_not(at.moves))
        def _():
            R.ow_in[l] = R.ow_out[l]

    def assemble(l):
        if not host:
            return
        back[l].wait()
        piece = [R.back[l].inbox[k].astype(F32)[0:wrows] for k in range(8)]
        join = lambda side, *spans: jnp.concatenate(
            [piece[2 * g + side][:, lo:hi] for g in range(4) for lo, hi in spans], axis=1)
        at_kv = quarter
        R.qkv_grad[l, :, 0:width] = join(1, (at_kv, at_kv + 192))
        R.qkv_grad[l, :, width : 2 * width] = join(0, (at_kv, at_kv + 128), (at_kv + 256, at_kv + 320))
        R.qkv_grad[l, :, 2 * width : 3 * width] = join(0, (at_kv + 128, at_kv + 256), (at_kv + 320, at_kv + 384))
        step = quarter // nz
        for side in range(2):
            for zz in range(nz):
                lo = (side * nz + zz) * 4 * step
                R.gu_grad[l, :, lo : lo + 4 * step] = join(side, (step * zz, step * zz + step))

        @pl.when(at.moves)
        def _():
            moved[l].wait_recv()
        R.out_grad[l] = R.ow_in[l, 0:wrows, :]

    def small_copy(j):
        k = 4 * at.c + j
        return remote(R.sm_out, R.sm_in.at[at.g], R.sm_send.at[j], R.sm_recv.at[at.g], at.of_plane(k)), k != at.member

    def small_from(g):
        k = 2 * g + at.x
        return remote(R.sm_out, R.sm_in.at[g], R.sm_send.at[0], R.sm_recv.at[g], at.of_plane(k)), k != at.member

    R.g[...] = R.grad[...].astype(F32)
    for l in reversed(range(layers)):
        top = l == layers - 1
        e2, d_gain, d_shift = norm_back(R.g[...], R.sum2[l][...], small(l, 1))
        put_small(l, 1, d_gain)
        put_small(l, 5, d_shift)
        low = e2.astype(BF)
        put_small(l, 4, jnp.sum(low.astype(F32), axis=0, keepdims=True))
        if not top:
            square_sum.finish()
        R.df[at.g] = low
        gather_df.start()
        R.e2[...] = e2
        for which in range(6):
            load(which, l).wait()
        serve(feed_forward_sums(l + 1), 1)
        gather_df.wait_near()
        for number, half in enumerate((at.x, 1 - at.x)):
            if number == 1:
                gather_df.wait_far()
                serve(attention_sums(l + 1), 1)
            here = half_at(half)
            dhid_all = dot(of(R.df, half), R.down_now[...], NT)
            for col in range(0, quarter, 256):
                dhid = dhid_all[:, col : col + 256]
                gate = R.mixed_now[here, col : col + 256]
                up = R.mixed_now[here, quarter + col : quarter + col + 256]
                cdf = normal_cdf(gate)
                act = gate * cdf
                R.hid[here, col : col + 256] = (act * up).astype(BF)
                R.dgu[here, col : col + 256] = (dhid * up * (cdf + gate * normal_pdf(gate))).astype(BF)
                R.dgu[here, quarter + col : quarter + col + 256] = (dhid * act).astype(BF)
            put_part(half, dot(R.dgu[here, :quarter], side_weight(R.gu_now, 0), NT)
                     + dot(R.dgu[here, quarter:], side_weight(R.gu_now, 1), NT))
            if number == 0:
                square_sum.send_near()
            else:
                square_sum.send_far()
        wgrad(R.hid, R.df[...].reshape(rows, width), R.dn[l].stage, None, 0, width)
        square_sum.relay()
        serve(feed_forward_sums(l + 1), 2)
        for p in range(3, nz - 1):
            serve(feed_forward_sums(l + 1), p)
        dy = R.e2[...] + square_sum.total()
        e1, d_gain, d_shift = norm_back(dy, R.sum1[l][...], small(l, 0))
        put_small(l, 0, d_gain)
        put_small(l, 3, d_shift)
        low = e1.astype(BF)
        put_small(l, 2, jnp.sum(low.astype(F32), axis=0, keepdims=True))
        R.da[at.g] = low
        gather_da.start()
        R.e1[...] = e1
        for cc in range(2):
            wgrad(R.yr_now, R.dgu, R.gu[l].stage, cc, quarter * cc, quarter * cc + quarter)
        gather_da.wait_near()
        gather_da.wait_far()
        for item in feed_forward_sums(l):
            item.start()
        if l > 0:
            for which in (mixed, yr, gu_w, down_w):
                load(which, l - 1).start()
        da_all = R.da[...].reshape(rows, width)
        dctx = dot(da_all, R.out_w[l][...], NT).astype(BF)
        ctxf = R.ctxf[l]
        wide = dctx.astype(F32)
        first_two = wide[:, :128]
        third = jnp.concatenate([jnp.zeros((rows, 64), F32), wide[:, 128:192]], axis=1)
        prod = first_two * ctxf[:, :128]
        low_half = in_half(0, rows)
        deltas = [
            jnp.sum(jnp.where(low_half, prod, 0.0), axis=1, keepdims=True),
            jnp.sum(jnp.where(low_half, 0.0, prod), axis=1, keepdims=True),
            jnp.sum(wide[:, 128:192] * ctxf[:, 128:192], axis=1, keepdims=True),
        ]
        for h in range(3):
            half = V_AT[h][1]
            base = jnp.where(in_half(half, rows), first_two if h < 2 else third, 0.0)
            R.do[h] = with_lanes(base, 0 if half else 64, split3(-deltas[h])).astype(BF)

        def begin(l=l):
            serve(attention_sums(l + 1), 2)
            for p in range(3, nz - 1):
                serve(attention_sums(l + 1), p)

        def out_grad(l=l):
            d_out = dot(R.ctx[l][...], R.da[...].reshape(rows, width), TN)
            if host:
                step = d_out.shape[0] // (2 * nz)
                for b in range(2 * nz):
                    R.ow[l].stage[b // 2, b % 2] = jnp.concatenate(
                        [d_out[step * b : step * b + step], jnp.zeros((OW_ROWS - step, width), F32)]).astype(BF)
            else:
                R.ow[l].stage[...] = d_out.astype(BF)

        def behind(i, l=l):
            pl.when(i == 0)(out_grad)
            if l < layers - 1:
                @pl.when(i == min(1, nz - 2))
                def _():
                    emit(l + 1)

                @pl.when(i == nz - 2)
                def _():
                    assemble(l + 1)

        def at_end(l=l):
            serve(feed_forward_sums(l), 0)
        attn_back(at, R, l, top, begin, behind, at_end)
        dproj = R.dproj
        gather_df.finish()
        gather_da.finish()
        square_sum.finish()
        for number, half in enumerate((1 - at.x, at.x)):
            put_part(half, dot(dproj[half_at(half), :384], side_weight(R.qkv_now, 0), NT)
                     + dot(dproj[half_at(half), 384:], side_weight(R.qkv_now, 1), NT))
            if number == 0:
                square_sum.send_far()
            else:
                square_sum.send_near()
        square_sum.relay()
        bias_sum = jnp.sum(dproj[...].astype(F32), axis=0, keepdims=True)
        for t, row in ((6, bias_sum[:, 384:576]), (7, jnp.concatenate([bias_sum[:, 128:256], bias_sum[:, 320:384]], axis=1))):
            put_small(l, t, jnp.concatenate([jnp.where(at.g == g, row, 0.0) for g in range(4)], axis=1))
        for cc in range(2):
            wgrad(R.xr_now, dproj, R.qk[l].stage, cc, 384 * cc, 384 * cc + 384)
        for item in attention_sums(l):
            item.start()
        serve(attention_sums(l), 0)
        if l > 0:
            load(xr, l - 1).start()
            load(qkv_w, l - 1).start()
        R.g[...] = R.e1[...] + square_sum.total()
    R.grad_in[...] = R.g[...]
    square_sum.finish()
    if host:
        for b in range(2 * nz):
            step = width // (2 * nz)
            sm_sum.stage[b // 2, b % 2, :, 0:step] = R.tok_small[:, step * b : step * b + step]
        sm_sum.start()
        last = feed_forward_sums(0) + attention_sums(0) + (sm_sum,)
        sm_sum.serve(0)
        for p in range(1, nz - 1):
            serve(last, p)
        R.sm_out[...] = sm_sum.total()
        for j in range(4):
            copy, away = small_copy(j)

            @pl.when(away)
            def _(copy=copy):
                copy.start()

            @pl.when(jnp.logical_not(away))
            def _():
                R.sm_in[at.g] = R.sm_out[...]
        emit(0)
        total = jnp.zeros(R.sm_out.shape, F32)
        for g in range(4):
            copy, away = small_from(g)

            @pl.when(away)
            def _(copy=copy):
                copy.wait_recv()
            total = total + R.sm_in[g]
        mine = jnp.zeros((8 * layers, wrows), F32)
        for k in range(4):
            mine = jnp.where(2 * at.y + at.c == k, total[:, wrows * k : wrows * k + wrows], mine)
        for l in range(layers):
            R.gains_grad[l] = mine[8 * l : 8 * l + 2]
            R.biases_grad[l] = jnp.concatenate([mine[8 * l + 6 : 8 * l + 8], mine[8 * l + 2 : 8 * l + 6]], axis=0)
        assemble(0)
        for l in range(layers):
            for item in feed_forward_sums(l) + attention_sums(l) + (back[l],):
                item.finish()

            @pl.when(at.moves)
            def _(l=l):
                moved[l].wait_send()
        for j in range(4):
            copy, away = small_copy(j)

            @pl.when(away)
            def _(copy=copy):
                copy.wait_send()
        sm_sum.finish()


def bwd(grad, saved, host):
    layers = len(saved.qkv_w)
    nz, _, rows, _ = saved.kaug.shape
    tokens, width = grad.shape
    quarter, group = width, width // 4
    quarter = saved.down_w[0].shape[0]
    r, rd = width // nz, quarter // (2 * nz)
    each = range(layers)
    out = dict(grad_in=shape(tokens, width, dtype=F32))
    scratch = {}
    if host:
        wrows, padded = width // (8 * nz), 32
        out.update(
            qkv_grad=shape(layers, wrows, 3 * width, dtype=F32), out_grad=shape(layers, wrows, width, dtype=F32),
            gu_grad=shape(layers, wrows, 8 * quarter, dtype=F32), dn_grad=shape(layers, rd, width, dtype=F32),
            gains_grad=shape(layers, 2, wrows, dtype=F32), biases_grad=shape(layers, 6, wrows, dtype=F32))
        scratch.update(
            back=[dict(out=keep(8, padded, quarter + 384), inbox=keep(8, padded, quarter + 384), send=copies(8), recv=copies(8))
                  for _ in each],
            ow_out=keep(layers, OW_ROWS, width, dtype=F32), ow_in=keep(layers, OW_ROWS, width, dtype=F32),
            ow_send=copies(layers), ow_recv=copies(layers),
            sm_out=keep(8 * layers, 128, dtype=F32), sm_in=keep(4, 8 * layers, 128, dtype=F32), sm_send=copies(4), sm_recv=copies(4))
        scratch.update(
            gu=[block_sum_item(nz, r, quarter) for _ in each], dn=[block_sum_item(nz, rd, width) for _ in each],
            qk=[block_sum_item(nz, r, 384) for _ in each], ow=[block_sum_item(nz, OW_ROWS, width) for _ in each],
            sm=block_sum_item(nz, 8 * layers, 128, dtype=F32), tok_small=keep(8 * layers, width, dtype=F32))
    else:
        out.update(
            gu=[dict(stage=shape(nz, 2, r, quarter)) for _ in each], dn=[dict(stage=shape(quarter, width)) for _ in each],
            qk=[dict(stage=shape(nz, 2, r, 384)) for _ in each], ow=[dict(stage=shape(group, width)) for _ in each],
            tok_small=shape(8 * layers, width, dtype=F32))
    like = lambda arrays: keep(*arrays[0].shape, dtype=arrays[0].dtype)
    scratch.update(
        mixed_now=like(saved.mixed), yr_now=like(saved.yr), xr_now=like(saved.xr), gu_now=like(saved.gu_w),
        down_now=like(saved.down_w), qkv_now=like(saved.qkv_w), load=copies(6), kvbuf=keep(2, rows, 384), augbuf=keep(2, rows, 128), kvsem=copies(2, 2),
        df=keep(4, tokens, width), df_send=copies(6), df_recv=copies(6),
        da=keep(4, tokens, width), da_send=copies(6), da_recv=copies(6),
        part=keep(4, tokens, width, dtype=F32), **square_sum_items(tokens, width),
        g=keep(tokens, width, dtype=F32), e1=keep(tokens, width, dtype=F32), e2=keep(tokens, width, dtype=F32),
        hid=keep(rows, quarter), dgu=keep(rows, 2 * quarter), do=keep(3, rows, 128),
        dqacc=keep(3, rows, 128, dtype=F32), dproj=keep(rows, 768),
        dkv=dict(block_sum_item(nz, rows, 384), free=pltpu.SemaphoreType.REGULAR))
    near = dict(grad=grad, small=saved.small, sum1=saved.sum1, sum2=saved.sum2, ctx=saved.ctx,
                ctxf=saved.ctxf, qb=saved.qb, out_w=saved.out_w)
    far = dict(mixed=saved.mixed, yr=saved.yr, xr=saved.xr, gu_w=saved.gu_w, down_w=saved.down_w, kv=saved.kv, kaug=saved.kaug,
               qkv_w=saved.qkv_w)
    return call(functools.partial(bwd_kernel, nz, layers, host), "backward", 1, near=near, far=far, out=out, scratch=scratch)


def shards(hidden_in, out_grad, segment_ids, alibi_slopes, qkv_weight, out_weight, gate_up_weight, down_weight, gains, biases):
    nz = lax.axis_size("z")
    nb = 2 * nz
    square, everyone, blocks = ("x", "y", "c"), ("z", "x", "y", "c"), ("z", "c")
    z, c = lax.axis_index("z"), lax.axis_index("c")
    tokens, width = hidden_in.shape
    layers, wrows = qkv_weight.shape[:2]
    ff = gate_up_weight.shape[2] // 2
    group, quarter = width // 4, ff // 4
    host = (width // nz) % 16 == 0 and down_weight.shape[1] % 16 == 0

    def to_groups(w):
        w = w.reshape(wrows, 3, 4, 3, 64)
        q, k, v = w[:, 0], w[:, 1], w[:, 2]
        kv = jnp.stack([k[:, :, 0], k[:, :, 1], v[:, :, 0], v[:, :, 1], k[:, :, 2], v[:, :, 2]], axis=2)
        return kv.reshape(wrows, 4, 384), q.reshape(wrows, 4, group)

    def from_groups(kv, q):
        kv, q = kv.reshape(4, wrows, 6, 64), q.reshape(4, wrows, 3, 64)
        k = jnp.stack([kv[:, :, 0], kv[:, :, 1], kv[:, :, 4]], axis=2)
        v = jnp.stack([kv[:, :, 2], kv[:, :, 3], kv[:, :, 5]], axis=2)
        return jnp.stack([q, k, v]).transpose(2, 0, 1, 3, 4).reshape(wrows, 3 * width)

    places = [(8 * zz + 2 * g + cc, g * nb + 2 * zz + cc) for zz in range(nz) for g in range(4) for cc in range(2)]
    gu0 = 384 * layers

    def gathered_outside():
        beside = jnp.broadcast_to(small[:, None], (wrows, 4, 192))
        nothing = jnp.zeros((wrows, 4, 192), BF)
        gu = gate_up_weight.reshape(layers, wrows, 2, nz, 4, quarter // nz).transpose(0, 1, 4, 2, 3, 5)
        gu = gu.reshape(layers, wrows, 4, 2, quarter)
        sides = [[], []]
        for l in range(layers):
            kv, q = to_groups(qkv_weight[l])
            sides[0].append(kv)
            sides[1] += [q, nothing if l else beside]
        for l in range(layers):
            for side in range(2):
                sides[side].append(gu[l, :, :, side])
        both = jnp.stack([jnp.concatenate(side, axis=2) for side in sides], axis=2).reshape(wrows, 8, -1)
        spread = lax.all_to_all(both, square, split_axis=1, concat_axis=0, tiled=True).reshape(8 * wrows, -1)
        ow_own = lax.ppermute(out_weight, everyone, [(chunk, device) for device, chunk in places])
        whole = lambda v: lax.all_gather(v, blocks, axis=0).reshape(nz, 2, *v.shape)
        flat = lambda v: lax.all_gather(v, blocks, axis=0, tiled=True)
        return types.SimpleNamespace(
            qkv_given=[whole(spread[:, 384 * l : 384 * l + 384]) for l in range(layers)],
            gu_given=[whole(spread[:, gu0 + quarter * l : gu0 + quarter * l + quarter]) for l in range(layers)],
            down_given=[flat(down_weight[l]) for l in range(layers)], out_given=[flat(ow_own[l]) for l in range(layers)])

    small = jnp.concatenate([gains, biases], axis=1).transpose(0, 2, 1)
    small = jnp.concatenate([small[l] for l in range(layers)], axis=1)
    small = jnp.pad(small, ((0, 0), (0, 192 - small.shape[1])))
    if host:
        weights = types.SimpleNamespace(
            qkv_mine=qkv_weight, gu_mine=gate_up_weight, down_mine=down_weight, small_mine=small,
            ow_mine=out_weight.reshape(layers * wrows, width))
    else:
        weights = gathered_outside()
    seg = segment_ids.reshape(8 * nz, tokens)
    saved = fwd(hidden_in, alibi_slopes, seg, weights, layers, host)
    done = bwd(out_grad, saved, host)
    if host:
        return (saved.output, done.grad_in, done.qkv_grad, done.out_grad, done.gu_grad, done.dn_grad, done.gains_grad,
                done.biases_grad)
    step = width // nb
    blocks_sum = lambda v: lax.psum_scatter(v, blocks, scatter_dimension=0, tiled=True)
    done.gu_sum = [blocks_sum(item.stage.reshape(nb, -1, quarter))[0] for item in done.gu]
    done.qk_sum = [blocks_sum(item.stage.reshape(nb, -1, 384))[0] for item in done.qk]
    done.dn_sum = [blocks_sum(item.stage) for item in done.dn]
    done.ow_sum = [blocks_sum(item.stage) for item in done.ow]
    sm = lax.psum_scatter(done.tok_small.reshape(-1, nb, step), blocks, scatter_dimension=1, tiled=True)[:, 0]
    sm = sm.T.reshape(4, wrows, 8 * layers)
    high = lax.reduce_precision(sm, 8, 7)
    sm = jnp.concatenate([high, sm - high], axis=2).astype(BF)
    sm = lax.dynamic_update_slice_in_dim(jnp.zeros((8, wrows, 16 * layers), BF), sm, 4 * c, 0)
    rows_of = lambda v: v.reshape(8, wrows, -1)
    back = jnp.concatenate([rows_of(v) for v in done.qk_sum + done.gu_sum] + [sm], axis=2)
    back = lax.all_to_all(back, square, split_axis=0, concat_axis=0, tiled=True)
    sides = back.astype(F32).reshape(4, 2, wrows, -1)
    qkv_grad = jnp.stack([from_groups(sides[:, 0, :, 384 * l : 384 * l + 384], sides[:, 1, :, 384 * l : 384 * l + group])
                          for l in range(layers)])
    gu_grad = jnp.stack([sides[:, :, :, gu0 + quarter * l : gu0 + quarter * l + quarter] for l in range(layers)])
    gu_grad = gu_grad.reshape(layers, 4, 2, wrows, nz, quarter // nz).transpose(0, 3, 2, 4, 1, 5).reshape(layers, wrows, 2 * ff)
    sm = jnp.sum(sides[..., gu0 + quarter * layers :], axis=(0, 1))
    sm = (sm[:, : 8 * layers] + sm[:, 8 * layers :]).T.reshape(layers, 8, wrows)
    out_grad_w = lax.ppermute(jnp.stack(done.ow_sum)[:, :wrows].astype(F32), everyone, places)
    return (saved.output, done.grad_in, qkv_grad, out_grad_w, gu_grad, jnp.stack(done.dn_sum).astype(F32), sm[:, 0:2],
            jnp.concatenate([sm[:, 6:8], sm[:, 2:6]], axis=1))


def solution(mesh):
    nb, nh = mesh.devices.shape
    everyone = ("z", "x", "y", "c")
    tok, mid, last = P(everyone, None), P(None, everyone, None), P(None, None, everyone)
    return jax.shard_map(
        shards, mesh=Mesh(mesh.devices.reshape(nb // 2, 2, nh // 2, 2), everyone),
        in_specs=(tok, tok, P(), P(), mid, mid, mid, mid, last, last),
        out_specs=(tok, tok, mid, mid, mid, mid, last, last),
        check_vma=False,
    )
```

```python
import functools
import types

import jax
import jax.numpy as jnp
from jax import lax
from jax.experimental import pallas as pl
from jax.experimental.pallas import tpu as pltpu
from jax.sharding import Mesh
from jax.sharding import PartitionSpec as P

MESH = pl.DeviceIdType.MESH
BF = jnp.bfloat16
F32 = jnp.float32
NT = (((1,), (1,)), ((), ()))
NN = (((1,), (0,)), ((), ()))
TN = (((0,), (0,)), ((), ()))
EPS = 1e-06
K_AT = ((0, 0), (0, 1), (2, 0))
V_AT = ((1, 0), (1, 1), (2, 1))
ROW_LANE, SEGMENT_LANE = 9, 12
OW_ROWS = 32
VMEM = pl.BlockSpec(memory_space=pltpu.VMEM)
ANY = pl.BlockSpec(memory_space=pl.ANY)


def dot(a, b, dims=NN):
    return lax.dot_general(a, b, dims, preferred_element_type=F32)


def lanes(rows):
    return lax.broadcasted_iota(jnp.int32, (rows, 128), 1)


def in_half(half, rows):
    return lanes(rows) >= 64 if half else lanes(rows) < 64


def ones_half(half, rows):
    first = 0 if half else 64
    lane = lanes(rows)
    return jnp.where((lane >= first) & (lane < first + 3), 1.0, 0.0).astype(BF)


def k_operand(kv, aug, h):
    col, half = K_AT[h]
    return jnp.where(in_half(half, kv.shape[0]), kv[:, 128 * col : 128 * col + 128], aug)


def v_operand(kv, h):
    col, half = V_AT[h]
    rows = kv.shape[0]
    return jnp.where(in_half(half, rows), kv[:, 128 * col : 128 * col + 128], ones_half(half, rows))


def split3(value):
    high = value.astype(BF).astype(F32)
    mid = (value - high).astype(BF).astype(F32)
    return high, mid, value - high - mid


def with_lanes(base, first, values):
    lane = lanes(base.shape[0])
    for i, v in enumerate(values):
        base = jnp.where(lane == first + i, v, base)
    return base


def layer_norm(total, gain, shift):
    centred = total - jnp.mean(total, axis=-1, keepdims=True)
    scale = lax.rsqrt(jnp.mean(centred * centred, axis=-1, keepdims=True) + EPS)
    return centred * scale * gain + shift


def norm_back(grad, total, gain):
    centred = total - jnp.mean(total, axis=-1, keepdims=True)
    scale = lax.rsqrt(jnp.mean(centred * centred, axis=-1, keepdims=True) + EPS)
    n = centred * scale
    dn = grad * gain
    e = scale * (dn - jnp.mean(dn, axis=-1, keepdims=True) - n * jnp.mean(dn * n, axis=-1, keepdims=True))
    return e, jnp.sum(grad * n, axis=0, keepdims=True), jnp.sum(grad, axis=0, keepdims=True)


def normal_cdf(u):
    return 0.5 * (1.0 + lax.erf(u * (0.5**0.5)))


def normal_pdf(u):
    return jnp.exp(-0.5 * u * u) * ((2.0 * jnp.pi) ** -0.5)


def remote(src, dst, send, recv, device):
    return pltpu.make_async_remote_copy(
        src_ref=src, dst_ref=dst, send_sem=send, recv_sem=recv, device_id=device, device_id_type=MESH)


def loop(first, last, do):
    def step(i, carry):
        do(i)
        return carry
    lax.fori_loop(first, last, step, 0)


class Place:
    def __init__(self, nz):
        self.nz = nz
        self.z, self.x, self.y, self.c = [lax.axis_index(name) for name in "zxyc"]
        self.g = 2 * self.x + self.y
        self.gx, self.gy = 2 * (1 - self.x) + self.y, 2 * self.x + 1 - self.y
        self.gd = 2 * (1 - self.x) + 1 - self.y
        self.oc = 1 - self.c
        self.beside = (self.z, self.x, self.y, self.oc)
        self.across_x = (self.z, 1 - self.x, self.y, self.c)
        self.across_y = (self.z, self.x, 1 - self.y, self.c)
        self.block = 2 * self.z + self.c
        self.member = 2 * self.g + self.c
        self.number = 8 * self.z + self.member
        nb = 2 * nz
        self.chunk = self.g * nb + self.block
        self.chunk_device = self.device(self.chunk)
        place = self.number % nb
        self.holder = (place // 2, self.number // nb // 2, self.number // nb % 2, place % 2)
        self.moves = self.chunk != self.number
        self.has_left, self.has_right = self.z > 0, self.z < nz - 1

    def column(self, zz):
        return (zz, self.x, self.y, self.c)

    def device(self, number):
        k = number % 8
        return (number // 8, k // 4, k // 2 % 2, k % 2)

    def of_plane(self, k):
        return (self.z, k // 4, k // 2 % 2, k % 2)

    def neighbours(self):
        return 3 - (self.z == 0).astype(jnp.int32) - (self.z == self.nz - 1).astype(jnp.int32)

    def signal_neighbours(self, semaphore):
        pl.semaphore_signal(semaphore, inc=1, device_id=self.beside, device_id_type=MESH)

        @pl.when(self.has_left)
        def _():
            pl.semaphore_signal(semaphore, inc=1, device_id=self.column(self.z - 1), device_id_type=MESH)

        @pl.when(self.has_right)
        def _():
            pl.semaphore_signal(semaphore, inc=1, device_id=self.column(self.z + 1), device_id_type=MESH)

    def enter(self, plane):
        barrier = pltpu.get_barrier_semaphore()

        def greet(device):
            pl.semaphore_signal(barrier, inc=1, device_id=device, device_id_type=MESH)

        if not plane:
            greet(self.across_x)
            greet(self.across_y)
            self.signal_neighbours(barrier)
            return lambda: pl.semaphore_wait(barrier, 2 + self.neighbours())
        loop(1, 8, lambda j: greet(self.of_plane((self.member + j) % 8)))
        self.signal_neighbours(barrier)

        @pl.when(self.moves)
        def _():
            greet(self.chunk_device)
            greet(self.holder)
        return lambda: pl.semaphore_wait(barrier, 7 + self.neighbours() + 2 * self.moves.astype(jnp.int32))

    def positions(self, zz, cc, tokens, rows):
        row = lax.broadcasted_iota(jnp.int32, (rows, 128), 0)
        return ((zz * 8 + (row // tokens) * 2 + cc) * tokens + row % tokens).astype(F32)


class SquareGather:
    def __init__(self, at, buf, send, recv):
        half = buf.shape[1] // 2
        first, second = pl.ds(0, half), pl.ds(half, half)

        def copy(i, g, rows, device):
            return remote(buf.at[g, rows], buf.at[g, rows], send.at[i], recv.at[i], device)
        self.x_first, self.x_second = copy(0, at.g, first, at.across_x), copy(1, at.g, second, at.across_x)
        self.y_second, self.y_first = copy(2, at.g, second, at.across_y), copy(3, at.g, first, at.across_y)
        self.on_y = copy(4, at.gx, first, at.across_y)
        self.on_x = copy(5, at.gy, second, at.across_x)

    def start(self):
        for copy in (self.x_first, self.y_second, self.x_second, self.y_first):
            copy.start()

    def wait_near(self):
        self.x_first.wait_recv()
        self.on_y.start()
        self.y_second.wait_recv()
        self.on_x.start()
        self.y_first.wait_recv()

    def wait_far(self):
        self.x_second.wait_recv()
        self.on_x.wait_recv()
        self.on_y.wait_recv()

    def finish(self):
        for copy in (self.x_first, self.x_second, self.y_first, self.y_second, self.on_x, self.on_y):
            copy.wait_send()


class SquareSum:
    def __init__(self, at, part, stage, inbox, send, recv):
        self.at, self.part, self.stage, self.inbox = at, part, stage, inbox
        self.half = part.shape[2] // 2
        to = (at.across_x, at.across_x, at.across_y, at.across_y, at.across_y, at.across_x)
        self.copies = [remote(stage.at[i], inbox.at[i], send.at[i], recv.at[i], to[i]) for i in range(6)]

    def left(self, g):
        return self.part[g, :, : self.half]

    def right(self, g):
        return self.part[g, :, self.half :]

    def post(self, i, value):
        self.stage[i] = value.astype(BF)
        self.copies[i].start()

    def came(self, i):
        self.copies[i].wait_recv()
        return self.inbox[i].astype(F32)

    def send_far(self):
        self.post(0, self.left(self.at.gd))
        self.post(2, self.right(self.at.gd))
        self.post(1, self.left(self.at.gx))

    def send_near(self):
        self.post(3, self.right(self.at.gy))

    def relay(self):
        self.post(4, self.left(self.at.gy) + self.came(0))
        self.post(5, self.right(self.at.gx) + self.came(2))

    def total(self):
        left = self.left(self.at.g) + self.came(1)
        right = self.right(self.at.g) + self.came(3)
        return jnp.concatenate([left + self.came(4), right + self.came(5)], axis=1)

    def finish(self):
        for copy in self.copies:
            copy.wait_send()


class BlockGather:
    def __init__(self, at, item):
        self.at, self.buf, self.zsend, self.csend, self.recv = at, item.buf, item.zsend, item.csend, item.recv
        self.parts = self.recv.shape[2]
        self.step = self.buf.shape[2] // self.parts

    def copy(self, zz, cc, part, send, device):
        block = self.buf.at[zz, cc, pl.ds(part * self.step, self.step)]
        return remote(block, block, send, self.recv.at[zz, cc, part], device)

    def to_right(self, zz, part):
        return self.copy(zz, self.at.c, part, self.zsend.at[0, zz, part], self.at.column(self.at.z + 1))

    def to_left(self, zz, part):
        return self.copy(zz, self.at.c, part, self.zsend.at[1, zz, part], self.at.column(self.at.z - 1))

    def to_beside(self, zz, part):
        return self.copy(zz, self.at.c, part, self.csend.at[zz, part], self.at.beside)

    def wait_part(self, zz, cc, part):
        self.copy(zz, cc, part, self.csend.at[zz, part], self.at.beside).wait_recv()

    def wait(self, zz, cc):
        for part in range(self.parts):
            self.wait_part(zz, cc, part)

    def put(self, value):
        self.buf[self.at.z, self.at.c] = value

    def start(self):
        at = self.at
        for part in range(self.parts):
            @pl.when(at.has_right)
            def _(part=part):
                self.to_right(at.z, part).start()

            @pl.when(at.has_left)
            def _(part=part):
                self.to_left(at.z, part).start()
            self.to_beside(at.z, part).start()

    def serve(self, d):
        at = self.at
        for part in range(self.parts):
            @pl.when(at.z - d >= 0)
            def _(part=part):
                self.wait_part(at.z - d, at.c, part)

                @pl.when(at.has_right)
                def _():
                    self.to_right(at.z - d, part).start()
                self.to_beside(at.z - d, part).start()

            @pl.when(at.z + d < at.nz)
            def _(part=part):
                self.wait_part(at.z + d, at.c, part)

                @pl.when(at.has_left)
                def _():
                    self.to_left(at.z + d, part).start()
                self.to_beside(at.z + d, part).start()

    def serve_all(self):
        loop(1, self.at.nz, self.serve)

    def collect(self):
        loop(0, self.at.nz, lambda zz: self.wait(zz, self.at.oc))

    def finish(self):
        at = self.at

        def drain(zz):
            for part in range(self.parts):
                self.to_beside(zz, part).wait_send()

                @pl.when((zz <= at.z) & at.has_right)
                def _(part=part):
                    self.to_right(zz, part).wait_send()

                @pl.when((zz >= at.z) & at.has_left)
                def _(part=part):
                    self.to_left(zz, part).wait_send()
        loop(0, at.nz, drain)


def block_gather_item(nz, *dims, parts=1):
    return dict(buf=keep(nz, 2, *dims), zsend=copies(2, nz, parts), csend=copies(nz, parts), recv=copies(nz, 2, parts))


class BlockSum:
    def __init__(self, at, item):
        self.at, self.stage, self.cin, self.zin = at, item.stage, item.cin, item.zin
        self.csend, self.crecv, self.zsend, self.zrecv = item.csend, item.crecv, item.zsend, item.zrecv
        self.parts = self.zsend.shape[1]
        self.step = self.stage.shape[2] // self.parts

    def rows(self, part):
        return pl.ds(part * self.step, self.step)

    def to_beside(self, t):
        return remote(self.stage.at[t, self.at.oc], self.cin.at[t], self.csend.at[t], self.crecv.at[t], self.at.beside)

    def along(self, t, slot, part, device):
        rows = self.rows(part)
        return remote(self.stage.at[t, self.at.c, rows], self.zin.at[slot, rows], self.zsend.at[t, part],
                      self.zrecv.at[slot, part], device)

    def to_right(self, t, part):
        return self.along(t, t + 1, part, self.at.column(self.at.z + 1))

    def to_left(self, t, part):
        return self.along(t, t, part, self.at.column(self.at.z - 1))

    def arrived(self, slot, part):
        block = self.zin.at[slot, self.rows(part)]
        remote(block, block, self.zsend.at[0, part], self.zrecv.at[slot, part], self.at.beside).wait_recv()

    def start(self):
        loop(0, self.at.nz, lambda t: self.to_beside(t).start())

    def add(self, t, part, slot=None):
        rows = self.rows(part)
        value = self.stage[t, self.at.c, rows].astype(F32) + self.cin[t, rows].astype(F32)
        if slot is not None:
            value = value + self.zin[slot, rows].astype(F32)
        self.stage[t, self.at.c, rows] = value.astype(self.stage.dtype)

    def go(self, t, slot, passed_on, send):
        self.to_beside(t).wait_recv()
        for part in range(self.parts):
            @pl.when(passed_on)
            def _(part=part):
                self.arrived(slot, part)
                self.add(t, part, slot)

            @pl.when(jnp.logical_not(passed_on))
            def _(part=part):
                self.add(t, part)
            send(t, part).start()

    def serve(self, p, source=True, relay=True):
        at = self.at
        right, left = p - at.z, p - (at.nz - 1 - at.z)
        go_r = (right >= 0) & (right < at.nz - 1 - at.z)
        go_l = (left >= 0) & (left < at.z)
        if not source:
            go_r, go_l = go_r & at.has_left, go_l & at.has_right
        if not relay:
            go_r, go_l = go_r & jnp.logical_not(at.has_left), go_l & jnp.logical_not(at.has_right)

        @pl.when(go_r)
        def _():
            self.go(at.nz - 1 - right, at.nz - right, at.has_left, self.to_right)

        @pl.when(go_l)
        def _():
            self.go(left, left, at.has_right, self.to_left)

    def total(self):
        at = self.at
        self.to_beside(at.z).wait_recv()
        for part in range(self.parts):
            @pl.when(at.has_left)
            def _(part=part):
                self.arrived(at.z + 1, part)

            @pl.when(at.has_right)
            def _(part=part):
                self.arrived(at.z, part)
        value = self.stage[at.z, at.c].astype(F32) + self.cin[at.z].astype(F32)
        from_left = jnp.where(at.has_left, self.zin[at.z + 1].astype(F32), 0.0)
        from_right = jnp.where(at.has_right, self.zin[at.z].astype(F32), 0.0)
        return value + from_left + from_right

    def finish(self):
        at = self.at

        def drain(t):
            self.to_beside(t).wait_send()
            for part in range(self.parts):
                @pl.when(t > at.z)
                def _(part=part):
                    self.to_right(t, part).wait_send()

                @pl.when(t < at.z)
                def _(part=part):
                    self.to_left(t, part).wait_send()
        loop(0, at.nz, drain)


class PlaneExchange:
    def __init__(self, at, out, inbox, send, recv, columns=None):
        self.at, self.out, self.inbox, self.send, self.recv, self.columns = at, out, inbox, send, recv, columns

    def source(self, k):
        return self.out.at[k] if self.columns is None else self.out.at[k, :, self.columns]

    def start(self):
        at = self.at

        def step(j):
            k = (at.member + j) % 8
            remote(self.source(k), self.inbox.at[at.member], self.send.at[k], self.recv.at[at.member], at.of_plane(k)).start()
        loop(1, 8, step)
        self.inbox[at.member] = self.source(at.member)[...]

    def each(self, do):
        at = self.at

        def step(j):
            k = (at.member + j) % 8
            do(remote(self.source(k), self.inbox.at[k], self.send.at[k], self.recv.at[k], at.of_plane(k)))
        loop(1, 8, step)

    def wait(self):
        self.each(lambda copy: copy.wait_recv())

    def finish(self):
        self.each(lambda copy: copy.wait_send())

    def rows(self, count):
        return jnp.concatenate([self.inbox[k].astype(F32)[0:count] for k in range(8)], axis=0)


def box(tree):
    if isinstance(tree, dict):
        return types.SimpleNamespace(**{k: box(v) for k, v in tree.items()})
    return [box(v) for v in tree] if isinstance(tree, list) else tree


def call(body, name, collective_id, near=None, far=None, table=None, out=None, far_out=None, scratch=None):
    groups = [near or {}, far or {}, table or {}, out or {}, far_out or {}, scratch or {}]
    flat, trees = zip(*[jax.tree.flatten(g) for g in groups])
    counts = [len(f) for f in flat]

    def kernel(*refs):
        named, first = {}, 0
        for tree, count in zip(trees, counts):
            named.update(jax.tree.unflatten(tree, refs[first : first + count]))
            first += count
        body(box(named))

    smem = pl.BlockSpec(memory_space=pltpu.SMEM)
    results = pl.pallas_call(
        kernel,
        out_shape=tuple(flat[3]) + tuple(flat[4]),
        in_specs=[VMEM] * counts[0] + [ANY] * counts[1] + [smem] * counts[2],
        out_specs=(VMEM,) * counts[3] + (ANY,) * counts[4],
        scratch_shapes=list(flat[5]),
        compiler_params=pltpu.CompilerParams(
            collective_id=collective_id, has_side_effects=True, vmem_limit_bytes=63 * 2**20),
        cost_estimate=pl.CostEstimate(flops=10**11, bytes_accessed=2 * 10**8, transcendentals=10**7),
        name=name,
    )(*flat[0], *flat[1], *flat[2])
    done = jax.tree.unflatten(trees[3], results[: counts[3]])
    done.update(jax.tree.unflatten(trees[4], results[counts[3] :]))
    return box(done)


def shape(*dims, dtype=BF):
    return jax.ShapeDtypeStruct(dims, dtype)


def keep(*dims, dtype=BF):
    return pltpu.VMEM(dims, dtype)


def copies(*dims):
    return pltpu.SemaphoreType.DMA(dims)


def square_sum_items(tokens, width):
    half = width // 2
    return dict(ss_stage=keep(6, tokens, half), ss_inbox=keep(6, tokens, half), ss_send=copies(6), ss_recv=copies(6))


def flat_weight(ref, lo=0, hi=None):
    if len(ref.shape) == 2:
        return ref[:, lo:hi]
    v = ref[:, :, :, lo:hi]
    return v.reshape(v.shape[0] * v.shape[1] * v.shape[2], v.shape[3])


def side_weight(ref, cc, lo=0, hi=None):
    v = ref[:, cc, :, lo:hi]
    return v.reshape(v.shape[0] * v.shape[1], v.shape[2])


def block_sum_item(nz, *dims, dtype=BF, parts=1):
    return dict(stage=keep(nz, 2, *dims, dtype=dtype), cin=keep(nz, *dims, dtype=dtype), zin=keep(nz + 1, *dims, dtype=dtype),
                csend=copies(nz), crecv=copies(nz), zsend=copies(nz, parts), zrecv=copies(nz + 1, parts))


def segment_row(seg, zz, cc):
    return jnp.concatenate([seg[pl.ds(zz * 8 + 2 * k + cc, 1), :] for k in range(4)], axis=1)


def key_columns(at, slopes, seg, zz, cc, tokens):
    rows = 4 * tokens
    column = lax.broadcasted_iota(jnp.int32, (128, rows), 0) % 64
    row = lax.broadcasted_iota(jnp.int32, (128, rows), 1)
    position = ((zz * 8 + (row // tokens) * 2 + cc) * tokens + row % tokens).astype(F32)
    value = jnp.where(segment_row(seg, zz, cc) == column - SEGMENT_LANE, 0.0, -1e30)
    value = jnp.where(column < SEGMENT_LANE + 5, value, 0.0)
    value = jnp.where(column < SEGMENT_LANE, 1.0, value)
    for h in range(3):
        for i, term in enumerate(split3(position * slopes[3 * at.g + h])):
            value = jnp.where(column == 3 * h + i, term, value)
    return value.T.astype(BF)


def segment_columns(at, seg, rows):
    column = lax.broadcasted_iota(jnp.int32, (128, rows), 0) % 64
    return jnp.where(segment_row(seg, at.z, at.c) == column - SEGMENT_LANE, 1.0, 0.0).T


def query_operand(at, q_ref, inside, slopes, side, h, tokens, lse=None):
    rows = 4 * tokens
    if h < 2:
        data = q_ref[:, 0:128]
    else:
        data = jnp.concatenate([q_ref[:, 128:192], jnp.zeros((rows, 64), q_ref.dtype)], axis=1)
    half = K_AT[h][1]
    sign = 1.0 if side == 0 else -1.0
    column = lanes(rows) % 64
    aug = jnp.where((column >= 3 * h) & (column < 3 * h + 3), sign, inside[...])
    term = at.positions(at.z, at.c, tokens, rows) * (slopes[3 * at.g + h] * -sign)
    if lse is not None:
        term = term - lse
    aug = with_lanes(aug, ROW_LANE if half else 64 + ROW_LANE, split3(term))
    return jnp.where(in_half(half, rows), data.astype(F32) * 0.125, aug).astype(BF)


def attention(at, gather, q_op, kaug, m_ref, acc_ref, behind):
    m_ref[...] = jnp.full(m_ref.shape, -1e30, F32)
    acc_ref[...] = jnp.zeros(acc_ref.shape, F32)

    def compute(zz, cc, same):
        kv, aug = gather.buf.at[zz, cc], kaug[zz, cc]
        side = (zz > at.z).astype(jnp.int32)
        for h in range(3):
            k = k_operand(kv, aug, h)
            if same:
                s = jnp.minimum(dot(q_op[0, h], k, NT), dot(q_op[1, h], k, NT))
            else:
                s = dot(q_op[side, h], k, NT)
            m_old = m_ref[h]
            m_new = jnp.maximum(m_old, jnp.max(s, axis=1, keepdims=True))
            p = jnp.exp(s - m_new[:, :1]).astype(BF)
            acc_ref[h] = acc_ref[h] * jnp.exp(m_old - m_new) + dot(p, v_operand(kv, h))
            m_ref[h] = m_new

    def here(i):
        cc = jnp.where(i == 0, at.c, at.oc)

        @pl.when(i == 1)
        def _():
            gather.wait(at.z, at.oc)
        compute(at.z, cc, True)
    loop(0, 2, here)

    def both(d):
        return (at.z - d >= 0) & (at.z + d < at.nz)

    def step(d):
        @pl.when(jnp.logical_not(both(d - 1)) | (d == 1))
        def _():
            gather.serve(d)
        behind(d)

        def visit(i):
            zz = jnp.where(i % 2 == 0, at.z - d, at.z + d)

            @pl.when((zz >= 0) & (zz < at.nz))
            def _():
                @pl.when(i >= 2)
                def _():
                    gather.wait(zz, at.oc)
                compute(zz, jnp.where(i < 2, at.c, at.oc), False)

            @pl.when((i == 1) & both(d) & (d + 1 < at.nz))
            def _():
                gather.serve(d + 1)
        loop(0, 4, visit)
    loop(1, at.nz, step)


def attention_end(m_ref, acc_ref, ctx_ref, ctxf_ref):
    for h in range(3):
        half = V_AT[h][1]
        first = 0 if half else 64
        acc = acc_ref[h]
        total = acc[:, first : first + 1]
        ctx = acc[:, 64 * half : 64 * half + 64] / total
        ctxf_ref[:, 64 * h : 64 * h + 64] = ctx
        ctx_ref[:, 64 * h : 64 * h + 64] = ctx.astype(BF)
        m_ref[h] = m_ref[h] + jnp.log(total)


def fwd_kernel(nz, layers, host, R):
    at = Place(nz)
    tokens = R.x0.shape[0]
    rows, half_rows = 4 * tokens, 2 * tokens
    quarter = R.hid.shape[1]
    group = R.ctx_now[0].shape[1]
    arrived = at.enter(host)
    part = R.part
    square_sum = SquareSum(at, part, R.ss_stage, R.ss_inbox, R.ss_send, R.ss_recv)
    gather_x = [SquareGather(at, R.xr_now[l], R.x_send.at[l], R.x_recv.at[l]) for l in range(layers)]
    gather_y = [SquareGather(at, R.yr_now[l], R.y_send.at[l], R.y_recv.at[l]) for l in range(layers)]
    kv = BlockGather(at, R.kv_now)
    saves, waited = [], []

    def save(source, target):
        saves.append(pltpu.make_async_copy(source, target, R.saved.at[len(saves)]))
        saves[-1].start()
        return len(saves) - 1

    def wait_saved(number):
        saves[number].wait()
        waited.append(number)

    if host:
        qkv, gu, down = [[BlockGather(at, item) for item in items] for items in (R.qkv_now, R.gu_now, R.down_now)]
        ow = BlockGather(at, R.ow_now)
        qkv_w, gu_w, down_w, out_w = [g.buf for g in qkv], [g.buf for g in gu], [g.buf for g in down], R.out_now
        wrows = R.ow_now.buf.shape[2] // layers
        lists = [qkv[l] for l in range(layers)] + [gu[l] for l in range(layers)]
        columns, first = [], 0
        for item in lists:
            columns.append(pl.ds(first, item.buf.shape[3]))
            first += item.buf.shape[3]
        spread = [PlaneExchange(at, R.spread, R.spread_in[i], R.spread_send.at[i], R.spread_recv.at[i], columns[i])
                  for i in range(len(lists))]

        def arrive(i):
            spread[i].wait()
            lists[i].put(spread[i].rows(wrows).astype(BF))

        def regroup():
            join = lambda *parts: jnp.concatenate(parts, axis=1)
            part_width = quarter // nz
            for l in range(layers):
                w = R.qkv_mine[l].astype(F32)
                for g in range(4):
                    q, k, v = [w[:, part * 4 * group + group * g : part * 4 * group + group * g + group] for part in range(3)]
                    beside = jnp.zeros(q.shape, F32) if l else R.small_mine[...].astype(F32)
                    at_l = 384 * l
                    R.spread[2 * g, 0:wrows, at_l : at_l + 384] = join(k[:, :128], v[:, :128], k[:, 128:], v[:, 128:]).astype(BF)
                    R.spread[2 * g + 1, 0:wrows, at_l : at_l + 384] = join(q, beside).astype(BF)
            for l in range(layers):
                w = R.gu_mine[l].astype(F32)
                lo = 384 * layers + quarter * l
                for g in range(4):
                    for side in range(2):
                        firsts = [((side * nz + zz) * 4 + g) * part_width for zz in range(nz)]
                        R.spread[2 * g + side, 0:wrows, lo : lo + quarter] = join(*[w[:, i : i + part_width] for i in firsts]).astype(BF)

        regroup()
        for l in range(layers):
            down[l].put(R.down_mine[l])
        arrived()
        down[0].start()
        to_holder = remote(R.ow_mine, R.ow_in, R.ow_send, R.ow_recv, at.holder)
        spread[0].start()
    else:
        arrived()
        qkv_w, gu_w, down_w, out_w = R.qkv_given, R.gu_given, R.down_given, R.out_given

    R.xr_now[0][at.g] = R.x0[...]
    gather_x[0].start()
    if host:
        spread[layers].start()

        @pl.when(at.moves)
        def _():
            to_holder.start()

        @pl.when(jnp.logical_not(at.moves))
        def _():
            R.ow_in[...] = R.ow_mine[...]
        arrive(0)
        qkv[0].start()

        @pl.when(at.moves)
        def _():
            to_holder.wait_recv()
        ow.put(R.ow_in[...])
        ow.start()

    def columns(b):
        R.kaug_now[b // 2, b % 2] = key_columns(at, R.slopes, R.seg, b // 2, b % 2, tokens)

    def columns_and_serve(zz):
        columns(2 * zz)
        columns(2 * zz + 1)
        if host:
            @pl.when(zz > 0)
            def _():
                qkv[0].serve(zz)
    loop(0, nz, columns_and_serve)
    save(R.kaug_now, R.kaug)
    R.inside[...] = segment_columns(at, R.seg, rows)

    def small(l, t):
        return R.small[8 * l + t : 8 * l + t + 1, :]

    def of(buf, half):
        v = buf[pl.ds(2 * half, 2)]
        return v.reshape(half_rows, v.shape[2])

    def half_at(half):
        return pl.ds(pl.multiple_of(half * half_rows, half_rows), half_rows)

    def put_part(half, value):
        part[pl.ds(2 * half, 2)] = value.reshape(2, tokens, value.shape[1])

    def of_group(row):
        value = jnp.zeros((1, group), F32)
        for g in range(4):
            value = jnp.where(at.g == g, row[:, group * g : group * g + group], value)
        return value

    if host:
        qkv[0].collect()
    R.small[...] = side_weight(qkv_w[0], 1, 128, 256).astype(F32).T[64 : 64 + 8 * layers, :]
    R.state[...] = R.x0[...].astype(F32)
    gather_x[0].wait_near()
    gather_x[0].wait_far()

    for l in range(layers):
        last = l == layers - 1
        x_all = R.xr_now[l][...].reshape(rows, -1)
        save(R.xr_now[l], R.xr[l])
        qb, vb = of_group(small(l, 2)), of_group(small(l, 3))
        none = jnp.zeros((1, 128), F32)
        kv_bias = jnp.concatenate([none, vb[:, :128], none[:, :64], vb[:, 128:192]], axis=1)
        if l:
            pl.semaphore_wait(R.kv_free, at.neighbours())
        kv.put((dot(x_all, side_weight(qkv_w[l], 0)) + kv_bias).astype(BF))
        kv.start()
        if host and not last:
            spread[l + 1].start()
            spread[layers + l + 1].start()
        R.q[...] = (dot(x_all, side_weight(qkv_w[l], 1, 0, group)) + qb).astype(BF)
        for side in range(2):
            for h in range(3):
                R.q_op[side, h] = query_operand(at, R.q, R.inside, R.slopes, side, h, tokens)

        def behind(d, l=l):
            if host:
                if l == 0:
                    ow.serve(d)

                @pl.when(d == min(2, nz - 1))
                def _():
                    arrive(layers + l)
                    gu[l].start()

        def later(p, l=l):
            if host:
                for step in range(p, nz if p == 3 else p + 1):
                    gu[l].serve(step)
                    if l == 0:
                        down[l].serve(step)

        def ahead(p, l=l):
            if host and l < layers - 1:
                if p == 0:
                    arrive(l + 1)
                    qkv[l + 1].start()
                    down[l + 1].start()
                for step in range(p, nz if p == 3 else p + 1):
                    if step:
                        qkv[l + 1].serve(step)
                        down[l + 1].serve(step)
        attention(at, kv, R.q_op, R.kaug_now, R.m, R.acc, behind)
        attention_end(R.m, R.acc, R.ctx_now[l], R.ctxf_now[l])
        kv_saved = save(kv.buf, R.kv[l])
        save(R.ctx_now[l], R.ctx[l])
        save(R.ctxf_now[l], R.ctxf[l])
        if l == 0 and host:
            ow.collect()
            step = group // (2 * nz)
            for i in range(layers):
                for b in range(2 * nz):
                    R.ow_wide[...] = ow.buf[b // 2, b % 2].astype(F32)
                    R.ow_flat[step * b : step * b + step, :] = R.ow_wide[step * i : step * i + step, :]
                R.out_now[i][...] = R.ow_flat[...].astype(BF)
                save(R.out_now[i], R.out_w[i])
        if l:
            square_sum.finish()
        for number, half in enumerate((1 - at.x, at.x)):
            put_part(half, dot(R.ctx_now[l][half_at(half), :], out_w[l][...]))
            if number == 0:
                square_sum.send_far()
            else:
                square_sum.send_near()
        later(1)
        square_sum.relay()
        kv.finish()
        for side in range(2):
            for h in range(3):
                R.qb_now[l][side, h] = query_operand(at, R.q, R.inside, R.slopes, side, h, tokens, R.m[h])
        save(R.qb_now[l], R.qb[l])
        later(2)
        wait_saved(kv_saved)
        if not last:
            at.signal_neighbours(R.kv_free)
        R.sum1_now[l][...] = R.state[...] + (square_sum.total() + small(l, 4))
        save(R.sum1_now[l], R.sum1[l])
        y = layer_norm(R.sum1_now[l][...], small(l, 0), small(l, 5))
        R.yr_now[l][at.g] = y.astype(BF)
        gather_y[l].start()
        R.state[...] = y
        later(3)
        ahead(0)
        if host:
            gu[l].collect()
            down[l].collect()
        gather_y[l].wait_near()
        if l:
            wait_saved(mixed_saved)
        square_sum.finish()
        for number, half in enumerate((at.x, 1 - at.x)):
            if number == 1:
                gather_y[l].wait_far()
                ahead(1)
            here = half_at(half)
            y_half = of(R.yr_now[l], half)
            for col in range(0, quarter, 256):
                gate = dot(y_half, side_weight(gu_w[l], 0, col, col + 256))
                up = dot(y_half, side_weight(gu_w[l], 1, col, col + 256))
                R.mixed_now[here, col : col + 256] = gate
                R.mixed_now[here, quarter + col : quarter + col + 256] = up
                R.hid[:, col : col + 256] = (gate * normal_cdf(gate) * up).astype(BF)
            put_part(half, dot(R.hid[...], flat_weight(down_w[l])))
            if number == 0:
                square_sum.send_near()
            else:
                square_sum.send_far()
        mixed_saved = save(R.mixed_now, R.mixed[l])
        save(R.yr_now[l], R.yr[l])
        if host:
            save(qkv[l].buf, R.qkv_w[l])
            save(gu[l].buf, R.gu_w[l])
            save(down[l].buf, R.down_w[l])
        square_sum.relay()
        ahead(2)
        R.sum2_now[l][...] = R.state[...] + (square_sum.total() + small(l, 6))
        save(R.sum2_now[l], R.sum2[l])
        state = layer_norm(R.sum2_now[l][...], small(l, 1), small(l, 7))
        R.state[...] = state
        if last:
            R.output[...] = state.astype(BF)
        else:
            R.xr_now[l + 1][at.g] = state.astype(BF)
            gather_x[l + 1].start()
            ahead(3)
            gather_x[l + 1].wait_near()
            gather_x[l + 1].wait_far()
            if host:
                qkv[l + 1].collect()
    for l in range(layers):
        gather_x[l].finish()
        gather_y[l].finish()
    square_sum.finish()
    if host:
        for items in (qkv, gu, down):
            for item in items:
                item.finish()
        ow.finish()
        for item in spread:
            item.finish()

        @pl.when(at.moves)
        def _():
            to_holder.wait_send()
    for number, copy in enumerate(saves):
        if number not in waited:
            copy.wait()


def fwd(x0, slopes, seg, weights, layers, host):
    nz = seg.shape[0] // 8
    tokens, width = x0.shape
    rows = 4 * tokens
    group = width // 4
    each = range(layers)
    quarter = weights.gu_mine.shape[2] // 8 if host else weights.gu_given[0].shape[3]
    r = width // nz
    keep_rows = lambda: [keep(4, tokens, width) for _ in each]
    keep_wide = lambda: [keep(tokens, width, dtype=F32) for _ in each]
    scratch = dict(
        xr_now=keep_rows(), x_send=copies(layers, 6), x_recv=copies(layers, 6),
        yr_now=keep_rows(), y_send=copies(layers, 6), y_recv=copies(layers, 6),
        part=keep(4, tokens, width, dtype=F32), state=keep(tokens, width, dtype=F32), **square_sum_items(tokens, width),
        kv_now=block_gather_item(nz, rows, 384, parts=2), kv_free=pltpu.SemaphoreType.REGULAR, saved=copies(16 * layers),
        kaug_now=keep(nz, 2, rows, 128), inside=keep(rows, 128, dtype=F32),
        q=keep(rows, group), q_op=keep(2, 3, rows, 128),
        m=keep(3, rows, 128, dtype=F32), acc=keep(3, rows, 128, dtype=F32),
        ctx_now=[keep(rows, group) for _ in each], ctxf_now=[keep(rows, group, dtype=F32) for _ in each],
        qb_now=[keep(2, 3, rows, 128) for _ in each], sum1_now=keep_wide(), sum2_now=keep_wide(),
        mixed_now=keep(rows, 2 * quarter, dtype=F32), hid=keep(2 * tokens, quarter))
    far_out = dict(
        xr=[shape(4, tokens, width) for _ in each], yr=[shape(4, tokens, width) for _ in each],
        kv=[shape(nz, 2, rows, 384) for _ in each], ctx=[shape(rows, group) for _ in each],
        ctxf=[shape(rows, group, dtype=F32) for _ in each], qb=[shape(2, 3, rows, 128) for _ in each],
        sum1=[shape(tokens, width, dtype=F32) for _ in each], sum2=[shape(tokens, width, dtype=F32) for _ in each],
        mixed=[shape(rows, 2 * quarter, dtype=F32) for _ in each], kaug=shape(nz, 2, rows, 128))
    near = dict(x0=x0, seg=seg, **vars(weights))
    if host:
        gathered = lambda *dims: [shape(nz, 2, *dims) for _ in each]
        items = lambda *dims: [block_gather_item(nz, *dims, parts=2) for _ in each]
        rd = weights.down_mine.shape[1]
        padded = 32
        far_out.update(qkv_w=gathered(r, 384), gu_w=gathered(r, quarter), down_w=gathered(rd, width),
                       out_w=[shape(group, width) for _ in each])
        scratch.update(
            qkv_now=items(r, 384), gu_now=items(r, quarter), down_now=items(rd, width),
            spread=keep(8, padded, layers * (384 + quarter)), spread_in=[keep(8, padded, 384) for _ in each] + [keep(8, padded, quarter) for _ in each],
            spread_send=copies(2 * layers, 8), spread_recv=copies(2 * layers, 8),
            ow_in=keep(*weights.ow_mine.shape), ow_send=pltpu.SemaphoreType.DMA, ow_recv=pltpu.SemaphoreType.DMA,
            ow_now=block_gather_item(nz, *weights.ow_mine.shape), out_now=[keep(group, width) for _ in each],
            ow_wide=keep(*weights.ow_mine.shape, dtype=F32), ow_flat=keep(group, width, dtype=F32))
    out = dict(output=shape(tokens, width), small=shape(8 * layers, width, dtype=F32))
    done = call(functools.partial(fwd_kernel, nz, layers, host), "forward", 0, near=near, table=dict(slopes=slopes),
                out=out, far_out=far_out, scratch=scratch)
    if not host:
        done.qkv_w, done.gu_w, done.down_w, done.out_w = weights.qkv_given, weights.gu_given, weights.down_given, weights.out_given
    done.down_w = [w.reshape(quarter, width) for w in done.down_w]
    done.xr = [v.reshape(rows, width) for v in done.xr]
    done.yr = [v.reshape(rows, width) for v in done.yr]
    return done


def attn_back(at, R, l, top, begin, behind, at_end):
    nz, rows = at.nz, R.kvbuf.shape[1]
    q_ref, do_ref, dqacc = R.qb[l], R.do, R.dqacc
    dkv = BlockSum(at, R.dkv)

    def target(i):
        right = nz - 1 - at.z
        from_right = jnp.where(i < right, nz - 1 - i, i - right)
        from_left = jnp.where(i < at.z, i, nz - 1 - (i - at.z))
        return jnp.where(i == nz - 1, at.z, jnp.where(at.z < nz // 2, from_right, from_left))

    class Load:
        def __init__(self, t, slot):
            cc = at.oc if slot == 0 else at.c
            self.copies = [pltpu.make_async_copy(source.at[t, cc], target.at[slot], R.kvsem.at[i, slot])
                           for i, (source, target) in enumerate(((R.kv[l], R.kvbuf), (R.kaug, R.augbuf)))]

        def start(self):
            for copy in self.copies:
                copy.start()

        def wait(self):
            for copy in self.copies:
                copy.wait()

    load = Load

    dqacc[...] = jnp.zeros(dqacc.shape, F32)

    def compute(t, slot, same):
        cc = at.oc if slot == 0 else at.c
        side = (t > at.z).astype(jnp.int32)
        kv, aug = R.kvbuf.at[slot], R.augbuf[slot]
        dks, dvs = [], []
        for h in range(3):
            k, v = k_operand(kv, aug, h), v_operand(kv, h)
            if same:
                s = jnp.minimum(dot(k, q_ref[0, h], NT), dot(k, q_ref[1, h], NT))
            else:
                s = dot(k, q_ref[side, h], NT)
            p = jnp.exp(s)
            ds = (p * dot(v, do_ref[h], NT)).astype(BF)
            dvs.append(dot(p.astype(BF), do_ref[h]))
            dks.append(dot(ds, q_ref[side, h]))
            dqacc[h] += dot(ds, k, TN)
        low = in_half(0, rows)
        dkv.stage[t, cc, :, 0:128] = jnp.where(low, dks[0], dks[1]).astype(BF)
        dkv.stage[t, cc, :, 128:256] = jnp.where(low, dvs[0], dvs[1]).astype(BF)
        dkv.stage[t, cc, :, 256:384] = jnp.where(low, dks[2], dvs[2]).astype(BF)

    def far(t, same):
        load(t, 1).start()
        load(t, 0).wait()
        compute(t, 0, same)
        dkv.to_beside(t).start()

    load(target(0), 0).start()
    begin()
    if not top:
        pl.semaphore_wait(R.dkv.free, at.neighbours())

    def step(i):
        t = target(i)
        far(t, False)
        load(target(i + 1), 0).start()
        load(t, 1).wait()
        compute(t, 1, False)
        dkv.serve(i)
        behind(i)
    loop(0, nz - 1, step)
    far(at.z, True)
    load(at.z, 1).wait()
    compute(at.z, 1, True)
    at_end()
    dq = jnp.where(in_half(0, rows), dqacc[0], dqacc[1]) * 0.125
    R.dproj[:, 384:512] = dq.astype(BF)
    R.dproj[:, 512:576] = (dqacc[2][:, 0:64] * 0.125).astype(BF)
    R.dproj[:, 0:384] = dkv.total().astype(BF)
    if l > 0:
        at.signal_neighbours(R.dkv.free)
    dkv.finish()


def bwd_kernel(nz, layers, host, R):
    at = Place(nz)
    tokens = R.grad.shape[0]
    rows, half_rows = 4 * tokens, 2 * tokens
    quarter = R.hid.shape[1]
    width = R.grad.shape[1]
    mixed, yr, xr, gu_w, down_w, qkv_w = range(6)
    streams = ((R.mixed, R.mixed_now), (R.yr, R.yr_now), (R.xr, R.xr_now), (R.gu_w, R.gu_now), (R.down_w, R.down_now),
               (R.qkv_w, R.qkv_now))

    def load(which, l):
        return pltpu.make_async_copy(streams[which][0][l], streams[which][1], R.load.at[which])

    for which in range(6):
        load(which, layers - 1).start()
    at.enter(host)()
    R.dproj[:, 576:768] = jnp.zeros((rows, 192), BF)
    gather_df = SquareGather(at, R.df, R.df_send, R.df_recv)
    gather_da = SquareGather(at, R.da, R.da_send, R.da_recv)
    part = R.part
    square_sum = SquareSum(at, part, R.ss_stage, R.ss_inbox, R.ss_send, R.ss_recv)
    if host:
        gu_sum, dn_sum, qk_sum, ow_sum = [[BlockSum(at, item) for item in items] for items in (R.gu, R.dn, R.qk, R.ow)]
        sm_sum = BlockSum(at, R.sm)
        back = [PlaneExchange(at, item.out, item.inbox, item.send, item.recv) for item in R.back]
        wrows = R.out_grad.shape[1]
        moved = [remote(R.ow_out.at[l], R.ow_in.at[l], R.ow_send.at[l], R.ow_recv.at[l], at.chunk_device) for l in range(layers)]

    def small(l, t):
        return R.small[8 * l + t : 8 * l + t + 1, :]

    def put_small(l, t, value):
        R.tok_small[8 * l + t : 8 * l + t + 1, :] = value

    def of(buf, half):
        v = buf[pl.ds(2 * half, 2)]
        return v.reshape(half_rows, v.shape[2])

    def half_at(half):
        return pl.ds(pl.multiple_of(half * half_rows, half_rows), half_rows)

    def put_part(half, value):
        part[pl.ds(2 * half, 2)] = value.reshape(2, tokens, value.shape[1])

    def wgrad(left, right, stage, cc, lo, hi):
        for first in range(0, left.shape[1], 384):
            v = dot(left[:, first : first + 384], right[:, lo:hi], TN)
            if len(stage.shape) == 2:
                stage[first : first + 384, :] = v.astype(BF)
                continue
            step = stage.shape[2]
            for i in range(384 // step):
                b = first // step + i
                zz, side = (b // 2, b % 2) if cc is None else (b, cc)
                stage[zz, side] = v[step * i : step * i + step].astype(BF)

    def feed_forward_sums(l):
        return (gu_sum[l], dn_sum[l]) if host and l < layers else ()

    def attention_sums(l):
        return (qk_sum[l], ow_sum[l]) if host and l < layers else ()

    def serve(items, p):
        for item in items:
            item.serve(p)

    def emit(l):
        if not host or l == layers:
            return
        pad = lambda v: jnp.concatenate([v, jnp.zeros((R.back[l].out.shape[1] - wrows, v.shape[1]), F32)], axis=0).astype(BF)
        for item, lo in ((gu_sum[l], 0), (qk_sum[l], quarter)):
            v = item.total()
            for k in range(8):
                R.back[l].out[k, :, lo : lo + v.shape[1]] = pad(v[wrows * k : wrows * k + wrows])
        back[l].start()
        R.dn_grad[l] = dn_sum[l].total()
        R.ow_out[l] = ow_sum[l].total()

        @pl.when(at.moves)
        def _():
            moved[l].start()

        @pl.when(jnp.logical_not(at.moves))
        def _():
            R.ow_in[l] = R.ow_out[l]

    def assemble(l):
        if not host:
            return
        back[l].wait()
        piece = [R.back[l].inbox[k].astype(F32)[0:wrows] for k in range(8)]
        join = lambda side, *spans: jnp.concatenate(
            [piece[2 * g + side][:, lo:hi] for g in range(4) for lo, hi in spans], axis=1)
        at_kv = quarter
        R.qkv_grad[l, :, 0:width] = join(1, (at_kv, at_kv + 192))
        R.qkv_grad[l, :, width : 2 * width] = join(0, (at_kv, at_kv + 128), (at_kv + 256, at_kv + 320))
        R.qkv_grad[l, :, 2 * width : 3 * width] = join(0, (at_kv + 128, at_kv + 256), (at_kv + 320, at_kv + 384))
        step = quarter // nz
        for side in range(2):
            for zz in range(nz):
                lo = (side * nz + zz) * 4 * step
                R.gu_grad[l, :, lo : lo + 4 * step] = join(side, (step * zz, step * zz + step))

        @pl.when(at.moves)
        def _():
            moved[l].wait_recv()
        R.out_grad[l] = R.ow_in[l, 0:wrows, :]

    def small_copy(j):
        k = 4 * at.c + j
        return remote(R.sm_out, R.sm_in.at[at.g], R.sm_send.at[j], R.sm_recv.at[at.g], at.of_plane(k)), k != at.member

    def small_from(g):
        k = 2 * g + at.x
        return remote(R.sm_out, R.sm_in.at[g], R.sm_send.at[0], R.sm_recv.at[g], at.of_plane(k)), k != at.member

    R.g[...] = R.grad[...].astype(F32)
    for l in reversed(range(layers)):
        top = l == layers - 1
        e2, d_gain, d_shift = norm_back(R.g[...], R.sum2[l][...], small(l, 1))
        put_small(l, 1, d_gain)
        put_small(l, 5, d_shift)
        low = e2.astype(BF)
        put_small(l, 4, jnp.sum(low.astype(F32), axis=0, keepdims=True))
        if not top:
            square_sum.finish()
        R.df[at.g] = low
        gather_df.start()
        R.e2[...] = e2
        for which in range(6):
            load(which, l).wait()
        serve(feed_forward_sums(l + 1), 1)
        gather_df.wait_near()
        for number, half in enumerate((at.x, 1 - at.x)):
            if number == 1:
                gather_df.wait_far()
                serve(attention_sums(l + 1), 1)
            here = half_at(half)
            dhid_all = dot(of(R.df, half), R.down_now[...], NT)
            for col in range(0, quarter, 256):
                dhid = dhid_all[:, col : col + 256]
                gate = R.mixed_now[here, col : col + 256]
                up = R.mixed_now[here, quarter + col : quarter + col + 256]
                cdf = normal_cdf(gate)
                act = gate * cdf
                R.hid[here, col : col + 256] = (act * up).astype(BF)
                R.dgu[here, col : col + 256] = (dhid * up * (cdf + gate * normal_pdf(gate))).astype(BF)
                R.dgu[here, quarter + col : quarter + col + 256] = (dhid * act).astype(BF)
            put_part(half, dot(R.dgu[here, :quarter], side_weight(R.gu_now, 0), NT)
                     + dot(R.dgu[here, quarter:], side_weight(R.gu_now, 1), NT))
            if number == 0:
                square_sum.send_near()
            else:
                square_sum.send_far()
        wgrad(R.hid, R.df[...].reshape(rows, width), R.dn[l].stage, None, 0, width)
        square_sum.relay()
        serve(feed_forward_sums(l + 1), 2)
        for p in range(3, nz - 1):
            serve(feed_forward_sums(l + 1), p)
        dy = R.e2[...] + square_sum.total()
        e1, d_gain, d_shift = norm_back(dy, R.sum1[l][...], small(l, 0))
        put_small(l, 0, d_gain)
        put_small(l, 3, d_shift)
        low = e1.astype(BF)
        put_small(l, 2, jnp.sum(low.astype(F32), axis=0, keepdims=True))
        R.da[at.g] = low
        gather_da.start()
        R.e1[...] = e1
        for cc in range(2):
            wgrad(R.yr_now, R.dgu, R.gu[l].stage, cc, quarter * cc, quarter * cc + quarter)
        gather_da.wait_near()
        gather_da.wait_far()
        for item in feed_forward_sums(l):
            item.start()
        if l > 0:
            for which in (mixed, yr, gu_w, down_w):
                load(which, l - 1).start()
        da_all = R.da[...].reshape(rows, width)
        dctx = dot(da_all, R.out_w[l][...], NT).astype(BF)
        ctxf = R.ctxf[l]
        wide = dctx.astype(F32)
        first_two = wide[:, :128]
        third = jnp.concatenate([jnp.zeros((rows, 64), F32), wide[:, 128:192]], axis=1)
        prod = first_two * ctxf[:, :128]
        low_half = in_half(0, rows)
        deltas = [
            jnp.sum(jnp.where(low_half, prod, 0.0), axis=1, keepdims=True),
            jnp.sum(jnp.where(low_half, 0.0, prod), axis=1, keepdims=True),
            jnp.sum(wide[:, 128:192] * ctxf[:, 128:192], axis=1, keepdims=True),
        ]
        for h in range(3):
            half = V_AT[h][1]
            base = jnp.where(in_half(half, rows), first_two if h < 2 else third, 0.0)
            R.do[h] = with_lanes(base, 0 if half else 64, split3(-deltas[h])).astype(BF)

        def begin(l=l):
            serve(attention_sums(l + 1), 2)
            for p in range(3, nz - 1):
                serve(attention_sums(l + 1), p)

        def out_grad(l=l):
            d_out = dot(R.ctx[l][...], R.da[...].reshape(rows, width), TN)
            if host:
                step = d_out.shape[0] // (2 * nz)
                for b in range(2 * nz):
                    R.ow[l].stage[b // 2, b % 2] = jnp.concatenate(
                        [d_out[step * b : step * b + step], jnp.zeros((OW_ROWS - step, width), F32)]).astype(BF)
            else:
                R.ow[l].stage[...] = d_out.astype(BF)

        def behind(i, l=l):
            pl.when(i == 0)(out_grad)
            if l < layers - 1:
                @pl.when(i == min(1, nz - 2))
                def _():
                    emit(l + 1)

                @pl.when(i == nz - 2)
                def _():
                    assemble(l + 1)

        def at_end(l=l):
            serve(feed_forward_sums(l), 0)
        attn_back(at, R, l, top, begin, behind, at_end)
        dproj = R.dproj
        gather_df.finish()
        gather_da.finish()
        square_sum.finish()
        for number, half in enumerate((1 - at.x, at.x)):
            put_part(half, dot(dproj[half_at(half), :384], side_weight(R.qkv_now, 0), NT)
                     + dot(dproj[half_at(half), 384:], side_weight(R.qkv_now, 1), NT))
            if number == 0:
                square_sum.send_far()
            else:
                square_sum.send_near()
        square_sum.relay()
        bias_sum = jnp.sum(dproj[...].astype(F32), axis=0, keepdims=True)
        for t, row in ((6, bias_sum[:, 384:576]), (7, jnp.concatenate([bias_sum[:, 128:256], bias_sum[:, 320:384]], axis=1))):
            put_small(l, t, jnp.concatenate([jnp.where(at.g == g, row, 0.0) for g in range(4)], axis=1))
        for cc in range(2):
            wgrad(R.xr_now, dproj, R.qk[l].stage, cc, 384 * cc, 384 * cc + 384)
        for item in attention_sums(l):
            item.start()
        serve(attention_sums(l), 0)
        if l > 0:
            load(xr, l - 1).start()
            load(qkv_w, l - 1).start()
        R.g[...] = R.e1[...] + square_sum.total()
    R.grad_in[...] = R.g[...]
    square_sum.finish()
    if host:
        for b in range(2 * nz):
            step = width // (2 * nz)
            sm_sum.stage[b // 2, b % 2, :, 0:step] = R.tok_small[:, step * b : step * b + step]
        sm_sum.start()
        last = feed_forward_sums(0) + attention_sums(0) + (sm_sum,)
        sm_sum.serve(0)
        for p in range(1, nz - 1):
            serve(last, p)
        R.sm_out[...] = sm_sum.total()
        for j in range(4):
            copy, away = small_copy(j)

            @pl.when(away)
            def _(copy=copy):
                copy.start()

            @pl.when(jnp.logical_not(away))
            def _():
                R.sm_in[at.g] = R.sm_out[...]
        emit(0)
        total = jnp.zeros(R.sm_out.shape, F32)
        for g in range(4):
            copy, away = small_from(g)

            @pl.when(away)
            def _(copy=copy):
                copy.wait_recv()
            total = total + R.sm_in[g]
        mine = jnp.zeros((8 * layers, wrows), F32)
        for k in range(4):
            mine = jnp.where(2 * at.y + at.c == k, total[:, wrows * k : wrows * k + wrows], mine)
        for l in range(layers):
            R.gains_grad[l] = mine[8 * l : 8 * l + 2]
            R.biases_grad[l] = jnp.concatenate([mine[8 * l + 6 : 8 * l + 8], mine[8 * l + 2 : 8 * l + 6]], axis=0)
        assemble(0)
        for l in range(layers):
            for item in feed_forward_sums(l) + attention_sums(l) + (back[l],):
                item.finish()

            @pl.when(at.moves)
            def _(l=l):
                moved[l].wait_send()
        for j in range(4):
            copy, away = small_copy(j)

            @pl.when(away)
            def _(copy=copy):
                copy.wait_send()
        sm_sum.finish()


def bwd(grad, saved, host):
    layers = len(saved.qkv_w)
    nz, _, rows, _ = saved.kaug.shape
    tokens, width = grad.shape
    quarter, group = width, width // 4
    quarter = saved.down_w[0].shape[0]
    r, rd = width // nz, quarter // (2 * nz)
    each = range(layers)
    out = dict(grad_in=shape(tokens, width, dtype=F32))
    scratch = {}
    if host:
        wrows, padded = width // (8 * nz), 32
        out.update(
            qkv_grad=shape(layers, wrows, 3 * width, dtype=F32), out_grad=shape(layers, wrows, width, dtype=F32),
            gu_grad=shape(layers, wrows, 8 * quarter, dtype=F32), dn_grad=shape(layers, rd, width, dtype=F32),
            gains_grad=shape(layers, 2, wrows, dtype=F32), biases_grad=shape(layers, 6, wrows, dtype=F32))
        scratch.update(
            back=[dict(out=keep(8, padded, quarter + 384), inbox=keep(8, padded, quarter + 384), send=copies(8), recv=copies(8))
                  for _ in each],
            ow_out=keep(layers, OW_ROWS, width, dtype=F32), ow_in=keep(layers, OW_ROWS, width, dtype=F32),
            ow_send=copies(layers), ow_recv=copies(layers),
            sm_out=keep(8 * layers, 128, dtype=F32), sm_in=keep(4, 8 * layers, 128, dtype=F32), sm_send=copies(4), sm_recv=copies(4))
        scratch.update(
            gu=[block_sum_item(nz, r, quarter, parts=2) for _ in each], dn=[block_sum_item(nz, rd, width, parts=2) for _ in each],
            qk=[block_sum_item(nz, r, 384, parts=2) for _ in each], ow=[block_sum_item(nz, OW_ROWS, width) for _ in each],
            sm=block_sum_item(nz, 8 * layers, 128, dtype=F32), tok_small=keep(8 * layers, width, dtype=F32))
    else:
        out.update(
            gu=[dict(stage=shape(nz, 2, r, quarter)) for _ in each], dn=[dict(stage=shape(quarter, width)) for _ in each],
            qk=[dict(stage=shape(nz, 2, r, 384)) for _ in each], ow=[dict(stage=shape(group, width)) for _ in each],
            tok_small=shape(8 * layers, width, dtype=F32))
    like = lambda arrays: keep(*arrays[0].shape, dtype=arrays[0].dtype)
    scratch.update(
        mixed_now=like(saved.mixed), yr_now=like(saved.yr), xr_now=like(saved.xr), gu_now=like(saved.gu_w),
        down_now=like(saved.down_w), qkv_now=like(saved.qkv_w), load=copies(6), kvbuf=keep(2, rows, 384), augbuf=keep(2, rows, 128), kvsem=copies(2, 2),
        df=keep(4, tokens, width), df_send=copies(6), df_recv=copies(6),
        da=keep(4, tokens, width), da_send=copies(6), da_recv=copies(6),
        part=keep(4, tokens, width, dtype=F32), **square_sum_items(tokens, width),
        g=keep(tokens, width, dtype=F32), e1=keep(tokens, width, dtype=F32), e2=keep(tokens, width, dtype=F32),
        hid=keep(rows, quarter), dgu=keep(rows, 2 * quarter), do=keep(3, rows, 128),
        dqacc=keep(3, rows, 128, dtype=F32), dproj=keep(rows, 768),
        dkv=dict(block_sum_item(nz, rows, 384, parts=2), free=pltpu.SemaphoreType.REGULAR))
    near = dict(grad=grad, small=saved.small, sum1=saved.sum1, sum2=saved.sum2, ctx=saved.ctx,
                ctxf=saved.ctxf, qb=saved.qb, out_w=saved.out_w)
    far = dict(mixed=saved.mixed, yr=saved.yr, xr=saved.xr, gu_w=saved.gu_w, down_w=saved.down_w, kv=saved.kv, kaug=saved.kaug,
               qkv_w=saved.qkv_w)
    return call(functools.partial(bwd_kernel, nz, layers, host), "backward", 1, near=near, far=far, out=out, scratch=scratch)


def shards(hidden_in, out_grad, segment_ids, alibi_slopes, qkv_weight, out_weight, gate_up_weight, down_weight, gains, biases):
    nz = lax.axis_size("z")
    nb = 2 * nz
    square, everyone, blocks = ("x", "y", "c"), ("z", "x", "y", "c"), ("z", "c")
    z, c = lax.axis_index("z"), lax.axis_index("c")
    tokens, width = hidden_in.shape
    layers, wrows = qkv_weight.shape[:2]
    ff = gate_up_weight.shape[2] // 2
    group, quarter = width // 4, ff // 4
    host = (width // nz) % 16 == 0 and down_weight.shape[1] % 16 == 0

    def to_groups(w):
        w = w.reshape(wrows, 3, 4, 3, 64)
        q, k, v = w[:, 0], w[:, 1], w[:, 2]
        kv = jnp.stack([k[:, :, 0], k[:, :, 1], v[:, :, 0], v[:, :, 1], k[:, :, 2], v[:, :, 2]], axis=2)
        return kv.reshape(wrows, 4, 384), q.reshape(wrows, 4, group)

    def from_groups(kv, q):
        kv, q = kv.reshape(4, wrows, 6, 64), q.reshape(4, wrows, 3, 64)
        k = jnp.stack([kv[:, :, 0], kv[:, :, 1], kv[:, :, 4]], axis=2)
        v = jnp.stack([kv[:, :, 2], kv[:, :, 3], kv[:, :, 5]], axis=2)
        return jnp.stack([q, k, v]).transpose(2, 0, 1, 3, 4).reshape(wrows, 3 * width)

    places = [(8 * zz + 2 * g + cc, g * nb + 2 * zz + cc) for zz in range(nz) for g in range(4) for cc in range(2)]
    gu0 = 384 * layers

    def gathered_outside():
        beside = jnp.broadcast_to(small[:, None], (wrows, 4, 192))
        nothing = jnp.zeros((wrows, 4, 192), BF)
        gu = gate_up_weight.reshape(layers, wrows, 2, nz, 4, quarter // nz).transpose(0, 1, 4, 2, 3, 5)
        gu = gu.reshape(layers, wrows, 4, 2, quarter)
        sides = [[], []]
        for l in range(layers):
            kv, q = to_groups(qkv_weight[l])
            sides[0].append(kv)
            sides[1] += [q, nothing if l else beside]
        for l in range(layers):
            for side in range(2):
                sides[side].append(gu[l, :, :, side])
        both = jnp.stack([jnp.concatenate(side, axis=2) for side in sides], axis=2).reshape(wrows, 8, -1)
        spread = lax.all_to_all(both, square, split_axis=1, concat_axis=0, tiled=True).reshape(8 * wrows, -1)
        ow_own = lax.ppermute(out_weight, everyone, [(chunk, device) for device, chunk in places])
        whole = lambda v: lax.all_gather(v, blocks, axis=0).reshape(nz, 2, *v.shape)
        flat = lambda v: lax.all_gather(v, blocks, axis=0, tiled=True)
        return types.SimpleNamespace(
            qkv_given=[whole(spread[:, 384 * l : 384 * l + 384]) for l in range(layers)],
            gu_given=[whole(spread[:, gu0 + quarter * l : gu0 + quarter * l + quarter]) for l in range(layers)],
            down_given=[flat(down_weight[l]) for l in range(layers)], out_given=[flat(ow_own[l]) for l in range(layers)])

    small = jnp.concatenate([gains, biases], axis=1).transpose(0, 2, 1)
    small = jnp.concatenate([small[l] for l in range(layers)], axis=1)
    small = jnp.pad(small, ((0, 0), (0, 192 - small.shape[1])))
    if host:
        weights = types.SimpleNamespace(
            qkv_mine=qkv_weight, gu_mine=gate_up_weight, down_mine=down_weight, small_mine=small,
            ow_mine=out_weight.reshape(layers * wrows, width))
    else:
        weights = gathered_outside()
    seg = segment_ids.reshape(8 * nz, tokens)
    saved = fwd(hidden_in, alibi_slopes, seg, weights, layers, host)
    done = bwd(out_grad, saved, host)
    if host:
        return (saved.output, done.grad_in, done.qkv_grad, done.out_grad, done.gu_grad, done.dn_grad, done.gains_grad,
                done.biases_grad)
    step = width // nb
    blocks_sum = lambda v: lax.psum_scatter(v, blocks, scatter_dimension=0, tiled=True)
    done.gu_sum = [blocks_sum(item.stage.reshape(nb, -1, quarter))[0] for item in done.gu]
    done.qk_sum = [blocks_sum(item.stage.reshape(nb, -1, 384))[0] for item in done.qk]
    done.dn_sum = [blocks_sum(item.stage) for item in done.dn]
    done.ow_sum = [blocks_sum(item.stage) for item in done.ow]
    sm = lax.psum_scatter(done.tok_small.reshape(-1, nb, step), blocks, scatter_dimension=1, tiled=True)[:, 0]
    sm = sm.T.reshape(4, wrows, 8 * layers)
    high = lax.reduce_precision(sm, 8, 7)
    sm = jnp.concatenate([high, sm - high], axis=2).astype(BF)
    sm = lax.dynamic_update_slice_in_dim(jnp.zeros((8, wrows, 16 * layers), BF), sm, 4 * c, 0)
    rows_of = lambda v: v.reshape(8, wrows, -1)
    back = jnp.concatenate([rows_of(v) for v in done.qk_sum + done.gu_sum] + [sm], axis=2)
    back = lax.all_to_all(back, square, split_axis=0, concat_axis=0, tiled=True)
    sides = back.astype(F32).reshape(4, 2, wrows, -1)
    qkv_grad = jnp.stack([from_groups(sides[:, 0, :, 384 * l : 384 * l + 384], sides[:, 1, :, 384 * l : 384 * l + group])
                          for l in range(layers)])
    gu_grad = jnp.stack([sides[:, :, :, gu0 + quarter * l : gu0 + quarter * l + quarter] for l in range(layers)])
    gu_grad = gu_grad.reshape(layers, 4, 2, wrows, nz, quarter // nz).transpose(0, 3, 2, 4, 1, 5).reshape(layers, wrows, 2 * ff)
    sm = jnp.sum(sides[..., gu0 + quarter * layers :], axis=(0, 1))
    sm = (sm[:, : 8 * layers] + sm[:, 8 * layers :]).T.reshape(layers, 8, wrows)
    out_grad_w = lax.ppermute(jnp.stack(done.ow_sum)[:, :wrows].astype(F32), everyone, places)
    return (saved.output, done.grad_in, qkv_grad, out_grad_w, gu_grad, jnp.stack(done.dn_sum).astype(F32), sm[:, 0:2],
            jnp.concatenate([sm[:, 6:8], sm[:, 2:6]], axis=1))


def solution(mesh):
    nb, nh = mesh.devices.shape
    everyone = ("z", "x", "y", "c")
    tok, mid, last = P(everyone, None), P(None, everyone, None), P(None, None, everyone)
    return jax.shard_map(
        shards, mesh=Mesh(mesh.devices.reshape(nb // 2, 2, nh // 2, 2), everyone),
        in_specs=(tok, tok, P(), P(), mid, mid, mid, mid, last, last),
        out_specs=(tok, tok, mid, mid, mid, mid, last, last),
        check_vma=False,
    )
```

```python
import functools
import types

import jax
import jax.numpy as jnp
from jax import lax
from jax.experimental import pallas as pl
from jax.experimental.pallas import tpu as pltpu
from jax.sharding import Mesh
from jax.sharding import PartitionSpec as P

MESH = pl.DeviceIdType.MESH
BF = jnp.bfloat16
F32 = jnp.float32
NT = (((1,), (1,)), ((), ()))
NN = (((1,), (0,)), ((), ()))
TN = (((0,), (0,)), ((), ()))
EPS = 1e-06
K_AT = ((0, 0), (0, 1), (2, 0))
V_AT = ((1, 0), (1, 1), (2, 1))
ROW_LANE, SEGMENT_LANE = 9, 12
OW_ROWS = 32
VMEM = pl.BlockSpec(memory_space=pltpu.VMEM)
ANY = pl.BlockSpec(memory_space=pl.ANY)


def dot(a, b, dims=NN):
    return lax.dot_general(a, b, dims, preferred_element_type=F32)


def lanes(rows):
    return lax.broadcasted_iota(jnp.int32, (rows, 128), 1)


def in_half(half, rows):
    return lanes(rows) >= 64 if half else lanes(rows) < 64


def ones_half(half, rows):
    first = 0 if half else 64
    lane = lanes(rows)
    return jnp.where((lane >= first) & (lane < first + 3), 1.0, 0.0).astype(BF)


def k_operand(kv, aug, h):
    col, half = K_AT[h]
    return jnp.where(in_half(half, kv.shape[0]), kv[:, 128 * col : 128 * col + 128], aug)


def v_operand(kv, h):
    col, half = V_AT[h]
    rows = kv.shape[0]
    return jnp.where(in_half(half, rows), kv[:, 128 * col : 128 * col + 128], ones_half(half, rows))


def split3(value):
    high = value.astype(BF).astype(F32)
    mid = (value - high).astype(BF).astype(F32)
    return high, mid, value - high - mid


def with_lanes(base, first, values):
    lane = lanes(base.shape[0])
    for i, v in enumerate(values):
        base = jnp.where(lane == first + i, v, base)
    return base


def layer_norm(total, gain, shift):
    centred = total - jnp.mean(total, axis=-1, keepdims=True)
    scale = lax.rsqrt(jnp.mean(centred * centred, axis=-1, keepdims=True) + EPS)
    return centred * scale * gain + shift


def norm_back(grad, total, gain):
    centred = total - jnp.mean(total, axis=-1, keepdims=True)
    scale = lax.rsqrt(jnp.mean(centred * centred, axis=-1, keepdims=True) + EPS)
    n = centred * scale
    dn = grad * gain
    e = scale * (dn - jnp.mean(dn, axis=-1, keepdims=True) - n * jnp.mean(dn * n, axis=-1, keepdims=True))
    return e, jnp.sum(grad * n, axis=0, keepdims=True), jnp.sum(grad, axis=0, keepdims=True)


def normal_cdf(u):
    return 0.5 * (1.0 + lax.erf(u * (0.5**0.5)))


def normal_pdf(u):
    return jnp.exp(-0.5 * u * u) * ((2.0 * jnp.pi) ** -0.5)


def remote(src, dst, send, recv, device):
    return pltpu.make_async_remote_copy(
        src_ref=src, dst_ref=dst, send_sem=send, recv_sem=recv, device_id=device, device_id_type=MESH)


def loop(first, last, do):
    def step(i, carry):
        do(i)
        return carry
    lax.fori_loop(first, last, step, 0)


class Place:
    def __init__(self, nz):
        self.nz = nz
        self.z, self.x, self.y, self.c = [lax.axis_index(name) for name in "zxyc"]
        self.g = 2 * self.x + self.y
        self.gx, self.gy = 2 * (1 - self.x) + self.y, 2 * self.x + 1 - self.y
        self.gd = 2 * (1 - self.x) + 1 - self.y
        self.oc = 1 - self.c
        self.beside = (self.z, self.x, self.y, self.oc)
        self.across_x = (self.z, 1 - self.x, self.y, self.c)
        self.across_y = (self.z, self.x, 1 - self.y, self.c)
        self.block = 2 * self.z + self.c
        self.member = 2 * self.g + self.c
        self.number = 8 * self.z + self.member
        nb = 2 * nz
        self.chunk = self.g * nb + self.block
        self.chunk_device = self.device(self.chunk)
        place = self.number % nb
        self.holder = (place // 2, self.number // nb // 2, self.number // nb % 2, place % 2)
        self.moves = self.chunk != self.number
        self.has_left, self.has_right = self.z > 0, self.z < nz - 1

    def column(self, zz):
        return (zz, self.x, self.y, self.c)

    def device(self, number):
        k = number % 8
        return (number // 8, k // 4, k // 2 % 2, k % 2)

    def of_plane(self, k):
        return (self.z, k // 4, k // 2 % 2, k % 2)

    def neighbours(self):
        return 3 - (self.z == 0).astype(jnp.int32) - (self.z == self.nz - 1).astype(jnp.int32)

    def signal_neighbours(self, semaphore):
        pl.semaphore_signal(semaphore, inc=1, device_id=self.beside, device_id_type=MESH)

        @pl.when(self.has_left)
        def _():
            pl.semaphore_signal(semaphore, inc=1, device_id=self.column(self.z - 1), device_id_type=MESH)

        @pl.when(self.has_right)
        def _():
            pl.semaphore_signal(semaphore, inc=1, device_id=self.column(self.z + 1), device_id_type=MESH)

    def enter(self, plane):
        barrier = pltpu.get_barrier_semaphore()

        def greet(device):
            pl.semaphore_signal(barrier, inc=1, device_id=device, device_id_type=MESH)

        if not plane:
            greet(self.across_x)
            greet(self.across_y)
            self.signal_neighbours(barrier)
            return lambda: pl.semaphore_wait(barrier, 2 + self.neighbours())
        loop(1, 8, lambda j: greet(self.of_plane((self.member + j) % 8)))
        self.signal_neighbours(barrier)

        @pl.when(self.moves)
        def _():
            greet(self.chunk_device)
            greet(self.holder)
        return lambda: pl.semaphore_wait(barrier, 7 + self.neighbours() + 2 * self.moves.astype(jnp.int32))

    def positions(self, zz, cc, tokens, rows):
        row = lax.broadcasted_iota(jnp.int32, (rows, 128), 0)
        return ((zz * 8 + (row // tokens) * 2 + cc) * tokens + row % tokens).astype(F32)


class SquareGather:
    def __init__(self, at, buf, send, recv):
        half = buf.shape[1] // 2
        first, second = pl.ds(0, half), pl.ds(half, half)

        def copy(i, g, rows, device):
            return remote(buf.at[g, rows], buf.at[g, rows], send.at[i], recv.at[i], device)
        self.x_first, self.x_second = copy(0, at.g, first, at.across_x), copy(1, at.g, second, at.across_x)
        self.y_second, self.y_first = copy(2, at.g, second, at.across_y), copy(3, at.g, first, at.across_y)
        self.on_y = copy(4, at.gx, first, at.across_y)
        self.on_x = copy(5, at.gy, second, at.across_x)

    def start(self):
        for copy in (self.x_first, self.y_second, self.x_second, self.y_first):
            copy.start()

    def wait_near(self):
        self.x_first.wait_recv()
        self.on_y.start()
        self.y_second.wait_recv()
        self.on_x.start()
        self.y_first.wait_recv()

    def wait_far(self):
        self.x_second.wait_recv()
        self.on_x.wait_recv()
        self.on_y.wait_recv()

    def finish(self):
        for copy in (self.x_first, self.x_second, self.y_first, self.y_second, self.on_x, self.on_y):
            copy.wait_send()


class SquareSum:
    def __init__(self, at, part, stage, inbox, send, recv):
        self.at, self.part, self.stage, self.inbox = at, part, stage, inbox
        self.half = part.shape[2] // 2
        to = (at.across_x, at.across_x, at.across_y, at.across_y, at.across_y, at.across_x)
        self.copies = [remote(stage.at[i], inbox.at[i], send.at[i], recv.at[i], to[i]) for i in range(6)]

    def left(self, g):
        return self.part[g, :, : self.half]

    def right(self, g):
        return self.part[g, :, self.half :]

    def post(self, i, value):
        self.stage[i] = value.astype(BF)
        self.copies[i].start()

    def came(self, i):
        self.copies[i].wait_recv()
        return self.inbox[i].astype(F32)

    def send_far(self):
        self.post(0, self.left(self.at.gd))
        self.post(2, self.right(self.at.gd))
        self.post(1, self.left(self.at.gx))

    def send_near(self):
        self.post(3, self.right(self.at.gy))

    def relay(self):
        self.post(4, self.left(self.at.gy) + self.came(0))
        self.post(5, self.right(self.at.gx) + self.came(2))

    def total(self):
        left = self.left(self.at.g) + self.came(1)
        right = self.right(self.at.g) + self.came(3)
        return jnp.concatenate([left + self.came(4), right + self.came(5)], axis=1)

    def finish(self):
        for copy in self.copies:
            copy.wait_send()


class BlockGather:
    def __init__(self, at, item):
        self.at, self.buf, self.zsend, self.csend, self.recv = at, item.buf, item.zsend, item.csend, item.recv
        self.parts = self.recv.shape[2]
        self.step = self.buf.shape[2] // self.parts

    def copy(self, zz, cc, part, send, device):
        block = self.buf.at[zz, cc, pl.ds(part * self.step, self.step)]
        return remote(block, block, send, self.recv.at[zz, cc, part], device)

    def to_right(self, zz, part):
        return self.copy(zz, self.at.c, part, self.zsend.at[0, zz, part], self.at.column(self.at.z + 1))

    def to_left(self, zz, part):
        return self.copy(zz, self.at.c, part, self.zsend.at[1, zz, part], self.at.column(self.at.z - 1))

    def to_beside(self, zz, part):
        return self.copy(zz, self.at.c, part, self.csend.at[zz, part], self.at.beside)

    def wait_part(self, zz, cc, part):
        self.copy(zz, cc, part, self.csend.at[zz, part], self.at.beside).wait_recv()

    def wait(self, zz, cc):
        for part in range(self.parts):
            self.wait_part(zz, cc, part)

    def put(self, value):
        self.buf[self.at.z, self.at.c] = value

    def start(self):
        at = self.at
        for part in range(self.parts):
            @pl.when(at.has_right)
            def _(part=part):
                self.to_right(at.z, part).start()

            @pl.when(at.has_left)
            def _(part=part):
                self.to_left(at.z, part).start()
            self.to_beside(at.z, part).start()

    def serve(self, d):
        at = self.at
        for part in range(self.parts):
            @pl.when(at.z - d >= 0)
            def _(part=part):
                self.wait_part(at.z - d, at.c, part)

                @pl.when(at.has_right)
                def _():
                    self.to_right(at.z - d, part).start()
                self.to_beside(at.z - d, part).start()

            @pl.when(at.z + d < at.nz)
            def _(part=part):
                self.wait_part(at.z + d, at.c, part)

                @pl.when(at.has_left)
                def _():
                    self.to_left(at.z + d, part).start()
                self.to_beside(at.z + d, part).start()

    def serve_all(self):
        loop(1, self.at.nz, self.serve)

    def collect(self):
        loop(0, self.at.nz, lambda zz: self.wait(zz, self.at.oc))

    def finish(self):
        at = self.at

        def drain(zz):
            for part in range(self.parts):
                self.to_beside(zz, part).wait_send()

                @pl.when((zz <= at.z) & at.has_right)
                def _(part=part):
                    self.to_right(zz, part).wait_send()

                @pl.when((zz >= at.z) & at.has_left)
                def _(part=part):
                    self.to_left(zz, part).wait_send()
        loop(0, at.nz, drain)


def block_gather_item(nz, *dims, parts=1):
    return dict(buf=keep(nz, 2, *dims), zsend=copies(2, nz, parts), csend=copies(nz, parts), recv=copies(nz, 2, parts))


class BlockSum:
    def __init__(self, at, item):
        self.at, self.stage, self.cin, self.zin = at, item.stage, item.cin, item.zin
        self.csend, self.crecv, self.zsend, self.zrecv = item.csend, item.crecv, item.zsend, item.zrecv
        self.parts = self.zsend.shape[1]
        self.step = self.stage.shape[2] // self.parts

    def rows(self, part):
        return pl.ds(part * self.step, self.step)

    def to_beside(self, t):
        return remote(self.stage.at[t, self.at.oc], self.cin.at[t], self.csend.at[t], self.crecv.at[t], self.at.beside)

    def along(self, t, slot, part, device):
        rows = self.rows(part)
        return remote(self.stage.at[t, self.at.c, rows], self.zin.at[slot, rows], self.zsend.at[t, part],
                      self.zrecv.at[slot, part], device)

    def to_right(self, t, part):
        return self.along(t, t + 1, part, self.at.column(self.at.z + 1))

    def to_left(self, t, part):
        return self.along(t, t, part, self.at.column(self.at.z - 1))

    def arrived(self, slot, part):
        block = self.zin.at[slot, self.rows(part)]
        remote(block, block, self.zsend.at[0, part], self.zrecv.at[slot, part], self.at.beside).wait_recv()

    def start(self):
        loop(0, self.at.nz, lambda t: self.to_beside(t).start())

    def add(self, t, part, slot=None):
        rows = self.rows(part)
        value = self.stage[t, self.at.c, rows].astype(F32) + self.cin[t, rows].astype(F32)
        if slot is not None:
            value = value + self.zin[slot, rows].astype(F32)
        self.stage[t, self.at.c, rows] = value.astype(self.stage.dtype)

    def go(self, t, slot, passed_on, send):
        self.to_beside(t).wait_recv()
        for part in range(self.parts):
            @pl.when(passed_on)
            def _(part=part):
                self.arrived(slot, part)
                self.add(t, part, slot)

            @pl.when(jnp.logical_not(passed_on))
            def _(part=part):
                self.add(t, part)
            send(t, part).start()

    def serve(self, p, source=True, relay=True):
        at = self.at
        right, left = p - at.z, p - (at.nz - 1 - at.z)
        go_r = (right >= 0) & (right < at.nz - 1 - at.z)
        go_l = (left >= 0) & (left < at.z)
        if not source:
            go_r, go_l = go_r & at.has_left, go_l & at.has_right
        if not relay:
            go_r, go_l = go_r & jnp.logical_not(at.has_left), go_l & jnp.logical_not(at.has_right)

        @pl.when(go_r)
        def _():
            self.go(at.nz - 1 - right, at.nz - right, at.has_left, self.to_right)

        @pl.when(go_l)
        def _():
            self.go(left, left, at.has_right, self.to_left)

    def total(self):
        at = self.at
        self.to_beside(at.z).wait_recv()
        for part in range(self.parts):
            @pl.when(at.has_left)
            def _(part=part):
                self.arrived(at.z + 1, part)

            @pl.when(at.has_right)
            def _(part=part):
                self.arrived(at.z, part)
        value = self.stage[at.z, at.c].astype(F32) + self.cin[at.z].astype(F32)
        from_left = jnp.where(at.has_left, self.zin[at.z + 1].astype(F32), 0.0)
        from_right = jnp.where(at.has_right, self.zin[at.z].astype(F32), 0.0)
        return value + from_left + from_right

    def finish(self):
        at = self.at

        def drain(t):
            self.to_beside(t).wait_send()
            for part in range(self.parts):
                @pl.when(t > at.z)
                def _(part=part):
                    self.to_right(t, part).wait_send()

                @pl.when(t < at.z)
                def _(part=part):
                    self.to_left(t, part).wait_send()
        loop(0, at.nz, drain)


class PlaneExchange:
    def __init__(self, at, out, inbox, send, recv, columns=None):
        self.at, self.out, self.inbox, self.send, self.recv, self.columns = at, out, inbox, send, recv, columns

    def source(self, k):
        return self.out.at[k] if self.columns is None else self.out.at[k, :, self.columns]

    def start(self):
        at = self.at

        def step(j):
            k = (at.member + j) % 8
            remote(self.source(k), self.inbox.at[at.member], self.send.at[k], self.recv.at[at.member], at.of_plane(k)).start()
        loop(1, 8, step)
        self.inbox[at.member] = self.source(at.member)[...]

    def each(self, do):
        at = self.at

        def step(j):
            k = (at.member + j) % 8
            do(remote(self.source(k), self.inbox.at[k], self.send.at[k], self.recv.at[k], at.of_plane(k)))
        loop(1, 8, step)

    def wait(self):
        self.each(lambda copy: copy.wait_recv())

    def finish(self):
        self.each(lambda copy: copy.wait_send())

    def rows(self, count):
        return jnp.concatenate([self.inbox[k].astype(F32)[0:count] for k in range(8)], axis=0)


def box(tree):
    if isinstance(tree, dict):
        return types.SimpleNamespace(**{k: box(v) for k, v in tree.items()})
    return [box(v) for v in tree] if isinstance(tree, list) else tree


def call(body, name, collective_id, near=None, far=None, table=None, out=None, far_out=None, scratch=None):
    groups = [near or {}, far or {}, table or {}, out or {}, far_out or {}, scratch or {}]
    flat, trees = zip(*[jax.tree.flatten(g) for g in groups])
    counts = [len(f) for f in flat]

    def kernel(*refs):
        named, first = {}, 0
        for tree, count in zip(trees, counts):
            named.update(jax.tree.unflatten(tree, refs[first : first + count]))
            first += count
        body(box(named))

    smem = pl.BlockSpec(memory_space=pltpu.SMEM)
    results = pl.pallas_call(
        kernel,
        out_shape=tuple(flat[3]) + tuple(flat[4]),
        in_specs=[VMEM] * counts[0] + [ANY] * counts[1] + [smem] * counts[2],
        out_specs=(VMEM,) * counts[3] + (ANY,) * counts[4],
        scratch_shapes=list(flat[5]),
        compiler_params=pltpu.CompilerParams(
            collective_id=collective_id, has_side_effects=True, vmem_limit_bytes=63 * 2**20),
        cost_estimate=pl.CostEstimate(flops=10**11, bytes_accessed=2 * 10**8, transcendentals=10**7),
        name=name,
    )(*flat[0], *flat[1], *flat[2])
    done = jax.tree.unflatten(trees[3], results[: counts[3]])
    done.update(jax.tree.unflatten(trees[4], results[counts[3] :]))
    return box(done)


def shape(*dims, dtype=BF):
    return jax.ShapeDtypeStruct(dims, dtype)


def keep(*dims, dtype=BF):
    return pltpu.VMEM(dims, dtype)


def copies(*dims):
    return pltpu.SemaphoreType.DMA(dims)


def square_sum_items(tokens, width):
    half = width // 2
    return dict(ss_stage=keep(6, tokens, half), ss_inbox=keep(6, tokens, half), ss_send=copies(6), ss_recv=copies(6))


def flat_weight(ref, lo=0, hi=None):
    if len(ref.shape) == 2:
        return ref[:, lo:hi]
    v = ref[:, :, :, lo:hi]
    return v.reshape(v.shape[0] * v.shape[1] * v.shape[2], v.shape[3])


def side_weight(ref, cc, lo=0, hi=None):
    v = ref[:, cc, :, lo:hi]
    return v.reshape(v.shape[0] * v.shape[1], v.shape[2])


def block_sum_item(nz, *dims, dtype=BF, parts=1):
    return dict(stage=keep(nz, 2, *dims, dtype=dtype), cin=keep(nz, *dims, dtype=dtype), zin=keep(nz + 1, *dims, dtype=dtype),
                csend=copies(nz), crecv=copies(nz), zsend=copies(nz, parts), zrecv=copies(nz + 1, parts))


def segment_row(seg, zz, cc):
    return jnp.concatenate([seg[pl.ds(zz * 8 + 2 * k + cc, 1), :] for k in range(4)], axis=1)


def key_columns(at, slopes, seg, zz, cc, tokens):
    rows = 4 * tokens
    column = lax.broadcasted_iota(jnp.int32, (128, rows), 0) % 64
    row = lax.broadcasted_iota(jnp.int32, (128, rows), 1)
    position = ((zz * 8 + (row // tokens) * 2 + cc) * tokens + row % tokens).astype(F32)
    value = jnp.where(segment_row(seg, zz, cc) == column - SEGMENT_LANE, 0.0, -1e30)
    value = jnp.where(column < SEGMENT_LANE + 5, value, 0.0)
    value = jnp.where(column < SEGMENT_LANE, 1.0, value)
    for h in range(3):
        for i, term in enumerate(split3(position * slopes[3 * at.g + h])):
            value = jnp.where(column == 3 * h + i, term, value)
    return value.T.astype(BF)


def segment_columns(at, seg, rows):
    column = lax.broadcasted_iota(jnp.int32, (128, rows), 0) % 64
    return jnp.where(segment_row(seg, at.z, at.c) == column - SEGMENT_LANE, 1.0, 0.0).T


def query_operand(at, q_ref, inside, slopes, side, h, tokens, lse=None):
    rows = 4 * tokens
    if h < 2:
        data = q_ref[:, 0:128]
    else:
        data = jnp.concatenate([q_ref[:, 128:192], jnp.zeros((rows, 64), q_ref.dtype)], axis=1)
    half = K_AT[h][1]
    sign = 1.0 if side == 0 else -1.0
    column = lanes(rows) % 64
    aug = jnp.where((column >= 3 * h) & (column < 3 * h + 3), sign, inside[...])
    term = at.positions(at.z, at.c, tokens, rows) * (slopes[3 * at.g + h] * -sign)
    if lse is not None:
        term = term - lse
    aug = with_lanes(aug, ROW_LANE if half else 64 + ROW_LANE, split3(term))
    return jnp.where(in_half(half, rows), data.astype(F32) * 0.125, aug).astype(BF)


def attention(at, gather, q_op, kaug, m_ref, acc_ref, behind):
    m_ref[...] = jnp.full(m_ref.shape, -1e30, F32)
    acc_ref[...] = jnp.zeros(acc_ref.shape, F32)

    def compute(zz, cc, same):
        kv, aug = gather.buf.at[zz, cc], kaug[zz, cc]
        side = (zz > at.z).astype(jnp.int32)
        for h in range(3):
            k = k_operand(kv, aug, h)
            if same:
                s = jnp.minimum(dot(q_op[0, h], k, NT), dot(q_op[1, h], k, NT))
            else:
                s = dot(q_op[side, h], k, NT)
            m_old = m_ref[h]
            m_new = jnp.maximum(m_old, jnp.max(s, axis=1, keepdims=True))
            p = jnp.exp(s - m_new[:, :1]).astype(BF)
            acc_ref[h] = acc_ref[h] * jnp.exp(m_old - m_new) + dot(p, v_operand(kv, h))
            m_ref[h] = m_new

    def here(i):
        cc = jnp.where(i == 0, at.c, at.oc)

        @pl.when(i == 1)
        def _():
            gather.wait(at.z, at.oc)
        compute(at.z, cc, True)
    loop(0, 2, here)

    def both(d):
        return (at.z - d >= 0) & (at.z + d < at.nz)

    def step(d):
        @pl.when(jnp.logical_not(both(d - 1)) | (d == 1))
        def _():
            gather.serve(d)
        behind(d)

        def visit(i):
            zz = jnp.where(i % 2 == 0, at.z - d, at.z + d)

            @pl.when((zz >= 0) & (zz < at.nz))
            def _():
                @pl.when(i >= 2)
                def _():
                    gather.wait(zz, at.oc)
                compute(zz, jnp.where(i < 2, at.c, at.oc), False)

            @pl.when((i == 1) & both(d) & (d + 1 < at.nz))
            def _():
                gather.serve(d + 1)
        loop(0, 4, visit)
    loop(1, at.nz, step)


def attention_end(m_ref, acc_ref, ctx_ref, ctxf_ref):
    for h in range(3):
        half = V_AT[h][1]
        first = 0 if half else 64
        acc = acc_ref[h]
        total = acc[:, first : first + 1]
        ctx = acc[:, 64 * half : 64 * half + 64] / total
        ctxf_ref[:, 64 * h : 64 * h + 64] = ctx
        ctx_ref[:, 64 * h : 64 * h + 64] = ctx.astype(BF)
        m_ref[h] = m_ref[h] + jnp.log(total)


def fwd_kernel(nz, layers, host, R):
    at = Place(nz)
    tokens = R.x0.shape[0]
    rows, half_rows = 4 * tokens, 2 * tokens
    quarter = R.hid.shape[1]
    group = R.ctx_now[0].shape[1]
    arrived = at.enter(host)
    part = R.part
    square_sum = SquareSum(at, part, R.ss_stage, R.ss_inbox, R.ss_send, R.ss_recv)
    gather_x = [SquareGather(at, R.xr_now[l], R.x_send.at[l], R.x_recv.at[l]) for l in range(layers)]
    gather_y = [SquareGather(at, R.yr_now[l], R.y_send.at[l], R.y_recv.at[l]) for l in range(layers)]
    kv = BlockGather(at, R.kv_now)
    saves, waited = [], []

    def save(source, target):
        saves.append(pltpu.make_async_copy(source, target, R.saved.at[len(saves)]))
        saves[-1].start()
        return len(saves) - 1

    def wait_saved(number):
        saves[number].wait()
        waited.append(number)

    if host:
        qkv, gu, down = [[BlockGather(at, item) for item in items] for items in (R.qkv_now, R.gu_now, R.down_now)]
        ow = BlockGather(at, R.ow_now)
        qkv_w, gu_w, down_w, out_w = [g.buf for g in qkv], [g.buf for g in gu], [g.buf for g in down], R.out_now
        wrows = R.ow_now.buf.shape[2] // layers
        lists = [qkv[l] for l in range(layers)] + [gu[l] for l in range(layers)]
        columns, first = [], 0
        for item in lists:
            columns.append(pl.ds(first, item.buf.shape[3]))
            first += item.buf.shape[3]
        spread = [PlaneExchange(at, R.spread, R.spread_in[i], R.spread_send.at[i], R.spread_recv.at[i], columns[i])
                  for i in range(len(lists))]

        def arrive(i):
            spread[i].wait()
            lists[i].put(spread[i].rows(wrows).astype(BF))

        def regroup():
            join = lambda *parts: jnp.concatenate(parts, axis=1)
            part_width = quarter // nz
            for l in range(layers):
                w = R.qkv_mine[l].astype(F32)
                for g in range(4):
                    q, k, v = [w[:, part * 4 * group + group * g : part * 4 * group + group * g + group] for part in range(3)]
                    beside = jnp.zeros(q.shape, F32) if l else R.small_mine[...].astype(F32)
                    at_l = 384 * l
                    R.spread[2 * g, 0:wrows, at_l : at_l + 384] = join(k[:, :128], v[:, :128], k[:, 128:], v[:, 128:]).astype(BF)
                    R.spread[2 * g + 1, 0:wrows, at_l : at_l + 384] = join(q, beside).astype(BF)
            for l in range(layers):
                w = R.gu_mine[l].astype(F32)
                lo = 384 * layers + quarter * l
                for g in range(4):
                    for side in range(2):
                        firsts = [((side * nz + zz) * 4 + g) * part_width for zz in range(nz)]
                        R.spread[2 * g + side, 0:wrows, lo : lo + quarter] = join(*[w[:, i : i + part_width] for i in firsts]).astype(BF)

        regroup()
        for l in range(layers):
            down[l].put(R.down_mine[l])
        arrived()
        down[0].start()
        to_holder = remote(R.ow_mine, R.ow_in, R.ow_send, R.ow_recv, at.holder)
        spread[0].start()
    else:
        arrived()
        qkv_w, gu_w, down_w, out_w = R.qkv_given, R.gu_given, R.down_given, R.out_given

    R.xr_now[0][at.g] = R.x0[...]
    gather_x[0].start()
    if host:
        spread[layers].start()

        @pl.when(at.moves)
        def _():
            to_holder.start()

        @pl.when(jnp.logical_not(at.moves))
        def _():
            R.ow_in[...] = R.ow_mine[...]
        arrive(0)
        qkv[0].start()

        @pl.when(at.moves)
        def _():
            to_holder.wait_recv()
        ow.put(R.ow_in[...])
        ow.start()

    def columns(b):
        R.kaug_now[b // 2, b % 2] = key_columns(at, R.slopes, R.seg, b // 2, b % 2, tokens)

    def columns_and_serve(zz):
        columns(2 * zz)
        columns(2 * zz + 1)
        if host:
            @pl.when(zz > 0)
            def _():
                qkv[0].serve(zz)
    loop(0, nz, columns_and_serve)
    save(R.kaug_now, R.kaug)
    R.inside[...] = segment_columns(at, R.seg, rows)

    def small(l, t):
        return R.small[8 * l + t : 8 * l + t + 1, :]

    def of(buf, half):
        v = buf[pl.ds(2 * half, 2)]
        return v.reshape(half_rows, v.shape[2])

    def half_at(half):
        return pl.ds(pl.multiple_of(half * half_rows, half_rows), half_rows)

    def put_part(half, value):
        part[pl.ds(2 * half, 2)] = value.reshape(2, tokens, value.shape[1])

    def of_group(row):
        value = jnp.zeros((1, group), F32)
        for g in range(4):
            value = jnp.where(at.g == g, row[:, group * g : group * g + group], value)
        return value

    if host:
        qkv[0].collect()
    R.small[...] = side_weight(qkv_w[0], 1, 128, 256).astype(F32).T[64 : 64 + 8 * layers, :]
    R.state[...] = R.x0[...].astype(F32)
    gather_x[0].wait_near()
    gather_x[0].wait_far()

    for l in range(layers):
        last = l == layers - 1
        x_all = R.xr_now[l][...].reshape(rows, -1)
        save(R.xr_now[l], R.xr[l])
        qb, vb = of_group(small(l, 2)), of_group(small(l, 3))
        none = jnp.zeros((1, 128), F32)
        kv_bias = jnp.concatenate([none, vb[:, :128], none[:, :64], vb[:, 128:192]], axis=1)
        if l:
            pl.semaphore_wait(R.kv_free, at.neighbours())
        kv.put((dot(x_all, side_weight(qkv_w[l], 0)) + kv_bias).astype(BF))
        kv.start()
        if host and not last:
            spread[l + 1].start()
            spread[layers + l + 1].start()
        R.q[...] = (dot(x_all, side_weight(qkv_w[l], 1, 0, group)) + qb).astype(BF)
        for side in range(2):
            for h in range(3):
                R.q_op[side, h] = query_operand(at, R.q, R.inside, R.slopes, side, h, tokens)

        def behind(d, l=l):
            if host:
                if l == 0:
                    ow.serve(d)

                @pl.when(d == min(2, nz - 1))
                def _():
                    arrive(layers + l)
                    gu[l].start()

        def later(p, l=l):
            if host:
                for step in range(p, nz if p == 3 else p + 1):
                    gu[l].serve(step)
                    if l == 0:
                        down[l].serve(step)

        def ahead(p, l=l):
            if host and l < layers - 1:
                if p == 0:
                    arrive(l + 1)
                    qkv[l + 1].start()
                    down[l + 1].start()
                for step in range(p, nz if p == 3 else p + 1):
                    if step:
                        qkv[l + 1].serve(step)
                        down[l + 1].serve(step)
        attention(at, kv, R.q_op, R.kaug_now, R.m, R.acc, behind)
        attention_end(R.m, R.acc, R.ctx_now[l], R.ctxf_now[l])
        kv_saved = save(kv.buf, R.kv[l])
        save(R.ctx_now[l], R.ctx[l])
        save(R.ctxf_now[l], R.ctxf[l])
        if l == 0 and host:
            ow.collect()
            step = group // (2 * nz)
            for i in range(layers):
                for b in range(2 * nz):
                    R.ow_wide[...] = ow.buf[b // 2, b % 2].astype(F32)
                    R.ow_flat[step * b : step * b + step, :] = R.ow_wide[step * i : step * i + step, :]
                R.out_now[i][...] = R.ow_flat[...].astype(BF)
                save(R.out_now[i], R.out_w[i])
        if l:
            square_sum.finish()
        for number, half in enumerate((1 - at.x, at.x)):
            put_part(half, dot(R.ctx_now[l][half_at(half), :], out_w[l][...]))
            if number == 0:
                square_sum.send_far()
            else:
                square_sum.send_near()
        later(1)
        square_sum.relay()
        kv.finish()
        for side in range(2):
            for h in range(3):
                R.qb_now[l][side, h] = query_operand(at, R.q, R.inside, R.slopes, side, h, tokens, R.m[h])
        save(R.qb_now[l], R.qb[l])
        later(2)
        wait_saved(kv_saved)
        if not last:
            at.signal_neighbours(R.kv_free)
        R.sum1_now[l][...] = R.state[...] + (square_sum.total() + small(l, 4))
        save(R.sum1_now[l], R.sum1[l])
        y = layer_norm(R.sum1_now[l][...], small(l, 0), small(l, 5))
        R.yr_now[l][at.g] = y.astype(BF)
        gather_y[l].start()
        R.state[...] = y
        later(3)
        ahead(0)
        if host:
            gu[l].collect()
            down[l].collect()
        gather_y[l].wait_near()
        if l:
            wait_saved(mixed_saved)
        square_sum.finish()
        for number, half in enumerate((at.x, 1 - at.x)):
            if number == 1:
                gather_y[l].wait_far()
                ahead(1)
            here = half_at(half)
            y_half = of(R.yr_now[l], half)
            for col in range(0, quarter, 256):
                gate = dot(y_half, side_weight(gu_w[l], 0, col, col + 256))
                up = dot(y_half, side_weight(gu_w[l], 1, col, col + 256))
                R.mixed_now[here, col : col + 256] = gate
                R.mixed_now[here, quarter + col : quarter + col + 256] = up
                R.hid[:, col : col + 256] = (gate * normal_cdf(gate) * up).astype(BF)
            put_part(half, dot(R.hid[...], flat_weight(down_w[l])))
            if number == 0:
                square_sum.send_near()
            else:
                square_sum.send_far()
        mixed_saved = save(R.mixed_now, R.mixed[l])
        save(R.yr_now[l], R.yr[l])
        if host:
            save(qkv[l].buf, R.qkv_w[l])
            save(gu[l].buf, R.gu_w[l])
            save(down[l].buf, R.down_w[l])
        square_sum.relay()
        ahead(2)
        R.sum2_now[l][...] = R.state[...] + (square_sum.total() + small(l, 6))
        save(R.sum2_now[l], R.sum2[l])
        state = layer_norm(R.sum2_now[l][...], small(l, 1), small(l, 7))
        R.state[...] = state
        if last:
            R.output[...] = state.astype(BF)
        else:
            R.xr_now[l + 1][at.g] = state.astype(BF)
            gather_x[l + 1].start()
            ahead(3)
            gather_x[l + 1].wait_near()
            gather_x[l + 1].wait_far()
            if host:
                qkv[l + 1].collect()
    for l in range(layers):
        gather_x[l].finish()
        gather_y[l].finish()
    square_sum.finish()
    if host:
        for items in (qkv, gu, down):
            for item in items:
                item.finish()
        ow.finish()
        for item in spread:
            item.finish()

        @pl.when(at.moves)
        def _():
            to_holder.wait_send()
    for number, copy in enumerate(saves):
        if number not in waited:
            copy.wait()


def fwd(x0, slopes, seg, weights, layers, host):
    nz = seg.shape[0] // 8
    tokens, width = x0.shape
    rows = 4 * tokens
    group = width // 4
    each = range(layers)
    quarter = weights.gu_mine.shape[2] // 8 if host else weights.gu_given[0].shape[3]
    r = width // nz
    keep_rows = lambda: [keep(4, tokens, width) for _ in each]
    keep_wide = lambda: [keep(tokens, width, dtype=F32) for _ in each]
    scratch = dict(
        xr_now=keep_rows(), x_send=copies(layers, 6), x_recv=copies(layers, 6),
        yr_now=keep_rows(), y_send=copies(layers, 6), y_recv=copies(layers, 6),
        part=keep(4, tokens, width, dtype=F32), state=keep(tokens, width, dtype=F32), **square_sum_items(tokens, width),
        kv_now=block_gather_item(nz, rows, 384, parts=2), kv_free=pltpu.SemaphoreType.REGULAR, saved=copies(16 * layers),
        kaug_now=keep(nz, 2, rows, 128), inside=keep(rows, 128, dtype=F32),
        q=keep(rows, group), q_op=keep(2, 3, rows, 128),
        m=keep(3, rows, 128, dtype=F32), acc=keep(3, rows, 128, dtype=F32),
        ctx_now=[keep(rows, group) for _ in each], ctxf_now=[keep(rows, group, dtype=F32) for _ in each],
        qb_now=[keep(2, 3, rows, 128) for _ in each], sum1_now=keep_wide(), sum2_now=keep_wide(),
        mixed_now=keep(rows, 2 * quarter, dtype=F32), hid=keep(2 * tokens, quarter))
    far_out = dict(
        xr=[shape(4, tokens, width) for _ in each], yr=[shape(4, tokens, width) for _ in each],
        kv=[shape(nz, 2, rows, 384) for _ in each], ctx=[shape(rows, group) for _ in each],
        ctxf=[shape(rows, group, dtype=F32) for _ in each], qb=[shape(2, 3, rows, 128) for _ in each],
        sum1=[shape(tokens, width, dtype=F32) for _ in each], sum2=[shape(tokens, width, dtype=F32) for _ in each],
        mixed=[shape(rows, 2 * quarter, dtype=F32) for _ in each], kaug=shape(nz, 2, rows, 128))
    near = dict(x0=x0, seg=seg, **vars(weights))
    if host:
        gathered = lambda *dims: [shape(nz, 2, *dims) for _ in each]
        items = lambda *dims: [block_gather_item(nz, *dims, parts=2) for _ in each]
        rd = weights.down_mine.shape[1]
        padded = 32
        far_out.update(qkv_w=gathered(r, 384), gu_w=gathered(r, quarter), down_w=gathered(rd, width),
                       out_w=[shape(group, width) for _ in each])
        scratch.update(
            qkv_now=items(r, 384), gu_now=items(r, quarter), down_now=items(rd, width),
            spread=keep(8, padded, layers * (384 + quarter)), spread_in=[keep(8, padded, 384) for _ in each] + [keep(8, padded, quarter) for _ in each],
            spread_send=copies(2 * layers, 8), spread_recv=copies(2 * layers, 8),
            ow_in=keep(*weights.ow_mine.shape), ow_send=pltpu.SemaphoreType.DMA, ow_recv=pltpu.SemaphoreType.DMA,
            ow_now=block_gather_item(nz, *weights.ow_mine.shape), out_now=[keep(group, width) for _ in each],
            ow_wide=keep(*weights.ow_mine.shape, dtype=F32), ow_flat=keep(group, width, dtype=F32))
    out = dict(output=shape(tokens, width), small=shape(8 * layers, width, dtype=F32))
    done = call(functools.partial(fwd_kernel, nz, layers, host), "forward", 0, near=near, table=dict(slopes=slopes),
                out=out, far_out=far_out, scratch=scratch)
    if not host:
        done.qkv_w, done.gu_w, done.down_w, done.out_w = weights.qkv_given, weights.gu_given, weights.down_given, weights.out_given
    done.down_w = [w.reshape(quarter, width) for w in done.down_w]
    done.xr = [v.reshape(rows, width) for v in done.xr]
    done.yr = [v.reshape(rows, width) for v in done.yr]
    return done


def attn_back(at, R, l, top, begin, behind, at_end):
    nz, rows = at.nz, R.kvbuf.shape[1]
    q_ref, do_ref, dqacc = R.qb_now, R.do, R.dqacc
    dkv = BlockSum(at, R.dkv)

    def target(i):
        right = nz - 1 - at.z
        from_right = jnp.where(i < right, nz - 1 - i, i - right)
        from_left = jnp.where(i < at.z, i, nz - 1 - (i - at.z))
        return jnp.where(i == nz - 1, at.z, jnp.where(at.z < nz // 2, from_right, from_left))

    class Load:
        def __init__(self, t, slot):
            cc = at.oc if slot == 0 else at.c
            self.copies = [pltpu.make_async_copy(source.at[t, cc], target.at[slot], R.kvsem.at[i, slot])
                           for i, (source, target) in enumerate(((R.kv[l], R.kvbuf), (R.kaug, R.augbuf)))]

        def start(self):
            for copy in self.copies:
                copy.start()

        def wait(self):
            for copy in self.copies:
                copy.wait()

    load = Load

    dqacc[...] = jnp.zeros(dqacc.shape, F32)

    def compute(t, slot, same):
        cc = at.oc if slot == 0 else at.c
        side = (t > at.z).astype(jnp.int32)
        kv, aug = R.kvbuf.at[slot], R.augbuf[slot]
        dks, dvs = [], []
        for h in range(3):
            k, v = k_operand(kv, aug, h), v_operand(kv, h)
            if same:
                s = jnp.minimum(dot(k, q_ref[0, h], NT), dot(k, q_ref[1, h], NT))
            else:
                s = dot(k, q_ref[side, h], NT)
            p = jnp.exp(s)
            ds = (p * dot(v, do_ref[h], NT)).astype(BF)
            dvs.append(dot(p.astype(BF), do_ref[h]))
            dks.append(dot(ds, q_ref[side, h]))
            dqacc[h] += dot(ds, k, TN)
        low = in_half(0, rows)
        dkv.stage[t, cc, :, 0:128] = jnp.where(low, dks[0], dks[1]).astype(BF)
        dkv.stage[t, cc, :, 128:256] = jnp.where(low, dvs[0], dvs[1]).astype(BF)
        dkv.stage[t, cc, :, 256:384] = jnp.where(low, dks[2], dvs[2]).astype(BF)

    def far(t, same):
        load(t, 1).start()
        load(t, 0).wait()
        compute(t, 0, same)
        dkv.to_beside(t).start()

    load(target(0), 0).start()
    begin()
    if not top:
        pl.semaphore_wait(R.dkv.free, at.neighbours())

    def step(i):
        t = target(i)
        far(t, False)
        load(target(i + 1), 0).start()
        load(t, 1).wait()
        compute(t, 1, False)
        dkv.serve(i)
        behind(i)
    loop(0, nz - 1, step)
    far(at.z, True)
    load(at.z, 1).wait()
    compute(at.z, 1, True)
    at_end()
    dq = jnp.where(in_half(0, rows), dqacc[0], dqacc[1]) * 0.125
    R.dproj[:, 384:512] = dq.astype(BF)
    R.dproj[:, 512:576] = (dqacc[2][:, 0:64] * 0.125).astype(BF)
    R.dproj[:, 0:384] = dkv.total().astype(BF)
    if l > 0:
        at.signal_neighbours(R.dkv.free)
    dkv.finish()


def bwd_kernel(nz, layers, host, R):
    at = Place(nz)
    tokens = R.grad.shape[0]
    rows, half_rows = 4 * tokens, 2 * tokens
    quarter = R.hid.shape[1]
    width = R.grad.shape[1]
    mixed, yr, xr, gu_w, down_w, qkv_w, qb, ctx, ctxf, out_w = range(10)
    streams = ((R.mixed, R.mixed_now), (R.yr, R.yr_now), (R.xr, R.xr_now), (R.gu_w, R.gu_now), (R.down_w, R.down_now),
               (R.qkv_w, R.qkv_now), (R.qb, R.qb_now), (R.ctx, R.ctx_now), (R.ctxf, R.ctxf_now), (R.out_w, R.out_now))

    def load(which, l):
        return pltpu.make_async_copy(streams[which][0][l], streams[which][1], R.load.at[which])

    for which in range(10):
        load(which, layers - 1).start()
    at.enter(host)()
    R.dproj[:, 576:768] = jnp.zeros((rows, 192), BF)
    gather_df = SquareGather(at, R.df, R.df_send, R.df_recv)
    gather_da = SquareGather(at, R.da, R.da_send, R.da_recv)
    part = R.part
    square_sum = SquareSum(at, part, R.ss_stage, R.ss_inbox, R.ss_send, R.ss_recv)
    if host:
        gu_sum, dn_sum, qk_sum, ow_sum = [[BlockSum(at, item) for item in items] for items in (R.gu, R.dn, R.qk, R.ow)]
        sm_sum = BlockSum(at, R.sm)
        back = [[PlaneExchange(at, item.out, item.inbox, item.send, item.recv) for item in items] for items in R.back]
        wrows = R.out_grad.shape[1]
        moved = [remote(R.ow_out.at[l], R.ow_in.at[l], R.ow_send.at[l], R.ow_recv.at[l], at.chunk_device) for l in range(layers)]

    def small(l, t):
        return R.small[8 * l + t : 8 * l + t + 1, :]

    def put_small(l, t, value):
        R.tok_small[8 * l + t : 8 * l + t + 1, :] = value

    def of(buf, half):
        v = buf[pl.ds(2 * half, 2)]
        return v.reshape(half_rows, v.shape[2])

    def half_at(half):
        return pl.ds(pl.multiple_of(half * half_rows, half_rows), half_rows)

    def put_part(half, value):
        part[pl.ds(2 * half, 2)] = value.reshape(2, tokens, value.shape[1])

    def wgrad(left, right, stage, cc, lo, hi):
        for first in range(0, left.shape[1], 384):
            v = dot(left[:, first : first + 384], right[:, lo:hi], TN)
            if len(stage.shape) == 2:
                stage[first : first + 384, :] = v.astype(BF)
                continue
            step = stage.shape[2]
            for i in range(384 // step):
                b = first // step + i
                zz, side = (b // 2, b % 2) if cc is None else (b, cc)
                stage[zz, side] = v[step * i : step * i + step].astype(BF)

    def feed_forward_sums(l):
        return (gu_sum[l], dn_sum[l]) if host and l < layers else ()

    def attention_sums(l):
        return (qk_sum[l], ow_sum[l]) if host and l < layers else ()

    def serve(items, p):
        for item in items:
            item.serve(p)

    def emit(l):
        if not host or l == layers:
            return
        for item, exchange in zip((gu_sum[l], qk_sum[l]), back[l]):
            v = item.total()
            rest = jnp.zeros((exchange.out.shape[1] - wrows, v.shape[1]), F32)
            for k in range(8):
                exchange.out[k] = jnp.concatenate([v[wrows * k : wrows * k + wrows], rest], axis=0).astype(BF)
            exchange.start()
        R.dn_grad[l] = dn_sum[l].total()
        R.ow_out[l] = ow_sum[l].total()

        @pl.when(at.moves)
        def _():
            moved[l].start()

        @pl.when(jnp.logical_not(at.moves))
        def _():
            R.ow_in[l] = R.ow_out[l]

    def assemble(l):
        if not host:
            return
        def pieces(exchange):
            exchange.wait()
            piece = [exchange.inbox[k].astype(F32)[0:wrows] for k in range(8)]
            return lambda side, *spans: jnp.concatenate(
                [piece[2 * g + side][:, lo:hi] for g in range(4) for lo, hi in spans], axis=1)

        join = pieces(back[l][0])
        step = quarter // nz
        for side in range(2):
            for zz in range(nz):
                lo = (side * nz + zz) * 4 * step
                R.gu_grad[l, :, lo : lo + 4 * step] = join(side, (step * zz, step * zz + step))
        join = pieces(back[l][1])
        at_kv = 0
        R.qkv_grad[l, :, 0:width] = join(1, (at_kv, at_kv + 192))
        R.qkv_grad[l, :, width : 2 * width] = join(0, (at_kv, at_kv + 128), (at_kv + 256, at_kv + 320))
        R.qkv_grad[l, :, 2 * width : 3 * width] = join(0, (at_kv + 128, at_kv + 256), (at_kv + 320, at_kv + 384))

        @pl.when(at.moves)
        def _():
            moved[l].wait_recv()
        R.out_grad[l] = R.ow_in[l, 0:wrows, :]

    def small_copy(j):
        k = 4 * at.c + j
        return remote(R.sm_out, R.sm_in.at[at.g], R.sm_send.at[j], R.sm_recv.at[at.g], at.of_plane(k)), k != at.member

    def small_from(g):
        k = 2 * g + at.x
        return remote(R.sm_out, R.sm_in.at[g], R.sm_send.at[0], R.sm_recv.at[g], at.of_plane(k)), k != at.member

    R.g[...] = R.grad[...].astype(F32)
    for l in reversed(range(layers)):
        top = l == layers - 1
        e2, d_gain, d_shift = norm_back(R.g[...], R.sum2[l][...], small(l, 1))
        put_small(l, 1, d_gain)
        put_small(l, 5, d_shift)
        low = e2.astype(BF)
        put_small(l, 4, jnp.sum(low.astype(F32), axis=0, keepdims=True))
        if not top:
            square_sum.finish()
        R.df[at.g] = low
        gather_df.start()
        R.e2[...] = e2
        for which in range(10):
            load(which, l).wait()
        serve(feed_forward_sums(l + 1), 1)
        gather_df.wait_near()
        for number, half in enumerate((at.x, 1 - at.x)):
            if number == 1:
                gather_df.wait_far()
                serve(attention_sums(l + 1), 1)
            here = half_at(half)
            dhid_all = dot(of(R.df, half), R.down_now[...], NT)
            for col in range(0, quarter, 256):
                dhid = dhid_all[:, col : col + 256]
                gate = R.mixed_now[here, col : col + 256]
                up = R.mixed_now[here, quarter + col : quarter + col + 256]
                cdf = normal_cdf(gate)
                act = gate * cdf
                R.hid[here, col : col + 256] = (act * up).astype(BF)
                R.dgu[here, col : col + 256] = (dhid * up * (cdf + gate * normal_pdf(gate))).astype(BF)
                R.dgu[here, quarter + col : quarter + col + 256] = (dhid * act).astype(BF)
            put_part(half, dot(R.dgu[here, :quarter], side_weight(R.gu_now, 0), NT)
                     + dot(R.dgu[here, quarter:], side_weight(R.gu_now, 1), NT))
            if number == 0:
                square_sum.send_near()
            else:
                square_sum.send_far()
        wgrad(R.hid, R.df[...].reshape(rows, width), R.dn[l].stage, None, 0, width)
        square_sum.relay()
        serve(feed_forward_sums(l + 1), 2)
        for p in range(3, nz - 1):
            serve(feed_forward_sums(l + 1), p)
        dy = R.e2[...] + square_sum.total()
        e1, d_gain, d_shift = norm_back(dy, R.sum1[l][...], small(l, 0))
        put_small(l, 0, d_gain)
        put_small(l, 3, d_shift)
        low = e1.astype(BF)
        put_small(l, 2, jnp.sum(low.astype(F32), axis=0, keepdims=True))
        R.da[at.g] = low
        gather_da.start()
        R.e1[...] = e1
        for cc in range(2):
            wgrad(R.yr_now, R.dgu, R.gu[l].stage, cc, quarter * cc, quarter * cc + quarter)
        gather_da.wait_near()
        gather_da.wait_far()
        for item in feed_forward_sums(l):
            item.start()
        if l > 0:
            for which in (mixed, yr, gu_w, down_w):
                load(which, l - 1).start()
        da_all = R.da[...].reshape(rows, width)
        dctx = dot(da_all, R.out_now[...], NT).astype(BF)
        heads_out = R.ctxf_now
        wide = dctx.astype(F32)
        first_two = wide[:, :128]
        third = jnp.concatenate([jnp.zeros((rows, 64), F32), wide[:, 128:192]], axis=1)
        prod = first_two * heads_out[:, :128]
        low_half = in_half(0, rows)
        deltas = [
            jnp.sum(jnp.where(low_half, prod, 0.0), axis=1, keepdims=True),
            jnp.sum(jnp.where(low_half, 0.0, prod), axis=1, keepdims=True),
            jnp.sum(wide[:, 128:192] * heads_out[:, 128:192], axis=1, keepdims=True),
        ]
        for h in range(3):
            half = V_AT[h][1]
            base = jnp.where(in_half(half, rows), first_two if h < 2 else third, 0.0)
            R.do[h] = with_lanes(base, 0 if half else 64, split3(-deltas[h])).astype(BF)

        def begin(l=l):
            serve(attention_sums(l + 1), 2)
            for p in range(3, nz - 1):
                serve(attention_sums(l + 1), p)

        def out_grad(l=l):
            d_out = dot(R.ctx_now[...], R.da[...].reshape(rows, width), TN)
            if host:
                step = d_out.shape[0] // (2 * nz)
                for b in range(2 * nz):
                    R.ow[l].stage[b // 2, b % 2] = jnp.concatenate(
                        [d_out[step * b : step * b + step], jnp.zeros((OW_ROWS - step, width), F32)]).astype(BF)
            else:
                R.ow[l].stage[...] = d_out.astype(BF)

        def behind(i, l=l):
            pl.when(i == 0)(out_grad)
            if l < layers - 1:
                @pl.when(i == min(1, nz - 2))
                def _():
                    emit(l + 1)

                @pl.when(i == nz - 2)
                def _():
                    assemble(l + 1)

        def at_end(l=l):
            serve(feed_forward_sums(l), 0)
        attn_back(at, R, l, top, begin, behind, at_end)
        dproj = R.dproj
        gather_df.finish()
        gather_da.finish()
        square_sum.finish()
        for number, half in enumerate((1 - at.x, at.x)):
            put_part(half, dot(dproj[half_at(half), :384], side_weight(R.qkv_now, 0), NT)
                     + dot(dproj[half_at(half), 384:], side_weight(R.qkv_now, 1), NT))
            if number == 0:
                square_sum.send_far()
            else:
                square_sum.send_near()
        square_sum.relay()
        bias_sum = jnp.sum(dproj[...].astype(F32), axis=0, keepdims=True)
        for t, row in ((6, bias_sum[:, 384:576]), (7, jnp.concatenate([bias_sum[:, 128:256], bias_sum[:, 320:384]], axis=1))):
            put_small(l, t, jnp.concatenate([jnp.where(at.g == g, row, 0.0) for g in range(4)], axis=1))
        for cc in range(2):
            wgrad(R.xr_now, dproj, R.qk[l].stage, cc, 384 * cc, 384 * cc + 384)
        for item in attention_sums(l):
            item.start()
        serve(attention_sums(l), 0)
        if l > 0:
            for which in (xr, qkv_w, qb, ctx, ctxf, out_w):
                load(which, l - 1).start()
        R.g[...] = R.e1[...] + square_sum.total()
    R.grad_in[...] = R.g[...]
    square_sum.finish()
    if host:
        for b in range(2 * nz):
            step = width // (2 * nz)
            sm_sum.stage[b // 2, b % 2, :, 0:step] = R.tok_small[:, step * b : step * b + step]
        sm_sum.start()
        last = feed_forward_sums(0) + attention_sums(0) + (sm_sum,)
        sm_sum.serve(0)
        for p in range(1, nz - 1):
            serve(last, p)
        R.sm_out[...] = sm_sum.total()
        for j in range(4):
            copy, away = small_copy(j)

            @pl.when(away)
            def _(copy=copy):
                copy.start()

            @pl.when(jnp.logical_not(away))
            def _():
                R.sm_in[at.g] = R.sm_out[...]
        emit(0)
        total = jnp.zeros(R.sm_out.shape, F32)
        for g in range(4):
            copy, away = small_from(g)

            @pl.when(away)
            def _(copy=copy):
                copy.wait_recv()
            total = total + R.sm_in[g]
        mine = jnp.zeros((8 * layers, wrows), F32)
        for k in range(4):
            mine = jnp.where(2 * at.y + at.c == k, total[:, wrows * k : wrows * k + wrows], mine)
        for l in range(layers):
            R.gains_grad[l] = mine[8 * l : 8 * l + 2]
            R.biases_grad[l] = jnp.concatenate([mine[8 * l + 6 : 8 * l + 8], mine[8 * l + 2 : 8 * l + 6]], axis=0)
        assemble(0)
        for l in range(layers):
            for item in feed_forward_sums(l) + attention_sums(l) + tuple(back[l]):
                item.finish()

            @pl.when(at.moves)
            def _(l=l):
                moved[l].wait_send()
        for j in range(4):
            copy, away = small_copy(j)

            @pl.when(away)
            def _(copy=copy):
                copy.wait_send()
        sm_sum.finish()


def bwd(grad, saved, host):
    layers = len(saved.qkv_w)
    nz, _, rows, _ = saved.kaug.shape
    tokens, width = grad.shape
    quarter, group = width, width // 4
    quarter = saved.down_w[0].shape[0]
    r, rd = width // nz, quarter // (2 * nz)
    each = range(layers)
    out = dict(grad_in=shape(tokens, width, dtype=F32))
    scratch = {}
    if host:
        wrows, padded = width // (8 * nz), 32
        out.update(
            qkv_grad=shape(layers, wrows, 3 * width, dtype=F32), out_grad=shape(layers, wrows, width, dtype=F32),
            gu_grad=shape(layers, wrows, 8 * quarter, dtype=F32), dn_grad=shape(layers, rd, width, dtype=F32),
            gains_grad=shape(layers, 2, wrows, dtype=F32), biases_grad=shape(layers, 6, wrows, dtype=F32))
        scratch.update(
            back=[[dict(out=keep(8, padded, cols), inbox=keep(8, padded, cols), send=copies(8), recv=copies(8))
                   for cols in (quarter, 384)] for _ in each],
            ow_out=keep(layers, OW_ROWS, width, dtype=F32), ow_in=keep(layers, OW_ROWS, width, dtype=F32),
            ow_send=copies(layers), ow_recv=copies(layers),
            sm_out=keep(8 * layers, 128, dtype=F32), sm_in=keep(4, 8 * layers, 128, dtype=F32), sm_send=copies(4), sm_recv=copies(4))
        scratch.update(
            gu=[block_sum_item(nz, r, quarter, parts=2) for _ in each], dn=[block_sum_item(nz, rd, width, parts=2) for _ in each],
            qk=[block_sum_item(nz, r, 384, parts=2) for _ in each], ow=[block_sum_item(nz, OW_ROWS, width) for _ in each],
            sm=block_sum_item(nz, 8 * layers, 128, dtype=F32), tok_small=keep(8 * layers, width, dtype=F32))
    else:
        out.update(
            gu=[dict(stage=shape(nz, 2, r, quarter)) for _ in each], dn=[dict(stage=shape(quarter, width)) for _ in each],
            qk=[dict(stage=shape(nz, 2, r, 384)) for _ in each], ow=[dict(stage=shape(group, width)) for _ in each],
            tok_small=shape(8 * layers, width, dtype=F32))
    like = lambda arrays: keep(*arrays[0].shape, dtype=arrays[0].dtype)
    scratch.update(
        mixed_now=like(saved.mixed), yr_now=like(saved.yr), xr_now=like(saved.xr), gu_now=like(saved.gu_w),
        down_now=like(saved.down_w), qkv_now=like(saved.qkv_w), qb_now=like(saved.qb),
        ctx_now=like(saved.ctx), ctxf_now=like(saved.ctxf), out_now=like(saved.out_w), load=copies(10), kvbuf=keep(2, rows, 384), augbuf=keep(2, rows, 128), kvsem=copies(2, 2),
        df=keep(4, tokens, width), df_send=copies(6), df_recv=copies(6),
        da=keep(4, tokens, width), da_send=copies(6), da_recv=copies(6),
        part=keep(4, tokens, width, dtype=F32), **square_sum_items(tokens, width),
        g=keep(tokens, width, dtype=F32), e1=keep(tokens, width, dtype=F32), e2=keep(tokens, width, dtype=F32),
        hid=keep(rows, quarter), dgu=keep(rows, 2 * quarter), do=keep(3, rows, 128),
        dqacc=keep(3, rows, 128, dtype=F32), dproj=keep(rows, 768),
        dkv=dict(block_sum_item(nz, rows, 384, parts=2), free=pltpu.SemaphoreType.REGULAR))
    near = dict(grad=grad, small=saved.small, sum1=saved.sum1, sum2=saved.sum2)
    far = dict(mixed=saved.mixed, yr=saved.yr, xr=saved.xr, gu_w=saved.gu_w, down_w=saved.down_w, kv=saved.kv, kaug=saved.kaug,
               qkv_w=saved.qkv_w, qb=saved.qb, ctx=saved.ctx, ctxf=saved.ctxf, out_w=saved.out_w)
    return call(functools.partial(bwd_kernel, nz, layers, host), "backward", 1, near=near, far=far, out=out, scratch=scratch)


def shards(hidden_in, out_grad, segment_ids, alibi_slopes, qkv_weight, out_weight, gate_up_weight, down_weight, gains, biases):
    nz = lax.axis_size("z")
    nb = 2 * nz
    square, everyone, blocks = ("x", "y", "c"), ("z", "x", "y", "c"), ("z", "c")
    z, c = lax.axis_index("z"), lax.axis_index("c")
    tokens, width = hidden_in.shape
    layers, wrows = qkv_weight.shape[:2]
    ff = gate_up_weight.shape[2] // 2
    group, quarter = width // 4, ff // 4
    host = (width // nz) % 16 == 0 and down_weight.shape[1] % 16 == 0

    def to_groups(w):
        w = w.reshape(wrows, 3, 4, 3, 64)
        q, k, v = w[:, 0], w[:, 1], w[:, 2]
        kv = jnp.stack([k[:, :, 0], k[:, :, 1], v[:, :, 0], v[:, :, 1], k[:, :, 2], v[:, :, 2]], axis=2)
        return kv.reshape(wrows, 4, 384), q.reshape(wrows, 4, group)

    def from_groups(kv, q):
        kv, q = kv.reshape(4, wrows, 6, 64), q.reshape(4, wrows, 3, 64)
        k = jnp.stack([kv[:, :, 0], kv[:, :, 1], kv[:, :, 4]], axis=2)
        v = jnp.stack([kv[:, :, 2], kv[:, :, 3], kv[:, :, 5]], axis=2)
        return jnp.stack([q, k, v]).transpose(2, 0, 1, 3, 4).reshape(wrows, 3 * width)

    places = [(8 * zz + 2 * g + cc, g * nb + 2 * zz + cc) for zz in range(nz) for g in range(4) for cc in range(2)]
    gu0 = 384 * layers

    def gathered_outside():
        beside = jnp.broadcast_to(small[:, None], (wrows, 4, 192))
        nothing = jnp.zeros((wrows, 4, 192), BF)
        gu = gate_up_weight.reshape(layers, wrows, 2, nz, 4, quarter // nz).transpose(0, 1, 4, 2, 3, 5)
        gu = gu.reshape(layers, wrows, 4, 2, quarter)
        sides = [[], []]
        for l in range(layers):
            kv, q = to_groups(qkv_weight[l])
            sides[0].append(kv)
            sides[1] += [q, nothing if l else beside]
        for l in range(layers):
            for side in range(2):
                sides[side].append(gu[l, :, :, side])
        both = jnp.stack([jnp.concatenate(side, axis=2) for side in sides], axis=2).reshape(wrows, 8, -1)
        spread = lax.all_to_all(both, square, split_axis=1, concat_axis=0, tiled=True).reshape(8 * wrows, -1)
        ow_own = lax.ppermute(out_weight, everyone, [(chunk, device) for device, chunk in places])
        whole = lambda v: lax.all_gather(v, blocks, axis=0).reshape(nz, 2, *v.shape)
        flat = lambda v: lax.all_gather(v, blocks, axis=0, tiled=True)
        return types.SimpleNamespace(
            qkv_given=[whole(spread[:, 384 * l : 384 * l + 384]) for l in range(layers)],
            gu_given=[whole(spread[:, gu0 + quarter * l : gu0 + quarter * l + quarter]) for l in range(layers)],
            down_given=[flat(down_weight[l]) for l in range(layers)], out_given=[flat(ow_own[l]) for l in range(layers)])

    small = jnp.concatenate([gains, biases], axis=1).transpose(0, 2, 1)
    small = jnp.concatenate([small[l] for l in range(layers)], axis=1)
    small = jnp.pad(small, ((0, 0), (0, 192 - small.shape[1])))
    if host:
        weights = types.SimpleNamespace(
            qkv_mine=qkv_weight, gu_mine=gate_up_weight, down_mine=down_weight, small_mine=small,
            ow_mine=out_weight.reshape(layers * wrows, width))
    else:
        weights = gathered_outside()
    seg = segment_ids.reshape(8 * nz, tokens)
    saved = fwd(hidden_in, alibi_slopes, seg, weights, layers, host)
    done = bwd(out_grad, saved, host)
    if host:
        return (saved.output, done.grad_in, done.qkv_grad, done.out_grad, done.gu_grad, done.dn_grad, done.gains_grad,
                done.biases_grad)
    step = width // nb
    blocks_sum = lambda v: lax.psum_scatter(v, blocks, scatter_dimension=0, tiled=True)
    done.gu_sum = [blocks_sum(item.stage.reshape(nb, -1, quarter))[0] for item in done.gu]
    done.qk_sum = [blocks_sum(item.stage.reshape(nb, -1, 384))[0] for item in done.qk]
    done.dn_sum = [blocks_sum(item.stage) for item in done.dn]
    done.ow_sum = [blocks_sum(item.stage) for item in done.ow]
    sm = lax.psum_scatter(done.tok_small.reshape(-1, nb, step), blocks, scatter_dimension=1, tiled=True)[:, 0]
    sm = sm.T.reshape(4, wrows, 8 * layers)
    high = lax.reduce_precision(sm, 8, 7)
    sm = jnp.concatenate([high, sm - high], axis=2).astype(BF)
    sm = lax.dynamic_update_slice_in_dim(jnp.zeros((8, wrows, 16 * layers), BF), sm, 4 * c, 0)
    rows_of = lambda v: v.reshape(8, wrows, -1)
    back = jnp.concatenate([rows_of(v) for v in done.qk_sum + done.gu_sum] + [sm], axis=2)
    back = lax.all_to_all(back, square, split_axis=0, concat_axis=0, tiled=True)
    sides = back.astype(F32).reshape(4, 2, wrows, -1)
    qkv_grad = jnp.stack([from_groups(sides[:, 0, :, 384 * l : 384 * l + 384], sides[:, 1, :, 384 * l : 384 * l + group])
                          for l in range(layers)])
    gu_grad = jnp.stack([sides[:, :, :, gu0 + quarter * l : gu0 + quarter * l + quarter] for l in range(layers)])
    gu_grad = gu_grad.reshape(layers, 4, 2, wrows, nz, quarter // nz).transpose(0, 3, 2, 4, 1, 5).reshape(layers, wrows, 2 * ff)
    sm = jnp.sum(sides[..., gu0 + quarter * layers :], axis=(0, 1))
    sm = (sm[:, : 8 * layers] + sm[:, 8 * layers :]).T.reshape(layers, 8, wrows)
    out_grad_w = lax.ppermute(jnp.stack(done.ow_sum)[:, :wrows].astype(F32), everyone, places)
    return (saved.output, done.grad_in, qkv_grad, out_grad_w, gu_grad, jnp.stack(done.dn_sum).astype(F32), sm[:, 0:2],
            jnp.concatenate([sm[:, 6:8], sm[:, 2:6]], axis=1))


def solution(mesh):
    nb, nh = mesh.devices.shape
    everyone = ("z", "x", "y", "c")
    tok, mid, last = P(everyone, None), P(None, everyone, None), P(None, None, everyone)
    return jax.shard_map(
        shards, mesh=Mesh(mesh.devices.reshape(nb // 2, 2, nh // 2, 2), everyone),
        in_specs=(tok, tok, P(), P(), mid, mid, mid, mid, last, last),
        out_specs=(tok, tok, mid, mid, mid, mid, last, last),
        check_vma=False,
    )
```

```python
import functools
import types

import jax
import jax.numpy as jnp
from jax import lax
from jax.experimental import pallas as pl
from jax.experimental.pallas import tpu as pltpu
from jax.sharding import Mesh
from jax.sharding import PartitionSpec as P

MESH = pl.DeviceIdType.MESH
BF = jnp.bfloat16
F32 = jnp.float32
NT = (((1,), (1,)), ((), ()))
NN = (((1,), (0,)), ((), ()))
TN = (((0,), (0,)), ((), ()))
EPS = 1e-06
K_AT = ((0, 0), (0, 1), (2, 0))
V_AT = ((1, 0), (1, 1), (2, 1))
ROW_LANE, SEGMENT_LANE = 9, 12
OW_ROWS = 32
VMEM = pl.BlockSpec(memory_space=pltpu.VMEM)
ANY = pl.BlockSpec(memory_space=pl.ANY)


def dot(a, b, dims=NN):
    return lax.dot_general(a, b, dims, preferred_element_type=F32)


def lanes(rows):
    return lax.broadcasted_iota(jnp.int32, (rows, 128), 1)


def in_half(half, rows):
    return lanes(rows) >= 64 if half else lanes(rows) < 64


def ones_half(half, rows):
    first = 0 if half else 64
    lane = lanes(rows)
    return jnp.where((lane >= first) & (lane < first + 3), 1.0, 0.0).astype(BF)


def k_operand(kv, aug, h):
    col, half = K_AT[h]
    return jnp.where(in_half(half, kv.shape[0]), kv[:, 128 * col : 128 * col + 128], aug)


def v_operand(kv, h):
    col, half = V_AT[h]
    rows = kv.shape[0]
    return jnp.where(in_half(half, rows), kv[:, 128 * col : 128 * col + 128], ones_half(half, rows))


def split3(value):
    high = value.astype(BF).astype(F32)
    mid = (value - high).astype(BF).astype(F32)
    return high, mid, value - high - mid


def with_lanes(base, first, values):
    lane = lanes(base.shape[0])
    for i, v in enumerate(values):
        base = jnp.where(lane == first + i, v, base)
    return base


def layer_norm(total, gain, shift):
    centred = total - jnp.mean(total, axis=-1, keepdims=True)
    scale = lax.rsqrt(jnp.mean(centred * centred, axis=-1, keepdims=True) + EPS)
    return centred * scale * gain + shift


def norm_back(grad, total, gain):
    centred = total - jnp.mean(total, axis=-1, keepdims=True)
    scale = lax.rsqrt(jnp.mean(centred * centred, axis=-1, keepdims=True) + EPS)
    n = centred * scale
    dn = grad * gain
    e = scale * (dn - jnp.mean(dn, axis=-1, keepdims=True) - n * jnp.mean(dn * n, axis=-1, keepdims=True))
    return e, jnp.sum(grad * n, axis=0, keepdims=True), jnp.sum(grad, axis=0, keepdims=True)


def normal_cdf(u):
    return 0.5 * (1.0 + lax.erf(u * (0.5**0.5)))


def normal_pdf(u):
    return jnp.exp(-0.5 * u * u) * ((2.0 * jnp.pi) ** -0.5)


def remote(src, dst, send, recv, device):
    return pltpu.make_async_remote_copy(
        src_ref=src, dst_ref=dst, send_sem=send, recv_sem=recv, device_id=device, device_id_type=MESH)


def loop(first, last, do):
    def step(i, carry):
        do(i)
        return carry
    lax.fori_loop(first, last, step, 0)


class Place:
    def __init__(self, nz):
        self.nz = nz
        self.z, self.x, self.y, self.c = [lax.axis_index(name) for name in "zxyc"]
        self.g = 2 * self.x + self.y
        self.gx, self.gy = 2 * (1 - self.x) + self.y, 2 * self.x + 1 - self.y
        self.gd = 2 * (1 - self.x) + 1 - self.y
        self.oc = 1 - self.c
        self.beside = (self.z, self.x, self.y, self.oc)
        self.across_x = (self.z, 1 - self.x, self.y, self.c)
        self.across_y = (self.z, self.x, 1 - self.y, self.c)
        self.block = 2 * self.z + self.c
        self.member = 2 * self.g + self.c
        self.number = 8 * self.z + self.member
        nb = 2 * nz
        self.chunk = self.g * nb + self.block
        self.chunk_device = self.device(self.chunk)
        place = self.number % nb
        self.holder = (place // 2, self.number // nb // 2, self.number // nb % 2, place % 2)
        self.moves = self.chunk != self.number
        self.has_left, self.has_right = self.z > 0, self.z < nz - 1

    def column(self, zz):
        return (zz, self.x, self.y, self.c)

    def device(self, number):
        k = number % 8
        return (number // 8, k // 4, k // 2 % 2, k % 2)

    def of_plane(self, k):
        return (self.z, k // 4, k // 2 % 2, k % 2)

    def neighbours(self):
        return 3 - (self.z == 0).astype(jnp.int32) - (self.z == self.nz - 1).astype(jnp.int32)

    def signal_neighbours(self, semaphore):
        pl.semaphore_signal(semaphore, inc=1, device_id=self.beside, device_id_type=MESH)

        @pl.when(self.has_left)
        def _():
            pl.semaphore_signal(semaphore, inc=1, device_id=self.column(self.z - 1), device_id_type=MESH)

        @pl.when(self.has_right)
        def _():
            pl.semaphore_signal(semaphore, inc=1, device_id=self.column(self.z + 1), device_id_type=MESH)

    def enter(self, plane):
        barrier = pltpu.get_barrier_semaphore()

        def greet(device):
            pl.semaphore_signal(barrier, inc=1, device_id=device, device_id_type=MESH)

        if not plane:
            greet(self.across_x)
            greet(self.across_y)
            self.signal_neighbours(barrier)
            return lambda: pl.semaphore_wait(barrier, 2 + self.neighbours())
        loop(1, 8, lambda j: greet(self.of_plane((self.member + j) % 8)))
        self.signal_neighbours(barrier)

        @pl.when(self.moves)
        def _():
            greet(self.chunk_device)
            greet(self.holder)
        return lambda: pl.semaphore_wait(barrier, 7 + self.neighbours() + 2 * self.moves.astype(jnp.int32))

    def positions(self, zz, cc, tokens, rows):
        row = lax.broadcasted_iota(jnp.int32, (rows, 128), 0)
        return ((zz * 8 + (row // tokens) * 2 + cc) * tokens + row % tokens).astype(F32)


class SquareGather:
    def __init__(self, at, buf, send, recv):
        half = buf.shape[1] // 2
        first, second = pl.ds(0, half), pl.ds(half, half)

        def copy(i, g, rows, device):
            return remote(buf.at[g, rows], buf.at[g, rows], send.at[i], recv.at[i], device)
        self.x_first, self.x_second = copy(0, at.g, first, at.across_x), copy(1, at.g, second, at.across_x)
        self.y_second, self.y_first = copy(2, at.g, second, at.across_y), copy(3, at.g, first, at.across_y)
        self.on_y = copy(4, at.gx, first, at.across_y)
        self.on_x = copy(5, at.gy, second, at.across_x)

    def start(self):
        for copy in (self.x_first, self.y_second, self.x_second, self.y_first):
            copy.start()

    def wait_near(self):
        self.x_first.wait_recv()
        self.on_y.start()
        self.y_second.wait_recv()
        self.on_x.start()
        self.y_first.wait_recv()

    def wait_far(self):
        self.x_second.wait_recv()
        self.on_x.wait_recv()
        self.on_y.wait_recv()

    def finish(self):
        for copy in (self.x_first, self.x_second, self.y_first, self.y_second, self.on_x, self.on_y):
            copy.wait_send()


class SquareSum:
    def __init__(self, at, part, stage, inbox, send, recv):
        self.at, self.part, self.stage, self.inbox = at, part, stage, inbox
        self.half = part.shape[2] // 2
        to = (at.across_x, at.across_x, at.across_y, at.across_y, at.across_y, at.across_x)
        self.copies = [remote(stage.at[i], inbox.at[i], send.at[i], recv.at[i], to[i]) for i in range(6)]

    def left(self, g):
        return self.part[g, :, : self.half]

    def right(self, g):
        return self.part[g, :, self.half :]

    def post(self, i, value):
        self.stage[i] = value.astype(BF)
        self.copies[i].start()

    def came(self, i):
        self.copies[i].wait_recv()
        return self.inbox[i].astype(F32)

    def send_far(self):
        self.post(0, self.left(self.at.gd))
        self.post(2, self.right(self.at.gd))
        self.post(1, self.left(self.at.gx))

    def send_near(self):
        self.post(3, self.right(self.at.gy))

    def relay(self):
        self.post(4, self.left(self.at.gy) + self.came(0))
        self.post(5, self.right(self.at.gx) + self.came(2))

    def total(self):
        left = self.left(self.at.g) + self.came(1)
        right = self.right(self.at.g) + self.came(3)
        return jnp.concatenate([left + self.came(4), right + self.came(5)], axis=1)

    def finish(self):
        for copy in self.copies:
            copy.wait_send()


class BlockGather:
    def __init__(self, at, item):
        self.at, self.buf, self.zsend, self.csend, self.recv = at, item.buf, item.zsend, item.csend, item.recv
        self.parts = self.recv.shape[2]
        self.step = self.buf.shape[2] // self.parts

    def copy(self, zz, cc, part, send, device):
        block = self.buf.at[zz, cc, pl.ds(part * self.step, self.step)]
        return remote(block, block, send, self.recv.at[zz, cc, part], device)

    def to_right(self, zz, part):
        return self.copy(zz, self.at.c, part, self.zsend.at[0, zz, part], self.at.column(self.at.z + 1))

    def to_left(self, zz, part):
        return self.copy(zz, self.at.c, part, self.zsend.at[1, zz, part], self.at.column(self.at.z - 1))

    def to_beside(self, zz, part):
        return self.copy(zz, self.at.c, part, self.csend.at[zz, part], self.at.beside)

    def wait_part(self, zz, cc, part):
        self.copy(zz, cc, part, self.csend.at[zz, part], self.at.beside).wait_recv()

    def wait(self, zz, cc):
        for part in range(self.parts):
            self.wait_part(zz, cc, part)

    def put(self, value):
        self.buf[self.at.z, self.at.c] = value

    def start(self):
        at = self.at
        for part in range(self.parts):
            @pl.when(at.has_right)
            def _(part=part):
                self.to_right(at.z, part).start()

            @pl.when(at.has_left)
            def _(part=part):
                self.to_left(at.z, part).start()
            self.to_beside(at.z, part).start()

    def serve(self, d):
        at = self.at
        for part in range(self.parts):
            @pl.when(at.z - d >= 0)
            def _(part=part):
                self.wait_part(at.z - d, at.c, part)

                @pl.when(at.has_right)
                def _():
                    self.to_right(at.z - d, part).start()
                self.to_beside(at.z - d, part).start()

            @pl.when(at.z + d < at.nz)
            def _(part=part):
                self.wait_part(at.z + d, at.c, part)

                @pl.when(at.has_left)
                def _():
                    self.to_left(at.z + d, part).start()
                self.to_beside(at.z + d, part).start()

    def serve_all(self):
        loop(1, self.at.nz, self.serve)

    def collect(self):
        loop(0, self.at.nz, lambda zz: self.wait(zz, self.at.oc))

    def finish(self):
        at = self.at

        def drain(zz):
            for part in range(self.parts):
                self.to_beside(zz, part).wait_send()

                @pl.when((zz <= at.z) & at.has_right)
                def _(part=part):
                    self.to_right(zz, part).wait_send()

                @pl.when((zz >= at.z) & at.has_left)
                def _(part=part):
                    self.to_left(zz, part).wait_send()
        loop(0, at.nz, drain)


def block_gather_item(nz, *dims, parts=1):
    return dict(buf=keep(nz, 2, *dims), zsend=copies(2, nz, parts), csend=copies(nz, parts), recv=copies(nz, 2, parts))


class BlockSum:
    def __init__(self, at, item):
        self.at, self.stage, self.cin, self.zin = at, item.stage, item.cin, item.zin
        self.csend, self.crecv, self.zsend, self.zrecv = item.csend, item.crecv, item.zsend, item.zrecv
        self.parts = self.zsend.shape[1]
        self.step = self.stage.shape[2] // self.parts

    def rows(self, part):
        return pl.ds(part * self.step, self.step)

    def to_beside(self, t):
        return remote(self.stage.at[t, self.at.oc], self.cin.at[t], self.csend.at[t], self.crecv.at[t], self.at.beside)

    def along(self, t, slot, part, device):
        rows = self.rows(part)
        return remote(self.stage.at[t, self.at.c, rows], self.zin.at[slot, rows], self.zsend.at[t, part],
                      self.zrecv.at[slot, part], device)

    def to_right(self, t, part):
        return self.along(t, t + 1, part, self.at.column(self.at.z + 1))

    def to_left(self, t, part):
        return self.along(t, t, part, self.at.column(self.at.z - 1))

    def arrived(self, slot, part):
        block = self.zin.at[slot, self.rows(part)]
        remote(block, block, self.zsend.at[0, part], self.zrecv.at[slot, part], self.at.beside).wait_recv()

    def start(self):
        loop(0, self.at.nz, lambda t: self.to_beside(t).start())

    def add(self, t, part, slot=None):
        rows = self.rows(part)
        value = self.stage[t, self.at.c, rows].astype(F32) + self.cin[t, rows].astype(F32)
        if slot is not None:
            value = value + self.zin[slot, rows].astype(F32)
        self.stage[t, self.at.c, rows] = value.astype(self.stage.dtype)

    def go(self, t, slot, passed_on, send):
        self.to_beside(t).wait_recv()
        for part in range(self.parts):
            @pl.when(passed_on)
            def _(part=part):
                self.arrived(slot, part)
                self.add(t, part, slot)

            @pl.when(jnp.logical_not(passed_on))
            def _(part=part):
                self.add(t, part)
            send(t, part).start()

    def serve(self, p, source=True, relay=True):
        at = self.at
        right, left = p - at.z, p - (at.nz - 1 - at.z)
        go_r = (right >= 0) & (right < at.nz - 1 - at.z)
        go_l = (left >= 0) & (left < at.z)
        if not source:
            go_r, go_l = go_r & at.has_left, go_l & at.has_right
        if not relay:
            go_r, go_l = go_r & jnp.logical_not(at.has_left), go_l & jnp.logical_not(at.has_right)

        @pl.when(go_r)
        def _():
            self.go(at.nz - 1 - right, at.nz - right, at.has_left, self.to_right)

        @pl.when(go_l)
        def _():
            self.go(left, left, at.has_right, self.to_left)

    def total(self):
        at = self.at
        self.to_beside(at.z).wait_recv()
        for part in range(self.parts):
            @pl.when(at.has_left)
            def _(part=part):
                self.arrived(at.z + 1, part)

            @pl.when(at.has_right)
            def _(part=part):
                self.arrived(at.z, part)
        value = self.stage[at.z, at.c].astype(F32) + self.cin[at.z].astype(F32)
        from_left = jnp.where(at.has_left, self.zin[at.z + 1].astype(F32), 0.0)
        from_right = jnp.where(at.has_right, self.zin[at.z].astype(F32), 0.0)
        return value + from_left + from_right

    def finish(self):
        at = self.at

        def drain(t):
            self.to_beside(t).wait_send()
            for part in range(self.parts):
                @pl.when(t > at.z)
                def _(part=part):
                    self.to_right(t, part).wait_send()

                @pl.when(t < at.z)
                def _(part=part):
                    self.to_left(t, part).wait_send()
        loop(0, at.nz, drain)


class PlaneExchange:
    def __init__(self, at, out, inbox, send, recv, columns=None):
        self.at, self.out, self.inbox, self.send, self.recv, self.columns = at, out, inbox, send, recv, columns

    def source(self, k):
        return self.out.at[k] if self.columns is None else self.out.at[k, :, self.columns]

    def start(self):
        at = self.at

        def step(j):
            k = (at.member + j) % 8
            remote(self.source(k), self.inbox.at[at.member], self.send.at[k], self.recv.at[at.member], at.of_plane(k)).start()
        loop(1, 8, step)
        self.inbox[at.member] = self.source(at.member)[...]

    def each(self, do):
        at = self.at

        def step(j):
            k = (at.member + j) % 8
            do(remote(self.source(k), self.inbox.at[k], self.send.at[k], self.recv.at[k], at.of_plane(k)))
        loop(1, 8, step)

    def wait(self):
        self.each(lambda copy: copy.wait_recv())

    def finish(self):
        self.each(lambda copy: copy.wait_send())

    def rows(self, count):
        return jnp.concatenate([self.inbox[k].astype(F32)[0:count] for k in range(8)], axis=0)


def box(tree):
    if isinstance(tree, dict):
        return types.SimpleNamespace(**{k: box(v) for k, v in tree.items()})
    return [box(v) for v in tree] if isinstance(tree, list) else tree


def call(body, name, collective_id, near=None, far=None, table=None, out=None, far_out=None, scratch=None):
    groups = [near or {}, far or {}, table or {}, out or {}, far_out or {}, scratch or {}]
    flat, trees = zip(*[jax.tree.flatten(g) for g in groups])
    counts = [len(f) for f in flat]

    def kernel(*refs):
        named, first = {}, 0
        for tree, count in zip(trees, counts):
            named.update(jax.tree.unflatten(tree, refs[first : first + count]))
            first += count
        body(box(named))

    smem = pl.BlockSpec(memory_space=pltpu.SMEM)
    results = pl.pallas_call(
        kernel,
        out_shape=tuple(flat[3]) + tuple(flat[4]),
        in_specs=[VMEM] * counts[0] + [ANY] * counts[1] + [smem] * counts[2],
        out_specs=(VMEM,) * counts[3] + (ANY,) * counts[4],
        scratch_shapes=list(flat[5]),
        compiler_params=pltpu.CompilerParams(
            collective_id=collective_id, has_side_effects=True, vmem_limit_bytes=63 * 2**20),
        cost_estimate=pl.CostEstimate(flops=10**11, bytes_accessed=2 * 10**8, transcendentals=10**7),
        name=name,
    )(*flat[0], *flat[1], *flat[2])
    done = jax.tree.unflatten(trees[3], results[: counts[3]])
    done.update(jax.tree.unflatten(trees[4], results[counts[3] :]))
    return box(done)


def shape(*dims, dtype=BF):
    return jax.ShapeDtypeStruct(dims, dtype)


def keep(*dims, dtype=BF):
    return pltpu.VMEM(dims, dtype)


def copies(*dims):
    return pltpu.SemaphoreType.DMA(dims)


def square_sum_items(tokens, width):
    half = width // 2
    return dict(ss_stage=keep(6, tokens, half), ss_inbox=keep(6, tokens, half), ss_send=copies(6), ss_recv=copies(6))


def flat_weight(ref, lo=0, hi=None):
    if len(ref.shape) == 2:
        return ref[:, lo:hi]
    v = ref[:, :, :, lo:hi]
    return v.reshape(v.shape[0] * v.shape[1] * v.shape[2], v.shape[3])


def side_weight(ref, cc, lo=0, hi=None):
    v = ref[:, cc, :, lo:hi]
    return v.reshape(v.shape[0] * v.shape[1], v.shape[2])


def block_sum_item(nz, *dims, dtype=BF, parts=1):
    return dict(stage=keep(nz, 2, *dims, dtype=dtype), cin=keep(nz, *dims, dtype=dtype), zin=keep(nz + 1, *dims, dtype=dtype),
                csend=copies(nz), crecv=copies(nz), zsend=copies(nz, parts), zrecv=copies(nz + 1, parts))


def segment_row(seg, zz, cc):
    return jnp.concatenate([seg[pl.ds(zz * 8 + 2 * k + cc, 1), :] for k in range(4)], axis=1)


def key_columns(at, slopes, seg, zz, cc, tokens):
    rows = 4 * tokens
    column = lax.broadcasted_iota(jnp.int32, (128, rows), 0) % 64
    row = lax.broadcasted_iota(jnp.int32, (128, rows), 1)
    position = ((zz * 8 + (row // tokens) * 2 + cc) * tokens + row % tokens).astype(F32)
    value = jnp.where(segment_row(seg, zz, cc) == column - SEGMENT_LANE, 0.0, -1e30)
    value = jnp.where(column < SEGMENT_LANE + 5, value, 0.0)
    value = jnp.where(column < SEGMENT_LANE, 1.0, value)
    for h in range(3):
        for i, term in enumerate(split3(position * slopes[3 * at.g + h])):
            value = jnp.where(column == 3 * h + i, term, value)
    return value.T.astype(BF)


def segment_columns(at, seg, rows):
    column = lax.broadcasted_iota(jnp.int32, (128, rows), 0) % 64
    return jnp.where(segment_row(seg, at.z, at.c) == column - SEGMENT_LANE, 1.0, 0.0).T


def query_operand(at, q_ref, inside, slopes, side, h, tokens, lse=None):
    rows = 4 * tokens
    if h < 2:
        data = q_ref[:, 0:128]
    else:
        data = jnp.concatenate([q_ref[:, 128:192], jnp.zeros((rows, 64), q_ref.dtype)], axis=1)
    half = K_AT[h][1]
    sign = 1.0 if side == 0 else -1.0
    column = lanes(rows) % 64
    aug = jnp.where((column >= 3 * h) & (column < 3 * h + 3), sign, inside[...])
    term = at.positions(at.z, at.c, tokens, rows) * (slopes[3 * at.g + h] * -sign)
    if lse is not None:
        term = term - lse
    aug = with_lanes(aug, ROW_LANE if half else 64 + ROW_LANE, split3(term))
    return jnp.where(in_half(half, rows), data.astype(F32) * 0.125, aug).astype(BF)


def attention(at, gather, q_op, kaug, m_ref, acc_ref, behind):
    m_ref[...] = jnp.full(m_ref.shape, -1e30, F32)
    acc_ref[...] = jnp.zeros(acc_ref.shape, F32)

    def compute(zz, cc, same):
        kv, aug = gather.buf.at[zz, cc], kaug[zz, cc]
        side = (zz > at.z).astype(jnp.int32)
        for h in range(3):
            k = k_operand(kv, aug, h)
            if same:
                s = jnp.minimum(dot(q_op[0, h], k, NT), dot(q_op[1, h], k, NT))
            else:
                s = dot(q_op[side, h], k, NT)
            m_old = m_ref[h]
            m_new = jnp.maximum(m_old, jnp.max(s, axis=1, keepdims=True))
            p = jnp.exp(s - m_new[:, :1]).astype(BF)
            acc_ref[h] = acc_ref[h] * jnp.exp(m_old - m_new) + dot(p, v_operand(kv, h))
            m_ref[h] = m_new

    def here(i):
        cc = jnp.where(i == 0, at.c, at.oc)

        @pl.when(i == 1)
        def _():
            gather.wait(at.z, at.oc)
        compute(at.z, cc, True)
    loop(0, 2, here)

    def both(d):
        return (at.z - d >= 0) & (at.z + d < at.nz)

    def step(d):
        @pl.when(jnp.logical_not(both(d - 1)) | (d == 1))
        def _():
            gather.serve(d)
        behind(d)

        def visit(i):
            zz = jnp.where(i % 2 == 0, at.z - d, at.z + d)

            @pl.when((zz >= 0) & (zz < at.nz))
            def _():
                @pl.when(i >= 2)
                def _():
                    gather.wait(zz, at.oc)
                compute(zz, jnp.where(i < 2, at.c, at.oc), False)

            @pl.when((i == 1) & both(d) & (d + 1 < at.nz))
            def _():
                gather.serve(d + 1)
        loop(0, 4, visit)
    loop(1, at.nz, step)


def attention_end(m_ref, acc_ref, ctx_ref, ctxf_ref):
    for h in range(3):
        half = V_AT[h][1]
        first = 0 if half else 64
        acc = acc_ref[h]
        total = acc[:, first : first + 1]
        ctx = acc[:, 64 * half : 64 * half + 64] / total
        ctxf_ref[:, 64 * h : 64 * h + 64] = ctx
        ctx_ref[:, 64 * h : 64 * h + 64] = ctx.astype(BF)
        m_ref[h] = m_ref[h] + jnp.log(total)


def fwd_kernel(nz, layers, host, R):
    at = Place(nz)
    tokens = R.x0.shape[0]
    rows, half_rows = 4 * tokens, 2 * tokens
    quarter = R.hid.shape[1]
    group = R.ctx_now[0].shape[1]
    arrived = at.enter(host)
    part = R.part
    square_sum = SquareSum(at, part, R.ss_stage, R.ss_inbox, R.ss_send, R.ss_recv)
    gather_x = [SquareGather(at, R.xr_now[l], R.x_send.at[l], R.x_recv.at[l]) for l in range(layers)]
    gather_y = [SquareGather(at, R.yr_now[l], R.y_send.at[l], R.y_recv.at[l]) for l in range(layers)]
    kv = BlockGather(at, R.kv_now)
    saves, waited = [], []

    def save(source, target):
        saves.append(pltpu.make_async_copy(source, target, R.saved.at[len(saves)]))
        saves[-1].start()
        return len(saves) - 1

    def wait_saved(number):
        saves[number].wait()
        waited.append(number)

    if host:
        qkv, gu, down = [[BlockGather(at, item) for item in items] for items in (R.qkv_now, R.gu_now, R.down_now)]
        ow = BlockGather(at, R.ow_now)
        qkv_w, gu_w, down_w, out_w = [g.buf for g in qkv], [g.buf for g in gu], [g.buf for g in down], R.out_now
        wrows = R.ow_now.buf.shape[2] // layers
        lists = [qkv[l] for l in range(layers)] + [gu[l] for l in range(layers)]
        columns, first = [], 0
        for item in lists:
            columns.append(pl.ds(first, item.buf.shape[3]))
            first += item.buf.shape[3]
        spread = [PlaneExchange(at, R.spread, R.spread_in[i], R.spread_send.at[i], R.spread_recv.at[i], columns[i])
                  for i in range(len(lists))]

        def arrive(i):
            spread[i].wait()
            lists[i].put(spread[i].rows(wrows).astype(BF))

        def regroup():
            join = lambda *parts: jnp.concatenate(parts, axis=1)
            part_width = quarter // nz
            for l in range(layers):
                w = R.qkv_mine[l].astype(F32)
                for g in range(4):
                    q, k, v = [w[:, part * 4 * group + group * g : part * 4 * group + group * g + group] for part in range(3)]
                    beside = jnp.zeros(q.shape, F32) if l else R.small_mine[...].astype(F32)
                    at_l = 384 * l
                    R.spread[2 * g, 0:wrows, at_l : at_l + 384] = join(k[:, :128], v[:, :128], k[:, 128:], v[:, 128:]).astype(BF)
                    R.spread[2 * g + 1, 0:wrows, at_l : at_l + 384] = join(q, beside).astype(BF)
            for l in range(layers):
                w = R.gu_mine[l].astype(F32)
                lo = 384 * layers + quarter * l
                for g in range(4):
                    for side in range(2):
                        firsts = [((side * nz + zz) * 4 + g) * part_width for zz in range(nz)]
                        R.spread[2 * g + side, 0:wrows, lo : lo + quarter] = join(*[w[:, i : i + part_width] for i in firsts]).astype(BF)

        regroup()
        for l in range(layers):
            down[l].put(R.down_mine[l])
        arrived()
        down[0].start()
        to_holder = remote(R.ow_mine, R.ow_in, R.ow_send, R.ow_recv, at.holder)
        spread[0].start()
    else:
        arrived()
        qkv_w, gu_w, down_w, out_w = R.qkv_given, R.gu_given, R.down_given, R.out_given

    R.xr_now[0][at.g] = R.x0[...]
    gather_x[0].start()
    if host:
        spread[layers].start()

        @pl.when(at.moves)
        def _():
            to_holder.start()

        @pl.when(jnp.logical_not(at.moves))
        def _():
            R.ow_in[...] = R.ow_mine[...]
        arrive(0)
        qkv[0].start()

        @pl.when(at.moves)
        def _():
            to_holder.wait_recv()
        ow.put(R.ow_in[...])
        ow.start()

    def columns(b):
        R.kaug_now[b // 2, b % 2] = key_columns(at, R.slopes, R.seg, b // 2, b % 2, tokens)

    def columns_and_serve(zz):
        columns(2 * zz)
        columns(2 * zz + 1)
        if host:
            @pl.when(zz > 0)
            def _():
                qkv[0].serve(zz)
    loop(0, nz, columns_and_serve)
    save(R.kaug_now, R.kaug)
    R.inside[...] = segment_columns(at, R.seg, rows)

    def small(l, t):
        return R.small[8 * l + t : 8 * l + t + 1, :]

    def of(buf, half):
        v = buf[pl.ds(2 * half, 2)]
        return v.reshape(half_rows, v.shape[2])

    def half_at(half):
        return pl.ds(pl.multiple_of(half * half_rows, half_rows), half_rows)

    def put_part(half, value):
        part[pl.ds(2 * half, 2)] = value.reshape(2, tokens, value.shape[1])

    def of_group(row):
        value = jnp.zeros((1, group), F32)
        for g in range(4):
            value = jnp.where(at.g == g, row[:, group * g : group * g + group], value)
        return value

    if host:
        qkv[0].collect()
    R.small[...] = side_weight(qkv_w[0], 1, 128, 256).astype(F32).T[64 : 64 + 8 * layers, :]
    R.state[...] = R.x0[...].astype(F32)
    gather_x[0].wait_near()
    gather_x[0].wait_far()

    for l in range(layers):
        last = l == layers - 1
        x_all = R.xr_now[l][...].reshape(rows, -1)
        save(R.xr_now[l], R.xr[l])
        qb, vb = of_group(small(l, 2)), of_group(small(l, 3))
        none = jnp.zeros((1, 128), F32)
        kv_bias = jnp.concatenate([none, vb[:, :128], none[:, :64], vb[:, 128:192]], axis=1)
        if l:
            pl.semaphore_wait(R.kv_free, at.neighbours())
        kv.put((dot(x_all, side_weight(qkv_w[l], 0)) + kv_bias).astype(BF))
        kv.start()
        if host and not last:
            spread[l + 1].start()
            spread[layers + l + 1].start()
        R.q[...] = (dot(x_all, side_weight(qkv_w[l], 1, 0, group)) + qb).astype(BF)
        for side in range(2):
            for h in range(3):
                R.q_op[side, h] = query_operand(at, R.q, R.inside, R.slopes, side, h, tokens)

        def behind(d, l=l):
            if host:
                if l == 0:
                    ow.serve(d)

                @pl.when(d == min(2, nz - 1))
                def _():
                    arrive(layers + l)
                    gu[l].start()

        def later(p, l=l):
            if host:
                for step in range(p, nz if p == 3 else p + 1):
                    gu[l].serve(step)
                    if l == 0:
                        down[l].serve(step)

        def ahead(p, l=l):
            if host and l < layers - 1:
                if p == 0:
                    arrive(l + 1)
                    qkv[l + 1].start()
                    down[l + 1].start()
                for step in range(p, nz if p == 3 else p + 1):
                    if step:
                        qkv[l + 1].serve(step)
                        down[l + 1].serve(step)
        attention(at, kv, R.q_op, R.kaug_now, R.m, R.acc, behind)
        attention_end(R.m, R.acc, R.ctx_now[l], R.ctxf_now[l])
        kv_saved = save(kv.buf, R.kv[l])
        save(R.ctx_now[l], R.ctx[l])
        save(R.ctxf_now[l], R.ctxf[l])
        if l == 0 and host:
            ow.collect()
            step = group // (2 * nz)
            for i in range(layers):
                for b in range(2 * nz):
                    R.ow_wide[...] = ow.buf[b // 2, b % 2].astype(F32)
                    R.ow_flat[step * b : step * b + step, :] = R.ow_wide[step * i : step * i + step, :]
                R.out_now[i][...] = R.ow_flat[...].astype(BF)
                save(R.out_now[i], R.out_w[i])
        if l:
            square_sum.finish()
        for number, half in enumerate((1 - at.x, at.x)):
            put_part(half, dot(R.ctx_now[l][half_at(half), :], out_w[l][...]))
            if number == 0:
                square_sum.send_far()
            else:
                square_sum.send_near()
        later(1)
        square_sum.relay()
        kv.finish()
        for side in range(2):
            for h in range(3):
                R.qb_now[l][side, h] = query_operand(at, R.q, R.inside, R.slopes, side, h, tokens, R.m[h])
        save(R.qb_now[l], R.qb[l])
        later(2)
        wait_saved(kv_saved)
        if not last:
            at.signal_neighbours(R.kv_free)
        R.sum1_now[l][...] = R.state[...] + (square_sum.total() + small(l, 4))
        save(R.sum1_now[l], R.sum1[l])
        y = layer_norm(R.sum1_now[l][...], small(l, 0), small(l, 5))
        R.yr_now[l][at.g] = y.astype(BF)
        gather_y[l].start()
        R.state[...] = y
        later(3)
        ahead(0)
        gather_y[l].wait_near()
        if host:
            gu[l].collect()
            down[l].collect()
        if l:
            wait_saved(mixed_saved)
        square_sum.finish()
        for number, half in enumerate((at.x, 1 - at.x)):
            if number == 1:
                gather_y[l].wait_far()
                ahead(1)
            here = half_at(half)
            y_half = of(R.yr_now[l], half)
            for col in range(0, quarter, 256):
                gate = dot(y_half, side_weight(gu_w[l], 0, col, col + 256))
                up = dot(y_half, side_weight(gu_w[l], 1, col, col + 256))
                R.mixed_now[here, col : col + 256] = gate
                R.mixed_now[here, quarter + col : quarter + col + 256] = up
                R.hid[:, col : col + 256] = (gate * normal_cdf(gate) * up).astype(BF)
            put_part(half, dot(R.hid[...], flat_weight(down_w[l])))
            if number == 0:
                square_sum.send_near()
            else:
                square_sum.send_far()
        mixed_saved = save(R.mixed_now, R.mixed[l])
        save(R.yr_now[l], R.yr[l])
        if host:
            save(qkv[l].buf, R.qkv_w[l])
            save(gu[l].buf, R.gu_w[l])
            save(down[l].buf, R.down_w[l])
        square_sum.relay()
        ahead(2)
        R.sum2_now[l][...] = R.state[...] + (square_sum.total() + small(l, 6))
        save(R.sum2_now[l], R.sum2[l])
        state = layer_norm(R.sum2_now[l][...], small(l, 1), small(l, 7))
        R.state[...] = state
        if last:
            R.output[...] = state.astype(BF)
        else:
            R.xr_now[l + 1][at.g] = state.astype(BF)
            gather_x[l + 1].start()
            gather_x[l + 1].wait_near()
            ahead(3)
            gather_x[l + 1].wait_far()
            if host:
                qkv[l + 1].collect()
    for l in range(layers):
        gather_x[l].finish()
        gather_y[l].finish()
    square_sum.finish()
    if host:
        for items in (qkv, gu, down):
            for item in items:
                item.finish()
        ow.finish()
        for item in spread:
            item.finish()

        @pl.when(at.moves)
        def _():
            to_holder.wait_send()
    for number, copy in enumerate(saves):
        if number not in waited:
            copy.wait()


def fwd(x0, slopes, seg, weights, layers, host):
    nz = seg.shape[0] // 8
    tokens, width = x0.shape
    rows = 4 * tokens
    group = width // 4
    each = range(layers)
    quarter = weights.gu_mine.shape[2] // 8 if host else weights.gu_given[0].shape[3]
    r = width // nz
    keep_rows = lambda: [keep(4, tokens, width) for _ in each]
    keep_wide = lambda: [keep(tokens, width, dtype=F32) for _ in each]
    scratch = dict(
        xr_now=keep_rows(), x_send=copies(layers, 6), x_recv=copies(layers, 6),
        yr_now=keep_rows(), y_send=copies(layers, 6), y_recv=copies(layers, 6),
        part=keep(4, tokens, width, dtype=F32), state=keep(tokens, width, dtype=F32), **square_sum_items(tokens, width),
        kv_now=block_gather_item(nz, rows, 384, parts=2), kv_free=pltpu.SemaphoreType.REGULAR, saved=copies(16 * layers),
        kaug_now=keep(nz, 2, rows, 128), inside=keep(rows, 128, dtype=F32),
        q=keep(rows, group), q_op=keep(2, 3, rows, 128),
        m=keep(3, rows, 128, dtype=F32), acc=keep(3, rows, 128, dtype=F32),
        ctx_now=[keep(rows, group) for _ in each], ctxf_now=[keep(rows, group, dtype=F32) for _ in each],
        qb_now=[keep(2, 3, rows, 128) for _ in each], sum1_now=keep_wide(), sum2_now=keep_wide(),
        mixed_now=keep(rows, 2 * quarter, dtype=F32), hid=keep(2 * tokens, quarter))
    far_out = dict(
        xr=[shape(4, tokens, width) for _ in each], yr=[shape(4, tokens, width) for _ in each],
        kv=[shape(nz, 2, rows, 384) for _ in each], ctx=[shape(rows, group) for _ in each],
        ctxf=[shape(rows, group, dtype=F32) for _ in each], qb=[shape(2, 3, rows, 128) for _ in each],
        sum1=[shape(tokens, width, dtype=F32) for _ in each], sum2=[shape(tokens, width, dtype=F32) for _ in each],
        mixed=[shape(rows, 2 * quarter, dtype=F32) for _ in each], kaug=shape(nz, 2, rows, 128))
    near = dict(x0=x0, seg=seg, **vars(weights))
    if host:
        gathered = lambda *dims: [shape(nz, 2, *dims) for _ in each]
        items = lambda *dims: [block_gather_item(nz, *dims, parts=2) for _ in each]
        rd = weights.down_mine.shape[1]
        padded = 32
        far_out.update(qkv_w=gathered(r, 384), gu_w=gathered(r, quarter), down_w=gathered(rd, width),
                       out_w=[shape(group, width) for _ in each])
        scratch.update(
            qkv_now=items(r, 384), gu_now=items(r, quarter), down_now=items(rd, width),
            spread=keep(8, padded, layers * (384 + quarter)), spread_in=[keep(8, padded, 384) for _ in each] + [keep(8, padded, quarter) for _ in each],
            spread_send=copies(2 * layers, 8), spread_recv=copies(2 * layers, 8),
            ow_in=keep(*weights.ow_mine.shape), ow_send=pltpu.SemaphoreType.DMA, ow_recv=pltpu.SemaphoreType.DMA,
            ow_now=block_gather_item(nz, *weights.ow_mine.shape), out_now=[keep(group, width) for _ in each],
            ow_wide=keep(*weights.ow_mine.shape, dtype=F32), ow_flat=keep(group, width, dtype=F32))
    out = dict(output=shape(tokens, width), small=shape(8 * layers, width, dtype=F32))
    done = call(functools.partial(fwd_kernel, nz, layers, host), "forward", 0, near=near, table=dict(slopes=slopes),
                out=out, far_out=far_out, scratch=scratch)
    if not host:
        done.qkv_w, done.gu_w, done.down_w, done.out_w = weights.qkv_given, weights.gu_given, weights.down_given, weights.out_given
    done.down_w = [w.reshape(quarter, width) for w in done.down_w]
    done.xr = [v.reshape(rows, width) for v in done.xr]
    done.yr = [v.reshape(rows, width) for v in done.yr]
    return done


def attn_back(at, R, l, top, begin, behind, at_end):
    nz, rows = at.nz, R.kvbuf.shape[1]
    q_ref, do_ref, dqacc = R.qb_now, R.do, R.dqacc
    dkv = BlockSum(at, R.dkv)

    def target(i):
        right = nz - 1 - at.z
        from_right = jnp.where(i < right, nz - 1 - i, i - right)
        from_left = jnp.where(i < at.z, i, nz - 1 - (i - at.z))
        return jnp.where(i == nz - 1, at.z, jnp.where(at.z < nz // 2, from_right, from_left))

    class Load:
        def __init__(self, t, slot):
            cc = at.oc if slot == 0 else at.c
            self.copies = [pltpu.make_async_copy(source.at[t, cc], target.at[slot], R.kvsem.at[i, slot])
                           for i, (source, target) in enumerate(((R.kv[l], R.kvbuf), (R.kaug, R.augbuf)))]

        def start(self):
            for copy in self.copies:
                copy.start()

        def wait(self):
            for copy in self.copies:
                copy.wait()

    load = Load

    dqacc[...] = jnp.zeros(dqacc.shape, F32)

    def compute(t, slot, same):
        cc = at.oc if slot == 0 else at.c
        side = (t > at.z).astype(jnp.int32)
        kv, aug = R.kvbuf.at[slot], R.augbuf[slot]
        dks, dvs = [], []
        for h in range(3):
            k, v = k_operand(kv, aug, h), v_operand(kv, h)
            if same:
                s = jnp.minimum(dot(k, q_ref[0, h], NT), dot(k, q_ref[1, h], NT))
            else:
                s = dot(k, q_ref[side, h], NT)
            p = jnp.exp(s)
            ds = (p * dot(v, do_ref[h], NT)).astype(BF)
            dvs.append(dot(p.astype(BF), do_ref[h]))
            dks.append(dot(ds, q_ref[side, h]))
            dqacc[h] += dot(ds, k, TN)
        low = in_half(0, rows)
        dkv.stage[t, cc, :, 0:128] = jnp.where(low, dks[0], dks[1]).astype(BF)
        dkv.stage[t, cc, :, 128:256] = jnp.where(low, dvs[0], dvs[1]).astype(BF)
        dkv.stage[t, cc, :, 256:384] = jnp.where(low, dks[2], dvs[2]).astype(BF)

    def far(t, same):
        load(t, 1).start()
        load(t, 0).wait()
        compute(t, 0, same)
        dkv.to_beside(t).start()

    load(target(0), 0).start()
    begin()
    if not top:
        pl.semaphore_wait(R.dkv.free, at.neighbours())

    def step(i):
        t = target(i)
        far(t, False)
        load(target(i + 1), 0).start()
        load(t, 1).wait()
        compute(t, 1, False)
        dkv.serve(i)
        behind(i)
    loop(0, nz - 1, step)
    far(at.z, True)
    load(at.z, 1).wait()
    compute(at.z, 1, True)
    at_end()
    dq = jnp.where(in_half(0, rows), dqacc[0], dqacc[1]) * 0.125
    R.dproj[:, 384:512] = dq.astype(BF)
    R.dproj[:, 512:576] = (dqacc[2][:, 0:64] * 0.125).astype(BF)
    R.dproj[:, 0:384] = dkv.total().astype(BF)
    if l > 0:
        at.signal_neighbours(R.dkv.free)
    dkv.finish()


def bwd_kernel(nz, layers, host, R):
    at = Place(nz)
    tokens = R.grad.shape[0]
    rows, half_rows = 4 * tokens, 2 * tokens
    quarter = R.hid.shape[1]
    width = R.grad.shape[1]
    mixed, yr, xr, gu_w, down_w, qkv_w, qb, ctx, ctxf, out_w = range(10)
    streams = ((R.mixed, R.mixed_now), (R.yr, R.yr_now), (R.xr, R.xr_now), (R.gu_w, R.gu_now), (R.down_w, R.down_now),
               (R.qkv_w, R.qkv_now), (R.qb, R.qb_now), (R.ctx, R.ctx_now), (R.ctxf, R.ctxf_now), (R.out_w, R.out_now))

    def load(which, l):
        return pltpu.make_async_copy(streams[which][0][l], streams[which][1], R.load.at[which])

    for which in range(10):
        load(which, layers - 1).start()
    at.enter(host)()
    R.dproj[:, 576:768] = jnp.zeros((rows, 192), BF)
    gather_df = SquareGather(at, R.df, R.df_send, R.df_recv)
    gather_da = SquareGather(at, R.da, R.da_send, R.da_recv)
    part = R.part
    square_sum = SquareSum(at, part, R.ss_stage, R.ss_inbox, R.ss_send, R.ss_recv)
    if host:
        gu_sum, dn_sum, qk_sum, ow_sum = [[BlockSum(at, item) for item in items] for items in (R.gu, R.dn, R.qk, R.ow)]
        sm_sum = BlockSum(at, R.sm)
        back = [[PlaneExchange(at, item.out, item.inbox, item.send, item.recv) for item in items] for items in R.back]
        wrows = R.out_grad.shape[1]
        moved = [remote(R.ow_out.at[l], R.ow_in.at[l], R.ow_send.at[l], R.ow_recv.at[l], at.chunk_device) for l in range(layers)]

    def small(l, t):
        return R.small[8 * l + t : 8 * l + t + 1, :]

    def put_small(l, t, value):
        R.tok_small[8 * l + t : 8 * l + t + 1, :] = value

    def of(buf, half):
        v = buf[pl.ds(2 * half, 2)]
        return v.reshape(half_rows, v.shape[2])

    def half_at(half):
        return pl.ds(pl.multiple_of(half * half_rows, half_rows), half_rows)

    def put_part(half, value):
        part[pl.ds(2 * half, 2)] = value.reshape(2, tokens, value.shape[1])

    def wgrad(left, right, stage, cc, lo, hi):
        for first in range(0, left.shape[1], 384):
            v = dot(left[:, first : first + 384], right[:, lo:hi], TN)
            if len(stage.shape) == 2:
                stage[first : first + 384, :] = v.astype(BF)
                continue
            step = stage.shape[2]
            for i in range(384 // step):
                b = first // step + i
                zz, side = (b // 2, b % 2) if cc is None else (b, cc)
                stage[zz, side] = v[step * i : step * i + step].astype(BF)

    def feed_forward_sums(l):
        return (gu_sum[l], dn_sum[l]) if host and l < layers else ()

    def attention_sums(l):
        return (qk_sum[l], ow_sum[l]) if host and l < layers else ()

    def serve(items, p):
        for item in items:
            item.serve(p)

    def emit(l):
        if not host or l == layers:
            return
        for item, exchange in zip((gu_sum[l], qk_sum[l]), back[l]):
            v = item.total()
            rest = jnp.zeros((exchange.out.shape[1] - wrows, v.shape[1]), F32)
            for k in range(8):
                exchange.out[k] = jnp.concatenate([v[wrows * k : wrows * k + wrows], rest], axis=0).astype(BF)
            exchange.start()
        R.dn_grad[l] = dn_sum[l].total()
        R.ow_out[l] = ow_sum[l].total()

        @pl.when(at.moves)
        def _():
            moved[l].start()

        @pl.when(jnp.logical_not(at.moves))
        def _():
            R.ow_in[l] = R.ow_out[l]

    def assemble(l):
        if not host:
            return
        def pieces(exchange):
            exchange.wait()
            piece = [exchange.inbox[k].astype(F32)[0:wrows] for k in range(8)]
            return lambda side, *spans: jnp.concatenate(
                [piece[2 * g + side][:, lo:hi] for g in range(4) for lo, hi in spans], axis=1)

        join = pieces(back[l][0])
        step = quarter // nz
        for side in range(2):
            for zz in range(nz):
                lo = (side * nz + zz) * 4 * step
                R.gu_grad[l, :, lo : lo + 4 * step] = join(side, (step * zz, step * zz + step))
        join = pieces(back[l][1])
        at_kv = 0
        R.qkv_grad[l, :, 0:width] = join(1, (at_kv, at_kv + 192))
        R.qkv_grad[l, :, width : 2 * width] = join(0, (at_kv, at_kv + 128), (at_kv + 256, at_kv + 320))
        R.qkv_grad[l, :, 2 * width : 3 * width] = join(0, (at_kv + 128, at_kv + 256), (at_kv + 320, at_kv + 384))

        @pl.when(at.moves)
        def _():
            moved[l].wait_recv()
        R.out_grad[l] = R.ow_in[l, 0:wrows, :]

    def small_copy(j):
        k = 4 * at.c + j
        return remote(R.sm_out, R.sm_in.at[at.g], R.sm_send.at[j], R.sm_recv.at[at.g], at.of_plane(k)), k != at.member

    def small_from(g):
        k = 2 * g + at.x
        return remote(R.sm_out, R.sm_in.at[g], R.sm_send.at[0], R.sm_recv.at[g], at.of_plane(k)), k != at.member

    R.g[...] = R.grad[...].astype(F32)
    for l in reversed(range(layers)):
        top = l == layers - 1
        e2, d_gain, d_shift = norm_back(R.g[...], R.sum2[l][...], small(l, 1))
        put_small(l, 1, d_gain)
        put_small(l, 5, d_shift)
        low = e2.astype(BF)
        put_small(l, 4, jnp.sum(low.astype(F32), axis=0, keepdims=True))
        if not top:
            square_sum.finish()
        R.df[at.g] = low
        gather_df.start()
        R.e2[...] = e2
        for which in range(10):
            load(which, l).wait()
        serve(feed_forward_sums(l + 1), 1)
        gather_df.wait_near()
        for number, half in enumerate((at.x, 1 - at.x)):
            if number == 1:
                gather_df.wait_far()
                serve(attention_sums(l + 1), 1)
            here = half_at(half)
            dhid_all = dot(of(R.df, half), R.down_now[...], NT)
            for col in range(0, quarter, 256):
                dhid = dhid_all[:, col : col + 256]
                gate = R.mixed_now[here, col : col + 256]
                up = R.mixed_now[here, quarter + col : quarter + col + 256]
                cdf = normal_cdf(gate)
                act = gate * cdf
                R.hid[here, col : col + 256] = (act * up).astype(BF)
                R.dgu[here, col : col + 256] = (dhid * up * (cdf + gate * normal_pdf(gate))).astype(BF)
                R.dgu[here, quarter + col : quarter + col + 256] = (dhid * act).astype(BF)
            put_part(half, dot(R.dgu[here, :quarter], side_weight(R.gu_now, 0), NT)
                     + dot(R.dgu[here, quarter:], side_weight(R.gu_now, 1), NT))
            if number == 0:
                square_sum.send_near()
            else:
                square_sum.send_far()
        wgrad(R.hid, R.df[...].reshape(rows, width), R.dn[l].stage, None, 0, width)
        square_sum.relay()
        serve(feed_forward_sums(l + 1), 2)
        for p in range(3, nz - 1):
            serve(feed_forward_sums(l + 1), p)
        dy = R.e2[...] + square_sum.total()
        e1, d_gain, d_shift = norm_back(dy, R.sum1[l][...], small(l, 0))
        put_small(l, 0, d_gain)
        put_small(l, 3, d_shift)
        low = e1.astype(BF)
        put_small(l, 2, jnp.sum(low.astype(F32), axis=0, keepdims=True))
        R.da[at.g] = low
        gather_da.start()
        R.e1[...] = e1
        for cc in range(2):
            wgrad(R.yr_now, R.dgu, R.gu[l].stage, cc, quarter * cc, quarter * cc + quarter)
        gather_da.wait_near()
        gather_da.wait_far()
        for item in feed_forward_sums(l):
            item.start()
        if l > 0:
            for which in (mixed, yr, gu_w, down_w):
                load(which, l - 1).start()
        da_all = R.da[...].reshape(rows, width)
        dctx = dot(da_all, R.out_now[...], NT).astype(BF)
        heads_out = R.ctxf_now
        wide = dctx.astype(F32)
        first_two = wide[:, :128]
        third = jnp.concatenate([jnp.zeros((rows, 64), F32), wide[:, 128:192]], axis=1)
        prod = first_two * heads_out[:, :128]
        low_half = in_half(0, rows)
        deltas = [
            jnp.sum(jnp.where(low_half, prod, 0.0), axis=1, keepdims=True),
            jnp.sum(jnp.where(low_half, 0.0, prod), axis=1, keepdims=True),
            jnp.sum(wide[:, 128:192] * heads_out[:, 128:192], axis=1, keepdims=True),
        ]
        for h in range(3):
            half = V_AT[h][1]
            base = jnp.where(in_half(half, rows), first_two if h < 2 else third, 0.0)
            R.do[h] = with_lanes(base, 0 if half else 64, split3(-deltas[h])).astype(BF)

        def begin(l=l):
            serve(attention_sums(l + 1), 2)
            for p in range(3, nz - 1):
                serve(attention_sums(l + 1), p)

        def out_grad(l=l):
            d_out = dot(R.ctx_now[...], R.da[...].reshape(rows, width), TN)
            if host:
                step = d_out.shape[0] // (2 * nz)
                for b in range(2 * nz):
                    R.ow[l].stage[b // 2, b % 2] = jnp.concatenate(
                        [d_out[step * b : step * b + step], jnp.zeros((OW_ROWS - step, width), F32)]).astype(BF)
            else:
                R.ow[l].stage[...] = d_out.astype(BF)

        def behind(i, l=l):
            pl.when(i == 0)(out_grad)
            if l < layers - 1:
                @pl.when(i == min(1, nz - 2))
                def _():
                    emit(l + 1)

                @pl.when(i == nz - 2)
                def _():
                    assemble(l + 1)

        def at_end(l=l):
            serve(feed_forward_sums(l), 0)
        attn_back(at, R, l, top, begin, behind, at_end)
        dproj = R.dproj
        gather_df.finish()
        gather_da.finish()
        square_sum.finish()
        for number, half in enumerate((1 - at.x, at.x)):
            put_part(half, dot(dproj[half_at(half), :384], side_weight(R.qkv_now, 0), NT)
                     + dot(dproj[half_at(half), 384:], side_weight(R.qkv_now, 1), NT))
            if number == 0:
                square_sum.send_far()
            else:
                square_sum.send_near()
        square_sum.relay()
        bias_sum = jnp.sum(dproj[...].astype(F32), axis=0, keepdims=True)
        for t, row in ((6, bias_sum[:, 384:576]), (7, jnp.concatenate([bias_sum[:, 128:256], bias_sum[:, 320:384]], axis=1))):
            put_small(l, t, jnp.concatenate([jnp.where(at.g == g, row, 0.0) for g in range(4)], axis=1))
        for cc in range(2):
            wgrad(R.xr_now, dproj, R.qk[l].stage, cc, 384 * cc, 384 * cc + 384)
        for item in attention_sums(l):
            item.start()
        serve(attention_sums(l), 0)
        if l > 0:
            for which in (xr, qkv_w, qb, ctx, ctxf, out_w):
                load(which, l - 1).start()
        R.g[...] = R.e1[...] + square_sum.total()
    R.grad_in[...] = R.g[...]
    square_sum.finish()
    if host:
        for b in range(2 * nz):
            step = width // (2 * nz)
            sm_sum.stage[b // 2, b % 2, :, 0:step] = R.tok_small[:, step * b : step * b + step]
        sm_sum.start()
        last = feed_forward_sums(0) + attention_sums(0) + (sm_sum,)
        sm_sum.serve(0)
        for p in range(1, nz - 1):
            serve(last, p)
        R.sm_out[...] = sm_sum.total()
        for j in range(4):
            copy, away = small_copy(j)

            @pl.when(away)
            def _(copy=copy):
                copy.start()

            @pl.when(jnp.logical_not(away))
            def _():
                R.sm_in[at.g] = R.sm_out[...]
        emit(0)
        total = jnp.zeros(R.sm_out.shape, F32)
        for g in range(4):
            copy, away = small_from(g)

            @pl.when(away)
            def _(copy=copy):
                copy.wait_recv()
            total = total + R.sm_in[g]
        mine = jnp.zeros((8 * layers, wrows), F32)
        for k in range(4):
            mine = jnp.where(2 * at.y + at.c == k, total[:, wrows * k : wrows * k + wrows], mine)
        for l in range(layers):
            R.gains_grad[l] = mine[8 * l : 8 * l + 2]
            R.biases_grad[l] = jnp.concatenate([mine[8 * l + 6 : 8 * l + 8], mine[8 * l + 2 : 8 * l + 6]], axis=0)
        assemble(0)
        for l in range(layers):
            for item in feed_forward_sums(l) + attention_sums(l) + tuple(back[l]):
                item.finish()

            @pl.when(at.moves)
            def _(l=l):
                moved[l].wait_send()
        for j in range(4):
            copy, away = small_copy(j)

            @pl.when(away)
            def _(copy=copy):
                copy.wait_send()
        sm_sum.finish()


def bwd(grad, saved, host):
    layers = len(saved.qkv_w)
    nz, _, rows, _ = saved.kaug.shape
    tokens, width = grad.shape
    quarter, group = width, width // 4
    quarter = saved.down_w[0].shape[0]
    r, rd = width // nz, quarter // (2 * nz)
    each = range(layers)
    out = dict(grad_in=shape(tokens, width, dtype=F32))
    scratch = {}
    if host:
        wrows, padded = width // (8 * nz), 32
        out.update(
            qkv_grad=shape(layers, wrows, 3 * width, dtype=F32), out_grad=shape(layers, wrows, width, dtype=F32),
            gu_grad=shape(layers, wrows, 8 * quarter, dtype=F32), dn_grad=shape(layers, rd, width, dtype=F32),
            gains_grad=shape(layers, 2, wrows, dtype=F32), biases_grad=shape(layers, 6, wrows, dtype=F32))
        scratch.update(
            back=[[dict(out=keep(8, padded, cols), inbox=keep(8, padded, cols), send=copies(8), recv=copies(8))
                   for cols in (quarter, 384)] for _ in each],
            ow_out=keep(layers, OW_ROWS, width, dtype=F32), ow_in=keep(layers, OW_ROWS, width, dtype=F32),
            ow_send=copies(layers), ow_recv=copies(layers),
            sm_out=keep(8 * layers, 128, dtype=F32), sm_in=keep(4, 8 * layers, 128, dtype=F32), sm_send=copies(4), sm_recv=copies(4))
        scratch.update(
            gu=[block_sum_item(nz, r, quarter, parts=2) for _ in each], dn=[block_sum_item(nz, rd, width, parts=2) for _ in each],
            qk=[block_sum_item(nz, r, 384, parts=2) for _ in each], ow=[block_sum_item(nz, OW_ROWS, width) for _ in each],
            sm=block_sum_item(nz, 8 * layers, 128, dtype=F32), tok_small=keep(8 * layers, width, dtype=F32))
    else:
        out.update(
            gu=[dict(stage=shape(nz, 2, r, quarter)) for _ in each], dn=[dict(stage=shape(quarter, width)) for _ in each],
            qk=[dict(stage=shape(nz, 2, r, 384)) for _ in each], ow=[dict(stage=shape(group, width)) for _ in each],
            tok_small=shape(8 * layers, width, dtype=F32))
    like = lambda arrays: keep(*arrays[0].shape, dtype=arrays[0].dtype)
    scratch.update(
        mixed_now=like(saved.mixed), yr_now=like(saved.yr), xr_now=like(saved.xr), gu_now=like(saved.gu_w),
        down_now=like(saved.down_w), qkv_now=like(saved.qkv_w), qb_now=like(saved.qb),
        ctx_now=like(saved.ctx), ctxf_now=like(saved.ctxf), out_now=like(saved.out_w), load=copies(10), kvbuf=keep(2, rows, 384), augbuf=keep(2, rows, 128), kvsem=copies(2, 2),
        df=keep(4, tokens, width), df_send=copies(6), df_recv=copies(6),
        da=keep(4, tokens, width), da_send=copies(6), da_recv=copies(6),
        part=keep(4, tokens, width, dtype=F32), **square_sum_items(tokens, width),
        g=keep(tokens, width, dtype=F32), e1=keep(tokens, width, dtype=F32), e2=keep(tokens, width, dtype=F32),
        hid=keep(rows, quarter), dgu=keep(rows, 2 * quarter), do=keep(3, rows, 128),
        dqacc=keep(3, rows, 128, dtype=F32), dproj=keep(rows, 768),
        dkv=dict(block_sum_item(nz, rows, 384, parts=2), free=pltpu.SemaphoreType.REGULAR))
    near = dict(grad=grad, small=saved.small, sum1=saved.sum1, sum2=saved.sum2)
    far = dict(mixed=saved.mixed, yr=saved.yr, xr=saved.xr, gu_w=saved.gu_w, down_w=saved.down_w, kv=saved.kv, kaug=saved.kaug,
               qkv_w=saved.qkv_w, qb=saved.qb, ctx=saved.ctx, ctxf=saved.ctxf, out_w=saved.out_w)
    return call(functools.partial(bwd_kernel, nz, layers, host), "backward", 1, near=near, far=far, out=out, scratch=scratch)


def shards(hidden_in, out_grad, segment_ids, alibi_slopes, qkv_weight, out_weight, gate_up_weight, down_weight, gains, biases):
    nz = lax.axis_size("z")
    nb = 2 * nz
    square, everyone, blocks = ("x", "y", "c"), ("z", "x", "y", "c"), ("z", "c")
    z, c = lax.axis_index("z"), lax.axis_index("c")
    tokens, width = hidden_in.shape
    layers, wrows = qkv_weight.shape[:2]
    ff = gate_up_weight.shape[2] // 2
    group, quarter = width // 4, ff // 4
    host = (width // nz) % 16 == 0 and down_weight.shape[1] % 16 == 0

    def to_groups(w):
        w = w.reshape(wrows, 3, 4, 3, 64)
        q, k, v = w[:, 0], w[:, 1], w[:, 2]
        kv = jnp.stack([k[:, :, 0], k[:, :, 1], v[:, :, 0], v[:, :, 1], k[:, :, 2], v[:, :, 2]], axis=2)
        return kv.reshape(wrows, 4, 384), q.reshape(wrows, 4, group)

    def from_groups(kv, q):
        kv, q = kv.reshape(4, wrows, 6, 64), q.reshape(4, wrows, 3, 64)
        k = jnp.stack([kv[:, :, 0], kv[:, :, 1], kv[:, :, 4]], axis=2)
        v = jnp.stack([kv[:, :, 2], kv[:, :, 3], kv[:, :, 5]], axis=2)
        return jnp.stack([q, k, v]).transpose(2, 0, 1, 3, 4).reshape(wrows, 3 * width)

    places = [(8 * zz + 2 * g + cc, g * nb + 2 * zz + cc) for zz in range(nz) for g in range(4) for cc in range(2)]
    gu0 = 384 * layers

    def gathered_outside():
        beside = jnp.broadcast_to(small[:, None], (wrows, 4, 192))
        nothing = jnp.zeros((wrows, 4, 192), BF)
        gu = gate_up_weight.reshape(layers, wrows, 2, nz, 4, quarter // nz).transpose(0, 1, 4, 2, 3, 5)
        gu = gu.reshape(layers, wrows, 4, 2, quarter)
        sides = [[], []]
        for l in range(layers):
            kv, q = to_groups(qkv_weight[l])
            sides[0].append(kv)
            sides[1] += [q, nothing if l else beside]
        for l in range(layers):
            for side in range(2):
                sides[side].append(gu[l, :, :, side])
        both = jnp.stack([jnp.concatenate(side, axis=2) for side in sides], axis=2).reshape(wrows, 8, -1)
        spread = lax.all_to_all(both, square, split_axis=1, concat_axis=0, tiled=True).reshape(8 * wrows, -1)
        ow_own = lax.ppermute(out_weight, everyone, [(chunk, device) for device, chunk in places])
        whole = lambda v: lax.all_gather(v, blocks, axis=0).reshape(nz, 2, *v.shape)
        flat = lambda v: lax.all_gather(v, blocks, axis=0, tiled=True)
        return types.SimpleNamespace(
            qkv_given=[whole(spread[:, 384 * l : 384 * l + 384]) for l in range(layers)],
            gu_given=[whole(spread[:, gu0 + quarter * l : gu0 + quarter * l + quarter]) for l in range(layers)],
            down_given=[flat(down_weight[l]) for l in range(layers)], out_given=[flat(ow_own[l]) for l in range(layers)])

    small = jnp.concatenate([gains, biases], axis=1).transpose(0, 2, 1)
    small = jnp.concatenate([small[l] for l in range(layers)], axis=1)
    small = jnp.pad(small, ((0, 0), (0, 192 - small.shape[1])))
    if host:
        weights = types.SimpleNamespace(
            qkv_mine=qkv_weight, gu_mine=gate_up_weight, down_mine=down_weight, small_mine=small,
            ow_mine=out_weight.reshape(layers * wrows, width))
    else:
        weights = gathered_outside()
    seg = segment_ids.reshape(8 * nz, tokens)
    saved = fwd(hidden_in, alibi_slopes, seg, weights, layers, host)
    done = bwd(out_grad, saved, host)
    if host:
        return (saved.output, done.grad_in, done.qkv_grad, done.out_grad, done.gu_grad, done.dn_grad, done.gains_grad,
                done.biases_grad)
    step = width // nb
    blocks_sum = lambda v: lax.psum_scatter(v, blocks, scatter_dimension=0, tiled=True)
    done.gu_sum = [blocks_sum(item.stage.reshape(nb, -1, quarter))[0] for item in done.gu]
    done.qk_sum = [blocks_sum(item.stage.reshape(nb, -1, 384))[0] for item in done.qk]
    done.dn_sum = [blocks_sum(item.stage) for item in done.dn]
    done.ow_sum = [blocks_sum(item.stage) for item in done.ow]
    sm = lax.psum_scatter(done.tok_small.reshape(-1, nb, step), blocks, scatter_dimension=1, tiled=True)[:, 0]
    sm = sm.T.reshape(4, wrows, 8 * layers)
    high = lax.reduce_precision(sm, 8, 7)
    sm = jnp.concatenate([high, sm - high], axis=2).astype(BF)
    sm = lax.dynamic_update_slice_in_dim(jnp.zeros((8, wrows, 16 * layers), BF), sm, 4 * c, 0)
    rows_of = lambda v: v.reshape(8, wrows, -1)
    back = jnp.concatenate([rows_of(v) for v in done.qk_sum + done.gu_sum] + [sm], axis=2)
    back = lax.all_to_all(back, square, split_axis=0, concat_axis=0, tiled=True)
    sides = back.astype(F32).reshape(4, 2, wrows, -1)
    qkv_grad = jnp.stack([from_groups(sides[:, 0, :, 384 * l : 384 * l + 384], sides[:, 1, :, 384 * l : 384 * l + group])
                          for l in range(layers)])
    gu_grad = jnp.stack([sides[:, :, :, gu0 + quarter * l : gu0 + quarter * l + quarter] for l in range(layers)])
    gu_grad = gu_grad.reshape(layers, 4, 2, wrows, nz, quarter // nz).transpose(0, 3, 2, 4, 1, 5).reshape(layers, wrows, 2 * ff)
    sm = jnp.sum(sides[..., gu0 + quarter * layers :], axis=(0, 1))
    sm = (sm[:, : 8 * layers] + sm[:, 8 * layers :]).T.reshape(layers, 8, wrows)
    out_grad_w = lax.ppermute(jnp.stack(done.ow_sum)[:, :wrows].astype(F32), everyone, places)
    return (saved.output, done.grad_in, qkv_grad, out_grad_w, gu_grad, jnp.stack(done.dn_sum).astype(F32), sm[:, 0:2],
            jnp.concatenate([sm[:, 6:8], sm[:, 2:6]], axis=1))


def solution(mesh):
    nb, nh = mesh.devices.shape
    everyone = ("z", "x", "y", "c")
    tok, mid, last = P(everyone, None), P(None, everyone, None), P(None, None, everyone)
    return jax.shard_map(
        shards, mesh=Mesh(mesh.devices.reshape(nb // 2, 2, nh // 2, 2), everyone),
        in_specs=(tok, tok, P(), P(), mid, mid, mid, mid, last, last),
        out_specs=(tok, tok, mid, mid, mid, mid, last, last),
        check_vma=False,
    )
```
